32 devices in a mesh: dp: 16 (over z, y, core), ctx: 2 (over x).
Axes of the slice: x: 2, y: 2, z: 4, core: 2. Of those that a mesh axis runs over, the one named last changes fastest.
Arguments:
- tokens: bfloat16 [16384, 576], P(('dp', 'ctx')), may hold values from -6 to 6
- q_weight: bfloat16 [331776], P(('dp', 'ctx')), may hold values from -0.25 to 0.25
- k_weight: bfloat16 [110592], P(('dp', 'ctx')), may hold values from -0.25 to 0.25
- v_weight: bfloat16 [110592], P(('dp', 'ctx')), may hold values from -0.25 to 0.25
- o_weight: bfloat16 [331776], P(('dp', 'ctx')), may hold values from -3 to 3
- gate_weight: bfloat16 [884736], P(('dp', 'ctx')), may hold values from -0.25 to 0.25
- up_weight: bfloat16 [884736], P(('dp', 'ctx')), may hold values from -0.25 to 0.25
- down_weight: bfloat16 [884736], P(('dp', 'ctx')), may hold values from -0.15625 to 0.15625
- vectors: bfloat16 [2112], P(('dp', 'ctx')), may hold values from -1.2 to 1.25
- doc_lengths: int32 [16, 4], P('dp'), may hold values from 1 to 1024, as said below
- cotangent: bfloat16 [16384, 576], P(('dp', 'ctx')), may hold values from -6 to 6
Outputs:
- layer_out: bfloat16 [16384, 576], P(('dp', 'ctx'))
- input_grad: float32 [16384, 576], P(('dp', 'ctx'))
- q_weight_grad: float32 [331776], P(('dp', 'ctx'))
- k_weight_grad: float32 [110592], P(('dp', 'ctx'))
- v_weight_grad: float32 [110592], P(('dp', 'ctx'))
- o_weight_grad: float32 [331776], P(('dp', 'ctx'))
- gate_weight_grad: float32 [884736], P(('dp', 'ctx'))
- up_weight_grad: float32 [884736], P(('dp', 'ctx'))
- down_weight_grad: float32 [884736], P(('dp', 'ctx'))
- vectors_grad: float32 [2112], P(('dp', 'ctx'))
The draws below stay inside these ranges and needn't reach their ends.
Inputs may be any that keep to these rules, and one draw needn't show every extreme that they name: `doc_lengths`: each row holds 4 document lengths that sum to 1024.
All inputs are finite; a program needn't handle non-finite values.
Results may differ from the reference program's by a relative error of at most 0.013.
Values may be sent and summed in bfloat16 or wider, within the bound.
No kernel may reach another device: no remote copies, remote signals or barrier semaphores. Data moves between devices by JAX's collectives and lax.ppermute only.
A program may use at most 128 MiB of HBM per device.

```python
import jax
import jax.numpy as jnp
from jax import lax

D = 576
HEADS = 9
KV_HEADS = 3
HEAD_DIM = 64
FF = 1536
DOCS = 4
SEQ_LEN = 1024
TOK_DEV = 512
SEQS = 16
TOKENS = 16384
VEC_PAD = 2112


def draw_vectors(key, part):
    key = jax.random.fold_in(key, 11)
    kv_width = KV_HEADS * HEAD_DIM
    place = jnp.arange(VEC_PAD)
    noise = jnp.clip(jax.random.normal(jax.random.fold_in(key, 1), (VEC_PAD,), jnp.float32), -4.0, 4.0)
    spread = jax.random.uniform(jax.random.fold_in(key, 2), (VEC_PAD,), jnp.float32, -1.0, 1.0)
    bias_qk = place < D + kv_width
    bias_value = (place >= D + kv_width) & (place < D + 2 * kv_width)
    values = jnp.where(bias_qk, 0.3 * noise, jnp.where(bias_value, 0.1 * noise, 1.0 + 0.25 * spread))
    return values.astype(jnp.bfloat16)


def draw_doc_lengths(key, part):
    key = jax.random.fold_in(key, 5)
    head_len = jax.random.randint(jax.random.fold_in(key, 1), (SEQS, 1), 1, max(TOK_DEV // 2, 1) + 1)
    tail_len = jax.random.randint(jax.random.fold_in(key, 2), (SEQS, DOCS - 2), 1, max(TOK_DEV // (2 * (DOCS - 2)), 1) + 1)
    middle = SEQ_LEN - head_len - jnp.sum(tail_len, axis=1, keepdims=True)
    return jnp.concatenate([head_len, middle, tail_len], axis=1).astype(jnp.int32)


def levels(own_key, shape, split, least, high):
    level, own = 1.0, jax.random.fold_in(own_key, 6)
    for axis_at, shards_of in split:
        draws = jnp.exp(jax.random.uniform(jax.random.fold_in(own, axis_at), (shards_of,), jnp.float32, least / len(split), high / len(split)))
        level = level * jnp.repeat(draws, shape[axis_at] // shards_of).reshape([-1 if axis == axis_at else 1 for axis in range(len(shape))])
    return level


def scatter_about(key, shape, width, limit, pieces=(), kind=jnp.bfloat16):
    level = levels(key, shape, pieces, -0.22, 0.18) if pieces else 1.0
    values = jax.random.normal(key, shape, jnp.float32) * width * level
    return jnp.minimum(jnp.maximum(values, -limit), limit).astype(kind)


def setup_inputs(seed: int = 0) -> dict:
    splits = jax.random.split(jax.random.key(seed), 12)
    tokens = scatter_about(splits[0], (TOKENS, D), 1.0, 6.0, ((0, 32),))
    q_weight = scatter_about(splits[1], (D * D,), D ** -0.5, 0.25, ((0, 32),))
    k_weight = scatter_about(splits[2], (D * KV_HEADS * HEAD_DIM,), D ** -0.5, 0.25, ((0, 32),))
    v_weight = scatter_about(splits[3], (D * KV_HEADS * HEAD_DIM,), D ** -0.5, 0.25, ((0, 32),))
    o_weight = scatter_about(splits[4], (D * D,), (max(SEQ_LEN // 256, 1)) ** -0.5, 3.0, ((0, 32),))
    gate_weight = scatter_about(splits[5], (D * FF,), D ** -0.5, 0.25, ((0, 32),))
    up_weight = scatter_about(splits[6], (D * FF,), D ** -0.5, 0.25, ((0, 32),))
    down_weight = scatter_about(splits[7], (FF * D,), FF ** -0.5, 0.15625, ((0, 32),))
    vectors = draw_vectors(jax.random.fold_in(splits[11], 71), 0)
    doc_lengths = draw_doc_lengths(jax.random.fold_in(splits[11], 71), 0)
    cotangent = scatter_about(splits[10], (TOKENS, D), 1.0, 6.0, ((0, 32),))
    return dict(tokens=tokens, q_weight=q_weight, k_weight=k_weight, v_weight=v_weight, o_weight=o_weight, gate_weight=gate_weight, up_weight=up_weight, down_weight=down_weight, vectors=vectors, doc_lengths=doc_lengths, cotangent=cotangent)


EPS = 1e-06
THETA = 100000.0
NEG_FILL = -1e+30
HIGH = lax.Precision.HIGHEST

@jax.custom_vjp
def low(v):
    return lax.optimization_barrier(v.astype(jnp.bfloat16)).astype(jnp.float32)

@jax.custom_vjp
def low_back(v):
    return v

def low_keep(v):
    return (low(v), None)

def low_pass(kept, grad):
    return (grad,)

def back_keep(v):
    return (v, None)

def back_low(kept, grad):
    return (low(grad),)
low.defvjp(low_keep, low_pass)
low_back.defvjp(back_keep, back_low)

def product(left, right):
    return jnp.dot(left, right, precision=HIGH)

def rms_scale(values, gain):
    return values * lax.rsqrt(lax.optimization_barrier(jnp.mean(values * values, axis=-1, keepdims=True)) + EPS) * gain

def rotary(values, position):
    half = values.shape[-1] // 2
    freq = THETA ** (-jnp.arange(half, dtype=jnp.float32) * 2.0 / values.shape[-1])
    angle = position.astype(jnp.float32)[:, None] * freq[None, :]
    cosine = jnp.cos(angle)[:, None, :]
    sine = jnp.sin(angle)[:, None, :]
    first = values[..., :half]
    second = values[..., half:]
    return jnp.concatenate([first * cosine - second * sine, second * cosine + first * sine], axis=-1)

def doc_layout(lengths, count):
    lengths = lengths.astype(jnp.int32)
    ends = jnp.cumsum(lengths).astype(jnp.int32)
    place = jnp.arange(count, dtype=jnp.int32)
    segment = lax.optimization_barrier(jnp.sum((place[:, None] >= ends[None, :-1]).astype(jnp.int32), axis=1)).astype(jnp.int32)
    starts = (ends - lengths).astype(jnp.int32)
    picked = segment[:, None] == jnp.arange(lengths.shape[0], dtype=jnp.int32)[None, :]
    first = lax.optimization_barrier(jnp.sum(jnp.where(picked, starts[None, :], 0), axis=1)).astype(jnp.int32)
    return (segment, (place - first).astype(jnp.int32))

def layer(inputs, params, segment, position):
    w_query, w_key, w_value, w_out, w_gate, w_up, w_down, flat = params
    kv_width = KV_HEADS * HEAD_DIM
    bias_q = flat[:D]
    bias_k = flat[D:D + kv_width]
    bias_v = flat[D + kv_width:D + 2 * kv_width]
    gain_attn = flat[D + 2 * kv_width:2 * D + 2 * kv_width]
    gain_mlp = flat[2 * D + 2 * kv_width:3 * D + 2 * kv_width]
    length = inputs.shape[0]
    group_size = HEADS // KV_HEADS
    n_first = low(rms_scale(inputs, gain_attn))
    q_pre = low_back(product(n_first, w_query) + bias_q)
    k_pre = low_back(product(n_first, w_key) + bias_k)
    v_low = low_back(low(product(n_first, w_value) + bias_v))
    q_rot = low(rotary(q_pre.reshape(length, HEADS, HEAD_DIM), position)).reshape(length, KV_HEADS, group_size, HEAD_DIM)
    k_rot = low(rotary(k_pre.reshape(length, KV_HEADS, HEAD_DIM), position))
    values = v_low.reshape(length, KV_HEADS, HEAD_DIM)
    block_rows = min(512, length)
    key_rows = jnp.arange(length, dtype=jnp.int32)
    score_scale = HEAD_DIM ** (-0.5)

    def block(start):
        query_block = lax.dynamic_slice_in_dim(q_rot, start, block_rows, 0)
        seg_query = lax.dynamic_slice_in_dim(segment, start, block_rows, 0)
        row_query = start + jnp.arange(block_rows, dtype=jnp.int32)
        scores = low_back(jnp.einsum('qkgd,skd->kgqs', query_block, k_rot, precision=HIGH) * score_scale)
        allowed = (seg_query[:, None] == segment[None, :]) & (row_query[:, None] >= key_rows[None, :])
        masked = jnp.where(allowed[None, None], scores, NEG_FILL)
        top = lax.optimization_barrier(jnp.max(masked, axis=-1, keepdims=True))
        weights = jnp.exp(masked - top)
        prob = weights / lax.optimization_barrier(jnp.sum(weights, axis=-1, keepdims=True))
        return jnp.einsum('kgqs,skd->qkgd', low(prob), values, precision=HIGH)
    starts = jnp.arange(length // block_rows, dtype=jnp.int32) * block_rows
    outs = lax.map(jax.checkpoint(block), starts)
    attn = low_back(low(outs.reshape(length, D)))
    mid = inputs + low_back(product(attn, w_out))
    n_second = low(rms_scale(mid, gain_mlp))
    gate = low_back(product(n_second, w_gate))
    up_val = low_back(product(n_second, w_up))
    hidden = low(jax.nn.silu(gate) * up_val)
    return mid + product(hidden, w_down)

def reference(tokens, q_weight, k_weight, v_weight, o_weight, gate_weight, up_weight, down_weight, vectors, doc_lengths, cotangent):
    kv_width = KV_HEADS * HEAD_DIM
    params = (q_weight.astype(jnp.float32).reshape(D, D), k_weight.astype(jnp.float32).reshape(D, kv_width), v_weight.astype(jnp.float32).reshape(D, kv_width), o_weight.astype(jnp.float32).reshape(D, D), gate_weight.astype(jnp.float32).reshape(D, FF), up_weight.astype(jnp.float32).reshape(D, FF), down_weight.astype(jnp.float32).reshape(FF, D), vectors.astype(jnp.float32))
    seq_tokens = tokens.reshape(SEQS, SEQ_LEN, D)
    seq_cot = cotangent.reshape(SEQS, SEQ_LEN, D)
    zeros = jax.tree.map(jnp.zeros_like, params)

    def one_seq(carry, item):
        x_seq, cot_seq, lengths = item
        segment, position = doc_layout(lengths, SEQ_LEN)

        def forward(inputs, weights):
            return layer(inputs, weights, segment, position)
        result, pull = jax.vjp(forward, x_seq.astype(jnp.float32), params)
        grad_x, grad_params = pull(cot_seq.astype(jnp.float32))
        return (jax.tree.map(jnp.add, carry, grad_params), (result.astype(jnp.bfloat16), grad_x))
    grads, (results, grad_inputs) = lax.scan(one_seq, zeros, (seq_tokens, seq_cot, doc_lengths))
    return (results.reshape(TOKENS, D), grad_inputs.reshape(TOKENS, D), grads[0].reshape(-1), grads[1].reshape(-1), grads[2].reshape(-1), grads[3].reshape(-1), grads[4].reshape(-1), grads[5].reshape(-1), grads[6].reshape(-1), grads[7])
```

```python
import functools

import jax
import jax.numpy as jnp
from jax import lax
from jax.experimental import pallas as pl
from jax.experimental.pallas import tpu as pltpu
from jax.sharding import PartitionSpec as P

KV_HEADS = 3
HEAD_DIM = 64

EPS = 1e-06
THETA = 100000.0
NEG_FILL = -1e30
AXES = ("dp", "ctx")
BF = jnp.bfloat16
F32 = jnp.float32


def times(left, right):
    return jnp.dot(left, right, preferred_element_type=F32)


def inner_rows(left, right):
    return lax.dot_general(left, right, (((0,), (0,)), ((), ())), preferred_element_type=F32)


def times_back(left, right):
    return lax.dot_general(left, right, (((1,), (1,)), ((), ())), preferred_element_type=F32)


def norm_back(values, inv, gain, grad):
    scaled = grad * gain
    dot = jnp.mean(scaled * values, axis=-1, keepdims=True)
    grad_values = inv * scaled - values * (inv * inv * inv * dot)
    grad_gain = jnp.sum(grad * values * inv, axis=0)
    return grad_values, grad_gain


def turn(values, cosine, sine):
    half = values.shape[-1] // 2
    first = values[..., :half]
    second = values[..., half:]
    return jnp.concatenate(
        [first * cosine - second * sine, second * cosine + first * sine], axis=-1
    )


def doc_layout(lengths, count):
    ends = jnp.cumsum(lengths)
    place = jnp.arange(count, dtype=jnp.int32)
    segment = jnp.sum((place[:, None] >= ends[None, :-1]).astype(jnp.int32), axis=1)
    starts = ends - lengths
    picked = segment[:, None] == jnp.arange(lengths.shape[0], dtype=jnp.int32)[None, :]
    first = jnp.sum(jnp.where(picked, starts[None, :], 0), axis=1)
    return (segment, place - first)


def fill_bias(bias, seg_k, row_k, seg_q, row_q):
    allowed = (seg_k[...] == seg_q[...]) & (row_k[...] <= row_q[...])
    bias[...] = jnp.where(allowed, 0.0, NEG_FILL)


def key_range(full, total, short, rows, block, at, causal):
    start = 0 if full else total - short
    stop = total - rows + (at + 1) * block if causal else total
    return start, stop


def attn_fwd_kernel(
    heads, block, short, causal, flag, q_ref, kv_ref, seg_k, row_k, seg_q, row_q,
    out_ref, lse_ref, qs, ks, vts, bias, out_t,
):
    rows = q_ref.shape[0]
    total = kv_ref.shape[0]
    kv_width = KV_HEADS * HEAD_DIM
    group = heads // KV_HEADS
    fill_bias(bias, seg_k, row_k, seg_q, row_q)
    for h in range(heads):
        qs[h] = q_ref[:, h * HEAD_DIM : (h + 1) * HEAD_DIM] * BF(HEAD_DIM**-0.5)
    for g in range(KV_HEADS):
        ks[g] = kv_ref[:, g * HEAD_DIM : (g + 1) * HEAD_DIM]
    vts[...] = jnp.transpose(kv_ref[:, kv_width:].astype(F32)).astype(BF)

    def run(full):
        @pl.loop(0, KV_HEADS)
        def _(g):
            v_rows = pl.ds(pl.multiple_of(g * HEAD_DIM, HEAD_DIM), HEAD_DIM)
            for j in range(group):
                h = g * group + j
                for at in range(rows // block):
                    start, stop = key_range(full, total, short, rows, block, at, causal)
                    cols = slice(at * block, (at + 1) * block)
                    s = times_back(ks[g, start:stop], qs[h, cols])
                    s = s + bias[start:stop, cols]
                    top = jnp.max(s, axis=0, keepdims=True)
                    p = jnp.exp(s - top)
                    total_p = jnp.sum(p, axis=0, keepdims=True)
                    o = times(vts[v_rows, start:stop], p.astype(BF))
                    out_rows = pl.ds(pl.multiple_of(h * HEAD_DIM, HEAD_DIM), HEAD_DIM)
                    out_t[out_rows, cols] = o / total_p
                    lse_ref[h, :, cols] = top + jnp.log(total_p)

    pl.when(flag[0] != 0)(lambda: run(True))
    pl.when(flag[0] == 0)(lambda: run(False))
    out_ref[...] = jnp.transpose(out_t[...]).astype(BF)


def attn_bwd_kernel(
    heads, block, short, causal, flag, q_ref, kv_ref, do_ref, lse_ref, seg_k, row_k, seg_q, row_q,
    dq_ref, dkv_ref, qs, ks, vs, kts, dos, bias, dq_t, dk, dv,
):
    rows = q_ref.shape[0]
    total = kv_ref.shape[0]
    kv_width = KV_HEADS * HEAD_DIM
    group = heads // KV_HEADS
    fill_bias(bias, seg_k, row_k, seg_q, row_q)
    for h in range(heads):
        lanes = slice(h * HEAD_DIM, (h + 1) * HEAD_DIM)
        qs[h] = q_ref[:, lanes] * BF(HEAD_DIM**-0.5)
        dos[h] = do_ref[:, lanes]
    for g in range(KV_HEADS):
        ks[g] = kv_ref[:, g * HEAD_DIM : (g + 1) * HEAD_DIM]
        vs[g] = kv_ref[:, kv_width + g * HEAD_DIM : kv_width + (g + 1) * HEAD_DIM]
    kts[...] = jnp.transpose(kv_ref[:, :kv_width].astype(F32)).astype(BF)
    dk[...] = jnp.zeros_like(dk)
    dv[...] = jnp.zeros_like(dv)

    def run(full):
        @pl.loop(0, KV_HEADS)
        def _(g):
            k_rows = pl.ds(pl.multiple_of(g * HEAD_DIM, HEAD_DIM), HEAD_DIM)
            for j in range(group):
                h = g * group + j
                for at in range(rows // block):
                    start, stop = key_range(full, total, short, rows, block, at, causal)
                    cols = slice(at * block, (at + 1) * block)
                    q = qs[h, cols]
                    do = dos[h, cols]
                    s = times_back(ks[g, start:stop], q)
                    p = jnp.exp(s + bias[start:stop, cols] - lse_ref[h, :, cols])
                    dp = times_back(vs[g, start:stop], do)
                    t = p * dp
                    inner = jnp.sum(t, axis=0, keepdims=True)
                    ds = (t - p * inner).astype(BF)
                    dk[g, start:stop] += times(ds, q)
                    dv[g, start:stop] += times(p.astype(BF), do)
                    dq = times(kts[k_rows, start:stop], ds)
                    out_rows = pl.ds(pl.multiple_of(h * HEAD_DIM, HEAD_DIM), HEAD_DIM)
                    dq_t[out_rows, cols] = dq * HEAD_DIM**-0.5

    pl.when(flag[0] != 0)(lambda: run(True))
    pl.when(flag[0] == 0)(lambda: run(False))
    dq_ref[...] = jnp.transpose(dq_t[...])
    for g in range(KV_HEADS):
        dkv_ref[:, g * HEAD_DIM : (g + 1) * HEAD_DIM] = dk[g]
        dkv_ref[:, kv_width + g * HEAD_DIM : kv_width + (g + 1) * HEAD_DIM] = dv[g]


VM = pl.BlockSpec(memory_space=pltpu.VMEM)
SM = pl.BlockSpec(memory_space=pltpu.SMEM)


def attn_cost(rows, total, heads, products):
    return pl.CostEstimate(
        flops=2 * products * rows * total * heads * HEAD_DIM,
        bytes_accessed=4 * (rows + total) * heads * HEAD_DIM,
        transcendentals=rows * total * heads,
    )


def attention(q, kv, places, flag, short, causal):
    rows, width = q.shape
    total = kv.shape[0]
    heads = width // HEAD_DIM
    block = min(rows, 256)
    return pl.pallas_call(
        functools.partial(attn_fwd_kernel, heads, block, short, causal),
        out_shape=(
            jax.ShapeDtypeStruct((rows, width), BF),
            jax.ShapeDtypeStruct((heads, 1, rows), F32),
        ),
        in_specs=[SM] + [VM] * 6,
        out_specs=(VM, VM),
        scratch_shapes=[
            pltpu.VMEM((heads, rows, HEAD_DIM), BF),
            pltpu.VMEM((KV_HEADS, total, HEAD_DIM), BF),
            pltpu.VMEM((KV_HEADS * HEAD_DIM, total), BF),
            pltpu.VMEM((total, rows), F32),
            pltpu.VMEM((width, rows), F32),
        ],
        compiler_params=pltpu.CompilerParams(vmem_limit_bytes=32 * 2**20),
        cost_estimate=attn_cost(rows, total, heads, 2),
        name="attn_fwd",
    )(flag, q, kv, *places)


def attention_back(q, kv, grad_out, lse, places, flag, short, causal):
    rows, width = q.shape
    total = kv.shape[0]
    heads = width // HEAD_DIM
    block = min(rows, 256)
    return pl.pallas_call(
        functools.partial(attn_bwd_kernel, heads, block, short, causal),
        out_shape=(
            jax.ShapeDtypeStruct((rows, width), F32),
            jax.ShapeDtypeStruct((total, 2 * KV_HEADS * HEAD_DIM), F32),
        ),
        in_specs=[SM] + [VM] * 8,
        out_specs=(VM, VM),
        scratch_shapes=[
            pltpu.VMEM((heads, rows, HEAD_DIM), BF),
            pltpu.VMEM((KV_HEADS, total, HEAD_DIM), BF),
            pltpu.VMEM((KV_HEADS, total, HEAD_DIM), BF),
            pltpu.VMEM((KV_HEADS * HEAD_DIM, total), BF),
            pltpu.VMEM((heads, rows, HEAD_DIM), BF),
            pltpu.VMEM((total, rows), F32),
            pltpu.VMEM((width, rows), F32),
            pltpu.VMEM((KV_HEADS, total, HEAD_DIM), F32),
            pltpu.VMEM((KV_HEADS, total, HEAD_DIM), F32),
        ],
        compiler_params=pltpu.CompilerParams(vmem_limit_bytes=32 * 2**20),
        cost_estimate=attn_cost(rows, total, heads, 5),
        name="attn_bwd",
    )(flag, q, kv, grad_out, lse, *places)


class Blocks:
    def __init__(self, dp_count, ctx_count):
        self.count = dp_count * ctx_count
        self.x = 1
        self.core = ctx_count
        self.y = 2 * ctx_count
        self.z = 4 * ctx_count
        self.zs = dp_count // 4

    def swap(self, values, mask):
        perm = [(i, i ^ mask) for i in range(self.count)]
        return lax.ppermute(values, AXES, perm)

    def gather(self, mine, y_first):
        held = jnp.stack([mine] + [self.swap(mine, d * self.z) for d in range(1, self.zs)])
        if y_first:
            held = jnp.stack([held, self.swap(held, self.y)], axis=1)
            held = jnp.stack([held, self.swap(held, self.x)], axis=2)
        else:
            held = jnp.stack([held, self.swap(held, self.x)], axis=1)
            held = jnp.stack([held, self.swap(held, self.y)], axis=1)
        held = jnp.stack([held, self.swap(held, self.core)], axis=2)
        return held.reshape((self.count,) + mine.shape)

    def scatter(self, terms, x_first):
        shape = terms.shape[1:]
        held = terms.reshape((self.zs, 2, 2, 2) + shape)

        def fold(keep, give, mask):
            got = self.swap(give, mask)
            return (keep.astype(F32) + got.astype(F32)).astype(BF)

        held = fold(held[:, :, 0], held[:, :, 1], self.core)
        if x_first:
            held = fold(held[:, :, 0], held[:, :, 1], self.x)
            held = fold(held[:, 0], held[:, 1], self.y)
        else:
            held = fold(held[:, 0], held[:, 1], self.y)
            held = fold(held[:, 0], held[:, 1], self.x)
        got = [self.swap(held[d], d * self.z).astype(F32) for d in range(1, self.zs)]
        return functools.reduce(jnp.add, got, held[0].astype(F32))


def pad_to(values, rows, columns):
    return jnp.pad(values, ((0, rows - values.shape[0]), (0, columns - values.shape[1])))


def local(
    tokens, q_weight, k_weight, v_weight, o_weight, gate_weight, up_weight, down_weight,
    vectors, doc_lengths, cotangent,
):
    tok_rows, width = tokens.shape
    ctx_count = lax.axis_size("ctx")
    dp_count = lax.axis_size("dp")
    count = dp_count * ctx_count
    seq_tokens = tok_rows * ctx_count
    ctx_index = lax.axis_index("ctx")
    me = lax.axis_index("dp") * ctx_count + ctx_index
    heads = width // HEAD_DIM
    kv_width = KV_HEADS * HEAD_DIM
    ff = gate_weight.shape[0] * count // width
    vec = vectors.shape[0]
    whole_rows = width % count == 0 and ff % count == 0
    fast = whole_rows and ctx_count == 2 and dp_count % 4 == 0 and count & (count - 1) == 0

    segment_all, position_all = doc_layout(doc_lengths[0], seq_tokens)
    offset = ctx_index * tok_rows
    row_all = jnp.arange(seq_tokens, dtype=jnp.int32)
    segment_mine = lax.dynamic_slice_in_dim(segment_all, offset, tok_rows)
    position_mine = lax.dynamic_slice_in_dim(position_all, offset, tok_rows)
    row_mine = offset + jnp.arange(tok_rows, dtype=jnp.int32)
    half = HEAD_DIM // 2
    freq = THETA ** (-jnp.arange(half, dtype=F32) * 2.0 / HEAD_DIM)
    angle = position_mine.astype(F32)[:, None] * freq[None, :]
    cosine = jnp.cos(angle)[:, None, :]
    sine = jnp.sin(angle)[:, None, :]

    inputs = tokens.astype(F32)
    inv_first = lax.rsqrt(jnp.mean(inputs * inputs, axis=-1, keepdims=True) + EPS)

    if fast:
        blocks = Blocks(dp_count, ctx_count)
        rows = width // count
        f_rows = ff // count
        tall = (rows + 1 + 7) // 8 * 8
        a_width = (width + 2 * kv_width + 127) // 128 * 128
        joined_w = jnp.concatenate(
            [w.reshape(rows, -1) for w in (q_weight, k_weight, v_weight)], axis=1
        )
        vec_row = pad_to(vectors.reshape(1, vec), tall - rows, a_width)
        wire_a = jnp.concatenate([pad_to(joined_w, rows, a_width), vec_row], axis=0)
        wire_o = pad_to(o_weight.reshape(rows, -1), tall, width)
        wire_g = pad_to(gate_weight.reshape(rows, -1), tall, ff)
        wire_u = pad_to(up_weight.reshape(rows, -1), tall, ff)
        wire_d = down_weight.reshape(f_rows, -1)
        got_a = blocks.gather(wire_a, True)
        got_o = blocks.gather(wire_o, False)
        got_g = blocks.gather(wire_g, False)
        got_u = blocks.gather(wire_u, True)
        got_d = blocks.gather(wire_d, False)
        order = me ^ jnp.arange(count, dtype=jnp.int32)
        slot = jnp.arange(count * tall, dtype=jnp.int32)
        inside = slot % tall
        feature = jnp.where(inside < rows, rows * (me ^ (slot // tall)) + inside, -1)
        place = (jnp.arange(width, dtype=jnp.int32)[:, None] == feature[None, :]).astype(BF)
        w_a = got_a.reshape(count * tall, a_width)
        w_qkv = w_a[:, : width + 2 * kv_width]
        w_out = got_o.reshape(count * tall, width)
        w_gate = got_g.reshape(count * tall, ff)
        w_up = got_u.reshape(count * tall, ff)
        w_down = got_d[order].reshape(ff, width)
        pick = (order[:, None] == jnp.arange(count, dtype=jnp.int32)[None, :]).astype(BF)
        flat = times(pick, got_a[:, rows, :vec]).reshape(-1)

        def spread(values):
            return times(values, place).astype(BF)

        def collect(values):
            return times_back(values.astype(BF), place)

    else:
        def whole(part):
            return lax.all_gather(part, AXES, axis=0, tiled=True)

        w_qkv = jnp.concatenate(
            [whole(w).reshape(width, -1) for w in (q_weight, k_weight, v_weight)], axis=1
        )
        w_out = whole(o_weight).reshape(width, width)
        w_gate = whole(gate_weight).reshape(width, ff)
        w_up = whole(up_weight).reshape(width, ff)
        w_down = whole(down_weight).reshape(ff, width)
        flat = whole(vectors).astype(F32)

        def spread(values):
            return values

        def collect(values):
            return values

    ends = [width, width + kv_width, width + 2 * kv_width, 2 * width + 2 * kv_width]
    bias_qkv = flat[: ends[2]]
    gain_attn = flat[ends[2] : ends[3]]
    gain_mlp = flat[ends[3] : ends[3] + width]

    n_first = spread((inputs * inv_first * gain_attn).astype(BF))
    qkv = times(n_first, w_qkv) + bias_qkv
    q_rot = turn(qkv[:, :width].reshape(tok_rows, heads, HEAD_DIM), cosine, sine)
    q_rot = q_rot.astype(BF).reshape(tok_rows, width)
    k_rot = turn(qkv[:, width : ends[1]].reshape(tok_rows, KV_HEADS, HEAD_DIM), cosine, sine)
    k_rot = k_rot.astype(BF).reshape(tok_rows, kv_width)
    kv_mine = jnp.concatenate([k_rot, qkv[:, ends[1] :].astype(BF)], axis=1)
    if fast:
        kv = jnp.concatenate([blocks.swap(kv_mine, blocks.x), kv_mine], axis=0)
        other = (1 - ctx_index) * tok_rows
        segment_k = jnp.concatenate(
            [lax.dynamic_slice_in_dim(segment_all, other, tok_rows), segment_mine]
        )
        row_k = jnp.concatenate([other + jnp.arange(tok_rows, dtype=jnp.int32), row_mine])
        flag = ctx_index.astype(jnp.int32).reshape(1)
        short = tok_rows
    else:
        kv = lax.all_gather(kv_mine, "ctx", axis=0, tiled=True)
        segment_k, row_k = segment_all, row_all
        flag = jnp.ones((1,), jnp.int32)
        short = seq_tokens
    places = (segment_k[:, None], row_k[:, None], segment_mine[None, :], row_mine[None, :])
    attn, lse = attention(q_rot, kv, places, flag, short, fast)
    attn_in = spread(attn)
    mid = inputs + times(attn_in, w_out)
    inv_second = lax.rsqrt(jnp.mean(mid * mid, axis=-1, keepdims=True) + EPS)
    n_second = spread((mid * inv_second * gain_mlp).astype(BF))
    gate = times(n_second, w_gate)
    up_val = times(n_second, w_up)
    sig = jax.nn.sigmoid(gate)
    act = gate * sig
    hidden = (act * up_val).astype(BF)
    layer_out = (mid + times(hidden, w_down)).astype(BF)

    grad_wdown = inner_rows(hidden, cotangent)
    grad_hidden = times_back(cotangent, w_down)
    grad_gate = (grad_hidden * up_val * (sig * (1.0 + gate * (1.0 - sig)))).astype(BF)
    grad_up = (grad_hidden * act).astype(BF)
    grad_wgate = inner_rows(n_second, grad_gate)
    grad_wup = inner_rows(n_second, grad_up)
    grad_n2 = collect(times_back(grad_gate, w_gate) + times_back(grad_up, w_up))
    grad_mid_norm, grad_gain_mlp = norm_back(mid, inv_second, gain_mlp, grad_n2)
    grad_mid = cotangent.astype(F32) + grad_mid_norm
    grad_branch = grad_mid.astype(BF)
    grad_wout = inner_rows(attn_in, grad_branch)
    grad_attn = collect(times_back(grad_branch, w_out)).astype(BF)

    if fast:
        def send(terms, rows_each, x_first):
            return blocks.scatter(terms.astype(BF).reshape(count, rows_each, -1), x_first)

        down_terms = grad_wdown.astype(BF).reshape(count, f_rows, width)[order]
        share_down = blocks.scatter(down_terms, False)
        share_gate = send(grad_wgate, tall, True)
        share_up = send(grad_wup, tall, False)
        share_out = send(grad_wout, tall, True)

    grad_q_rot, grad_kv = attention_back(q_rot, kv, grad_attn, lse, places, flag, short, fast)
    if fast:
        got = blocks.swap(grad_kv[:tok_rows].astype(BF), blocks.x)
        grad_kv_mine = grad_kv[tok_rows:] + got.astype(F32)
    else:
        grad_kv_mine = lax.psum_scatter(
            grad_kv.astype(BF), "ctx", scatter_dimension=0, tiled=True
        ).astype(F32)
    grad_q = turn(grad_q_rot.reshape(tok_rows, heads, HEAD_DIM), cosine, -sine)
    grad_k = turn(
        grad_kv_mine[:, :kv_width].reshape(tok_rows, KV_HEADS, HEAD_DIM), cosine, -sine
    )
    grad_qkv = jnp.concatenate(
        [
            grad_q.reshape(tok_rows, width).astype(BF),
            grad_k.reshape(tok_rows, kv_width).astype(BF),
            grad_kv_mine[:, kv_width:].astype(BF),
        ],
        axis=1,
    )
    grad_wqkv = inner_rows(n_first, grad_qkv)
    grad_bias = jnp.sum(grad_qkv.astype(F32), axis=0)
    grad_n1 = collect(times_back(grad_qkv, w_qkv))
    grad_x_norm, grad_gain_attn = norm_back(inputs, inv_first, gain_attn, grad_n1)
    input_grad = grad_mid + grad_x_norm
    used = 3 * width + 2 * kv_width
    vector_term = jnp.concatenate(
        [grad_bias, grad_gain_attn, grad_gain_mlp, jnp.zeros((vec * count - used,), F32)]
    )

    if fast:
        vec_terms = times(pick, vector_term.astype(BF).reshape(count, vec)).astype(BF)
        terms = grad_wqkv.astype(BF).reshape(count, tall, -1)[:, :rows]
        terms = jnp.pad(terms, ((0, 0), (0, 0), (0, a_width - terms.shape[2])))
        extra = jnp.pad(vec_terms[:, None], ((0, 0), (0, tall - rows - 1), (0, a_width - vec)))
        share_a = blocks.scatter(jnp.concatenate([terms, extra], axis=1), False)
        share_q = share_a[:rows, :width].reshape(-1)
        share_k = share_a[:rows, width : ends[1]].reshape(-1)
        share_v = share_a[:rows, ends[1] : ends[2]].reshape(-1)
        share_vec = share_a[rows, :vec]
        share_out = share_out[:rows].reshape(-1)
        share_gate = share_gate[:rows].reshape(-1)
        share_up = share_up[:rows].reshape(-1)
        share_down = share_down.reshape(-1)
    else:
        def shares(term):
            return lax.psum_scatter(term.reshape(-1), AXES, scatter_dimension=0, tiled=True)

        share_q = shares(grad_wqkv[:, :width])
        share_k = shares(grad_wqkv[:, width : ends[1]])
        share_v = shares(grad_wqkv[:, ends[1] :])
        share_out = shares(grad_wout)
        share_gate = shares(grad_wgate)
        share_up = shares(grad_wup)
        share_down = shares(grad_wdown)
        share_vec = shares(vector_term)
    return (
        layer_out, input_grad, share_q, share_k, share_v, share_out, share_gate, share_up,
        share_down, share_vec,
    )


def solution(mesh):
    split = P(AXES)
    rows = P(AXES, None)
    in_specs = (rows,) + (split,) * 8 + (P("dp", None), rows)
    out_specs = (rows, rows) + (split,) * 8
    return jax.shard_map(local, mesh=mesh, in_specs=in_specs, out_specs=out_specs, check_vma=False)
```

```python
import functools

import jax
import jax.numpy as jnp
import numpy as np
from jax import lax
from jax.experimental import pallas as pl
from jax.experimental.pallas import tpu as pltpu
from jax.sharding import PartitionSpec as P

KV_HEADS = 3
HEAD_DIM = 64

EPS = 1e-06
THETA = 100000.0
NEG_FILL = -1e30
AXES = ("dp", "ctx")
BF = jnp.bfloat16
F32 = jnp.float32


def times(left, right):
    return jnp.dot(left, right, preferred_element_type=F32)


def inner_rows(left, right):
    return lax.dot_general(left, right, (((0,), (0,)), ((), ())), preferred_element_type=F32)


def times_back(left, right):
    return lax.dot_general(left, right, (((1,), (1,)), ((), ())), preferred_element_type=F32)


def norm_back(values, inv, gain, grad):
    scaled = grad * gain
    dot = jnp.mean(scaled * values, axis=-1, keepdims=True)
    grad_values = inv * scaled - values * (inv * inv * inv * dot)
    grad_gain = jnp.sum(grad * values * inv, axis=0)
    return grad_values, grad_gain


def turn(values, cosine, sine):
    half = values.shape[-1] // 2
    first = values[..., :half]
    second = values[..., half:]
    return jnp.concatenate(
        [first * cosine - second * sine, second * cosine + first * sine], axis=-1
    )


def doc_layout(lengths, count):
    ends = jnp.cumsum(lengths)
    place = jnp.arange(count, dtype=jnp.int32)
    segment = jnp.sum((place[:, None] >= ends[None, :-1]).astype(jnp.int32), axis=1)
    starts = ends - lengths
    picked = segment[:, None] == jnp.arange(lengths.shape[0], dtype=jnp.int32)[None, :]
    first = jnp.sum(jnp.where(picked, starts[None, :], 0), axis=1)
    return (segment, place - first)


def fill_bias(bias, seg_k, row_k, seg_q, row_q):
    allowed = (seg_k[...] == seg_q[...]) & (row_k[...] <= row_q[...])
    bias[...] = jnp.where(allowed, 0.0, NEG_FILL)


def key_range(full, total, short, rows, block, at, causal):
    start = 0 if full else total - short
    stop = total - rows + (at + 1) * block if causal else total
    return start, stop


def attn_fwd_kernel(
    heads, block, short, causal, flag, q_ref, kv_ref, seg_k, row_k, seg_q, row_q,
    out_ref, lse_ref, qs, ks, vts, bias, out_t,
):
    rows = q_ref.shape[0]
    total = kv_ref.shape[0]
    kv_width = KV_HEADS * HEAD_DIM
    group = heads // KV_HEADS
    fill_bias(bias, seg_k, row_k, seg_q, row_q)
    for h in range(heads):
        qs[h] = q_ref[:, h * HEAD_DIM : (h + 1) * HEAD_DIM] * BF(HEAD_DIM**-0.5)
    for g in range(KV_HEADS):
        ks[g] = kv_ref[:, g * HEAD_DIM : (g + 1) * HEAD_DIM]
    vts[...] = jnp.transpose(kv_ref[:, kv_width:].astype(F32)).astype(BF)

    def run(full):
        @pl.loop(0, KV_HEADS)
        def _(g):
            v_rows = pl.ds(pl.multiple_of(g * HEAD_DIM, HEAD_DIM), HEAD_DIM)
            for j in range(group):
                h = g * group + j
                for at in range(rows // block):
                    start, stop = key_range(full, total, short, rows, block, at, causal)
                    cols = slice(at * block, (at + 1) * block)
                    s = times_back(ks[g, start:stop], qs[h, cols])
                    s = s + bias[start:stop, cols]
                    top = jnp.max(s, axis=0, keepdims=True)
                    p = jnp.exp(s - top)
                    total_p = jnp.sum(p, axis=0, keepdims=True)
                    o = times(vts[v_rows, start:stop], p.astype(BF))
                    out_rows = pl.ds(pl.multiple_of(h * HEAD_DIM, HEAD_DIM), HEAD_DIM)
                    out_t[out_rows, cols] = o / total_p
                    lse_ref[h, :, cols] = top + jnp.log(total_p)

    pl.when(flag[0] != 0)(lambda: run(True))
    pl.when(flag[0] == 0)(lambda: run(False))
    out_ref[...] = jnp.transpose(out_t[...]).astype(BF)


def attn_bwd_kernel(
    heads, block, short, causal, flag, q_ref, kv_ref, do_ref, lse_ref, seg_k, row_k, seg_q, row_q,
    dq_ref, dkv_ref, qs, ks, vs, kts, dos, bias, dq_t, dk, dv,
):
    rows = q_ref.shape[0]
    total = kv_ref.shape[0]
    kv_width = KV_HEADS * HEAD_DIM
    group = heads // KV_HEADS
    fill_bias(bias, seg_k, row_k, seg_q, row_q)
    for h in range(heads):
        lanes = slice(h * HEAD_DIM, (h + 1) * HEAD_DIM)
        qs[h] = q_ref[:, lanes] * BF(HEAD_DIM**-0.5)
        dos[h] = do_ref[:, lanes]
    for g in range(KV_HEADS):
        ks[g] = kv_ref[:, g * HEAD_DIM : (g + 1) * HEAD_DIM]
        vs[g] = kv_ref[:, kv_width + g * HEAD_DIM : kv_width + (g + 1) * HEAD_DIM]
    kts[...] = jnp.transpose(kv_ref[:, :kv_width].astype(F32)).astype(BF)
    dk[...] = jnp.zeros_like(dk)
    dv[...] = jnp.zeros_like(dv)

    def run(full):
        @pl.loop(0, KV_HEADS)
        def _(g):
            k_rows = pl.ds(pl.multiple_of(g * HEAD_DIM, HEAD_DIM), HEAD_DIM)
            for j in range(group):
                h = g * group + j
                for at in range(rows // block):
                    start, stop = key_range(full, total, short, rows, block, at, causal)
                    cols = slice(at * block, (at + 1) * block)
                    q = qs[h, cols]
                    do = dos[h, cols]
                    s = times_back(ks[g, start:stop], q)
                    p = jnp.exp(s + bias[start:stop, cols] - lse_ref[h, :, cols])
                    dp = times_back(vs[g, start:stop], do)
                    t = p * dp
                    inner = jnp.sum(t, axis=0, keepdims=True)
                    ds = (t - p * inner).astype(BF)
                    dk[g, start:stop] += times(ds, q)
                    dv[g, start:stop] += times(p.astype(BF), do)
                    dq = times(kts[k_rows, start:stop], ds)
                    out_rows = pl.ds(pl.multiple_of(h * HEAD_DIM, HEAD_DIM), HEAD_DIM)
                    dq_t[out_rows, cols] = dq * HEAD_DIM**-0.5

    pl.when(flag[0] != 0)(lambda: run(True))
    pl.when(flag[0] == 0)(lambda: run(False))
    dq_ref[...] = jnp.transpose(dq_t[...])
    for g in range(KV_HEADS):
        dkv_ref[:, g * HEAD_DIM : (g + 1) * HEAD_DIM] = dk[g]
        dkv_ref[:, kv_width + g * HEAD_DIM : kv_width + (g + 1) * HEAD_DIM] = dv[g]


VM = pl.BlockSpec(memory_space=pltpu.VMEM)
SM = pl.BlockSpec(memory_space=pltpu.SMEM)


def attn_cost(rows, total, heads, products):
    return pl.CostEstimate(
        flops=2 * products * rows * total * heads * HEAD_DIM,
        bytes_accessed=4 * (rows + total) * heads * HEAD_DIM,
        transcendentals=rows * total * heads,
    )


def attention(q, kv, places, flag, short, causal):
    rows, width = q.shape
    total = kv.shape[0]
    heads = width // HEAD_DIM
    block = min(rows, 256)
    return pl.pallas_call(
        functools.partial(attn_fwd_kernel, heads, block, short, causal),
        out_shape=(
            jax.ShapeDtypeStruct((rows, width), BF),
            jax.ShapeDtypeStruct((heads, 1, rows), F32),
        ),
        in_specs=[SM] + [VM] * 6,
        out_specs=(VM, VM),
        scratch_shapes=[
            pltpu.VMEM((heads, rows, HEAD_DIM), BF),
            pltpu.VMEM((KV_HEADS, total, HEAD_DIM), BF),
            pltpu.VMEM((KV_HEADS * HEAD_DIM, total), BF),
            pltpu.VMEM((total, rows), F32),
            pltpu.VMEM((width, rows), F32),
        ],
        compiler_params=pltpu.CompilerParams(vmem_limit_bytes=32 * 2**20),
        cost_estimate=attn_cost(rows, total, heads, 2),
        name="attn_fwd",
    )(flag, q, kv, *places)


def attention_back(q, kv, grad_out, lse, places, flag, short, causal):
    rows, width = q.shape
    total = kv.shape[0]
    heads = width // HEAD_DIM
    block = min(rows, 256)
    return pl.pallas_call(
        functools.partial(attn_bwd_kernel, heads, block, short, causal),
        out_shape=(
            jax.ShapeDtypeStruct((rows, width), F32),
            jax.ShapeDtypeStruct((total, 2 * KV_HEADS * HEAD_DIM), F32),
        ),
        in_specs=[SM] + [VM] * 8,
        out_specs=(VM, VM),
        scratch_shapes=[
            pltpu.VMEM((heads, rows, HEAD_DIM), BF),
            pltpu.VMEM((KV_HEADS, total, HEAD_DIM), BF),
            pltpu.VMEM((KV_HEADS, total, HEAD_DIM), BF),
            pltpu.VMEM((KV_HEADS * HEAD_DIM, total), BF),
            pltpu.VMEM((heads, rows, HEAD_DIM), BF),
            pltpu.VMEM((total, rows), F32),
            pltpu.VMEM((width, rows), F32),
            pltpu.VMEM((KV_HEADS, total, HEAD_DIM), F32),
            pltpu.VMEM((KV_HEADS, total, HEAD_DIM), F32),
        ],
        compiler_params=pltpu.CompilerParams(vmem_limit_bytes=32 * 2**20),
        cost_estimate=attn_cost(rows, total, heads, 5),
        name="attn_bwd",
    )(flag, q, kv, grad_out, lse, *places)


TAIL = 2
MAIN = 16
PIECES = MAIN // TAIL


class Blocks:
    def __init__(self, dp_count, ctx_count):
        self.count = dp_count * ctx_count
        self.x = 1
        self.core = ctx_count
        self.y = 2 * ctx_count
        self.z = 4 * ctx_count
        self.zs = dp_count // 4
        self.masks = []
        for p in range(self.count):
            z, x = p % self.zs, p // self.zs % 2
            y, core = p // (2 * self.zs) % 2, p // (4 * self.zs)
            self.masks.append(x * self.x + y * self.y + core * self.core + z * self.z)

    def swap(self, values, mask):
        perm = [(i, i ^ mask) for i in range(self.count)]
        return lax.ppermute(values, AXES, perm)

    def along_z(self, mine):
        return jnp.stack([mine] + [self.swap(mine, d * self.z) for d in range(1, self.zs)])

    def add(self, keep, got):
        return (keep.astype(F32) + got.astype(F32)).astype(BF)

    def sum_z(self, held):
        got = [self.swap(held[d], d * self.z).astype(F32) for d in range(1, self.zs)]
        return functools.reduce(jnp.add, got, held[0].astype(F32))


class Sizes:
    def __init__(self, width, ff, count, vec, kv_width):
        self.width, self.ff, self.count, self.vec = width, ff, count, vec
        self.rows = width // count
        self.f_rows = ff // count
        up = lambda n: (n + 127) // 128 * 128
        self.wide = up(width)
        self.qkv = width + 2 * kv_width
        self.a_width = up(self.qkv)
        self.tall = (self.rows + 1 + 7) // 8 * 8
        self.downs = self.f_rows // MAIN
        self.piece = 2 * ff // PIECES
        self.gate = 0
        self.tail = ff
        self.tail_o = self.tail + self.piece
        self.out = self.tail_o + 128
        self.down0 = self.out + self.wide
        self.first = self.down0 + self.wide
        self.up = self.first
        self.down1 = self.up + ff
        self.total = self.down1 + (self.downs - 1) * self.wide
        self.flat = self.a_width + 2 * self.wide

    def down_at(self, c):
        return self.down0 if c == 0 else self.down1 + (c - 1) * self.wide

    def fits(self):
        return (
            self.rows == MAIN + TAIL
            and self.f_rows % MAIN == 0
            and self.piece % 128 == 0
            and self.ff % 256 == 0
            and self.wide <= 128 * PIECES
            and self.vec <= 128
        )


def slot_tables(size, masks):
    far = -(2**20)
    a = [(masks[s // size.tall], s % size.tall) for s in range(size.count * size.tall)]
    a = [(m, i if i < size.rows else far) for m, i in a]
    b = [(masks[s // MAIN], s % MAIN) for s in range(size.count * MAIN)]
    b += [(masks[s // TAIL], MAIN + s % TAIL) for s in range(size.count * TAIL)]
    flat = []
    natural = [(0, size.qkv, size.a_width), (size.qkv, size.width, size.wide)]
    natural += [(size.qkv + size.width, size.width, size.wide)]
    for start, used, room in natural:
        for c in range(room):
            at = start + c
            flat.append((at // size.vec, at % size.vec) if c < used else (far, far))
    owners = np.asarray(masks, np.int32)[:, None]
    as_rows = lambda pairs: np.ascontiguousarray(np.asarray(pairs, np.int32).T)
    return as_rows(a), as_rows(b), as_rows(flat), owners


def place_matrix(size, me, table):
    feature = size.rows * (me ^ table[0:1, :]) + table[1:2, :]
    shape = (size.width, feature.shape[1])
    at = lax.broadcasted_iota(jnp.int32, shape, 0)
    return jnp.where(at == feature, 1.0, 0.0).astype(BF)


def vector_lanes(table):
    inside = lax.broadcasted_iota(jnp.int32, (128, table.shape[1]), 0)
    return jnp.where(inside == table[1:2, :], 1.0, 0.0).astype(BF)


def split_two(values):
    high = values.astype(BF)
    return high, (values - high.astype(F32)).astype(BF)


def swap_halves(u):
    rolled_back = pltpu.roll(u, 128 - HEAD_DIM // 2, 1)
    rolled = pltpu.roll(u, HEAD_DIM // 2, 1)
    lane = lax.broadcasted_iota(jnp.int32, u.shape, 1)
    return jnp.where(lane % HEAD_DIM < HEAD_DIM // 2, rolled_back, rolled)


def pre_kernel(
    size, me_ref, x_ref, wm_ref, wo_ref, cos_ref, sin_ref, table_a, table_f, owner_ref,
    q_ref, kv_ref, n1t_ref, flat_ref, w, qkv,
):
    me = me_ref[0]
    half = wm_ref.shape[0]
    w[:half] = wm_ref[...]
    w[half:] = wo_ref[...]
    shape = (size.count, 2 * half)
    row = lax.broadcasted_iota(jnp.int32, shape, 0) * size.tall + size.rows
    row = lax.broadcasted_iota(jnp.int32, shape, 1) == row
    packed = times(jnp.where(row, 1.0, 0.0).astype(BF), w[:, :128]).astype(BF)
    table = table_f[...]
    spread = times(packed, vector_lanes(table))
    mine = table[0:1, :] == (me ^ owner_ref[...])
    flat = jnp.sum(jnp.where(mine, spread, 0.0), axis=0, keepdims=True)
    flat_ref[...] = flat
    gain = flat[:, size.a_width : size.a_width + size.width]
    x = x_ref[...].astype(F32)
    inv = lax.rsqrt(jnp.mean(x * x, axis=-1, keepdims=True) + EPS)
    n1 = (x * inv * gain).astype(BF)
    n1a = times(n1, place_matrix(size, me, table_a[...]))
    qkv[...] = times(n1a.astype(BF), w[...]) + flat[:, : size.a_width]
    n1t_ref[...] = jnp.transpose(n1a).astype(BF)
    kv_width = kv_ref.shape[1] // 2
    for t in range((size.width + kv_width) // 128):
        u = qkv[:, t * 128 : (t + 1) * 128]
        qkv[:, t * 128 : (t + 1) * 128] = u * cos_ref[...] + swap_halves(u) * sin_ref[...]
    q_ref[...] = qkv[:, : size.width].astype(BF)
    kv_ref[...] = qkv[:, size.width : size.qkv].astype(BF)


def tail_place(size, c):
    shape = (size.count * TAIL, size.count * MAIN)
    q = lax.broadcasted_iota(jnp.int32, shape, 0)
    at = lax.broadcasted_iota(jnp.int32, shape, 1)
    want = (q // TAIL) * MAIN + c * TAIL + q % TAIL
    return jnp.where(at == want, 1.0, 0.0).astype(BF)


def tail_place_back(size, c):
    shape = (size.count * MAIN, size.count * TAIL)
    at = lax.broadcasted_iota(jnp.int32, shape, 0)
    q = lax.broadcasted_iota(jnp.int32, shape, 1)
    want = (q // TAIL) * MAIN + c * TAIL + q % TAIL
    return jnp.where(at == want, 1.0, 0.0).astype(BF)


def mlp_kernel(
    size, masks, me_ref, attn_ref, x_ref, cot_ref, flat_ref, b1m, b1o, b2m, b2o, table_b,
    out_ref, keep_ref, give_ref, gmid_ref, gattn_ref, ggain_ref,
    wg, wu, wo, wd, mid, n2s, n2t, place, acc, gacc, dwd, tails, tail_o,
):
    me = me_ref[0]
    width, ff = size.width, size.ff
    half = b1m.shape[0]
    main = 2 * half
    halves = ((slice(0, half), b1m, b2m, keep_ref), (slice(half, main), b1o, b2o, give_ref))
    place[...] = place_matrix(size, me, table_b[...])
    for part, b1, b2, _ in halves:
        wg[part] = b1[:, size.gate : size.gate + ff]
        wu[part] = b2[:, : ff]
        wo[part] = b1[:, size.out : size.out + size.wide]
    for c in range(PIECES):
        sel = tail_place(size, c)
        cols = slice(size.tail, size.tail + size.piece)
        got = times(sel[:, :half], b1m[:, cols]) + times(sel[:, half:], b1o[:, cols])
        target = wg if c * size.piece < ff else wu
        at = c * size.piece % ff
        target[main:, at : at + size.piece] = got.astype(BF)
        if c * 128 < size.wide:
            cols = slice(size.tail_o, size.tail_o + 128)
            got = times(sel[:, :half], b1m[:, cols]) + times(sel[:, half:], b1o[:, cols])
            wo[main:, c * 128 : (c + 1) * 128] = got.astype(BF)
    for p in range(size.count):
        _, b1, b2, _ = halves[p // (size.count // 2)]
        rows = slice(p * MAIN % half, p * MAIN % half + MAIN)
        owner = me ^ masks[p]
        for c in range(size.downs):
            at = size.down_at(c)
            src = b1[rows, at : at + size.wide] if c == 0 else (
                b2[rows, at - size.up : at - size.up + size.wide]
            )
            to = pl.multiple_of(owner * size.f_rows + c * MAIN, MAIN)
            wd[pl.ds(to, MAIN), :] = src
    attn_s = times(attn_ref[...], place[...])
    m = x_ref[...].astype(F32) + times(attn_s.astype(BF), wo[:, :width])
    mid[...] = m
    inv = lax.rsqrt(jnp.mean(m * m, axis=-1, keepdims=True) + EPS)
    lo = size.a_width + size.wide
    gain = flat_ref[:, lo : lo + width]
    n2 = (m * inv * gain).astype(BF)
    spread = times(n2, place[...])
    n2s[...] = spread.astype(BF)
    n2t[...] = jnp.transpose(spread).astype(BF)
    acc[...] = jnp.zeros_like(acc)
    gacc[...] = jnp.zeros_like(gacc)
    step = 256

    @pl.loop(0, ff // step)
    def _(b):
        at = pl.multiple_of(b * step, step)
        cols = pl.ds(at, step)
        gate = times(n2s[...], wg[:, cols])
        up = times(n2s[...], wu[:, cols])
        sig = 1.0 / (1.0 + jnp.exp(-gate))
        act = gate * sig
        h = act * up
        gh = times_back(cot_ref[...], wd[cols, :width])
        gg = (gh * up * (sig * (1.0 + gate * (1.0 - sig)))).astype(BF)
        gu = (gh * act).astype(BF)
        acc[...] += times(h.astype(BF), wd[cols, :width])
        dwd[cols, :width] = times(jnp.transpose(h).astype(BF), cot_ref[...]).astype(BF)
        gacc[...] += times_back(gg, wg[:, cols]) + times_back(gu, wu[:, cols])
        for k, (grad, base) in enumerate(((gg, size.gate), (gu, size.up))):
            dw = times(n2t[...], grad).astype(BF)
            keep_ref[:, pl.ds(pl.multiple_of(base + at, 128), step)] = dw[:half]
            give_ref[:, pl.ds(pl.multiple_of(base + at, 128), step)] = dw[half:main]
            tails[:, pl.ds(pl.multiple_of(k * ff + at, 128), step)] = dw[main:]

    m = mid[...]
    inv = lax.rsqrt(jnp.mean(m * m, axis=-1, keepdims=True) + EPS)
    out_ref[...] = (m + acc[...]).astype(BF)
    high, low = split_two(gacc[...])
    gn2 = times_back(high, place[...]) + times_back(low, place[...])
    scaled = gn2 * gain
    dot = jnp.mean(scaled * m, axis=-1, keepdims=True)
    ggain_ref[...] = jnp.sum(gn2 * m * inv, axis=0, keepdims=True)
    gmid = cot_ref[...].astype(F32) + inv * scaled - m * (inv * inv * inv * dot)
    gmid_ref[...] = gmid
    branch = gmid.astype(BF)
    gattn = times_back(branch, wo[:, :width]).astype(BF)
    gattn_ref[...] = times_back(gattn, place[...]).astype(BF)
    dwo = times(jnp.transpose(attn_s).astype(BF), branch).astype(BF)
    tail_o[...] = jnp.zeros_like(tail_o)
    tail_o[:, :width] = dwo[main:]
    for part, _, _, term in halves:
        term[:, size.out : size.out + width] = dwo[part]
    wire = jnp.zeros((main, size.piece), F32)
    wire_o = jnp.zeros((main, 128), F32)
    for c in range(PIECES):
        sel = tail_place_back(size, c)
        wire += times(sel, tails[:, c * size.piece : (c + 1) * size.piece])
        if c * 128 < size.wide:
            wire_o += times(sel, tail_o[:, c * 128 : (c + 1) * 128])
    for part, _, _, term in halves:
        term[:, size.tail : size.tail + size.piece] = wire[part].astype(BF)
        term[:, size.tail_o : size.tail_o + 128] = wire_o[part].astype(BF)
    for p in range(size.count):
        _, _, _, term = halves[p // (size.count // 2)]
        rows = slice(p * MAIN % half, p * MAIN % half + MAIN)
        owner = me ^ masks[p]
        for c in range(size.downs):
            at = size.down_at(c)
            src = pl.multiple_of(owner * size.f_rows + c * MAIN, MAIN)
            term[rows, at : at + size.wide] = dwd[pl.ds(src, MAIN), :]


def post_kernel(
    size, me_ref, dq_ref, dkv_ref, got_ref, cos_ref, sin_ref, n1t_ref, wm_ref, wo_ref, x_ref,
    gmid_ref, flat_ref, ggain_ref, table_a, table_f, owner_ref,
    gx_ref, keep_ref, give_ref, turn_buf, grad, vec_row,
):
    me = me_ref[0]
    width = size.width
    half = wm_ref.shape[0]
    kv_width = dkv_ref.shape[1] // 2
    turned = width + kv_width
    turn_buf[:, :width] = dq_ref[...]
    dkv = dkv_ref[...] + got_ref[...].astype(F32)
    turn_buf[:, width:] = dkv[:, :kv_width]
    grad[...] = jnp.zeros_like(grad)
    for t in range(turned // 128):
        u = turn_buf[:, t * 128 : (t + 1) * 128]
        back = u * cos_ref[...] - swap_halves(u) * sin_ref[...]
        grad[:, t * 128 : (t + 1) * 128] = back.astype(BF)
    grad[:, turned : turned + kv_width] = dkv[:, kv_width:].astype(BF)
    g = grad[...]
    place = place_matrix(size, me, table_a[...])
    high_m, low_m = split_two(times_back(g, wm_ref[...]))
    high_o, low_o = split_two(times_back(g, wo_ref[...]))
    gn1 = times_back(high_m, place[:, :half]) + times_back(high_o, place[:, half:])
    gn1 += times_back(low_m, place[:, :half]) + times_back(low_o, place[:, half:])
    x = x_ref[...].astype(F32)
    inv = lax.rsqrt(jnp.mean(x * x, axis=-1, keepdims=True) + EPS)
    gain = flat_ref[:, size.a_width : size.a_width + width]
    scaled = gn1 * gain
    dot = jnp.mean(scaled * x, axis=-1, keepdims=True)
    gx_ref[...] = gmid_ref[...] + inv * scaled - x * (inv * inv * inv * dot)
    vec_row[...] = jnp.zeros_like(vec_row)
    vec_row[:, : size.a_width] = jnp.sum(g.astype(F32), axis=0, keepdims=True)
    vec_row[:, size.a_width : size.a_width + width] = jnp.sum(gn1 * x * inv, axis=0, keepdims=True)
    lo = size.a_width + size.wide
    vec_row[:, lo : lo + width] = ggain_ref[...]
    table = table_f[...]
    mine = table[0:1, :] == (me ^ owner_ref[...])
    packed = times_back(jnp.where(mine, vec_row[...], 0.0).astype(BF), vector_lanes(table))
    shape = (half, size.count)
    for part, term in ((0, keep_ref), (1, give_ref)):
        rows = slice(part * half, (part + 1) * half)
        dw = times(n1t_ref[rows], g)
        term[...] = dw.astype(BF)
        want = lax.broadcasted_iota(jnp.int32, shape, 1) * size.tall + size.rows - part * half
        here = lax.broadcasted_iota(jnp.int32, shape, 0) == want
        extra = times(jnp.where(here, 1.0, 0.0).astype(BF), packed.astype(BF))
        term[:, :128] = (dw[:, :128] + extra).astype(BF)


def call(kernel, name, out_shape, scratch, flops, args, vmem=48):
    shapes = [jax.ShapeDtypeStruct(s, t) for s, t in out_shape]
    total = sum(int(np.prod(a.shape)) * a.dtype.itemsize for a in args)
    return pl.pallas_call(
        kernel,
        out_shape=shapes,
        in_specs=[SM] + [VM] * (len(args) - 1),
        out_specs=[VM] * len(shapes),
        scratch_shapes=[pltpu.VMEM(s, t) for s, t in scratch],
        compiler_params=pltpu.CompilerParams(vmem_limit_bytes=vmem * 2**20),
        cost_estimate=pl.CostEstimate(flops=flops, bytes_accessed=total, transcendentals=0),
        name=name,
    )(*args)


def pad_to(values, rows, columns):
    return jnp.pad(values, ((0, rows - values.shape[0]), (0, columns - values.shape[1])))


def tail_pack(rows, piece):
    rows = pad_to(rows, TAIL, PIECES * piece)
    return rows.reshape(TAIL, PIECES, piece).transpose(1, 0, 2).reshape(MAIN, piece)


def tail_unpack(wire, used):
    piece = wire.shape[1]
    rows = wire.reshape(PIECES, TAIL, piece).transpose(1, 0, 2).reshape(TAIL, PIECES * piece)
    return rows[:, :used]


def after(value, *others):
    return lax.optimization_barrier((value,) + others)[0]


def local_blocks(size, blocks, pos, args):
    (
        tokens, q_weight, k_weight, v_weight, o_weight, gate_weight, up_weight, down_weight,
        vectors, cotangent,
    ) = args
    tok_rows, width = tokens.shape
    ff, rows = size.ff, size.rows
    kv_width = KV_HEADS * HEAD_DIM
    ctx_index = lax.axis_index("ctx")
    me = (lax.axis_index("dp") * lax.axis_size("ctx") + ctx_index).astype(jnp.int32).reshape(1)
    masks = blocks.masks
    half = size.count // 2
    table_a, table_b, table_f, owners = slot_tables(size, masks)
    segment_all, segment_mine, row_mine, cos, sin = pos

    joined_w = jnp.concatenate(
        [w.reshape(rows, -1) for w in (q_weight, k_weight, v_weight)], axis=1
    )
    vec_row = pad_to(vectors.reshape(1, -1), size.tall - rows, size.a_width)
    wire_a = jnp.concatenate([pad_to(joined_w, rows, size.a_width), vec_row], axis=0)
    za = blocks.along_z(wire_a)
    w_g, w_u = gate_weight.reshape(rows, ff), up_weight.reshape(rows, ff)
    w_o = o_weight.reshape(rows, width)
    w_d = pad_to(down_weight.reshape(size.f_rows, width), size.f_rows, size.wide)
    d_parts = [w_d[c * MAIN : (c + 1) * MAIN] for c in range(size.downs)]
    wire_b = jnp.concatenate(
        [
            w_g[:MAIN],
            tail_pack(jnp.concatenate([w_g[MAIN:], w_u[MAIN:]], axis=1), size.piece),
            tail_pack(w_o[MAIN:], 128),
            pad_to(w_o[:MAIN], MAIN, size.wide),
            d_parts[0],
            w_u[:MAIN],
        ]
        + d_parts[1:],
        axis=1,
    )
    zb = blocks.along_z(wire_b)
    ya = jnp.stack([za, blocks.swap(za, blocks.y)])
    b1, b2 = zb[:, :, : size.first], zb[:, :, size.first :]
    b1 = jnp.stack([b1, blocks.swap(b1, blocks.y)])
    b2 = jnp.stack([b2, blocks.swap(b2, blocks.x)])
    xa = jnp.stack([ya, blocks.swap(ya, blocks.x)], axis=1)
    a_mine = xa.reshape(half * size.tall, size.a_width)
    a_other = blocks.swap(a_mine, blocks.core)
    b1_all = jnp.stack([b1, blocks.swap(b1, blocks.x)], axis=1)
    b2_all = jnp.stack([b2, blocks.swap(b2, blocks.y)])
    b1_mine = b1_all.reshape(half * MAIN, -1)
    b2_mine = b2_all.reshape(half * MAIN, -1)
    b1_other = blocks.swap(b1_mine, blocks.core)
    b2_other = blocks.swap(b2_mine, blocks.core)

    a_rows = size.count * size.tall
    a_other = after(a_other, b1, b2)
    q_rot, kv_mine, n1t, flat = call(
        functools.partial(pre_kernel, size),
        "norm_qkv",
        [
            ((tok_rows, width), BF), ((tok_rows, 2 * kv_width), BF), ((a_rows, tok_rows), BF),
            ((1, size.flat), F32),
        ],
        [((a_rows, size.a_width), BF), ((tok_rows, size.a_width), F32)],
        4 * tok_rows * width * size.a_width,
        (me, tokens, a_mine, a_other, cos, sin, table_a, table_f, owners),
    )
    kv_got = blocks.swap(kv_mine, blocks.x)
    kv = jnp.concatenate([kv_got, kv_mine], axis=0)
    kv = after(kv, b1_mine, b2_mine)
    other = (1 - ctx_index) * tok_rows
    segment_k = jnp.concatenate(
        [lax.dynamic_slice_in_dim(segment_all, other, tok_rows), segment_mine]
    )
    row_k = jnp.concatenate([other + jnp.arange(tok_rows, dtype=jnp.int32), row_mine])
    flag = ctx_index.astype(jnp.int32).reshape(1)
    places = (segment_k[:, None], row_k[:, None], segment_mine[None, :], row_mine[None, :])
    attn, lse = attention(q_rot, kv, places, flag, tok_rows, True)

    main = size.count * MAIN
    slots = main + size.count * TAIL
    layer_out, keep_b, give_b, grad_mid, grad_attn, grad_gain = call(
        functools.partial(mlp_kernel, size, masks),
        "feed_forward",
        [
            ((tok_rows, width), BF), ((main // 2, size.total), BF), ((main // 2, size.total), BF),
            ((tok_rows, width), F32), ((tok_rows, width), BF), ((1, width), F32),
        ],
        [
            ((slots, ff), BF), ((slots, ff), BF), ((slots, size.wide), BF), ((ff, size.wide), BF),
            ((tok_rows, width), F32), ((tok_rows, slots), BF), ((slots, tok_rows), BF),
            ((width, slots), BF), ((tok_rows, width), F32), ((tok_rows, slots), F32),
            ((ff, size.wide), BF), ((size.count * TAIL, 2 * ff), BF),
            ((size.count * TAIL, size.wide), BF),
        ],
        2 * tok_rows * width * (9 * ff + 5 * width),
        (
            me, attn, tokens, cotangent, flat, b1_mine, b1_other, b2_mine, b2_other, table_b,
        ),
    )

    got_b = blocks.swap(give_b, blocks.core)
    grad_q_rot, grad_kv = attention_back(
        q_rot, kv, grad_attn, lse, places, flag, tok_rows, True
    )
    held = blocks.add(keep_b, got_b).reshape(2, 2, blocks.zs, MAIN, size.total)
    h1, h2 = held[..., : size.first], held[..., size.first :]
    give_kv = after(grad_kv[:tok_rows].astype(BF), h1, h2)
    got_kv = blocks.swap(give_kv, blocks.x)
    h1 = blocks.add(h1[:, 0], blocks.swap(h1[:, 1], blocks.x))
    h2 = blocks.add(h2[0], blocks.swap(h2[1], blocks.y))
    got_kv = after(got_kv, h1, h2)

    gx, keep_a, give_a = call(
        functools.partial(post_kernel, size),
        "norm_qkv_back",
        [
            ((tok_rows, width), F32), ((a_rows // 2, size.a_width), BF),
            ((a_rows // 2, size.a_width), BF),
        ],
        [
            ((tok_rows, width + kv_width), F32), ((tok_rows, size.a_width), BF),
            ((1, size.flat), F32),
        ],
        6 * tok_rows * width * size.a_width,
        (
            me, grad_q_rot, grad_kv[tok_rows:], got_kv, cos, sin, n1t, a_mine, a_other, tokens,
            grad_mid, flat, grad_gain, table_a, table_f, owners,
        ),
    )
    h1 = blocks.add(h1[0], blocks.swap(h1[1], blocks.y))
    h2 = blocks.add(h2[0], blocks.swap(h2[1], blocks.x))
    share_b = blocks.sum_z(jnp.concatenate([h1, h2], axis=-1))

    held = blocks.add(keep_a, blocks.swap(give_a, blocks.core))
    held = held.reshape(2, 2, blocks.zs, size.tall, size.a_width)
    held = blocks.add(held[0], blocks.swap(held[1], blocks.y))
    held = blocks.add(held[0], blocks.swap(held[1], blocks.x))
    share_a = blocks.sum_z(held)

    tails = tail_unpack(share_b[:, size.tail : size.tail + size.piece], 2 * ff)
    tail_o = tail_unpack(share_b[:, size.tail_o : size.tail_o + 128], width)
    share_out = jnp.concatenate([share_b[:, size.out : size.out + width], tail_o], axis=0)
    share_gate = jnp.concatenate([share_b[:, :ff], tails[:, :ff]], axis=0)
    share_up = jnp.concatenate([share_b[:, size.up : size.up + ff], tails[:, ff:]], axis=0)
    share_down = jnp.concatenate(
        [share_b[:, size.down_at(c) : size.down_at(c) + width] for c in range(size.downs)], axis=0
    )
    ends = (width, width + kv_width, size.qkv)
    return (
        layer_out, gx, share_a[:rows, : ends[0]].reshape(-1),
        share_a[:rows, ends[0] : ends[1]].reshape(-1),
        share_a[:rows, ends[1] : ends[2]].reshape(-1),
        share_out.reshape(-1), share_gate.reshape(-1), share_up.reshape(-1),
        share_down.reshape(-1), share_a[rows, : size.vec],
    )


def local(
    tokens, q_weight, k_weight, v_weight, o_weight, gate_weight, up_weight, down_weight,
    vectors, doc_lengths, cotangent,
):
    tok_rows, width = tokens.shape
    ctx_count = lax.axis_size("ctx")
    dp_count = lax.axis_size("dp")
    count = dp_count * ctx_count
    seq_tokens = tok_rows * ctx_count
    ctx_index = lax.axis_index("ctx")
    heads = width // HEAD_DIM
    kv_width = KV_HEADS * HEAD_DIM
    ff = gate_weight.shape[0] * count // width

    segment_all, position_all = doc_layout(doc_lengths[0], seq_tokens)
    offset = ctx_index * tok_rows
    row_all = jnp.arange(seq_tokens, dtype=jnp.int32)
    segment_mine = lax.dynamic_slice_in_dim(segment_all, offset, tok_rows)
    position_mine = lax.dynamic_slice_in_dim(position_all, offset, tok_rows)
    row_mine = offset + jnp.arange(tok_rows, dtype=jnp.int32)
    half = HEAD_DIM // 2
    freq = THETA ** (-jnp.arange(half, dtype=F32) * 2.0 / HEAD_DIM)
    position_f = position_mine.astype(F32)[:, None]

    whole_rows = width % count == 0 and ff % count == 0
    if whole_rows and ctx_count == 2 and dp_count % 4 == 0 and count & (count - 1) == 0:
        size = Sizes(width, ff, count, vectors.shape[0], kv_width)
        if size.fits() and (width + kv_width) % 128 == 0:
            angle = position_f * jnp.tile(freq, 128 // half)[None, :]
            sign = np.where(np.arange(128) % HEAD_DIM < half, -1.0, 1.0).astype(np.float32)
            pos = (segment_all, segment_mine, row_mine, jnp.cos(angle), jnp.sin(angle) * sign)
            args = (
                tokens, q_weight, k_weight, v_weight, o_weight, gate_weight, up_weight,
                down_weight, vectors, cotangent,
            )
            return local_blocks(size, Blocks(dp_count, ctx_count), pos, args)

    angle = position_f * freq[None, :]
    cosine = jnp.cos(angle)[:, None, :]
    sine = jnp.sin(angle)[:, None, :]
    inputs = tokens.astype(F32)
    inv_first = lax.rsqrt(jnp.mean(inputs * inputs, axis=-1, keepdims=True) + EPS)

    def whole(part):
        return lax.all_gather(part, AXES, axis=0, tiled=True)

    w_qkv = jnp.concatenate(
        [whole(w).reshape(width, -1) for w in (q_weight, k_weight, v_weight)], axis=1
    )
    w_out = whole(o_weight).reshape(width, width)
    w_gate = whole(gate_weight).reshape(width, ff)
    w_up = whole(up_weight).reshape(width, ff)
    w_down = whole(down_weight).reshape(ff, width)
    flat = whole(vectors).astype(F32)
    ends = [width, width + kv_width, width + 2 * kv_width, 2 * width + 2 * kv_width]
    gain_attn = flat[ends[2] : ends[3]]
    gain_mlp = flat[ends[3] : ends[3] + width]

    n_first = (inputs * inv_first * gain_attn).astype(BF)
    qkv = times(n_first, w_qkv) + flat[: ends[2]]
    q_rot = turn(qkv[:, :width].reshape(tok_rows, heads, HEAD_DIM), cosine, sine)
    q_rot = q_rot.astype(BF).reshape(tok_rows, width)
    k_rot = turn(qkv[:, width : ends[1]].reshape(tok_rows, KV_HEADS, HEAD_DIM), cosine, sine)
    k_rot = k_rot.astype(BF).reshape(tok_rows, kv_width)
    kv_mine = jnp.concatenate([k_rot, qkv[:, ends[1] :].astype(BF)], axis=1)
    kv = lax.all_gather(kv_mine, "ctx", axis=0, tiled=True)
    flag = jnp.ones((1,), jnp.int32)
    places = (segment_all[:, None], row_all[:, None], segment_mine[None, :], row_mine[None, :])
    attn, lse = attention(q_rot, kv, places, flag, seq_tokens, False)
    mid = inputs + times(attn, w_out)
    inv_second = lax.rsqrt(jnp.mean(mid * mid, axis=-1, keepdims=True) + EPS)
    n_second = (mid * inv_second * gain_mlp).astype(BF)
    gate = times(n_second, w_gate)
    up_val = times(n_second, w_up)
    sig = jax.nn.sigmoid(gate)
    act = gate * sig
    hidden = (act * up_val).astype(BF)
    layer_out = (mid + times(hidden, w_down)).astype(BF)

    grad_wdown = inner_rows(hidden, cotangent)
    grad_hidden = times_back(cotangent, w_down)
    grad_gate = (grad_hidden * up_val * (sig * (1.0 + gate * (1.0 - sig)))).astype(BF)
    grad_up = (grad_hidden * act).astype(BF)
    grad_wgate = inner_rows(n_second, grad_gate)
    grad_wup = inner_rows(n_second, grad_up)
    grad_n2 = times_back(grad_gate, w_gate) + times_back(grad_up, w_up)
    grad_mid_norm, grad_gain_mlp = norm_back(mid, inv_second, gain_mlp, grad_n2)
    grad_mid = cotangent.astype(F32) + grad_mid_norm
    grad_branch = grad_mid.astype(BF)
    grad_wout = inner_rows(attn, grad_branch)
    grad_attn = times_back(grad_branch, w_out).astype(BF)
    grad_q_rot, grad_kv = attention_back(
        q_rot, kv, grad_attn, lse, places, flag, seq_tokens, False
    )
    grad_kv_mine = lax.psum_scatter(
        grad_kv.astype(BF), "ctx", scatter_dimension=0, tiled=True
    ).astype(F32)
    grad_q = turn(grad_q_rot.reshape(tok_rows, heads, HEAD_DIM), cosine, -sine)
    grad_k = turn(
        grad_kv_mine[:, :kv_width].reshape(tok_rows, KV_HEADS, HEAD_DIM), cosine, -sine
    )
    grad_qkv = jnp.concatenate(
        [
            grad_q.reshape(tok_rows, width).astype(BF),
            grad_k.reshape(tok_rows, kv_width).astype(BF),
            grad_kv_mine[:, kv_width:].astype(BF),
        ],
        axis=1,
    )
    grad_wqkv = inner_rows(n_first, grad_qkv)
    grad_bias = jnp.sum(grad_qkv.astype(F32), axis=0)
    grad_n1 = times_back(grad_qkv, w_qkv)
    grad_x_norm, grad_gain_attn = norm_back(inputs, inv_first, gain_attn, grad_n1)
    input_grad = grad_mid + grad_x_norm
    used = 3 * width + 2 * kv_width
    padding = jnp.zeros((vectors.shape[0] * count - used,), F32)
    vector_term = jnp.concatenate([grad_bias, grad_gain_attn, grad_gain_mlp, padding])

    def shares(term):
        return lax.psum_scatter(term.reshape(-1), AXES, scatter_dimension=0, tiled=True)

    return (
        layer_out, input_grad, shares(grad_wqkv[:, :width]),
        shares(grad_wqkv[:, width : ends[1]]), shares(grad_wqkv[:, ends[1] :]),
        shares(grad_wout), shares(grad_wgate), shares(grad_wup), shares(grad_wdown),
        shares(vector_term),
    )


def solution(mesh):
    split = P(AXES)
    rows = P(AXES, None)
    in_specs = (rows,) + (split,) * 8 + (P("dp", None), rows)
    out_specs = (rows, rows) + (split,) * 8
    return jax.shard_map(local, mesh=mesh, in_specs=in_specs, out_specs=out_specs, check_vma=False)
```

```python
import functools

import jax
import jax.numpy as jnp
import numpy as np
from jax import lax
from jax.experimental import pallas as pl
from jax.experimental.pallas import tpu as pltpu
from jax.sharding import PartitionSpec as P

KV_HEADS = 3
HEAD_DIM = 64

EPS = 1e-06
THETA = 100000.0
NEG_FILL = -1e30
AXES = ("dp", "ctx")
BF = jnp.bfloat16
F32 = jnp.float32


def times(left, right):
    return jnp.dot(left, right, preferred_element_type=F32)


def inner_rows(left, right):
    return lax.dot_general(left, right, (((0,), (0,)), ((), ())), preferred_element_type=F32)


def times_back(left, right):
    return lax.dot_general(left, right, (((1,), (1,)), ((), ())), preferred_element_type=F32)


def norm_back(values, inv, gain, grad):
    scaled = grad * gain
    dot = jnp.mean(scaled * values, axis=-1, keepdims=True)
    grad_values = inv * scaled - values * (inv * inv * inv * dot)
    grad_gain = jnp.sum(grad * values * inv, axis=0)
    return grad_values, grad_gain


def turn(values, cosine, sine):
    half = values.shape[-1] // 2
    first = values[..., :half]
    second = values[..., half:]
    return jnp.concatenate(
        [first * cosine - second * sine, second * cosine + first * sine], axis=-1
    )


def doc_layout(lengths, count):
    ends = jnp.cumsum(lengths)
    place = jnp.arange(count, dtype=jnp.int32)
    segment = jnp.sum((place[:, None] >= ends[None, :-1]).astype(jnp.int32), axis=1)
    starts = ends - lengths
    picked = segment[:, None] == jnp.arange(lengths.shape[0], dtype=jnp.int32)[None, :]
    first = jnp.sum(jnp.where(picked, starts[None, :], 0), axis=1)
    return (segment, place - first)


def fill_bias(bias, seg_k, row_k, seg_q, row_q):
    allowed = (seg_k[...] == seg_q[...]) & (row_k[...] <= row_q[...])
    bias[...] = jnp.where(allowed, 0.0, NEG_FILL)


def key_range(full, total, short, rows, block, at, causal):
    start = 0 if full else total - short
    stop = total - rows + (at + 1) * block if causal else total
    return start, stop


def attn_fwd_kernel(
    heads, block, short, causal, flag, q_ref, kv_ref, seg_k, row_k, seg_q, row_q,
    out_ref, lse_ref, qs, ks, vts, bias, out_t,
):
    rows = q_ref.shape[0]
    total = kv_ref.shape[0]
    kv_width = KV_HEADS * HEAD_DIM
    group = heads // KV_HEADS
    fill_bias(bias, seg_k, row_k, seg_q, row_q)
    for h in range(heads):
        qs[h] = q_ref[:, h * HEAD_DIM : (h + 1) * HEAD_DIM] * BF(HEAD_DIM**-0.5)
    for g in range(KV_HEADS):
        ks[g] = kv_ref[:, g * HEAD_DIM : (g + 1) * HEAD_DIM]
    vts[...] = jnp.transpose(kv_ref[:, kv_width:].astype(F32)).astype(BF)

    def run(full):
        @pl.loop(0, KV_HEADS)
        def _(g):
            v_rows = pl.ds(pl.multiple_of(g * HEAD_DIM, HEAD_DIM), HEAD_DIM)
            for j in range(group):
                h = g * group + j
                for at in range(rows // block):
                    start, stop = key_range(full, total, short, rows, block, at, causal)
                    cols = slice(at * block, (at + 1) * block)
                    s = times_back(ks[g, start:stop], qs[h, cols])
                    s = s + bias[start:stop, cols]
                    top = jnp.max(s, axis=0, keepdims=True)
                    p = jnp.exp(s - top)
                    total_p = jnp.sum(p, axis=0, keepdims=True)
                    o = times(vts[v_rows, start:stop], p.astype(BF))
                    out_rows = pl.ds(pl.multiple_of(h * HEAD_DIM, HEAD_DIM), HEAD_DIM)
                    out_t[out_rows, cols] = o / total_p
                    lse_ref[h, :, cols] = top + jnp.log(total_p)

    pl.when(flag[0] != 0)(lambda: run(True))
    pl.when(flag[0] == 0)(lambda: run(False))
    out_ref[...] = jnp.transpose(out_t[...]).astype(BF)


def attn_bwd_kernel(
    heads, block, short, causal, g0, g1,
    flag, q_ref, kv_ref, do_ref, lse_ref, seg_k, row_k, seg_q, row_q,
    dq_ref, dk_ref, dv_ref, qs, ks, vs, kts, dos, bias, dq_t, dk, dv,
):
    rows = q_ref.shape[0]
    total = kv_ref.shape[0]
    kv_width = KV_HEADS * HEAD_DIM
    group = heads // KV_HEADS
    fill_bias(bias, seg_k, row_k, seg_q, row_q)
    for h in range(g0 * group, g1 * group):
        lanes = slice(h * HEAD_DIM, (h + 1) * HEAD_DIM)
        qs[h - g0 * group] = q_ref[:, lanes] * BF(HEAD_DIM**-0.5)
        dos[h - g0 * group] = do_ref[:, lanes]
    for g in range(g0, g1):
        ks[g - g0] = kv_ref[:, g * HEAD_DIM : (g + 1) * HEAD_DIM]
        vs[g - g0] = kv_ref[:, kv_width + g * HEAD_DIM : kv_width + (g + 1) * HEAD_DIM]
    for g in range(g1 - g0):
        kts[g] = jnp.transpose(ks[g].astype(F32)).astype(BF)
    dk[...] = jnp.zeros_like(dk)
    dv[...] = jnp.zeros_like(dv)

    def run(full):
        @pl.loop(0, g1 - g0)
        def _(g):
            for j in range(group):
                h = g * group + j
                for at in range(rows // block):
                    start, stop = key_range(full, total, short, rows, block, at, causal)
                    cols = slice(at * block, (at + 1) * block)
                    q = qs[h, cols]
                    do = dos[h, cols]
                    s = times_back(ks[g, start:stop], q)
                    p = jnp.exp(s + bias[start:stop, cols] - lse_ref[g0 * group + h, :, cols])
                    dp = times_back(vs[g, start:stop], do)
                    t = p * dp
                    inner = jnp.sum(t, axis=0, keepdims=True)
                    ds = (t - p * inner).astype(BF)
                    dk[g, start:stop] += times(ds, q)
                    dv[g, start:stop] += times(p.astype(BF), do)
                    dq = times(kts[g, :, start:stop], ds)
                    out_rows = pl.ds(pl.multiple_of(h * HEAD_DIM, HEAD_DIM), HEAD_DIM)
                    dq_t[out_rows, cols] = dq * HEAD_DIM**-0.5

    pl.when(flag[0] != 0)(lambda: run(True))
    pl.when(flag[0] == 0)(lambda: run(False))
    dq_ref[...] = jnp.transpose(dq_t[...])
    for g in range(g1 - g0):
        dk_ref[:, g * HEAD_DIM : (g + 1) * HEAD_DIM] = dk[g]
        dv_ref[:, g * HEAD_DIM : (g + 1) * HEAD_DIM] = dv[g]


VM = pl.BlockSpec(memory_space=pltpu.VMEM)
SM = pl.BlockSpec(memory_space=pltpu.SMEM)


def attn_cost(rows, total, heads, products):
    return pl.CostEstimate(
        flops=8 * products * rows * total * heads * HEAD_DIM,
        bytes_accessed=4 * (rows + total) * heads * HEAD_DIM,
        transcendentals=rows * total * heads,
    )


def attention(q, kv, places, flag, short, causal):
    rows, width = q.shape
    total = kv.shape[0]
    heads = width // HEAD_DIM
    block = min(rows, 256)
    return pl.pallas_call(
        functools.partial(attn_fwd_kernel, heads, block, short, causal),
        out_shape=(
            jax.ShapeDtypeStruct((rows, width), BF),
            jax.ShapeDtypeStruct((heads, 1, rows), F32),
        ),
        in_specs=[SM] + [VM] * 6,
        out_specs=(VM, VM),
        scratch_shapes=[
            pltpu.VMEM((heads, rows, HEAD_DIM), BF),
            pltpu.VMEM((KV_HEADS, total, HEAD_DIM), BF),
            pltpu.VMEM((KV_HEADS * HEAD_DIM, total), BF),
            pltpu.VMEM((total, rows), F32),
            pltpu.VMEM((width, rows), F32),
        ],
        compiler_params=pltpu.CompilerParams(vmem_limit_bytes=32 * 2**20),
        cost_estimate=attn_cost(rows, total, heads, 2),
        name="attn_fwd",
    )(flag, q, kv, *places)


def attention_back(q, kv, grad_out, lse, places, flag, short, causal, g0, g1):
    rows, width = q.shape
    total = kv.shape[0]
    heads = width // HEAD_DIM
    block = min(rows, 256)
    keys = g1 - g0
    mine = heads // KV_HEADS * keys
    return pl.pallas_call(
        functools.partial(attn_bwd_kernel, heads, block, short, causal, g0, g1),
        out_shape=(
            jax.ShapeDtypeStruct((rows, mine * HEAD_DIM), F32),
            jax.ShapeDtypeStruct((total, keys * HEAD_DIM), F32),
            jax.ShapeDtypeStruct((total, keys * HEAD_DIM), F32),
        ),
        in_specs=[SM] + [VM] * 8,
        out_specs=(VM, VM, VM),
        scratch_shapes=[
            pltpu.VMEM((mine, rows, HEAD_DIM), BF),
            pltpu.VMEM((keys, total, HEAD_DIM), BF),
            pltpu.VMEM((keys, total, HEAD_DIM), BF),
            pltpu.VMEM((keys, HEAD_DIM, total), BF),
            pltpu.VMEM((mine, rows, HEAD_DIM), BF),
            pltpu.VMEM((total, rows), F32),
            pltpu.VMEM((mine * HEAD_DIM, rows), F32),
            pltpu.VMEM((keys, total, HEAD_DIM), F32),
            pltpu.VMEM((keys, total, HEAD_DIM), F32),
        ],
        compiler_params=pltpu.CompilerParams(vmem_limit_bytes=32 * 2**20),
        cost_estimate=attn_cost(rows, total, mine, 5),
        name="attn_bwd",
    )(flag, q, kv, grad_out, lse, *places)


TAIL = 2
MAIN = 16
PIECES = MAIN // TAIL


class Blocks:
    def __init__(self, dp_count, ctx_count):
        self.count = dp_count * ctx_count
        self.x = 1
        self.core = ctx_count
        self.y = 2 * ctx_count
        self.z = 4 * ctx_count
        self.zs = dp_count // 4
        self.masks = []
        for p in range(self.count):
            z, x = p % self.zs, p // self.zs % 2
            y, core = p // (2 * self.zs) % 2, p // (4 * self.zs)
            self.masks.append(x * self.x + y * self.y + core * self.core + z * self.z)

    def swap(self, values, mask):
        perm = [(i, i ^ mask) for i in range(self.count)]
        return lax.ppermute(values, AXES, perm)

    def along_z(self, mine):
        return jnp.stack([mine] + [self.swap(mine, d * self.z) for d in range(1, self.zs)])

    def add(self, keep, got):
        return (keep.astype(F32) + got.astype(F32)).astype(BF)

    def sum_z(self, held):
        got = [self.swap(held[d], d * self.z).astype(F32) for d in range(1, self.zs)]
        return functools.reduce(jnp.add, got, held[0].astype(F32))


class Sizes:
    def __init__(self, width, ff, count, vec, kv_width):
        self.width, self.ff, self.count, self.vec = width, ff, count, vec
        self.rows = width // count
        self.f_rows = ff // count
        up = lambda n: (n + 127) // 128 * 128
        self.wide = up(width)
        self.qkv = width + 2 * kv_width
        self.a_width = up(self.qkv)
        self.tall = (self.rows + 1 + 7) // 8 * 8
        self.downs = self.f_rows // MAIN
        self.piece = 2 * ff // PIECES
        self.gate = 0
        self.tail = ff
        self.tail_o = self.tail + self.piece
        self.out = self.tail_o + 128
        self.down0 = self.out + self.wide
        self.first = self.down0 + self.wide
        self.second = ff + (self.downs - 1) * self.wide
        self.flat = self.a_width + 2 * self.wide

    def down_at(self, c):
        return (0, self.down0) if c == 0 else (1, self.ff + (c - 1) * self.wide)

    def fits(self):
        return (
            self.rows == MAIN + TAIL
            and self.f_rows % MAIN == 0
            and self.piece % 128 == 0
            and self.ff % 256 == 0
            and self.wide <= 128 * PIECES
            and self.vec <= 128
        )


def slot_tables(size, masks):
    far = -(2**20)
    a = [(masks[s // size.tall], s % size.tall) for s in range(size.count * size.tall)]
    a = [(m, i if i < size.rows else far) for m, i in a]
    b = [(masks[s // MAIN], s % MAIN) for s in range(size.count * MAIN)]
    b += [(masks[s // TAIL], MAIN + s % TAIL) for s in range(size.count * TAIL)]
    flat = []
    natural = [(0, size.qkv, size.a_width), (size.qkv, size.width, size.wide)]
    natural += [(size.qkv + size.width, size.width, size.wide)]
    for start, used, room in natural:
        for c in range(room):
            at = start + c
            flat.append((at // size.vec, at % size.vec) if c < used else (far, far))
    owners = np.asarray(masks, np.int32)[:, None]
    as_rows = lambda pairs: np.ascontiguousarray(np.asarray(pairs, np.int32).T)
    return as_rows(a), as_rows(b), as_rows(flat), owners


def place_matrix(size, me, table):
    feature = size.rows * (me ^ table[0:1, :]) + table[1:2, :]
    shape = (size.width, feature.shape[1])
    at = lax.broadcasted_iota(jnp.int32, shape, 0)
    return jnp.where(at == feature, 1.0, 0.0).astype(BF)


def vector_lanes(table):
    inside = lax.broadcasted_iota(jnp.int32, (128, table.shape[1]), 0)
    return jnp.where(inside == table[1:2, :], 1.0, 0.0).astype(BF)


def split_two(values):
    high = values.astype(BF)
    return high, (values - high.astype(F32)).astype(BF)


def swap_halves(u):
    rolled_back = pltpu.roll(u, 128 - HEAD_DIM // 2, 1)
    rolled = pltpu.roll(u, HEAD_DIM // 2, 1)
    lane = lax.broadcasted_iota(jnp.int32, u.shape, 1)
    return jnp.where(lane % HEAD_DIM < HEAD_DIM // 2, rolled_back, rolled)


def pre_kernel(
    size, me_ref, x_ref, wm_ref, wo_ref, cos_ref, sin_ref, table_a, table_f, owner_ref,
    q_ref, kv_ref, n1t_ref, flat_ref, w, qkv,
):
    me = me_ref[0]
    half = wm_ref.shape[0]
    w[:half] = wm_ref[...]
    w[half:] = wo_ref[...]
    shape = (size.count, 2 * half)
    row = lax.broadcasted_iota(jnp.int32, shape, 0) * size.tall + size.rows
    row = lax.broadcasted_iota(jnp.int32, shape, 1) == row
    packed = times(jnp.where(row, 1.0, 0.0).astype(BF), w[:, :128]).astype(BF)
    table = table_f[...]
    spread = times(packed, vector_lanes(table))
    mine = table[0:1, :] == (me ^ owner_ref[...])
    flat = jnp.sum(jnp.where(mine, spread, 0.0), axis=0, keepdims=True)
    flat_ref[...] = flat
    gain = flat[:, size.a_width : size.a_width + size.width]
    x = x_ref[...].astype(F32)
    inv = lax.rsqrt(jnp.mean(x * x, axis=-1, keepdims=True) + EPS)
    n1 = (x * inv * gain).astype(BF)
    n1a = times(n1, place_matrix(size, me, table_a[...]))
    qkv[...] = times(n1a.astype(BF), w[...]) + flat[:, : size.a_width]
    n1t_ref[...] = jnp.transpose(n1a).astype(BF)
    kv_width = kv_ref.shape[1] // 2
    for t in range((size.width + kv_width) // 128):
        u = qkv[:, t * 128 : (t + 1) * 128]
        qkv[:, t * 128 : (t + 1) * 128] = u * cos_ref[...] + swap_halves(u) * sin_ref[...]
    q_ref[...] = qkv[:, : size.width].astype(BF)
    kv_ref[...] = qkv[:, size.width : size.qkv].astype(BF)


def tail_place(size, c):
    shape = (size.count * TAIL, size.count * MAIN)
    q = lax.broadcasted_iota(jnp.int32, shape, 0)
    at = lax.broadcasted_iota(jnp.int32, shape, 1)
    want = (q // TAIL) * MAIN + c * TAIL + q % TAIL
    return jnp.where(at == want, 1.0, 0.0).astype(BF)


def tail_place_back(size, c):
    shape = (size.count * MAIN, size.count * TAIL)
    at = lax.broadcasted_iota(jnp.int32, shape, 0)
    q = lax.broadcasted_iota(jnp.int32, shape, 1)
    want = (q // TAIL) * MAIN + c * TAIL + q % TAIL
    return jnp.where(at == want, 1.0, 0.0).astype(BF)


def mlp_kernel(
    size, masks, me_ref, attn_ref, x_ref, cot_ref, flat_ref, b1m, b1o, b2m, b2o, table_b,
    out_ref, keep1, give1, keep2, give2, gmid_ref, gattn_ref, ggain_ref,
    wg, wu, wo, wd, mid, n2s, n2t, place, acc, gacc, dwd, tails, tail_o,
):
    me = me_ref[0]
    width, ff = size.width, size.ff
    half = b1m.shape[0]
    main = 2 * half
    halves = (
        (slice(0, half), (b1m, b2m), (keep1, keep2)),
        (slice(half, main), (b1o, b2o), (give1, give2)),
    )
    place[...] = place_matrix(size, me, table_b[...])
    for part, (b1, b2), _ in halves:
        wg[part] = b1[:, size.gate : size.gate + ff]
        wu[part] = b2[:, : ff]
        wo[part] = b1[:, size.out : size.out + size.wide]
    for c in range(PIECES):
        sel = tail_place(size, c)
        cols = slice(size.tail, size.tail + size.piece)
        got = times(sel[:, :half], b1m[:, cols]) + times(sel[:, half:], b1o[:, cols])
        target = wg if c * size.piece < ff else wu
        at = c * size.piece % ff
        target[main:, at : at + size.piece] = got.astype(BF)
        if c * 128 < size.wide:
            cols = slice(size.tail_o, size.tail_o + 128)
            got = times(sel[:, :half], b1m[:, cols]) + times(sel[:, half:], b1o[:, cols])
            wo[main:, c * 128 : (c + 1) * 128] = got.astype(BF)
    for p in range(size.count):
        _, got, _ = halves[p // (size.count // 2)]
        rows = slice(p * MAIN % half, p * MAIN % half + MAIN)
        owner = me ^ masks[p]
        for c in range(size.downs):
            which, at = size.down_at(c)
            src = got[which][rows, at : at + size.wide]
            to = pl.multiple_of(owner * size.f_rows + c * MAIN, MAIN)
            wd[pl.ds(to, MAIN), :] = src
    attn_s = times(attn_ref[...], place[...])
    m = x_ref[...].astype(F32) + times(attn_s.astype(BF), wo[:, :width])
    mid[...] = m
    inv = lax.rsqrt(jnp.mean(m * m, axis=-1, keepdims=True) + EPS)
    lo = size.a_width + size.wide
    gain = flat_ref[:, lo : lo + width]
    n2 = (m * inv * gain).astype(BF)
    spread = times(n2, place[...])
    n2s[...] = spread.astype(BF)
    n2t[...] = jnp.transpose(spread).astype(BF)
    acc[...] = jnp.zeros_like(acc)
    gacc[...] = jnp.zeros_like(gacc)
    step = 512 if ff % 512 == 0 else 256

    @pl.loop(0, ff // step)
    def _(b):
        at = pl.multiple_of(b * step, step)
        cols = pl.ds(at, step)
        gate = times(n2s[...], wg[:, cols])
        up = times(n2s[...], wu[:, cols])
        sig = 1.0 / (1.0 + jnp.exp(-gate))
        act = gate * sig
        h = act * up
        gh = times_back(cot_ref[...], wd[cols, :width])
        gg = (gh * up * (sig * (1.0 + gate * (1.0 - sig)))).astype(BF)
        gu = (gh * act).astype(BF)
        acc[...] += times(h.astype(BF), wd[cols, :width])
        dwd[cols, :width] = times(jnp.transpose(h).astype(BF), cot_ref[...]).astype(BF)
        gacc[...] += times_back(gg, wg[:, cols]) + times_back(gu, wu[:, cols])
        for k, (grad, keep, give) in enumerate(((gg, keep1, give1), (gu, keep2, give2))):
            dw = times(n2t[...], grad).astype(BF)
            keep[:, cols] = dw[:half]
            give[:, cols] = dw[half:main]
            tails[:, pl.ds(pl.multiple_of(k * ff + at, 128), step)] = dw[main:]

    m = mid[...]
    inv = lax.rsqrt(jnp.mean(m * m, axis=-1, keepdims=True) + EPS)
    out_ref[...] = (m + acc[...]).astype(BF)
    high, low = split_two(gacc[...])
    gn2 = times_back(high, place[...]) + times_back(low, place[...])
    scaled = gn2 * gain
    dot = jnp.mean(scaled * m, axis=-1, keepdims=True)
    ggain_ref[...] = jnp.sum(gn2 * m * inv, axis=0, keepdims=True)
    gmid = cot_ref[...].astype(F32) + inv * scaled - m * (inv * inv * inv * dot)
    gmid_ref[...] = gmid
    branch = gmid.astype(BF)
    gattn = times_back(branch, wo[:, :width]).astype(BF)
    gattn_ref[...] = times_back(gattn, place[...]).astype(BF)
    dwo = times(jnp.transpose(attn_s).astype(BF), branch).astype(BF)
    tail_o[...] = jnp.zeros_like(tail_o)
    tail_o[:, :width] = dwo[main:]
    for part, _, (term, _) in halves:
        term[:, size.out : size.out + width] = dwo[part]
    wire = jnp.zeros((main, size.piece), F32)
    wire_o = jnp.zeros((main, 128), F32)
    for c in range(PIECES):
        sel = tail_place_back(size, c)
        wire += times(sel, tails[:, c * size.piece : (c + 1) * size.piece])
        if c * 128 < size.wide:
            wire_o += times(sel, tail_o[:, c * 128 : (c + 1) * 128])
    for part, _, (term, _) in halves:
        term[:, size.tail : size.tail + size.piece] = wire[part].astype(BF)
        term[:, size.tail_o : size.tail_o + 128] = wire_o[part].astype(BF)
    for p in range(size.count):
        _, _, terms = halves[p // (size.count // 2)]
        rows = slice(p * MAIN % half, p * MAIN % half + MAIN)
        owner = me ^ masks[p]
        for c in range(size.downs):
            which, at = size.down_at(c)
            src = pl.multiple_of(owner * size.f_rows + c * MAIN, MAIN)
            terms[which][rows, at : at + size.wide] = dwd[pl.ds(src, MAIN), :]


def post_kernel(
    size, me_ref, dq_ref, dkv_ref, got_ref, cos_ref, sin_ref, n1t_ref, wm_ref, wo_ref, x_ref,
    gmid_ref, flat_ref, ggain_ref, table_a, table_f, owner_ref,
    gx_ref, keep_ref, give_ref, turn_buf, grad, vec_row,
):
    me = me_ref[0]
    width = size.width
    half = wm_ref.shape[0]
    kv_width = dkv_ref.shape[1] // 2
    turned = width + kv_width
    turn_buf[:, :width] = dq_ref[...]
    dkv = dkv_ref[...] + got_ref[...].astype(F32)
    turn_buf[:, width:] = dkv[:, :kv_width]
    grad[...] = jnp.zeros_like(grad)
    for t in range(turned // 128):
        u = turn_buf[:, t * 128 : (t + 1) * 128]
        back = u * cos_ref[...] - swap_halves(u) * sin_ref[...]
        grad[:, t * 128 : (t + 1) * 128] = back.astype(BF)
    grad[:, turned : turned + kv_width] = dkv[:, kv_width:].astype(BF)
    g = grad[...]
    place = place_matrix(size, me, table_a[...])
    high_m, low_m = split_two(times_back(g, wm_ref[...]))
    high_o, low_o = split_two(times_back(g, wo_ref[...]))
    gn1 = times_back(high_m, place[:, :half]) + times_back(high_o, place[:, half:])
    gn1 += times_back(low_m, place[:, :half]) + times_back(low_o, place[:, half:])
    x = x_ref[...].astype(F32)
    inv = lax.rsqrt(jnp.mean(x * x, axis=-1, keepdims=True) + EPS)
    gain = flat_ref[:, size.a_width : size.a_width + width]
    scaled = gn1 * gain
    dot = jnp.mean(scaled * x, axis=-1, keepdims=True)
    gx_ref[...] = gmid_ref[...] + inv * scaled - x * (inv * inv * inv * dot)
    vec_row[...] = jnp.zeros_like(vec_row)
    vec_row[:, : size.a_width] = jnp.sum(g.astype(F32), axis=0, keepdims=True)
    vec_row[:, size.a_width : size.a_width + width] = jnp.sum(gn1 * x * inv, axis=0, keepdims=True)
    lo = size.a_width + size.wide
    vec_row[:, lo : lo + width] = ggain_ref[...]
    table = table_f[...]
    mine = table[0:1, :] == (me ^ owner_ref[...])
    packed = times_back(jnp.where(mine, vec_row[...], 0.0).astype(BF), vector_lanes(table))
    shape = (half, size.count)
    for part, term in ((0, keep_ref), (1, give_ref)):
        rows = slice(part * half, (part + 1) * half)
        dw = times(n1t_ref[rows], g)
        term[...] = dw.astype(BF)
        want = lax.broadcasted_iota(jnp.int32, shape, 1) * size.tall + size.rows - part * half
        here = lax.broadcasted_iota(jnp.int32, shape, 0) == want
        extra = times(jnp.where(here, 1.0, 0.0).astype(BF), packed.astype(BF))
        term[:, :128] = (dw[:, :128] + extra).astype(BF)


def call(kernel, name, out_shape, scratch, flops, args, vmem=48):
    shapes = [jax.ShapeDtypeStruct(s, t) for s, t in out_shape]
    total = sum(int(np.prod(a.shape)) * a.dtype.itemsize for a in args)
    return pl.pallas_call(
        kernel,
        out_shape=shapes,
        in_specs=[SM] + [VM] * (len(args) - 1),
        out_specs=[VM] * len(shapes),
        scratch_shapes=[pltpu.VMEM(s, t) for s, t in scratch],
        compiler_params=pltpu.CompilerParams(vmem_limit_bytes=vmem * 2**20),
        cost_estimate=pl.CostEstimate(flops=flops, bytes_accessed=total, transcendentals=0),
        name=name,
    )(*args)


def pad_to(values, rows, columns):
    return jnp.pad(values, ((0, rows - values.shape[0]), (0, columns - values.shape[1])))


def tail_pack(rows, piece):
    rows = pad_to(rows, TAIL, PIECES * piece)
    return rows.reshape(TAIL, PIECES, piece).transpose(1, 0, 2).reshape(MAIN, piece)


def tail_unpack(wire, used):
    piece = wire.shape[1]
    rows = wire.reshape(PIECES, TAIL, piece).transpose(1, 0, 2).reshape(TAIL, PIECES * piece)
    return rows[:, :used]


def tie(*values):
    return lax.optimization_barrier(values)


def local_blocks(size, blocks, pos, args):
    (
        tokens, q_weight, k_weight, v_weight, o_weight, gate_weight, up_weight, down_weight,
        vectors, cotangent,
    ) = args
    tok_rows, width = tokens.shape
    ff, rows = size.ff, size.rows
    kv_width = KV_HEADS * HEAD_DIM
    ctx_index = lax.axis_index("ctx")
    me = (lax.axis_index("dp") * lax.axis_size("ctx") + ctx_index).astype(jnp.int32).reshape(1)
    masks = blocks.masks
    half = size.count // 2
    table_a, table_b, table_f, owners = slot_tables(size, masks)
    segment_all, segment_mine, row_mine, cos, sin = pos

    joined_w = jnp.concatenate(
        [w.reshape(rows, -1) for w in (q_weight, k_weight, v_weight)], axis=1
    )
    vec_row = pad_to(vectors.reshape(1, -1), size.tall - rows, size.a_width)
    wire_a = jnp.concatenate([pad_to(joined_w, rows, size.a_width), vec_row], axis=0)
    za = blocks.along_z(wire_a)
    w_g, w_u = gate_weight.reshape(rows, ff), up_weight.reshape(rows, ff)
    w_o = o_weight.reshape(rows, width)
    w_d = pad_to(down_weight.reshape(size.f_rows, width), size.f_rows, size.wide)
    d_parts = [w_d[c * MAIN : (c + 1) * MAIN] for c in range(size.downs)]
    wire_1 = jnp.concatenate(
        [
            w_g[:MAIN],
            tail_pack(jnp.concatenate([w_g[MAIN:], w_u[MAIN:]], axis=1), size.piece),
            tail_pack(w_o[MAIN:], 128),
            pad_to(w_o[:MAIN], MAIN, size.wide),
        ]
        + d_parts[:1],
        axis=1,
    )
    wire_2 = jnp.concatenate([w_u[:MAIN]] + d_parts[1:], axis=1)
    xa = jnp.stack([za, blocks.swap(za, blocks.x)])
    xa, wire_1, wire_2 = tie(xa, wire_1, wire_2)
    z1 = blocks.along_z(wire_1)
    z2 = blocks.along_z(wire_2)
    x1 = jnp.stack([z1, blocks.swap(z1, blocks.x)])
    y2 = jnp.stack([z2, blocks.swap(z2, blocks.y)])
    a_all = jnp.stack([xa, blocks.swap(xa, blocks.y)])
    a_mine = a_all.reshape(half * size.tall, size.a_width)
    a_other = blocks.swap(a_mine, blocks.core)
    a_rows = size.count * size.tall
    q_rot, kv_mine, n1t, flat = call(
        functools.partial(pre_kernel, size),
        "norm_qkv",
        [
            ((tok_rows, width), BF), ((tok_rows, 2 * kv_width), BF), ((a_rows, tok_rows), BF),
            ((1, size.flat), F32),
        ],
        [((a_rows, size.a_width), BF), ((tok_rows, size.a_width), F32)],
        4 * tok_rows * width * size.a_width,
        (me, tokens, a_mine, a_other, cos, sin, table_a, table_f, owners),
    )
    kv_got = blocks.swap(kv_mine, blocks.x)
    kv_got, x1, y2 = tie(kv_got, x1, y2)
    b1_all = jnp.stack([x1, blocks.swap(x1, blocks.y)])
    b2_all = jnp.stack([y2, blocks.swap(y2, blocks.x)], axis=1)
    b1_mine = b1_all.reshape(half * MAIN, -1)
    b2_mine = b2_all.reshape(half * MAIN, -1)
    kv = jnp.concatenate([kv_got, kv_mine], axis=0)
    other = (1 - ctx_index) * tok_rows
    segment_k = jnp.concatenate(
        [lax.dynamic_slice_in_dim(segment_all, other, tok_rows), segment_mine]
    )
    row_k = jnp.concatenate([other + jnp.arange(tok_rows, dtype=jnp.int32), row_mine])
    flag = ctx_index.astype(jnp.int32).reshape(1)
    places = (segment_k[:, None], row_k[:, None], segment_mine[None, :], row_mine[None, :])
    attn, lse = attention(q_rot, kv, places, flag, tok_rows, True)

    attn, b2_mine = tie(attn, b2_mine)
    attn, b1_mine = tie(attn, b1_mine)
    b1_other = blocks.swap(b1_mine, blocks.core)
    b2_other = blocks.swap(b2_mine, blocks.core)
    main = size.count * MAIN
    slots = main + size.count * TAIL
    layer_out, keep1, give1, keep2, give2, grad_mid, grad_attn, grad_gain = call(
        functools.partial(mlp_kernel, size, masks),
        "feed_forward",
        [
            ((tok_rows, width), BF),
            ((main // 2, size.first), BF), ((main // 2, size.first), BF),
            ((main // 2, size.second), BF), ((main // 2, size.second), BF),
            ((tok_rows, width), F32), ((tok_rows, width), BF), ((1, width), F32),
        ],
        [
            ((slots, ff), BF), ((slots, ff), BF), ((slots, size.wide), BF), ((ff, size.wide), BF),
            ((tok_rows, width), F32), ((tok_rows, slots), BF), ((slots, tok_rows), BF),
            ((width, slots), BF), ((tok_rows, width), F32), ((tok_rows, slots), F32),
            ((ff, size.wide), BF), ((size.count * TAIL, 2 * ff), BF),
            ((size.count * TAIL, size.wide), BF),
        ],
        2 * tok_rows * width * (9 * ff + 5 * width),
        (
            me, attn, tokens, cotangent, flat, b1_mine, b1_other, b2_mine, b2_other, table_b,
        ),
    )

    got1 = blocks.swap(give1, blocks.core)
    got2 = blocks.swap(give2, blocks.core)
    grads = [
        attention_back(q_rot, kv, grad_attn, lse, places, flag, tok_rows, True, g, g + 1)
        for g in range(KV_HEADS - 1)
    ]
    shape = (2, 2, blocks.zs, MAIN, -1)
    h1 = blocks.add(keep1, got1).reshape(shape)
    h2 = blocks.add(keep2, got2).reshape(shape)
    grad_last, h1, h2 = tie(grad_attn, h1, h2)
    grads.append(
        attention_back(
            q_rot, kv, grad_last, lse, places, flag, tok_rows, True, KV_HEADS - 1, KV_HEADS
        )
    )
    grad_q_rot = jnp.concatenate([g[0] for g in grads], axis=1)
    grad_kv = jnp.concatenate([g[1] for g in grads] + [g[2] for g in grads], axis=1)
    h1 = blocks.add(h1[0], blocks.swap(h1[1], blocks.y))
    h2 = blocks.add(h2[:, 0], blocks.swap(h2[:, 1], blocks.x))
    give_kv, h1, h2 = tie(grad_kv[:tok_rows].astype(BF), h1, h2)
    got_kv = blocks.swap(give_kv, blocks.x)

    gx, keep_a, give_a = call(
        functools.partial(post_kernel, size),
        "norm_qkv_back",
        [
            ((tok_rows, width), F32), ((a_rows // 2, size.a_width), BF),
            ((a_rows // 2, size.a_width), BF),
        ],
        [
            ((tok_rows, width + kv_width), F32), ((tok_rows, size.a_width), BF),
            ((1, size.flat), F32),
        ],
        6 * tok_rows * width * size.a_width,
        (
            me, grad_q_rot, grad_kv[tok_rows:], got_kv, cos, sin, n1t, a_mine, a_other, tokens,
            grad_mid, flat, grad_gain, table_a, table_f, owners,
        ),
    )
    h1 = blocks.add(h1[0], blocks.swap(h1[1], blocks.x))
    h2 = blocks.add(h2[0], blocks.swap(h2[1], blocks.y))
    share2 = blocks.sum_z(h2)
    held = blocks.add(keep_a, blocks.swap(give_a, blocks.core))
    held, share2, h1 = tie(held, share2, h1)
    held = held.reshape(2, 2, blocks.zs, size.tall, size.a_width)
    held = blocks.add(held[0], blocks.swap(held[1], blocks.y))
    share1 = blocks.sum_z(h1)
    held, share1 = tie(held, share1)
    held = blocks.add(held[0], blocks.swap(held[1], blocks.x))
    share_a = blocks.sum_z(held)

    tails = tail_unpack(share1[:, size.tail : size.tail + size.piece], 2 * ff)
    tail_o = tail_unpack(share1[:, size.tail_o : size.tail_o + 128], width)
    share_out = jnp.concatenate([share1[:, size.out : size.out + width], tail_o], axis=0)
    share_gate = jnp.concatenate([share1[:, :ff], tails[:, :ff]], axis=0)
    share_up = jnp.concatenate([share2[:, :ff], tails[:, ff:]], axis=0)
    downs = [size.down_at(c) for c in range(size.downs)]
    share_down = jnp.concatenate(
        [(share1, share2)[which][:, at : at + width] for which, at in downs], axis=0
    )
    ends = (width, width + kv_width, size.qkv)
    return (
        layer_out, gx, share_a[:rows, : ends[0]].reshape(-1),
        share_a[:rows, ends[0] : ends[1]].reshape(-1),
        share_a[:rows, ends[1] : ends[2]].reshape(-1),
        share_out.reshape(-1), share_gate.reshape(-1), share_up.reshape(-1),
        share_down.reshape(-1), share_a[rows, : size.vec],
    )


def local(
    tokens, q_weight, k_weight, v_weight, o_weight, gate_weight, up_weight, down_weight,
    vectors, doc_lengths, cotangent,
):
    tok_rows, width = tokens.shape
    ctx_count = lax.axis_size("ctx")
    dp_count = lax.axis_size("dp")
    count = dp_count * ctx_count
    seq_tokens = tok_rows * ctx_count
    ctx_index = lax.axis_index("ctx")
    heads = width // HEAD_DIM
    kv_width = KV_HEADS * HEAD_DIM
    ff = gate_weight.shape[0] * count // width

    segment_all, position_all = doc_layout(doc_lengths[0], seq_tokens)
    offset = ctx_index * tok_rows
    row_all = jnp.arange(seq_tokens, dtype=jnp.int32)
    segment_mine = lax.dynamic_slice_in_dim(segment_all, offset, tok_rows)
    position_mine = lax.dynamic_slice_in_dim(position_all, offset, tok_rows)
    row_mine = offset + jnp.arange(tok_rows, dtype=jnp.int32)
    half = HEAD_DIM // 2
    freq = THETA ** (-jnp.arange(half, dtype=F32) * 2.0 / HEAD_DIM)
    position_f = position_mine.astype(F32)[:, None]

    whole_rows = width % count == 0 and ff % count == 0
    if whole_rows and ctx_count == 2 and dp_count % 4 == 0 and count & (count - 1) == 0:
        size = Sizes(width, ff, count, vectors.shape[0], kv_width)
        if size.fits() and (width + kv_width) % 128 == 0:
            angle = position_f * jnp.tile(freq, 128 // half)[None, :]
            sign = np.where(np.arange(128) % HEAD_DIM < half, -1.0, 1.0).astype(np.float32)
            pos = (segment_all, segment_mine, row_mine, jnp.cos(angle), jnp.sin(angle) * sign)
            args = (
                tokens, q_weight, k_weight, v_weight, o_weight, gate_weight, up_weight,
                down_weight, vectors, cotangent,
            )
            return local_blocks(size, Blocks(dp_count, ctx_count), pos, args)

    angle = position_f * freq[None, :]
    cosine = jnp.cos(angle)[:, None, :]
    sine = jnp.sin(angle)[:, None, :]
    inputs = tokens.astype(F32)
    inv_first = lax.rsqrt(jnp.mean(inputs * inputs, axis=-1, keepdims=True) + EPS)

    def whole(part):
        return lax.all_gather(part, AXES, axis=0, tiled=True)

    w_qkv = jnp.concatenate(
        [whole(w).reshape(width, -1) for w in (q_weight, k_weight, v_weight)], axis=1
    )
    w_out = whole(o_weight).reshape(width, width)
    w_gate = whole(gate_weight).reshape(width, ff)
    w_up = whole(up_weight).reshape(width, ff)
    w_down = whole(down_weight).reshape(ff, width)
    flat = whole(vectors).astype(F32)
    ends = [width, width + kv_width, width + 2 * kv_width, 2 * width + 2 * kv_width]
    gain_attn = flat[ends[2] : ends[3]]
    gain_mlp = flat[ends[3] : ends[3] + width]

    n_first = (inputs * inv_first * gain_attn).astype(BF)
    qkv = times(n_first, w_qkv) + flat[: ends[2]]
    q_rot = turn(qkv[:, :width].reshape(tok_rows, heads, HEAD_DIM), cosine, sine)
    q_rot = q_rot.astype(BF).reshape(tok_rows, width)
    k_rot = turn(qkv[:, width : ends[1]].reshape(tok_rows, KV_HEADS, HEAD_DIM), cosine, sine)
    k_rot = k_rot.astype(BF).reshape(tok_rows, kv_width)
    kv_mine = jnp.concatenate([k_rot, qkv[:, ends[1] :].astype(BF)], axis=1)
    kv = lax.all_gather(kv_mine, "ctx", axis=0, tiled=True)
    flag = jnp.ones((1,), jnp.int32)
    places = (segment_all[:, None], row_all[:, None], segment_mine[None, :], row_mine[None, :])
    attn, lse = attention(q_rot, kv, places, flag, seq_tokens, False)
    mid = inputs + times(attn, w_out)
    inv_second = lax.rsqrt(jnp.mean(mid * mid, axis=-1, keepdims=True) + EPS)
    n_second = (mid * inv_second * gain_mlp).astype(BF)
    gate = times(n_second, w_gate)
    up_val = times(n_second, w_up)
    sig = jax.nn.sigmoid(gate)
    act = gate * sig
    hidden = (act * up_val).astype(BF)
    layer_out = (mid + times(hidden, w_down)).astype(BF)

    grad_wdown = inner_rows(hidden, cotangent)
    grad_hidden = times_back(cotangent, w_down)
    grad_gate = (grad_hidden * up_val * (sig * (1.0 + gate * (1.0 - sig)))).astype(BF)
    grad_up = (grad_hidden * act).astype(BF)
    grad_wgate = inner_rows(n_second, grad_gate)
    grad_wup = inner_rows(n_second, grad_up)
    grad_n2 = times_back(grad_gate, w_gate) + times_back(grad_up, w_up)
    grad_mid_norm, grad_gain_mlp = norm_back(mid, inv_second, gain_mlp, grad_n2)
    grad_mid = cotangent.astype(F32) + grad_mid_norm
    grad_branch = grad_mid.astype(BF)
    grad_wout = inner_rows(attn, grad_branch)
    grad_attn = times_back(grad_branch, w_out).astype(BF)
    grad_q_rot, grad_k, grad_v = attention_back(
        q_rot, kv, grad_attn, lse, places, flag, seq_tokens, False, 0, KV_HEADS
    )
    grad_kv = jnp.concatenate([grad_k, grad_v], axis=1)
    grad_kv_mine = lax.psum_scatter(
        grad_kv.astype(BF), "ctx", scatter_dimension=0, tiled=True
    ).astype(F32)
    grad_q = turn(grad_q_rot.reshape(tok_rows, heads, HEAD_DIM), cosine, -sine)
    grad_k = turn(
        grad_kv_mine[:, :kv_width].reshape(tok_rows, KV_HEADS, HEAD_DIM), cosine, -sine
    )
    grad_qkv = jnp.concatenate(
        [
            grad_q.reshape(tok_rows, width).astype(BF),
            grad_k.reshape(tok_rows, kv_width).astype(BF),
            grad_kv_mine[:, kv_width:].astype(BF),
        ],
        axis=1,
    )
    grad_wqkv = inner_rows(n_first, grad_qkv)
    grad_bias = jnp.sum(grad_qkv.astype(F32), axis=0)
    grad_n1 = times_back(grad_qkv, w_qkv)
    grad_x_norm, grad_gain_attn = norm_back(inputs, inv_first, gain_attn, grad_n1)
    input_grad = grad_mid + grad_x_norm
    used = 3 * width + 2 * kv_width
    padding = jnp.zeros((vectors.shape[0] * count - used,), F32)
    vector_term = jnp.concatenate([grad_bias, grad_gain_attn, grad_gain_mlp, padding])

    def shares(term):
        return lax.psum_scatter(term.reshape(-1), AXES, scatter_dimension=0, tiled=True)

    return (
        layer_out, input_grad, shares(grad_wqkv[:, :width]),
        shares(grad_wqkv[:, width : ends[1]]), shares(grad_wqkv[:, ends[1] :]),
        shares(grad_wout), shares(grad_wgate), shares(grad_wup), shares(grad_wdown),
        shares(vector_term),
    )


def solution(mesh):
    split = P(AXES)
    rows = P(AXES, None)
    in_specs = (rows,) + (split,) * 8 + (P("dp", None), rows)
    out_specs = (rows, rows) + (split,) * 8
    return jax.shard_map(local, mesh=mesh, in_specs=in_specs, out_specs=out_specs, check_vma=False)
```

```python
import functools

import jax
import jax.numpy as jnp
import numpy as np
from jax import lax
from jax.experimental import pallas as pl
from jax.experimental.pallas import tpu as pltpu
from jax.sharding import PartitionSpec as P

KV_HEADS = 3
HEAD_DIM = 64

EPS = 1e-06
THETA = 100000.0
NEG_FILL = -1e30
AXES = ("dp", "ctx")
BF = jnp.bfloat16
F32 = jnp.float32


def times(left, right):
    return jnp.dot(left, right, preferred_element_type=F32)


def inner_rows(left, right):
    return lax.dot_general(left, right, (((0,), (0,)), ((), ())), preferred_element_type=F32)


def times_back(left, right):
    return lax.dot_general(left, right, (((1,), (1,)), ((), ())), preferred_element_type=F32)


def norm_back(values, inv, gain, grad):
    scaled = grad * gain
    dot = jnp.mean(scaled * values, axis=-1, keepdims=True)
    grad_values = inv * scaled - values * (inv * inv * inv * dot)
    grad_gain = jnp.sum(grad * values * inv, axis=0)
    return grad_values, grad_gain


def turn(values, cosine, sine):
    half = values.shape[-1] // 2
    first = values[..., :half]
    second = values[..., half:]
    return jnp.concatenate(
        [first * cosine - second * sine, second * cosine + first * sine], axis=-1
    )


def doc_layout(lengths, count):
    ends = jnp.cumsum(lengths)
    place = jnp.arange(count, dtype=jnp.int32)
    segment = jnp.sum((place[:, None] >= ends[None, :-1]).astype(jnp.int32), axis=1)
    starts = ends - lengths
    picked = segment[:, None] == jnp.arange(lengths.shape[0], dtype=jnp.int32)[None, :]
    first = jnp.sum(jnp.where(picked, starts[None, :], 0), axis=1)
    return (segment, place - first)


def fill_bias(bias, seg_k, row_k, seg_q, row_q):
    allowed = (seg_k[...] == seg_q[...]) & (row_k[...] <= row_q[...])
    bias[...] = jnp.where(allowed, 0.0, NEG_FILL)


def key_range(full, total, short, rows, block, at, causal):
    start = 0 if full else total - short
    stop = total - rows + (at + 1) * block if causal else total
    return start, stop


def attn_fwd_kernel(
    heads, block, short, causal, flag, q_ref, kv_ref, seg_k, row_k, seg_q, row_q,
    out_ref, lse_ref, qs, ks, vts, bias, out_t,
):
    rows = q_ref.shape[0]
    total = kv_ref.shape[0]
    kv_width = KV_HEADS * HEAD_DIM
    group = heads // KV_HEADS
    fill_bias(bias, seg_k, row_k, seg_q, row_q)
    for h in range(heads):
        qs[h] = q_ref[:, h * HEAD_DIM : (h + 1) * HEAD_DIM] * BF(HEAD_DIM**-0.5)
    for g in range(KV_HEADS):
        ks[g] = kv_ref[:, g * HEAD_DIM : (g + 1) * HEAD_DIM]
    vts[...] = jnp.transpose(kv_ref[:, kv_width:].astype(F32)).astype(BF)

    def run(full):
        @pl.loop(0, heads)
        def _(h):
            g = h // group
            v_rows = pl.ds(pl.multiple_of(g * HEAD_DIM, HEAD_DIM), HEAD_DIM)
            out_rows = pl.ds(pl.multiple_of(h * HEAD_DIM, HEAD_DIM), HEAD_DIM)
            for at in range(rows // block):
                start, stop = key_range(full, total, short, rows, block, at, causal)
                cols = slice(at * block, (at + 1) * block)
                s = times_back(ks[g, start:stop], qs[h, cols])
                s = s + bias[start:stop, cols]
                top = jnp.max(s, axis=0, keepdims=True)
                p = jnp.exp(s - top)
                total_p = jnp.sum(p, axis=0, keepdims=True)
                o = times(vts[v_rows, start:stop], p.astype(BF))
                out_t[out_rows, cols] = o / total_p
                lse_ref[h, :, cols] = top + jnp.log(total_p)

    pl.when(flag[0] != 0)(lambda: run(True))
    pl.when(flag[0] == 0)(lambda: run(False))
    out_ref[...] = jnp.transpose(out_t[...]).astype(BF)


def attn_bwd_kernel(
    heads, block, short, causal, g0, g1,
    flag, q_ref, kv_ref, do_ref, lse_ref, seg_k, row_k, seg_q, row_q, *refs,
):
    outs, scratch = refs[:-9], refs[-9:]
    qs, ks, vs, kts, dos, bias, dq_t, dk, dv = scratch
    rows = q_ref.shape[0]
    total = kv_ref.shape[0]
    kv_width = KV_HEADS * HEAD_DIM
    group = heads // KV_HEADS
    keys = g1 - g0
    fill_bias(bias, seg_k, row_k, seg_q, row_q)
    for h in range(keys * group):
        lanes = slice((g0 * group + h) * HEAD_DIM, (g0 * group + h + 1) * HEAD_DIM)
        qs[h] = q_ref[:, lanes] * BF(HEAD_DIM**-0.5)
        dos[h] = do_ref[:, lanes]
    for g in range(keys):
        lo = (g0 + g) * HEAD_DIM
        ks[g] = kv_ref[:, lo : lo + HEAD_DIM]
        vs[g] = kv_ref[:, kv_width + lo : kv_width + lo + HEAD_DIM]
        kts[g] = jnp.transpose(ks[g].astype(F32)).astype(BF)
    dk[...] = jnp.zeros_like(dk)
    dv[...] = jnp.zeros_like(dv)

    def run(full):
        @pl.loop(0, keys * group)
        def _(h):
            g = h // group if keys > 1 else 0
            out_rows = pl.ds(pl.multiple_of(h * HEAD_DIM, HEAD_DIM), HEAD_DIM)
            for at in range(rows // block):
                start, stop = key_range(full, total, short, rows, block, at, causal)
                cols = slice(at * block, (at + 1) * block)
                q = qs[h, cols]
                do = dos[h, cols]
                s = times_back(ks[g, start:stop], q)
                p = jnp.exp(s + bias[start:stop, cols] - lse_ref[g0 * group + h, :, cols])
                dp = times_back(vs[g, start:stop], do)
                t = p * dp
                inner = jnp.sum(t, axis=0, keepdims=True)
                ds = (t - p * inner).astype(BF)
                dk[g, start:stop] += times(ds, q)
                dv[g, start:stop] += times(p.astype(BF), do)
                dq_t[out_rows, cols] = times(kts[g, :, start:stop], ds) * HEAD_DIM**-0.5

    pl.when(flag[0] != 0)(lambda: run(True))
    pl.when(flag[0] == 0)(lambda: run(False))
    outs[0][...] = jnp.transpose(dq_t[...])
    cut = total - outs[1].shape[0]
    for part, out in ((slice(cut, total), outs[1]),) + tuple((slice(0, cut), o) for o in outs[2:]):
        for g in range(keys):
            lo = g * HEAD_DIM
            out[:, lo : lo + HEAD_DIM] = dk[g, part].astype(out.dtype)
            lo += keys * HEAD_DIM
            out[:, lo : lo + HEAD_DIM] = dv[g, part].astype(out.dtype)


VM = pl.BlockSpec(memory_space=pltpu.VMEM)
SM = pl.BlockSpec(memory_space=pltpu.SMEM)


def attn_cost(rows, total, heads, products):
    return pl.CostEstimate(
        flops=8 * products * rows * total * heads * HEAD_DIM,
        bytes_accessed=4 * (rows + total) * heads * HEAD_DIM,
        transcendentals=rows * total * heads,
    )


def attention(q, kv, places, flag, short, causal):
    rows, width = q.shape
    total = kv.shape[0]
    heads = width // HEAD_DIM
    block = min(rows, 256)
    return pl.pallas_call(
        functools.partial(attn_fwd_kernel, heads, block, short, causal),
        out_shape=(
            jax.ShapeDtypeStruct((rows, width), BF),
            jax.ShapeDtypeStruct((heads, 1, rows), F32),
        ),
        in_specs=[SM] + [VM] * 6,
        out_specs=(VM, VM),
        scratch_shapes=[
            pltpu.VMEM((heads, rows, HEAD_DIM), BF),
            pltpu.VMEM((KV_HEADS, total, HEAD_DIM), BF),
            pltpu.VMEM((KV_HEADS * HEAD_DIM, total), BF),
            pltpu.VMEM((total, rows), F32),
            pltpu.VMEM((width, rows), F32),
        ],
        compiler_params=pltpu.CompilerParams(vmem_limit_bytes=20 * 2**20),
        cost_estimate=attn_cost(rows, total, heads, 2),
        name="attn_fwd",
    )(flag, q, kv, *places)


def attention_back(q, kv, grad_out, lse, places, flag, short, causal, g0, g1):
    rows, width = q.shape
    total = kv.shape[0]
    heads = width // HEAD_DIM
    block = min(rows, 256)
    keys = g1 - g0
    mine = heads // KV_HEADS * keys
    outs = [jax.ShapeDtypeStruct((rows, mine * HEAD_DIM), F32)]
    if causal:
        outs.append(jax.ShapeDtypeStruct((rows, 2 * keys * HEAD_DIM), F32))
        outs.append(jax.ShapeDtypeStruct((total - rows, 2 * keys * HEAD_DIM), BF))
    else:
        outs.append(jax.ShapeDtypeStruct((total, 2 * keys * HEAD_DIM), F32))
    return pl.pallas_call(
        functools.partial(attn_bwd_kernel, heads, block, short, causal, g0, g1),
        out_shape=outs,
        in_specs=[SM] + [VM] * 8,
        out_specs=[VM] * len(outs),
        scratch_shapes=[
            pltpu.VMEM((mine, rows, HEAD_DIM), BF),
            pltpu.VMEM((keys, total, HEAD_DIM), BF),
            pltpu.VMEM((keys, total, HEAD_DIM), BF),
            pltpu.VMEM((keys, HEAD_DIM, total), BF),
            pltpu.VMEM((mine, rows, HEAD_DIM), BF),
            pltpu.VMEM((total, rows), F32),
            pltpu.VMEM((mine * HEAD_DIM, rows), F32),
            pltpu.VMEM((keys, total, HEAD_DIM), F32),
            pltpu.VMEM((keys, total, HEAD_DIM), F32),
        ],
        compiler_params=pltpu.CompilerParams(vmem_limit_bytes=20 * 2**20),
        cost_estimate=attn_cost(rows, total, mine, 5),
        name="attn_bwd",
    )(flag, q, kv, grad_out, lse, *places)


TAIL = 2
MAIN = 16
PIECES = MAIN // TAIL


class Blocks:
    def __init__(self, dp_count, ctx_count):
        self.count = dp_count * ctx_count
        self.x = 1
        self.core = ctx_count
        self.y = 2 * ctx_count
        self.z = 4 * ctx_count
        self.zs = dp_count // 4
        self.masks = []
        for p in range(self.count):
            z, x = p % self.zs, p // self.zs % 2
            y, core = p // (2 * self.zs) % 2, p // (4 * self.zs)
            self.masks.append(x * self.x + y * self.y + core * self.core + z * self.z)

    def swap(self, values, mask):
        perm = [(i, i ^ mask) for i in range(self.count)]
        return lax.ppermute(values, AXES, perm)

    def along_z(self, mine):
        return jnp.stack([mine] + [self.swap(mine, d * self.z) for d in range(1, self.zs)])

    def add(self, keep, got):
        return (keep.astype(F32) + got.astype(F32)).astype(BF)

    def sum_z(self, held):
        got = [self.swap(held[d], d * self.z).astype(F32) for d in range(1, self.zs)]
        return functools.reduce(jnp.add, got, held[0].astype(F32))


class Sizes:
    def __init__(self, width, ff, count, vec, kv_width):
        self.width, self.ff, self.count, self.vec = width, ff, count, vec
        self.rows = width // count
        self.f_rows = ff // count
        up = lambda n: (n + 127) // 128 * 128
        self.wide = up(width)
        self.qkv = width + 2 * kv_width
        self.a_width = up(self.qkv)
        self.tall = (self.rows + 1 + 7) // 8 * 8
        self.downs = self.f_rows // MAIN
        self.piece = 2 * ff // PIECES
        self.gate = 0
        self.tail = ff
        self.tail_o = self.tail + self.piece
        self.out = self.tail_o + 128
        self.down0 = self.out + self.wide
        self.first = self.down0 + self.wide
        self.second = ff + (self.downs - 1) * self.wide
        self.flat = self.a_width + 2 * self.wide

    def down_at(self, c):
        return (0, self.down0) if c == 0 else (1, self.ff + (c - 1) * self.wide)

    def fits(self):
        return (
            self.rows == MAIN + TAIL
            and self.f_rows % MAIN == 0
            and self.piece % 128 == 0
            and self.ff % 256 == 0
            and self.wide <= 128 * PIECES
            and self.vec <= 128
        )


def slot_tables(size, masks):
    far = -(2**20)
    a = [(masks[s // size.tall], s % size.tall) for s in range(size.count * size.tall)]
    a = [(m, i if i < size.rows else far) for m, i in a]
    b = [(masks[s // MAIN], s % MAIN) for s in range(size.count * MAIN)]
    b += [(masks[s // TAIL], MAIN + s % TAIL) for s in range(size.count * TAIL)]
    flat = []
    natural = [(0, size.qkv, size.a_width), (size.qkv, size.width, size.wide)]
    natural += [(size.qkv + size.width, size.width, size.wide)]
    for start, used, room in natural:
        for c in range(room):
            at = start + c
            flat.append((at // size.vec, at % size.vec) if c < used else (far, far))
    owners = np.asarray(masks, np.int32)[:, None]
    as_rows = lambda pairs: np.ascontiguousarray(np.asarray(pairs, np.int32).T)
    return as_rows(a), as_rows(b), as_rows(flat), owners


def wire_kernel(size, g_ref, u_ref, o_ref, d_ref, out1, out2, tail, tail_o):
    ff, width = size.ff, size.width
    out1[:, : ff] = g_ref[:MAIN]
    out2[:, : ff] = u_ref[:MAIN]
    out1[:, size.out : size.out + size.wide] = jnp.zeros((MAIN, size.wide), BF)
    out1[:, size.out : size.out + width] = o_ref[:MAIN]
    tail_o[...] = jnp.zeros_like(tail_o)
    odd = [ref[MAIN:].astype(F32) for ref in (g_ref, u_ref, o_ref)]
    for c in range(PIECES):
        src = odd[c * size.piece // ff]
        at = c * size.piece % ff
        tail[c * TAIL : (c + 1) * TAIL] = src[:, at : at + size.piece]
        used = min(128, width - c * 128)
        if used > 0:
            tail_o[c * TAIL : (c + 1) * TAIL, :used] = odd[2][:, c * 128 : c * 128 + used]
    out1[:, size.tail : size.tail + size.piece] = tail[...].astype(BF)
    out1[:, size.tail_o : size.tail_o + 128] = tail_o[...].astype(BF)
    for c in range(size.downs):
        which, at = size.down_at(c)
        out = (out1, out2)[which]
        out[:, at : at + size.wide] = jnp.zeros((MAIN, size.wide), BF)
        out[:, at : at + width] = d_ref[c * MAIN : (c + 1) * MAIN]


def place_matrix(size, me, table):
    feature = size.rows * (me ^ table[0:1, :]) + table[1:2, :]
    shape = (size.width, feature.shape[1])
    at = lax.broadcasted_iota(jnp.int32, shape, 0)
    return jnp.where(at == feature, 1.0, 0.0).astype(BF)


def vector_lanes(table):
    inside = lax.broadcasted_iota(jnp.int32, (128, table.shape[1]), 0)
    return jnp.where(inside == table[1:2, :], 1.0, 0.0).astype(BF)


def split_two(values):
    high = values.astype(BF)
    return high, (values - high.astype(F32)).astype(BF)


def swap_halves(u):
    rolled_back = pltpu.roll(u, 128 - HEAD_DIM // 2, 1)
    rolled = pltpu.roll(u, HEAD_DIM // 2, 1)
    lane = lax.broadcasted_iota(jnp.int32, u.shape, 1)
    return jnp.where(lane % HEAD_DIM < HEAD_DIM // 2, rolled_back, rolled)


def pre_kernel(
    size, me_ref, x_ref, wm_ref, wo_ref, cos_ref, sin_ref, table_a, table_f, owner_ref,
    q_ref, kv_ref, n1t_ref, flat_ref, w, qkv,
):
    me = me_ref[0]
    half = wm_ref.shape[0]
    w[:half] = wm_ref[...]
    w[half:] = wo_ref[...]
    shape = (size.count, 2 * half)
    row = lax.broadcasted_iota(jnp.int32, shape, 0) * size.tall + size.rows
    row = lax.broadcasted_iota(jnp.int32, shape, 1) == row
    packed = times(jnp.where(row, 1.0, 0.0).astype(BF), w[:, :128]).astype(BF)
    table = table_f[...]
    spread = times(packed, vector_lanes(table))
    mine = table[0:1, :] == (me ^ owner_ref[...])
    flat = jnp.sum(jnp.where(mine, spread, 0.0), axis=0, keepdims=True)
    flat_ref[...] = flat
    gain = flat[:, size.a_width : size.a_width + size.width]
    x = x_ref[...].astype(F32)
    inv = lax.rsqrt(jnp.mean(x * x, axis=-1, keepdims=True) + EPS)
    n1 = (x * inv * gain).astype(BF)
    n1a = times(n1, place_matrix(size, me, table_a[...]))
    qkv[...] = times(n1a.astype(BF), w[...]) + flat[:, : size.a_width]
    n1t_ref[...] = jnp.transpose(n1a).astype(BF)
    kv_width = kv_ref.shape[1] // 2
    for t in range((size.width + kv_width) // 128):
        u = qkv[:, t * 128 : (t + 1) * 128]
        qkv[:, t * 128 : (t + 1) * 128] = u * cos_ref[...] + swap_halves(u) * sin_ref[...]
    q_ref[...] = qkv[:, : size.width].astype(BF)
    kv_ref[...] = qkv[:, size.width : size.qkv].astype(BF)


def tail_place(size, c):
    shape = (size.count * TAIL, size.count * MAIN)
    q = lax.broadcasted_iota(jnp.int32, shape, 0)
    at = lax.broadcasted_iota(jnp.int32, shape, 1)
    want = (q // TAIL) * MAIN + c * TAIL + q % TAIL
    return jnp.where(at == want, 1.0, 0.0).astype(BF)


def tail_place_back(size, c):
    shape = (size.count * MAIN, size.count * TAIL)
    at = lax.broadcasted_iota(jnp.int32, shape, 0)
    q = lax.broadcasted_iota(jnp.int32, shape, 1)
    want = (q // TAIL) * MAIN + c * TAIL + q % TAIL
    return jnp.where(at == want, 1.0, 0.0).astype(BF)


def mlp_kernel(
    size, masks, me_ref, attn_ref, x_ref, cot_ref, flat_ref, b1m, b1o, b2m, b2o, table_b,
    out_ref, keep1, give1, keep2, give2, gmid_ref, gattn_ref, ggain_ref,
    wg, wu, wo, wd, mid, n2s, n2t, place, acc, gacc, dwd, tails, tail_o,
):
    me = me_ref[0]
    width, ff = size.width, size.ff
    half = b1m.shape[0]
    main = 2 * half
    halves = (
        (slice(0, half), (b1m, b2m), (keep1, keep2)),
        (slice(half, main), (b1o, b2o), (give1, give2)),
    )
    place[...] = place_matrix(size, me, table_b[...])
    for part, (b1, b2), _ in halves:
        wg[part] = b1[:, size.gate : size.gate + ff]
        wu[part] = b2[:, : ff]
        wo[part] = b1[:, size.out : size.out + size.wide]
    for c in range(PIECES):
        sel = tail_place(size, c)
        cols = slice(size.tail, size.tail + size.piece)
        got = times(sel[:, :half], b1m[:, cols]) + times(sel[:, half:], b1o[:, cols])
        target = wg if c * size.piece < ff else wu
        at = c * size.piece % ff
        target[main:, at : at + size.piece] = got.astype(BF)
        if c * 128 < size.wide:
            cols = slice(size.tail_o, size.tail_o + 128)
            got = times(sel[:, :half], b1m[:, cols]) + times(sel[:, half:], b1o[:, cols])
            wo[main:, c * 128 : (c + 1) * 128] = got.astype(BF)
    for p in range(size.count):
        _, got, _ = halves[p // (size.count // 2)]
        rows = slice(p * MAIN % half, p * MAIN % half + MAIN)
        owner = me ^ masks[p]
        for c in range(size.downs):
            which, at = size.down_at(c)
            src = got[which][rows, at : at + size.wide]
            to = pl.multiple_of(owner * size.f_rows + c * MAIN, MAIN)
            wd[pl.ds(to, MAIN), :] = src
    attn_s = times(attn_ref[...], place[...])
    m = x_ref[...].astype(F32) + times(attn_s.astype(BF), wo[:, :width])
    mid[...] = m
    inv = lax.rsqrt(jnp.mean(m * m, axis=-1, keepdims=True) + EPS)
    lo = size.a_width + size.wide
    gain = flat_ref[:, lo : lo + width]
    n2 = (m * inv * gain).astype(BF)
    spread = times(n2, place[...])
    n2s[...] = spread.astype(BF)
    n2t[...] = jnp.transpose(spread).astype(BF)
    acc[...] = jnp.zeros_like(acc)
    gacc[...] = jnp.zeros_like(gacc)
    step = 512 if ff % 512 == 0 else 256

    @pl.loop(0, ff // step)
    def _(b):
        at = pl.multiple_of(b * step, step)
        cols = pl.ds(at, step)
        gate = times(n2s[...], wg[:, cols])
        up = times(n2s[...], wu[:, cols])
        sig = 1.0 / (1.0 + jnp.exp(-gate))
        act = gate * sig
        h = act * up
        gh = times_back(cot_ref[...], wd[cols, :width])
        gg = (gh * up * (sig * (1.0 + gate * (1.0 - sig)))).astype(BF)
        gu = (gh * act).astype(BF)
        acc[...] += times(h.astype(BF), wd[cols, :width])
        dwd[cols, :width] = times(jnp.transpose(h).astype(BF), cot_ref[...]).astype(BF)
        gacc[...] += times_back(gg, wg[:, cols]) + times_back(gu, wu[:, cols])
        for k, (grad, keep, give) in enumerate(((gg, keep1, give1), (gu, keep2, give2))):
            dw = times(n2t[...], grad).astype(BF)
            keep[:, cols] = dw[:half]
            give[:, cols] = dw[half:main]
            tails[:, pl.ds(pl.multiple_of(k * ff + at, 128), step)] = dw[main:]

    m = mid[...]
    inv = lax.rsqrt(jnp.mean(m * m, axis=-1, keepdims=True) + EPS)
    out_ref[...] = (m + acc[...]).astype(BF)
    high, low = split_two(gacc[...])
    gn2 = times_back(high, place[...]) + times_back(low, place[...])
    scaled = gn2 * gain
    dot = jnp.mean(scaled * m, axis=-1, keepdims=True)
    ggain_ref[...] = jnp.sum(gn2 * m * inv, axis=0, keepdims=True)
    gmid = cot_ref[...].astype(F32) + inv * scaled - m * (inv * inv * inv * dot)
    gmid_ref[...] = gmid
    branch = gmid.astype(BF)
    gattn = times_back(branch, wo[:, :width]).astype(BF)
    gattn_ref[...] = times_back(gattn, place[...]).astype(BF)
    dwo = times(jnp.transpose(attn_s).astype(BF), branch).astype(BF)
    tail_o[...] = jnp.zeros_like(tail_o)
    tail_o[:, :width] = dwo[main:]
    for part, _, (term, _) in halves:
        term[:, size.out : size.out + width] = dwo[part]
    wire = jnp.zeros((main, size.piece), F32)
    wire_o = jnp.zeros((main, 128), F32)
    for c in range(PIECES):
        sel = tail_place_back(size, c)
        wire += times(sel, tails[:, c * size.piece : (c + 1) * size.piece])
        if c * 128 < size.wide:
            wire_o += times(sel, tail_o[:, c * 128 : (c + 1) * 128])
    for part, _, (term, _) in halves:
        term[:, size.tail : size.tail + size.piece] = wire[part].astype(BF)
        term[:, size.tail_o : size.tail_o + 128] = wire_o[part].astype(BF)
    for p in range(size.count):
        _, _, terms = halves[p // (size.count // 2)]
        rows = slice(p * MAIN % half, p * MAIN % half + MAIN)
        owner = me ^ masks[p]
        for c in range(size.downs):
            which, at = size.down_at(c)
            src = pl.multiple_of(owner * size.f_rows + c * MAIN, MAIN)
            terms[which][rows, at : at + size.wide] = dwd[pl.ds(src, MAIN), :]


def post_kernel(
    size, me_ref, dq0, dq1, dq2, own0, own1, own2, got0, got1, got2, cos_ref, sin_ref, n1t_ref, wm_ref, wo_ref, x_ref,
    gmid_ref, flat_ref, ggain_ref, table_a, table_f, owner_ref,
    gx_ref, keep_ref, give_ref, turn_buf, grad, vec_row,
):
    me = me_ref[0]
    width = size.width
    half = wm_ref.shape[0]
    kv_width = KV_HEADS * HEAD_DIM
    turned = width + kv_width
    third = width // KV_HEADS
    grad[...] = jnp.zeros_like(grad)
    parts = ((dq0, own0, got0), (dq1, own1, got1), (dq2, own2, got2))
    for g, (dq, own, got) in enumerate(parts):
        turn_buf[:, g * third : (g + 1) * third] = dq[...]
        dkv = own[...] + got[...].astype(F32)
        lo = width + g * HEAD_DIM
        turn_buf[:, lo : lo + HEAD_DIM] = dkv[:, :HEAD_DIM]
        lo += kv_width
        grad[:, lo : lo + HEAD_DIM] = dkv[:, HEAD_DIM:].astype(BF)
    for t in range(turned // 128):
        u = turn_buf[:, t * 128 : (t + 1) * 128]
        back = u * cos_ref[...] - swap_halves(u) * sin_ref[...]
        grad[:, t * 128 : (t + 1) * 128] = back.astype(BF)
    g = grad[...]
    place = place_matrix(size, me, table_a[...])
    high_m, low_m = split_two(times_back(g, wm_ref[...]))
    high_o, low_o = split_two(times_back(g, wo_ref[...]))
    gn1 = times_back(high_m, place[:, :half]) + times_back(high_o, place[:, half:])
    gn1 += times_back(low_m, place[:, :half]) + times_back(low_o, place[:, half:])
    x = x_ref[...].astype(F32)
    inv = lax.rsqrt(jnp.mean(x * x, axis=-1, keepdims=True) + EPS)
    gain = flat_ref[:, size.a_width : size.a_width + width]
    scaled = gn1 * gain
    dot = jnp.mean(scaled * x, axis=-1, keepdims=True)
    gx_ref[...] = gmid_ref[...] + inv * scaled - x * (inv * inv * inv * dot)
    vec_row[...] = jnp.zeros_like(vec_row)
    vec_row[:, : size.a_width] = jnp.sum(g.astype(F32), axis=0, keepdims=True)
    vec_row[:, size.a_width : size.a_width + width] = jnp.sum(gn1 * x * inv, axis=0, keepdims=True)
    lo = size.a_width + size.wide
    vec_row[:, lo : lo + width] = ggain_ref[...]
    table = table_f[...]
    mine = table[0:1, :] == (me ^ owner_ref[...])
    packed = times_back(jnp.where(mine, vec_row[...], 0.0).astype(BF), vector_lanes(table))
    shape = (half, size.count)
    for part, term in ((0, keep_ref), (1, give_ref)):
        rows = slice(part * half, (part + 1) * half)
        dw = times(n1t_ref[rows], g)
        term[...] = dw.astype(BF)
        want = lax.broadcasted_iota(jnp.int32, shape, 1) * size.tall + size.rows - part * half
        here = lax.broadcasted_iota(jnp.int32, shape, 0) == want
        extra = times(jnp.where(here, 1.0, 0.0).astype(BF), packed.astype(BF))
        term[:, :128] = (dw[:, :128] + extra).astype(BF)


def call(kernel, name, out_shape, scratch, flops, args, vmem, scalar=True):
    shapes = [jax.ShapeDtypeStruct(s, t) for s, t in out_shape]
    total = sum(int(np.prod(a.shape)) * a.dtype.itemsize for a in args)
    return pl.pallas_call(
        kernel,
        out_shape=shapes,
        in_specs=[SM if scalar and i == 0 else VM for i in range(len(args))],
        out_specs=[VM] * len(shapes),
        scratch_shapes=[pltpu.VMEM(s, t) for s, t in scratch],
        compiler_params=pltpu.CompilerParams(vmem_limit_bytes=vmem * 2**20),
        cost_estimate=pl.CostEstimate(flops=flops, bytes_accessed=total, transcendentals=0),
        name=name,
    )(*args)


def pad_to(values, rows, columns):
    return jnp.pad(values, ((0, rows - values.shape[0]), (0, columns - values.shape[1])))


def tail_pack(rows, piece):
    rows = pad_to(rows, TAIL, PIECES * piece)
    return rows.reshape(TAIL, PIECES, piece).transpose(1, 0, 2).reshape(MAIN, piece)


def tail_unpack(wire, used):
    piece = wire.shape[1]
    rows = wire.reshape(PIECES, TAIL, piece).transpose(1, 0, 2).reshape(TAIL, PIECES * piece)
    return rows[:, :used]


def tie(*values):
    return lax.optimization_barrier(values)


def local_blocks(size, blocks, pos, args):
    (
        tokens, q_weight, k_weight, v_weight, o_weight, gate_weight, up_weight, down_weight,
        vectors, cotangent,
    ) = args
    tok_rows, width = tokens.shape
    ff, rows = size.ff, size.rows
    kv_width = KV_HEADS * HEAD_DIM
    ctx_index = lax.axis_index("ctx")
    me = (lax.axis_index("dp") * lax.axis_size("ctx") + ctx_index).astype(jnp.int32).reshape(1)
    masks = blocks.masks
    half = size.count // 2
    table_a, table_b, table_f, owners = slot_tables(size, masks)
    segment_all, segment_mine, row_mine, cos, sin = pos

    joined_w = jnp.concatenate(
        [w.reshape(rows, -1) for w in (q_weight, k_weight, v_weight)], axis=1
    )
    vec_row = pad_to(vectors.reshape(1, -1), size.tall - rows, size.a_width)
    wire_a = jnp.concatenate([pad_to(joined_w, rows, size.a_width), vec_row], axis=0)
    za = blocks.along_z(wire_a)
    w_rows = [w.reshape(rows, -1) for w in (gate_weight, up_weight, o_weight)]
    wire_1, wire_2 = call(
        functools.partial(wire_kernel, size),
        "wire",
        [((MAIN, size.first), BF), ((MAIN, size.second), BF)],
        [((MAIN, size.piece), F32), ((MAIN, 128), F32)],
        0,
        w_rows + [down_weight.reshape(size.f_rows, width)],
        4,
        scalar=False,
    )
    xa = jnp.stack([za, blocks.swap(za, blocks.x)])
    xa, wire_1, wire_2 = tie(xa, wire_1, wire_2)
    z1 = blocks.along_z(wire_1)
    z2 = blocks.along_z(wire_2)
    x1 = jnp.stack([z1, blocks.swap(z1, blocks.x)])
    y2 = jnp.stack([z2, blocks.swap(z2, blocks.y)])
    a_all = jnp.stack([xa, blocks.swap(xa, blocks.y)])
    a_mine = a_all.reshape(half * size.tall, size.a_width)
    a_other = blocks.swap(a_mine, blocks.core)
    a_rows = size.count * size.tall
    q_rot, kv_mine, n1t, flat = call(
        functools.partial(pre_kernel, size),
        "norm_qkv",
        [
            ((tok_rows, width), BF), ((tok_rows, 2 * kv_width), BF), ((a_rows, tok_rows), BF),
            ((1, size.flat), F32),
        ],
        [((a_rows, size.a_width), BF), ((tok_rows, size.a_width), F32)],
        4 * tok_rows * width * size.a_width,
        (me, tokens, a_mine, a_other, cos, sin, table_a, table_f, owners),
        16,
    )
    kv_got = blocks.swap(kv_mine, blocks.x)
    q_rot, x1, y2 = tie(q_rot, x1, y2)
    b1_all = jnp.stack([x1, blocks.swap(x1, blocks.y)])
    b2_all = jnp.stack([y2, blocks.swap(y2, blocks.x)], axis=1)
    b1_mine = b1_all.reshape(half * MAIN, -1)
    b2_mine = b2_all.reshape(half * MAIN, -1)
    kv = jnp.concatenate([kv_got, kv_mine], axis=0)
    other = (1 - ctx_index) * tok_rows
    segment_k = jnp.concatenate(
        [lax.dynamic_slice_in_dim(segment_all, other, tok_rows), segment_mine]
    )
    row_k = jnp.concatenate([other + jnp.arange(tok_rows, dtype=jnp.int32), row_mine])
    flag = ctx_index.astype(jnp.int32).reshape(1)
    places = (segment_k[:, None], row_k[:, None], segment_mine[None, :], row_mine[None, :])
    attn, lse = attention(q_rot, kv, places, flag, tok_rows, True)

    attn, b2_mine = tie(attn, b2_mine)
    attn, b1_mine = tie(attn, b1_mine)
    b1_other = blocks.swap(b1_mine, blocks.core)
    b2_other = blocks.swap(b2_mine, blocks.core)
    main = size.count * MAIN
    slots = main + size.count * TAIL
    layer_out, keep1, give1, keep2, give2, grad_mid, grad_attn, grad_gain = call(
        functools.partial(mlp_kernel, size, masks),
        "feed_forward",
        [
            ((tok_rows, width), BF),
            ((main // 2, size.first), BF), ((main // 2, size.first), BF),
            ((main // 2, size.second), BF), ((main // 2, size.second), BF),
            ((tok_rows, width), F32), ((tok_rows, width), BF), ((1, width), F32),
        ],
        [
            ((slots, ff), BF), ((slots, ff), BF), ((slots, size.wide), BF), ((ff, size.wide), BF),
            ((tok_rows, width), F32), ((tok_rows, slots), BF), ((slots, tok_rows), BF),
            ((width, slots), BF), ((tok_rows, width), F32), ((tok_rows, slots), F32),
            ((ff, size.wide), BF), ((size.count * TAIL, 2 * ff), BF),
            ((size.count * TAIL, size.wide), BF),
        ],
        2 * tok_rows * width * (9 * ff + 5 * width),
        (
            me, attn, tokens, cotangent, flat, b1_mine, b1_other, b2_mine, b2_other, table_b,
        ),
        32,
    )

    got1 = blocks.swap(give1, blocks.core)
    got2 = blocks.swap(give2, blocks.core)
    shape = (2, 2, blocks.zs, MAIN, -1)
    h1 = blocks.add(keep1, got1).reshape(shape)
    h2 = blocks.add(keep2, got2).reshape(shape)
    grads, got_kv = [], []
    for g in range(KV_HEADS):
        if g == 1:
            grad_attn, h1, h2 = tie(grad_attn, h1, h2)
            h1 = blocks.add(h1[0], blocks.swap(h1[1], blocks.y))
            h2 = blocks.add(h2[:, 0], blocks.swap(h2[:, 1], blocks.x))
        dq, own, other = attention_back(
            q_rot, kv, grad_attn, lse, places, flag, tok_rows, True, g, g + 1
        )
        if g == KV_HEADS - 1:
            other, h1, h2 = tie(other, h1, h2)
        grads.append((dq, own))
        got_kv.append(blocks.swap(other, blocks.x))
    h1 = blocks.add(h1[0], blocks.swap(h1[1], blocks.x))
    h2 = blocks.add(h2[0], blocks.swap(h2[1], blocks.y))

    gx, keep_a, give_a = call(
        functools.partial(post_kernel, size),
        "norm_qkv_back",
        [
            ((tok_rows, width), F32), ((a_rows // 2, size.a_width), BF),
            ((a_rows // 2, size.a_width), BF),
        ],
        [
            ((tok_rows, width + kv_width), F32), ((tok_rows, size.a_width), BF),
            ((1, size.flat), F32),
        ],
        6 * tok_rows * width * size.a_width,
        (
            me, *[g[0] for g in grads], *[g[1] for g in grads], *got_kv, cos, sin, n1t, a_mine,
            a_other, tokens, grad_mid, flat, grad_gain, table_a, table_f, owners,
        ),
        24,
    )
    held = blocks.add(keep_a, blocks.swap(give_a, blocks.core))
    held, h1, h2 = tie(held, h1, h2)
    held = held.reshape(2, 2, blocks.zs, size.tall, size.a_width)
    held = blocks.add(held[0], blocks.swap(held[1], blocks.y))
    held, share2 = tie(held, blocks.sum_z(h2))
    held = blocks.add(held[0], blocks.swap(held[1], blocks.x))
    held, share1 = tie(held, blocks.sum_z(h1))
    share_a = blocks.sum_z(held)

    tails = tail_unpack(share1[:, size.tail : size.tail + size.piece], 2 * ff)
    tail_o = tail_unpack(share1[:, size.tail_o : size.tail_o + 128], width)
    share_out = jnp.concatenate([share1[:, size.out : size.out + width], tail_o], axis=0)
    share_gate = jnp.concatenate([share1[:, :ff], tails[:, :ff]], axis=0)
    share_up = jnp.concatenate([share2[:, :ff], tails[:, ff:]], axis=0)
    downs = [size.down_at(c) for c in range(size.downs)]
    share_down = jnp.concatenate(
        [(share1, share2)[which][:, at : at + width] for which, at in downs], axis=0
    )
    ends = (width, width + kv_width, size.qkv)
    return (
        layer_out, gx, share_a[:rows, : ends[0]].reshape(-1),
        share_a[:rows, ends[0] : ends[1]].reshape(-1),
        share_a[:rows, ends[1] : ends[2]].reshape(-1),
        share_out.reshape(-1), share_gate.reshape(-1), share_up.reshape(-1),
        share_down.reshape(-1), share_a[rows, : size.vec],
    )


def local(
    tokens, q_weight, k_weight, v_weight, o_weight, gate_weight, up_weight, down_weight,
    vectors, doc_lengths, cotangent,
):
    tok_rows, width = tokens.shape
    ctx_count = lax.axis_size("ctx")
    dp_count = lax.axis_size("dp")
    count = dp_count * ctx_count
    seq_tokens = tok_rows * ctx_count
    ctx_index = lax.axis_index("ctx")
    heads = width // HEAD_DIM
    kv_width = KV_HEADS * HEAD_DIM
    ff = gate_weight.shape[0] * count // width

    segment_all, position_all = doc_layout(doc_lengths[0], seq_tokens)
    offset = ctx_index * tok_rows
    row_all = jnp.arange(seq_tokens, dtype=jnp.int32)
    segment_mine = lax.dynamic_slice_in_dim(segment_all, offset, tok_rows)
    position_mine = lax.dynamic_slice_in_dim(position_all, offset, tok_rows)
    row_mine = offset + jnp.arange(tok_rows, dtype=jnp.int32)
    half = HEAD_DIM // 2
    freq = THETA ** (-jnp.arange(half, dtype=F32) * 2.0 / HEAD_DIM)
    position_f = position_mine.astype(F32)[:, None]

    whole_rows = width % count == 0 and ff % count == 0
    if whole_rows and ctx_count == 2 and dp_count % 4 == 0 and count & (count - 1) == 0:
        size = Sizes(width, ff, count, vectors.shape[0], kv_width)
        if size.fits() and (width + kv_width) % 128 == 0:
            angle = position_f * jnp.tile(freq, 128 // half)[None, :]
            sign = np.where(np.arange(128) % HEAD_DIM < half, -1.0, 1.0).astype(np.float32)
            pos = (segment_all, segment_mine, row_mine, jnp.cos(angle), jnp.sin(angle) * sign)
            args = (
                tokens, q_weight, k_weight, v_weight, o_weight, gate_weight, up_weight,
                down_weight, vectors, cotangent,
            )
            return local_blocks(size, Blocks(dp_count, ctx_count), pos, args)

    angle = position_f * freq[None, :]
    cosine = jnp.cos(angle)[:, None, :]
    sine = jnp.sin(angle)[:, None, :]
    inputs = tokens.astype(F32)
    inv_first = lax.rsqrt(jnp.mean(inputs * inputs, axis=-1, keepdims=True) + EPS)

    def whole(part):
        return lax.all_gather(part, AXES, axis=0, tiled=True)

    w_qkv = jnp.concatenate(
        [whole(w).reshape(width, -1) for w in (q_weight, k_weight, v_weight)], axis=1
    )
    w_out = whole(o_weight).reshape(width, width)
    w_gate = whole(gate_weight).reshape(width, ff)
    w_up = whole(up_weight).reshape(width, ff)
    w_down = whole(down_weight).reshape(ff, width)
    flat = whole(vectors).astype(F32)
    ends = [width, width + kv_width, width + 2 * kv_width, 2 * width + 2 * kv_width]
    gain_attn = flat[ends[2] : ends[3]]
    gain_mlp = flat[ends[3] : ends[3] + width]

    n_first = (inputs * inv_first * gain_attn).astype(BF)
    qkv = times(n_first, w_qkv) + flat[: ends[2]]
    q_rot = turn(qkv[:, :width].reshape(tok_rows, heads, HEAD_DIM), cosine, sine)
    q_rot = q_rot.astype(BF).reshape(tok_rows, width)
    k_rot = turn(qkv[:, width : ends[1]].reshape(tok_rows, KV_HEADS, HEAD_DIM), cosine, sine)
    k_rot = k_rot.astype(BF).reshape(tok_rows, kv_width)
    kv_mine = jnp.concatenate([k_rot, qkv[:, ends[1] :].astype(BF)], axis=1)
    kv = lax.all_gather(kv_mine, "ctx", axis=0, tiled=True)
    flag = jnp.ones((1,), jnp.int32)
    places = (segment_all[:, None], row_all[:, None], segment_mine[None, :], row_mine[None, :])
    attn, lse = attention(q_rot, kv, places, flag, seq_tokens, False)
    mid = inputs + times(attn, w_out)
    inv_second = lax.rsqrt(jnp.mean(mid * mid, axis=-1, keepdims=True) + EPS)
    n_second = (mid * inv_second * gain_mlp).astype(BF)
    gate = times(n_second, w_gate)
    up_val = times(n_second, w_up)
    sig = jax.nn.sigmoid(gate)
    act = gate * sig
    hidden = (act * up_val).astype(BF)
    layer_out = (mid + times(hidden, w_down)).astype(BF)

    grad_wdown = inner_rows(hidden, cotangent)
    grad_hidden = times_back(cotangent, w_down)
    grad_gate = (grad_hidden * up_val * (sig * (1.0 + gate * (1.0 - sig)))).astype(BF)
    grad_up = (grad_hidden * act).astype(BF)
    grad_wgate = inner_rows(n_second, grad_gate)
    grad_wup = inner_rows(n_second, grad_up)
    grad_n2 = times_back(grad_gate, w_gate) + times_back(grad_up, w_up)
    grad_mid_norm, grad_gain_mlp = norm_back(mid, inv_second, gain_mlp, grad_n2)
    grad_mid = cotangent.astype(F32) + grad_mid_norm
    grad_branch = grad_mid.astype(BF)
    grad_wout = inner_rows(attn, grad_branch)
    grad_attn = times_back(grad_branch, w_out).astype(BF)
    grad_q_rot, grad_kv = attention_back(
        q_rot, kv, grad_attn, lse, places, flag, seq_tokens, False, 0, KV_HEADS
    )
    grad_kv_mine = lax.psum_scatter(
        grad_kv.astype(BF), "ctx", scatter_dimension=0, tiled=True
    ).astype(F32)
    grad_q = turn(grad_q_rot.reshape(tok_rows, heads, HEAD_DIM), cosine, -sine)
    grad_k = turn(
        grad_kv_mine[:, :kv_width].reshape(tok_rows, KV_HEADS, HEAD_DIM), cosine, -sine
    )
    grad_qkv = jnp.concatenate(
        [
            grad_q.reshape(tok_rows, width).astype(BF),
            grad_k.reshape(tok_rows, kv_width).astype(BF),
            grad_kv_mine[:, kv_width:].astype(BF),
        ],
        axis=1,
    )
    grad_wqkv = inner_rows(n_first, grad_qkv)
    grad_bias = jnp.sum(grad_qkv.astype(F32), axis=0)
    grad_n1 = times_back(grad_qkv, w_qkv)
    grad_x_norm, grad_gain_attn = norm_back(inputs, inv_first, gain_attn, grad_n1)
    input_grad = grad_mid + grad_x_norm
    used = 3 * width + 2 * kv_width
    padding = jnp.zeros((vectors.shape[0] * count - used,), F32)
    vector_term = jnp.concatenate([grad_bias, grad_gain_attn, grad_gain_mlp, padding])

    def shares(term):
        return lax.psum_scatter(term.reshape(-1), AXES, scatter_dimension=0, tiled=True)

    return (
        layer_out, input_grad, shares(grad_wqkv[:, :width]),
        shares(grad_wqkv[:, width : ends[1]]), shares(grad_wqkv[:, ends[1] :]),
        shares(grad_wout), shares(grad_wgate), shares(grad_wup), shares(grad_wdown),
        shares(vector_term),
    )


def solution(mesh):
    split = P(AXES)
    rows = P(AXES, None)
    in_specs = (rows,) + (split,) * 8 + (P("dp", None), rows)
    out_specs = (rows, rows) + (split,) * 8
    return jax.shard_map(local, mesh=mesh, in_specs=in_specs, out_specs=out_specs, check_vma=False)
```

```python
import functools

import jax
import jax.numpy as jnp
import numpy as np
from jax import lax
from jax.experimental import pallas as pl
from jax.experimental.pallas import tpu as pltpu
from jax.sharding import PartitionSpec as P

KV_HEADS = 3
HEAD_DIM = 64

EPS = 1e-06
THETA = 100000.0
NEG_FILL = -1e30
AXES = ("dp", "ctx")
BF = jnp.bfloat16
F32 = jnp.float32


def times(left, right):
    return jnp.dot(left, right, preferred_element_type=F32)


def inner_rows(left, right):
    return lax.dot_general(left, right, (((0,), (0,)), ((), ())), preferred_element_type=F32)


def times_back(left, right):
    return lax.dot_general(left, right, (((1,), (1,)), ((), ())), preferred_element_type=F32)


def norm_back(values, inv, gain, grad):
    scaled = grad * gain
    dot = jnp.mean(scaled * values, axis=-1, keepdims=True)
    grad_values = inv * scaled - values * (inv * inv * inv * dot)
    grad_gain = jnp.sum(grad * values * inv, axis=0)
    return grad_values, grad_gain


def turn(values, cosine, sine):
    half = values.shape[-1] // 2
    first = values[..., :half]
    second = values[..., half:]
    return jnp.concatenate(
        [first * cosine - second * sine, second * cosine + first * sine], axis=-1
    )


def doc_layout(lengths, count):
    ends = jnp.cumsum(lengths)
    place = jnp.arange(count, dtype=jnp.int32)
    segment = jnp.sum((place[:, None] >= ends[None, :-1]).astype(jnp.int32), axis=1)
    starts = ends - lengths
    picked = segment[:, None] == jnp.arange(lengths.shape[0], dtype=jnp.int32)[None, :]
    first = jnp.sum(jnp.where(picked, starts[None, :], 0), axis=1)
    return place - first


def segment_of(row, info, docs):
    return sum(jnp.where(row >= info[3 + j], 1, 0) for j in range(docs - 1))


def fill_bias(bias, info, docs, short):
    total, rows = bias.shape
    at = lax.broadcasted_iota(jnp.int32, (total, 1), 0)
    row_k = at + jnp.where(at < total - short, info[1], info[2] - (total - short))
    row_q = lax.broadcasted_iota(jnp.int32, (1, rows), 1) + info[2]
    if short == total:
        row_k = at
    same = segment_of(row_k, info, docs) == segment_of(row_q, info, docs)
    bias[...] = jnp.where(same & (row_k <= row_q), 0.0, NEG_FILL)


def key_range(full, total, short, rows, block, at, causal):
    start = 0 if full else total - short
    stop = total - rows + (at + 1) * block if causal else total
    return start, stop


def attn_fwd_kernel(
    heads, block, short, causal, docs, info, q_ref, kv_ref, out_ref, lse_ref, qs, ks, vts, bias, out_t,
):
    rows = q_ref.shape[0]
    total = kv_ref.shape[0]
    kv_width = KV_HEADS * HEAD_DIM
    group = heads // KV_HEADS
    fill_bias(bias, info, docs, short)
    for h in range(heads):
        qs[h] = q_ref[:, h * HEAD_DIM : (h + 1) * HEAD_DIM] * BF(HEAD_DIM**-0.5)
    for g in range(KV_HEADS):
        ks[g] = kv_ref[:, g * HEAD_DIM : (g + 1) * HEAD_DIM]
    vts[...] = jnp.transpose(kv_ref[:, kv_width:].astype(F32)).astype(BF)

    def run(full):
        @pl.loop(0, heads)
        def _(h):
            g = h // group
            v_rows = pl.ds(pl.multiple_of(g * HEAD_DIM, HEAD_DIM), HEAD_DIM)
            out_rows = pl.ds(pl.multiple_of(h * HEAD_DIM, HEAD_DIM), HEAD_DIM)
            for at in range(rows // block):
                start, stop = key_range(full, total, short, rows, block, at, causal)
                cols = slice(at * block, (at + 1) * block)
                s = times_back(ks[g, start:stop], qs[h, cols])
                s = s + bias[start:stop, cols]
                top = jnp.max(s, axis=0, keepdims=True)
                p = jnp.exp(s - top)
                total_p = jnp.sum(p, axis=0, keepdims=True)
                o = times(vts[v_rows, start:stop], p.astype(BF))
                out_t[out_rows, cols] = o / total_p
                lse_ref[h, :, cols] = top + jnp.log(total_p)

    pl.when(info[0] != 0)(lambda: run(True))
    pl.when(info[0] == 0)(lambda: run(False))
    out_ref[...] = jnp.transpose(out_t[...]).astype(BF)


def attn_bwd_kernel(
    heads, block, short, causal, docs, g0, g1, info, q_ref, kv_ref, do_ref, lse_ref, *refs,
):
    outs, scratch = refs[:-9], refs[-9:]
    qs, ks, vs, kts, dos, bias, dq_t, dk, dv = scratch
    rows = q_ref.shape[0]
    total = kv_ref.shape[0]
    kv_width = KV_HEADS * HEAD_DIM
    group = heads // KV_HEADS
    keys = g1 - g0
    fill_bias(bias, info, docs, short)
    for h in range(keys * group):
        lanes = slice((g0 * group + h) * HEAD_DIM, (g0 * group + h + 1) * HEAD_DIM)
        qs[h] = q_ref[:, lanes] * BF(HEAD_DIM**-0.5)
        dos[h] = do_ref[:, lanes]
    for g in range(keys):
        lo = (g0 + g) * HEAD_DIM
        ks[g] = kv_ref[:, lo : lo + HEAD_DIM]
        vs[g] = kv_ref[:, kv_width + lo : kv_width + lo + HEAD_DIM]
        kts[g] = jnp.transpose(ks[g].astype(F32)).astype(BF)
    dk[...] = jnp.zeros_like(dk)
    dv[...] = jnp.zeros_like(dv)

    def run(full):
        @pl.loop(0, keys * group)
        def _(h):
            g = h // group if keys > 1 else 0
            out_rows = pl.ds(pl.multiple_of(h * HEAD_DIM, HEAD_DIM), HEAD_DIM)
            for at in range(rows // block):
                start, stop = key_range(full, total, short, rows, block, at, causal)
                cols = slice(at * block, (at + 1) * block)
                q = qs[h, cols]
                do = dos[h, cols]
                s = times_back(ks[g, start:stop], q)
                p = jnp.exp(s + bias[start:stop, cols] - lse_ref[g0 * group + h, :, cols])
                dp = times_back(vs[g, start:stop], do)
                t = p * dp
                inner = jnp.sum(t, axis=0, keepdims=True)
                ds = (t - p * inner).astype(BF)
                dk[g, start:stop] += times(ds, q)
                dv[g, start:stop] += times(p.astype(BF), do)
                dq_t[out_rows, cols] = times(kts[g, :, start:stop], ds) * HEAD_DIM**-0.5

    pl.when(info[0] != 0)(lambda: run(True))
    pl.when(info[0] == 0)(lambda: run(False))
    outs[0][...] = jnp.transpose(dq_t[...])
    cut = total - outs[1].shape[0]
    for part, out in ((slice(cut, total), outs[1]),) + tuple((slice(0, cut), o) for o in outs[2:]):
        for g in range(keys):
            lo = g * HEAD_DIM
            out[:, lo : lo + HEAD_DIM] = dk[g, part].astype(out.dtype)
            lo += keys * HEAD_DIM
            out[:, lo : lo + HEAD_DIM] = dv[g, part].astype(out.dtype)


VM = pl.BlockSpec(memory_space=pltpu.VMEM)
SM = pl.BlockSpec(memory_space=pltpu.SMEM)


def attn_cost(rows, total, heads, products):
    return pl.CostEstimate(
        flops=8 * products * rows * total * heads * HEAD_DIM,
        bytes_accessed=4 * (rows + total) * heads * HEAD_DIM,
        transcendentals=rows * total * heads,
    )


def attention(q, kv, info, docs, short, causal):
    rows, width = q.shape
    total = kv.shape[0]
    heads = width // HEAD_DIM
    block = min(rows, 256)
    return pl.pallas_call(
        functools.partial(attn_fwd_kernel, heads, block, short, causal, docs),
        out_shape=(
            jax.ShapeDtypeStruct((rows, width), BF),
            jax.ShapeDtypeStruct((heads, 1, rows), F32),
        ),
        in_specs=[SM] + [VM] * 2,
        out_specs=(VM, VM),
        scratch_shapes=[
            pltpu.VMEM((heads, rows, HEAD_DIM), BF),
            pltpu.VMEM((KV_HEADS, total, HEAD_DIM), BF),
            pltpu.VMEM((KV_HEADS * HEAD_DIM, total), BF),
            pltpu.VMEM((total, rows), F32),
            pltpu.VMEM((width, rows), F32),
        ],
        compiler_params=pltpu.CompilerParams(vmem_limit_bytes=20 * 2**20),
        cost_estimate=attn_cost(rows, total, heads, 2),
        name="attn_fwd",
    )(info, q, kv)


def attention_back(q, kv, grad_out, lse, info, docs, short, causal, g0, g1):
    rows, width = q.shape
    total = kv.shape[0]
    heads = width // HEAD_DIM
    block = min(rows, 256)
    keys = g1 - g0
    mine = heads // KV_HEADS * keys
    outs = [jax.ShapeDtypeStruct((rows, mine * HEAD_DIM), F32)]
    if causal:
        outs.append(jax.ShapeDtypeStruct((rows, 2 * keys * HEAD_DIM), F32))
        outs.append(jax.ShapeDtypeStruct((total - rows, 2 * keys * HEAD_DIM), BF))
    else:
        outs.append(jax.ShapeDtypeStruct((total, 2 * keys * HEAD_DIM), F32))
    return pl.pallas_call(
        functools.partial(attn_bwd_kernel, heads, block, short, causal, docs, g0, g1),
        out_shape=outs,
        in_specs=[SM] + [VM] * 4,
        out_specs=[VM] * len(outs),
        scratch_shapes=[
            pltpu.VMEM((mine, rows, HEAD_DIM), BF),
            pltpu.VMEM((keys, total, HEAD_DIM), BF),
            pltpu.VMEM((keys, total, HEAD_DIM), BF),
            pltpu.VMEM((keys, HEAD_DIM, total), BF),
            pltpu.VMEM((mine, rows, HEAD_DIM), BF),
            pltpu.VMEM((total, rows), F32),
            pltpu.VMEM((mine * HEAD_DIM, rows), F32),
            pltpu.VMEM((keys, total, HEAD_DIM), F32),
            pltpu.VMEM((keys, total, HEAD_DIM), F32),
        ],
        compiler_params=pltpu.CompilerParams(vmem_limit_bytes=20 * 2**20),
        cost_estimate=attn_cost(rows, total, mine, 5),
        name="attn_bwd",
    )(info, q, kv, grad_out, lse)


TAIL = 2
MAIN = 16
PIECES = MAIN // TAIL


class Blocks:
    def __init__(self, dp_count, ctx_count):
        self.count = dp_count * ctx_count
        self.x = 1
        self.core = ctx_count
        self.y = 2 * ctx_count
        self.z = 4 * ctx_count
        self.zs = dp_count // 4
        self.masks = []
        for p in range(self.count):
            z, x = p % self.zs, p // self.zs % 2
            y, core = p // (2 * self.zs) % 2, p // (4 * self.zs)
            self.masks.append(x * self.x + y * self.y + core * self.core + z * self.z)

    def swap(self, values, mask):
        perm = [(i, i ^ mask) for i in range(self.count)]
        return lax.ppermute(values, AXES, perm)

    def along_z(self, mine):
        return jnp.stack([mine] + [self.swap(mine, d * self.z) for d in range(1, self.zs)])

    def add(self, keep, got):
        return (keep.astype(F32) + got.astype(F32)).astype(BF)

    def sum_z(self, held):
        got = [self.swap(held[d], d * self.z).astype(F32) for d in range(1, self.zs)]
        return functools.reduce(jnp.add, got, held[0].astype(F32))


class Sizes:
    def __init__(self, width, ff, count, vec, kv_width):
        self.width, self.ff, self.count, self.vec = width, ff, count, vec
        self.rows = width // count
        self.f_rows = ff // count
        up = lambda n: (n + 127) // 128 * 128
        self.wide = up(width)
        self.qkv = width + 2 * kv_width
        self.a_width = up(self.qkv)
        self.tall = (self.rows + 1 + 7) // 8 * 8
        self.downs = self.f_rows // MAIN
        self.piece = 2 * ff // PIECES
        self.gate = 0
        self.tail = ff
        self.tail_o = self.tail + self.piece
        self.out = self.tail_o + 128
        self.down0 = self.out + self.wide
        self.first = self.down0 + self.wide
        self.second = ff + (self.downs - 1) * self.wide
        self.flat = self.a_width + 2 * self.wide

    def down_at(self, c):
        return (0, self.down0) if c == 0 else (1, self.ff + (c - 1) * self.wide)

    def fits(self):
        return (
            self.rows == MAIN + TAIL
            and self.f_rows % MAIN == 0
            and self.piece % 128 == 0
            and self.ff % 256 == 0
            and self.wide <= 128 * PIECES
            and self.vec <= 128
        )


def slot_tables(size, masks):
    far = -(2**20)
    a = [(masks[s // size.tall], s % size.tall) for s in range(size.count * size.tall)]
    a = [(m, i if i < size.rows else far) for m, i in a]
    b = [(masks[s // MAIN], s % MAIN) for s in range(size.count * MAIN)]
    b += [(masks[s // TAIL], MAIN + s % TAIL) for s in range(size.count * TAIL)]
    flat = []
    natural = [(0, size.qkv, size.a_width), (size.qkv, size.width, size.wide)]
    natural += [(size.qkv + size.width, size.width, size.wide)]
    for start, used, room in natural:
        for c in range(room):
            at = start + c
            flat.append((at // size.vec, at % size.vec) if c < used else (far, far))
    owners = np.asarray(masks, np.int32)[:, None]
    as_rows = lambda pairs: np.ascontiguousarray(np.asarray(pairs, np.int32).T)
    return as_rows(a), as_rows(b), as_rows(flat), owners


def wire_kernel(
    size, g_ref, u_ref, o_ref, d_ref, xt_ref, cott_ref, out1, out2, x_ref, cot_ref, tail, tail_o
):
    ff, width = size.ff, size.width
    x_ref[...] = jnp.transpose(xt_ref[...].astype(F32)).astype(BF)
    cot_ref[...] = jnp.transpose(cott_ref[...].astype(F32)).astype(BF)
    out1[:, : ff] = g_ref[:MAIN]
    out2[:, : ff] = u_ref[:MAIN]
    out1[:, size.out : size.out + size.wide] = jnp.zeros((MAIN, size.wide), BF)
    out1[:, size.out : size.out + width] = o_ref[:MAIN]
    tail_o[...] = jnp.zeros_like(tail_o)
    odd = [ref[MAIN:].astype(F32) for ref in (g_ref, u_ref, o_ref)]
    for c in range(PIECES):
        src = odd[c * size.piece // ff]
        at = c * size.piece % ff
        tail[c * TAIL : (c + 1) * TAIL] = src[:, at : at + size.piece]
        used = min(128, width - c * 128)
        if used > 0:
            tail_o[c * TAIL : (c + 1) * TAIL, :used] = odd[2][:, c * 128 : c * 128 + used]
    out1[:, size.tail : size.tail + size.piece] = tail[...].astype(BF)
    out1[:, size.tail_o : size.tail_o + 128] = tail_o[...].astype(BF)
    for c in range(size.downs):
        which, at = size.down_at(c)
        out = (out1, out2)[which]
        out[:, at : at + size.wide] = jnp.zeros((MAIN, size.wide), BF)
        out[:, at : at + width] = d_ref[c * MAIN : (c + 1) * MAIN]


def place_matrix(size, me, table):
    feature = size.rows * (me ^ table[0:1, :]) + table[1:2, :]
    shape = (size.width, feature.shape[1])
    at = lax.broadcasted_iota(jnp.int32, shape, 0)
    return jnp.where(at == feature, 1.0, 0.0).astype(BF)


def vector_lanes(table):
    inside = lax.broadcasted_iota(jnp.int32, (128, table.shape[1]), 0)
    return jnp.where(inside == table[1:2, :], 1.0, 0.0).astype(BF)


def split_two(values):
    high = values.astype(BF)
    return high, (values - high.astype(F32)).astype(BF)


def swap_halves(u):
    rolled_back = pltpu.roll(u, 128 - HEAD_DIM // 2, 1)
    rolled = pltpu.roll(u, HEAD_DIM // 2, 1)
    lane = lax.broadcasted_iota(jnp.int32, u.shape, 1)
    return jnp.where(lane % HEAD_DIM < HEAD_DIM // 2, rolled_back, rolled)


def pre_kernel(
    size, me_ref, x_ref, w00, w01, w10, w11, cos_ref, sin_ref, table_a, table_f, owner_ref,
    q_ref, kv_ref, n1t_ref, flat_ref, w, qkv,
):
    me = me_ref[0]
    quarter = w00.shape[0]
    for i, part in enumerate((w00, w01, w10, w11)):
        w[i * quarter : (i + 1) * quarter] = part[...]
    shape = (size.count, 4 * quarter)
    row = lax.broadcasted_iota(jnp.int32, shape, 0) * size.tall + size.rows
    row = lax.broadcasted_iota(jnp.int32, shape, 1) == row
    packed = times(jnp.where(row, 1.0, 0.0).astype(BF), w[:, :128]).astype(BF)
    table = table_f[...]
    spread = times(packed, vector_lanes(table))
    mine = table[0:1, :] == (me ^ owner_ref[...])
    flat = jnp.sum(jnp.where(mine, spread, 0.0), axis=0, keepdims=True)
    flat_ref[...] = flat
    gain = flat[:, size.a_width : size.a_width + size.width]
    x = x_ref[...].astype(F32)
    inv = lax.rsqrt(jnp.mean(x * x, axis=-1, keepdims=True) + EPS)
    n1 = (x * inv * gain).astype(BF)
    n1a = times(n1, place_matrix(size, me, table_a[...]))
    qkv[...] = times(n1a.astype(BF), w[...]) + flat[:, : size.a_width]
    n1t_ref[...] = jnp.transpose(n1a).astype(BF)
    kv_width = kv_ref.shape[1] // 2
    for t in range((size.width + kv_width) // 128):
        u = qkv[:, t * 128 : (t + 1) * 128]
        qkv[:, t * 128 : (t + 1) * 128] = u * cos_ref[...] + swap_halves(u) * sin_ref[...]
    q_ref[...] = qkv[:, : size.width].astype(BF)
    kv_ref[...] = qkv[:, size.width : size.qkv].astype(BF)


def tail_place(size, c):
    shape = (size.count * TAIL, size.count * MAIN)
    q = lax.broadcasted_iota(jnp.int32, shape, 0)
    at = lax.broadcasted_iota(jnp.int32, shape, 1)
    want = (q // TAIL) * MAIN + c * TAIL + q % TAIL
    return jnp.where(at == want, 1.0, 0.0).astype(BF)


def tail_place_back(size, c):
    shape = (size.count * MAIN, size.count * TAIL)
    at = lax.broadcasted_iota(jnp.int32, shape, 0)
    q = lax.broadcasted_iota(jnp.int32, shape, 1)
    want = (q // TAIL) * MAIN + c * TAIL + q % TAIL
    return jnp.where(at == want, 1.0, 0.0).astype(BF)


def mlp_kernel(
    size, masks, me_ref, attn_ref, x_ref, cot_ref, flat_ref,
    b1_00, b1_01, b1_10, b1_11, b2_00, b2_01, b2_10, b2_11, table_b,
    out_ref, keep1, give1, keep2, give2, gmid_ref, gattn_ref, ggain_ref,
    wg, wu, wo, wd, mid, n2s, n2t, place, acc, gacc, dwd, tails, tail_o, packed,
):
    me = me_ref[0]
    width, ff = size.width, size.ff
    part = b1_00.shape[0]
    half, main = 2 * part, 4 * part
    rows_z = part // 2
    place[...] = place_matrix(size, me, table_b[...])
    first = (b1_00, b1_01, b1_10, b1_11)
    second = (b2_00, b2_01, b2_10, b2_11)
    room = size.piece + 128
    for i, b1 in enumerate(first):
        rows = slice(i * part, (i + 1) * part)
        wg[rows] = b1[:, :ff]
        wo[rows] = b1[:, size.out : size.out + size.wide]
        packed[rows] = b1[:, size.tail : size.tail + room]
    for i, b2 in enumerate(second):
        for y in range(2):
            at = (i // 2) * half + y * part + (i % 2) * rows_z
            wu[at : at + rows_z] = b2[y * rows_z : (y + 1) * rows_z, :ff]
    for c in range(PIECES):
        sel = tail_place(size, c)
        target = wg if c * size.piece < ff else wu
        at = c * size.piece % ff
        got = times(sel, packed[:, : size.piece])
        target[main:, at : at + size.piece] = got.astype(BF)
        if c * 128 < size.wide:
            got = times(sel, packed[:, size.piece : room])
            wo[main:, c * 128 : (c + 1) * 128] = got.astype(BF)
    zs = rows_z // MAIN
    for p in range(size.count):
        z, x, y, core = p % zs, p // zs % 2, p // (2 * zs) % 2, p // (4 * zs)
        owner = me ^ masks[p]
        for c in range(size.downs):
            which, at = size.down_at(c)
            src, row = (second[2 * core + x], y * zs + z) if which else (
                first[2 * core + y], x * zs + z
            )
            to = pl.multiple_of(owner * size.f_rows + c * MAIN, MAIN)
            wd[pl.ds(to, MAIN), :] = src[row * MAIN : (row + 1) * MAIN, at : at + size.wide]
    attn_s = times(attn_ref[...], place[...])
    m = x_ref[...].astype(F32) + times(attn_s.astype(BF), wo[:, :width])
    mid[...] = m
    inv = lax.rsqrt(jnp.mean(m * m, axis=-1, keepdims=True) + EPS)
    lo = size.a_width + size.wide
    gain = flat_ref[:, lo : lo + width]
    n2 = (m * inv * gain).astype(BF)
    spread = times(n2, place[...])
    n2s[...] = spread.astype(BF)
    n2t[...] = jnp.transpose(spread).astype(BF)
    acc[...] = jnp.zeros_like(acc)
    gacc[...] = jnp.zeros_like(gacc)
    step = 512 if ff % 512 == 0 else 256

    @pl.loop(0, ff // step)
    def _(b):
        at = pl.multiple_of(b * step, step)
        cols = pl.ds(at, step)
        gate = times(n2s[...], wg[:, cols])
        up = times(n2s[...], wu[:, cols])
        sig = 1.0 / (1.0 + jnp.exp(-gate))
        act = gate * sig
        h = act * up
        gh = times_back(cot_ref[...], wd[cols, :width])
        gg = (gh * up * (sig * (1.0 + gate * (1.0 - sig)))).astype(BF)
        gu = (gh * act).astype(BF)
        acc[...] += times(h.astype(BF), wd[cols, :width])
        dwd[cols, :width] = times(jnp.transpose(h).astype(BF), cot_ref[...]).astype(BF)
        gacc[...] += times_back(gg, wg[:, cols]) + times_back(gu, wu[:, cols])
        for k, (grad, keep, give) in enumerate(((gg, keep1, give1), (gu, keep2, give2))):
            dw = times(n2t[...], grad).astype(BF)
            keep[:, cols] = dw[:half]
            give[:, cols] = dw[half:main]
            tails[:, pl.ds(pl.multiple_of(k * ff + at, 128), step)] = dw[main:]

    m = mid[...]
    inv = lax.rsqrt(jnp.mean(m * m, axis=-1, keepdims=True) + EPS)
    out_ref[...] = jnp.transpose(m + acc[...]).astype(BF)
    high, low = split_two(gacc[...])
    gn2 = times_back(high, place[...]) + times_back(low, place[...])
    scaled = gn2 * gain
    dot = jnp.mean(scaled * m, axis=-1, keepdims=True)
    ggain_ref[...] = jnp.sum(gn2 * m * inv, axis=0, keepdims=True)
    gmid = cot_ref[...].astype(F32) + inv * scaled - m * (inv * inv * inv * dot)
    gmid_ref[...] = gmid
    branch = gmid.astype(BF)
    gattn = times_back(branch, wo[:, :width]).astype(BF)
    gattn_ref[...] = times_back(gattn, place[...]).astype(BF)
    dwo = times(jnp.transpose(attn_s).astype(BF), branch).astype(BF)
    tail_o[...] = jnp.zeros_like(tail_o)
    tail_o[:, :width] = dwo[main:]
    terms = ((keep1, keep2), (give1, give2))
    for i, (term, _) in enumerate(terms):
        term[:, size.out : size.out + width] = dwo[i * half : (i + 1) * half]
    wire = jnp.zeros((main, size.piece), F32)
    wire_o = jnp.zeros((main, 128), F32)
    for c in range(PIECES):
        sel = tail_place_back(size, c)
        wire += times(sel, tails[:, c * size.piece : (c + 1) * size.piece])
        if c * 128 < size.wide:
            wire_o += times(sel, tail_o[:, c * 128 : (c + 1) * 128])
    for i, (term, _) in enumerate(terms):
        rows = slice(i * half, (i + 1) * half)
        term[:, size.tail : size.tail + size.piece] = wire[rows].astype(BF)
        term[:, size.tail_o : size.tail_o + 128] = wire_o[rows].astype(BF)
    for p in range(size.count):
        to = terms[p // (size.count // 2)]
        rows = slice(p * MAIN % half, p * MAIN % half + MAIN)
        owner = me ^ masks[p]
        for c in range(size.downs):
            which, at = size.down_at(c)
            src = pl.multiple_of(owner * size.f_rows + c * MAIN, MAIN)
            to[which][rows, at : at + size.wide] = dwd[pl.ds(src, MAIN), :]


def post_kernel(
    size, me_ref, dq0, dq1, dq2, own0, own1, own2, got0, got1, got2, cos_ref, sin_ref, n1t_ref, w_ref, x_ref,
    gmid_ref, flat_ref, ggain_ref, table_a, table_f, owner_ref,
    gx_ref, keep_ref, give_ref, turn_buf, grad, vec_row,
):
    me = me_ref[0]
    width = size.width
    half = w_ref.shape[0] // 2
    kv_width = KV_HEADS * HEAD_DIM
    turned = width + kv_width
    third = width // KV_HEADS
    grad[...] = jnp.zeros_like(grad)
    parts = ((dq0, own0, got0), (dq1, own1, got1), (dq2, own2, got2))
    for g, (dq, own, got) in enumerate(parts):
        turn_buf[:, g * third : (g + 1) * third] = dq[...]
        dkv = own[...] + got[...].astype(F32)
        lo = width + g * HEAD_DIM
        turn_buf[:, lo : lo + HEAD_DIM] = dkv[:, :HEAD_DIM]
        lo += kv_width
        grad[:, lo : lo + HEAD_DIM] = dkv[:, HEAD_DIM:].astype(BF)
    for t in range(turned // 128):
        u = turn_buf[:, t * 128 : (t + 1) * 128]
        back = u * cos_ref[...] - swap_halves(u) * sin_ref[...]
        grad[:, t * 128 : (t + 1) * 128] = back.astype(BF)
    g = grad[...]
    place = place_matrix(size, me, table_a[...])
    high, low = split_two(times_back(g, w_ref[...]))
    gn1 = times_back(high, place) + times_back(low, place)
    x = x_ref[...].astype(F32)
    inv = lax.rsqrt(jnp.mean(x * x, axis=-1, keepdims=True) + EPS)
    gain = flat_ref[:, size.a_width : size.a_width + width]
    scaled = gn1 * gain
    dot = jnp.mean(scaled * x, axis=-1, keepdims=True)
    gx_ref[...] = jnp.transpose(gmid_ref[...] + inv * scaled - x * (inv * inv * inv * dot))
    vec_row[...] = jnp.zeros_like(vec_row)
    vec_row[:, : size.a_width] = jnp.sum(g.astype(F32), axis=0, keepdims=True)
    vec_row[:, size.a_width : size.a_width + width] = jnp.sum(gn1 * x * inv, axis=0, keepdims=True)
    lo = size.a_width + size.wide
    vec_row[:, lo : lo + width] = ggain_ref[...]
    table = table_f[...]
    mine = table[0:1, :] == (me ^ owner_ref[...])
    packed = times_back(jnp.where(mine, vec_row[...], 0.0).astype(BF), vector_lanes(table))
    shape = (half, size.count)
    for part, term in ((0, keep_ref), (1, give_ref)):
        rows = slice(part * half, (part + 1) * half)
        dw = times(n1t_ref[rows], g)
        term[...] = dw.astype(BF)
        want = lax.broadcasted_iota(jnp.int32, shape, 1) * size.tall + size.rows - part * half
        here = lax.broadcasted_iota(jnp.int32, shape, 0) == want
        extra = times(jnp.where(here, 1.0, 0.0).astype(BF), packed.astype(BF))
        term[:, :128] = (dw[:, :128] + extra).astype(BF)


def call(kernel, name, out_shape, scratch, flops, args, vmem, scalar=True):
    shapes = [jax.ShapeDtypeStruct(s, t) for s, t in out_shape]
    total = sum(int(np.prod(a.shape)) * a.dtype.itemsize for a in args)
    return pl.pallas_call(
        kernel,
        out_shape=shapes,
        in_specs=[SM if scalar and i == 0 else VM for i in range(len(args))],
        out_specs=[VM] * len(shapes),
        scratch_shapes=[pltpu.VMEM(s, t) for s, t in scratch],
        compiler_params=pltpu.CompilerParams(vmem_limit_bytes=vmem * 2**20),
        cost_estimate=pl.CostEstimate(flops=flops, bytes_accessed=total, transcendentals=0),
        name=name,
    )(*args)


def pad_to(values, rows, columns):
    return jnp.pad(values, ((0, rows - values.shape[0]), (0, columns - values.shape[1])))


def tail_pack(rows, piece):
    rows = pad_to(rows, TAIL, PIECES * piece)
    return rows.reshape(TAIL, PIECES, piece).transpose(1, 0, 2).reshape(MAIN, piece)


def tail_unpack(wire, used):
    piece = wire.shape[1]
    rows = wire.reshape(PIECES, TAIL, piece).transpose(1, 0, 2).reshape(TAIL, PIECES * piece)
    return rows[:, :used]


def tie(*values):
    return lax.optimization_barrier(values)


def local_blocks(size, blocks, pos, args):
    (
        tokens, q_weight, k_weight, v_weight, o_weight, gate_weight, up_weight, down_weight,
        vectors, cotangent,
    ) = args
    tok_rows, width = tokens.shape
    ff, rows = size.ff, size.rows
    kv_width = KV_HEADS * HEAD_DIM
    ctx_index = lax.axis_index("ctx")
    me = (lax.axis_index("dp") * lax.axis_size("ctx") + ctx_index).astype(jnp.int32).reshape(1)
    masks = blocks.masks
    half = size.count // 2
    table_a, table_b, table_f, owners = slot_tables(size, masks)
    info, docs, cos, sin = pos

    joined_w = jnp.concatenate(
        [w.reshape(rows, -1) for w in (q_weight, k_weight, v_weight)], axis=1
    )
    vec_row = pad_to(vectors.reshape(1, -1), size.tall - rows, size.a_width)
    wire_a = jnp.concatenate([pad_to(joined_w, rows, size.a_width), vec_row], axis=0)
    za = blocks.along_z(wire_a)
    xa = jnp.stack([za, blocks.swap(za, blocks.x)])
    _, flat_w = tie(za, (gate_weight, up_weight, o_weight, down_weight))
    w_rows = [w.reshape(rows, -1) for w in flat_w[:3]]
    wire_1, wire_2, tokens, cotangent = call(
        functools.partial(wire_kernel, size),
        "wire",
        [
            ((MAIN, size.first), BF), ((MAIN, size.second), BF), ((tok_rows, width), BF),
            ((tok_rows, width), BF),
        ],
        [((MAIN, size.piece), F32), ((MAIN, 128), F32)],
        0,
        w_rows + [flat_w[3].reshape(size.f_rows, width), tokens.T, cotangent.T],
        8,
        scalar=False,
    )
    xa, wire_1, wire_2 = tie(xa, wire_1, wire_2)
    ya = blocks.swap(xa, blocks.y)
    z1 = blocks.along_z(wire_1)
    z1, wire_2, ya = tie(z1, wire_2, ya)
    z2 = blocks.along_z(wire_2)
    x1 = jnp.stack([z1, blocks.swap(z1, blocks.x)])
    a_parts = [a.reshape(half // 2 * size.tall, size.a_width) for a in (xa, ya)]
    a_parts += [blocks.swap(a, blocks.core) for a in a_parts]

    a_rows = size.count * size.tall
    q_rot, kv_mine, n1t, flat, w_a = call(
        functools.partial(pre_kernel, size),
        "norm_qkv",
        [
            ((tok_rows, width), BF), ((tok_rows, 2 * kv_width), BF), ((a_rows, tok_rows), BF),
            ((1, size.flat), F32), ((a_rows, size.a_width), BF),
        ],
        [((tok_rows, size.a_width), F32)],
        4 * tok_rows * width * size.a_width,
        (me, tokens, *a_parts, cos, sin, table_a, table_f, owners),
        16,
    )
    kv_got = blocks.swap(kv_mine, blocks.x)
    z2, x1, kv_got = tie(z2, x1, kv_mine)[:2] + (kv_got,)
    y2 = jnp.stack([z2, blocks.swap(z2, blocks.y)])
    y2, kv_got = tie(y2, kv_got)
    b1_parts = [b.reshape(half // 2 * MAIN, -1) for b in (x1, blocks.swap(x1, blocks.y))]
    b2_parts = [b.reshape(half // 2 * MAIN, -1) for b in (y2, blocks.swap(y2, blocks.x))]
    kv = jnp.concatenate([kv_got, kv_mine], axis=0)
    attn, lse = attention(q_rot, kv, info, docs, tok_rows, True)

    b1_parts[1:] = [b1_parts[1], blocks.swap(b1_parts[0], blocks.core)]
    b2_parts[1:] = [b2_parts[1], blocks.swap(b2_parts[0], blocks.core)]
    attn, b2_parts[1] = tie(attn, b2_parts[1])
    attn, b1_parts[1] = tie(attn, b1_parts[1])
    b2_parts.append(blocks.swap(b2_parts[1], blocks.core))
    b1_parts.append(blocks.swap(b1_parts[1], blocks.core))
    main = size.count * MAIN
    slots = main + size.count * TAIL
    layer_out, keep1, give1, keep2, give2, grad_mid, grad_attn, grad_gain = call(
        functools.partial(mlp_kernel, size, masks),
        "feed_forward",
        [
            ((width, tok_rows), BF),
            ((main // 2, size.first), BF), ((main // 2, size.first), BF),
            ((main // 2, size.second), BF), ((main // 2, size.second), BF),
            ((tok_rows, width), F32), ((tok_rows, width), BF), ((1, width), F32),
        ],
        [
            ((slots, ff), BF), ((slots, ff), BF), ((slots, size.wide), BF), ((ff, size.wide), BF),
            ((tok_rows, width), F32), ((tok_rows, slots), BF), ((slots, tok_rows), BF),
            ((width, slots), BF), ((tok_rows, width), F32), ((tok_rows, slots), F32),
            ((ff, size.wide), BF), ((size.count * TAIL, 2 * ff), BF),
            ((size.count * TAIL, size.wide), BF), ((main, size.piece + 128), BF),
        ],
        2 * tok_rows * width * (9 * ff + 5 * width),
        (
            me, attn, tokens, cotangent, flat, *b1_parts, *b2_parts, table_b,
        ),
        28,
    )

    got1 = blocks.swap(give1, blocks.core)
    got2 = blocks.swap(give2, blocks.core)
    shape = (2, 2, blocks.zs, MAIN, -1)
    h1 = blocks.add(keep1, got1).reshape(shape)
    h2 = blocks.add(keep2, got2).reshape(shape)
    grads, got_kv = [], []
    for g in range(KV_HEADS):
        if g == 1:
            grad_attn, h1, h2 = tie(grad_attn, h1, h2)
            h1 = blocks.add(h1[0], blocks.swap(h1[1], blocks.y))
            h2 = blocks.add(h2[:, 0], blocks.swap(h2[:, 1], blocks.x))
        dq, own, other = attention_back(
            q_rot, kv, grad_attn, lse, info, docs, tok_rows, True, g, g + 1
        )
        if g == KV_HEADS - 1:
            other, h1, h2 = tie(other, h1, h2)
        grads.append((dq, own))
        got_kv.append(blocks.swap(other, blocks.x))
    h1 = blocks.add(h1[0], blocks.swap(h1[1], blocks.x))
    h2 = blocks.add(h2[0], blocks.swap(h2[1], blocks.y))

    gx, keep_a, give_a = call(
        functools.partial(post_kernel, size),
        "norm_qkv_back",
        [
            ((width, tok_rows), F32), ((a_rows // 2, size.a_width), BF),
            ((a_rows // 2, size.a_width), BF),
        ],
        [
            ((tok_rows, width + kv_width), F32), ((tok_rows, size.a_width), BF),
            ((1, size.flat), F32),
        ],
        6 * tok_rows * width * size.a_width,
        (
            me, *[g[0] for g in grads], *[g[1] for g in grads], *got_kv, cos, sin, n1t, w_a,
            tokens, grad_mid, flat, grad_gain, table_a, table_f, owners,
        ),
        24,
    )
    held = blocks.add(keep_a, blocks.swap(give_a, blocks.core))
    held, h2 = tie(held, h2)
    held = held.reshape(2, 2, blocks.zs, size.tall, size.a_width)
    held = blocks.add(held[0], blocks.swap(held[1], blocks.y))
    held, share2, h1 = tie(held, blocks.sum_z(h2), h1)
    held = blocks.add(held[0], blocks.swap(held[1], blocks.x))
    held, share1 = tie(held, blocks.sum_z(h1))
    share_a = blocks.sum_z(held)

    tails = tail_unpack(share1[:, size.tail : size.tail + size.piece], 2 * ff)
    tail_o = tail_unpack(share1[:, size.tail_o : size.tail_o + 128], width)
    share_out = jnp.concatenate([share1[:, size.out : size.out + width], tail_o], axis=0)
    share_gate = jnp.concatenate([share1[:, :ff], tails[:, :ff]], axis=0)
    share_up = jnp.concatenate([share2[:, :ff], tails[:, ff:]], axis=0)
    downs = [size.down_at(c) for c in range(size.downs)]
    share_down = jnp.concatenate(
        [(share1, share2)[which][:, at : at + width] for which, at in downs], axis=0
    )
    ends = (width, width + kv_width, size.qkv)
    return (
        layer_out.T, gx.T, share_a[:rows, : ends[0]].reshape(-1),
        share_a[:rows, ends[0] : ends[1]].reshape(-1),
        share_a[:rows, ends[1] : ends[2]].reshape(-1),
        share_out.reshape(-1), share_gate.reshape(-1), share_up.reshape(-1),
        share_down.reshape(-1), share_a[rows, : size.vec],
    )


def local(
    tokens, q_weight, k_weight, v_weight, o_weight, gate_weight, up_weight, down_weight,
    vectors, doc_lengths, cotangent,
):
    tok_rows, width = tokens.shape
    ctx_count = lax.axis_size("ctx")
    dp_count = lax.axis_size("dp")
    count = dp_count * ctx_count
    seq_tokens = tok_rows * ctx_count
    ctx_index = lax.axis_index("ctx")
    heads = width // HEAD_DIM
    kv_width = KV_HEADS * HEAD_DIM
    ff = gate_weight.shape[0] * count // width

    position_all = doc_layout(doc_lengths[0], seq_tokens)
    offset = ctx_index * tok_rows
    position_mine = lax.dynamic_slice_in_dim(position_all, offset, tok_rows)
    docs = doc_lengths.shape[1]
    others = (ctx_count - 1 - ctx_index) * tok_rows
    heads_of = jnp.stack([ctx_index, others, offset]).astype(jnp.int32)
    info = jnp.concatenate([heads_of, jnp.cumsum(doc_lengths[0])[:-1].astype(jnp.int32)])
    half = HEAD_DIM // 2
    freq = THETA ** (-jnp.arange(half, dtype=F32) * 2.0 / HEAD_DIM)
    position_f = position_mine.astype(F32)[:, None]

    whole_rows = width % count == 0 and ff % count == 0
    if whole_rows and ctx_count == 2 and dp_count % 4 == 0 and count & (count - 1) == 0:
        size = Sizes(width, ff, count, vectors.shape[0], kv_width)
        if size.fits() and (width + kv_width) % 128 == 0:
            angle = position_f * jnp.tile(freq, 128 // half)[None, :]
            sign = np.where(np.arange(128) % HEAD_DIM < half, -1.0, 1.0).astype(np.float32)
            pos = (info, docs, jnp.cos(angle), jnp.sin(angle) * sign)
            args = (
                tokens, q_weight, k_weight, v_weight, o_weight, gate_weight, up_weight,
                down_weight, vectors, cotangent,
            )
            return local_blocks(size, Blocks(dp_count, ctx_count), pos, args)

    angle = position_f * freq[None, :]
    cosine = jnp.cos(angle)[:, None, :]
    sine = jnp.sin(angle)[:, None, :]
    inputs = tokens.astype(F32)
    inv_first = lax.rsqrt(jnp.mean(inputs * inputs, axis=-1, keepdims=True) + EPS)

    def whole(part):
        return lax.all_gather(part, AXES, axis=0, tiled=True)

    w_qkv = jnp.concatenate(
        [whole(w).reshape(width, -1) for w in (q_weight, k_weight, v_weight)], axis=1
    )
    w_out = whole(o_weight).reshape(width, width)
    w_gate = whole(gate_weight).reshape(width, ff)
    w_up = whole(up_weight).reshape(width, ff)
    w_down = whole(down_weight).reshape(ff, width)
    flat = whole(vectors).astype(F32)
    ends = [width, width + kv_width, width + 2 * kv_width, 2 * width + 2 * kv_width]
    gain_attn = flat[ends[2] : ends[3]]
    gain_mlp = flat[ends[3] : ends[3] + width]

    n_first = (inputs * inv_first * gain_attn).astype(BF)
    qkv = times(n_first, w_qkv) + flat[: ends[2]]
    q_rot = turn(qkv[:, :width].reshape(tok_rows, heads, HEAD_DIM), cosine, sine)
    q_rot = q_rot.astype(BF).reshape(tok_rows, width)
    k_rot = turn(qkv[:, width : ends[1]].reshape(tok_rows, KV_HEADS, HEAD_DIM), cosine, sine)
    k_rot = k_rot.astype(BF).reshape(tok_rows, kv_width)
    kv_mine = jnp.concatenate([k_rot, qkv[:, ends[1] :].astype(BF)], axis=1)
    kv = lax.all_gather(kv_mine, "ctx", axis=0, tiled=True)
    info = info.at[0].set(1)
    attn, lse = attention(q_rot, kv, info, docs, seq_tokens, False)
    mid = inputs + times(attn, w_out)
    inv_second = lax.rsqrt(jnp.mean(mid * mid, axis=-1, keepdims=True) + EPS)
    n_second = (mid * inv_second * gain_mlp).astype(BF)
    gate = times(n_second, w_gate)
    up_val = times(n_second, w_up)
    sig = jax.nn.sigmoid(gate)
    act = gate * sig
    hidden = (act * up_val).astype(BF)
    layer_out = (mid + times(hidden, w_down)).astype(BF)

    grad_wdown = inner_rows(hidden, cotangent)
    grad_hidden = times_back(cotangent, w_down)
    grad_gate = (grad_hidden * up_val * (sig * (1.0 + gate * (1.0 - sig)))).astype(BF)
    grad_up = (grad_hidden * act).astype(BF)
    grad_wgate = inner_rows(n_second, grad_gate)
    grad_wup = inner_rows(n_second, grad_up)
    grad_n2 = times_back(grad_gate, w_gate) + times_back(grad_up, w_up)
    grad_mid_norm, grad_gain_mlp = norm_back(mid, inv_second, gain_mlp, grad_n2)
    grad_mid = cotangent.astype(F32) + grad_mid_norm
    grad_branch = grad_mid.astype(BF)
    grad_wout = inner_rows(attn, grad_branch)
    grad_attn = times_back(grad_branch, w_out).astype(BF)
    grad_q_rot, grad_kv = attention_back(
        q_rot, kv, grad_attn, lse, info, docs, seq_tokens, False, 0, KV_HEADS
    )
    grad_kv_mine = lax.psum_scatter(
        grad_kv.astype(BF), "ctx", scatter_dimension=0, tiled=True
    ).astype(F32)
    grad_q = turn(grad_q_rot.reshape(tok_rows, heads, HEAD_DIM), cosine, -sine)
    grad_k = turn(
        grad_kv_mine[:, :kv_width].reshape(tok_rows, KV_HEADS, HEAD_DIM), cosine, -sine
    )
    grad_qkv = jnp.concatenate(
        [
            grad_q.reshape(tok_rows, width).astype(BF),
            grad_k.reshape(tok_rows, kv_width).astype(BF),
            grad_kv_mine[:, kv_width:].astype(BF),
        ],
        axis=1,
    )
    grad_wqkv = inner_rows(n_first, grad_qkv)
    grad_bias = jnp.sum(grad_qkv.astype(F32), axis=0)
    grad_n1 = times_back(grad_qkv, w_qkv)
    grad_x_norm, grad_gain_attn = norm_back(inputs, inv_first, gain_attn, grad_n1)
    input_grad = grad_mid + grad_x_norm
    used = 3 * width + 2 * kv_width
    padding = jnp.zeros((vectors.shape[0] * count - used,), F32)
    vector_term = jnp.concatenate([grad_bias, grad_gain_attn, grad_gain_mlp, padding])

    def shares(term):
        return lax.psum_scatter(term.reshape(-1), AXES, scatter_dimension=0, tiled=True)

    return (
        layer_out, input_grad, shares(grad_wqkv[:, :width]),
        shares(grad_wqkv[:, width : ends[1]]), shares(grad_wqkv[:, ends[1] :]),
        shares(grad_wout), shares(grad_wgate), shares(grad_wup), shares(grad_wdown),
        shares(vector_term),
    )


def solution(mesh):
    split = P(AXES)
    rows = P(AXES, None)
    in_specs = (rows,) + (split,) * 8 + (P("dp", None), rows)
    out_specs = (rows, rows) + (split,) * 8
    return jax.shard_map(local, mesh=mesh, in_specs=in_specs, out_specs=out_specs, check_vma=False)
```

```python
import functools

import jax
import jax.numpy as jnp
import numpy as np
from jax import lax
from jax.experimental import pallas as pl
from jax.experimental.pallas import tpu as pltpu
from jax.sharding import PartitionSpec as P

KV_HEADS = 3
HEAD_DIM = 64

EPS = 1e-06
THETA = 100000.0
NEG_FILL = -1e30
AXES = ("dp", "ctx")
BF = jnp.bfloat16
F32 = jnp.float32


def times(left, right):
    return jnp.dot(left, right, preferred_element_type=F32)


def inner_rows(left, right):
    return lax.dot_general(left, right, (((0,), (0,)), ((), ())), preferred_element_type=F32)


def times_back(left, right):
    return lax.dot_general(left, right, (((1,), (1,)), ((), ())), preferred_element_type=F32)


def norm_back(values, inv, gain, grad):
    scaled = grad * gain
    dot = jnp.mean(scaled * values, axis=-1, keepdims=True)
    grad_values = inv * scaled - values * (inv * inv * inv * dot)
    grad_gain = jnp.sum(grad * values * inv, axis=0)
    return grad_values, grad_gain


def turn(values, cosine, sine):
    half = values.shape[-1] // 2
    first = values[..., :half]
    second = values[..., half:]
    return jnp.concatenate(
        [first * cosine - second * sine, second * cosine + first * sine], axis=-1
    )


def doc_layout(lengths, count):
    ends = jnp.cumsum(lengths)
    place = jnp.arange(count, dtype=jnp.int32)
    segment = jnp.sum((place[:, None] >= ends[None, :-1]).astype(jnp.int32), axis=1)
    starts = ends - lengths
    picked = segment[:, None] == jnp.arange(lengths.shape[0], dtype=jnp.int32)[None, :]
    first = jnp.sum(jnp.where(picked, starts[None, :], 0), axis=1)
    return place - first


def fill_bias(bias, info, docs, short):
    total, rows = bias.shape
    row_q = lax.broadcasted_iota(jnp.int32, (1, rows), 1) + info[2]
    first = jnp.zeros_like(row_q)
    for j in range(docs - 1):
        first = jnp.where(row_q >= info[3 + j], info[3 + j], first)
    parts = ((0, total, 0),)
    if short < total:
        parts = ((0, total - short, info[1]), (total - short, total, info[2]))
    for start, stop, base in parts:
        row_k = lax.broadcasted_iota(jnp.int32, (stop - start, rows), 0)
        allowed = (row_k >= first - base) & (row_k <= row_q - base)
        bias[start:stop] = jnp.where(allowed, 0.0, NEG_FILL)


def key_range(full, total, short, rows, block, at, causal):
    start = 0 if full else total - short
    stop = total - rows + (at + 1) * block if causal else total
    return start, stop


def key_parts(kv_refs):
    at = 0
    for kv_ref in kv_refs:
        yield slice(at, at + kv_ref.shape[0]), kv_ref
        at += kv_ref.shape[0]


def attn_fwd_kernel(
    heads, block, short, causal, docs, info, q_ref, *refs,
):
    kv_refs, (out_ref, lse_ref, qs, ks, vts, bias, out_t) = refs[:-7], refs[-7:]
    rows = q_ref.shape[0]
    total = bias.shape[0]
    kv_width = KV_HEADS * HEAD_DIM
    group = heads // KV_HEADS
    fill_bias(bias, info, docs, short)
    for h in range(heads):
        qs[h] = q_ref[:, h * HEAD_DIM : (h + 1) * HEAD_DIM] * BF(HEAD_DIM**-0.5)
    for at, kv_ref in key_parts(kv_refs):
        for g in range(KV_HEADS):
            ks[g, at] = kv_ref[:, g * HEAD_DIM : (g + 1) * HEAD_DIM]
        vts[:, at] = jnp.transpose(kv_ref[:, kv_width:].astype(F32)).astype(BF)

    def run(full):
        @pl.loop(0, KV_HEADS)
        def _(g):
            v_rows = pl.ds(pl.multiple_of(g * HEAD_DIM, HEAD_DIM), HEAD_DIM)
            for j in range(group):
                h = g * group + j
                out_rows = pl.ds(pl.multiple_of(h * HEAD_DIM, HEAD_DIM), HEAD_DIM)
                for at in range(rows // block):
                    start, stop = key_range(full, total, short, rows, block, at, causal)
                    cols = slice(at * block, (at + 1) * block)
                    s = times_back(ks[g, start:stop], qs[h, cols])
                    s = s + bias[start:stop, cols]
                    top = jnp.max(s, axis=0, keepdims=True)
                    p = jnp.exp(s - top)
                    total_p = jnp.sum(p, axis=0, keepdims=True)
                    o = times(vts[v_rows, start:stop], p.astype(BF))
                    out_t[out_rows, cols] = o / total_p
                    lse_ref[h, :, cols] = top + jnp.log(total_p)

    pl.when(info[0] != 0)(lambda: run(True))
    pl.when(info[0] == 0)(lambda: run(False))
    out_ref[...] = jnp.transpose(out_t[...]).astype(BF)


def attn_bwd_kernel(
    heads, block, short, causal, docs, g0, g1, parts, info, q_ref, do_ref, lse_ref, *refs,
):
    kv_refs, outs, scratch = refs[:parts], refs[parts:-9], refs[-9:]
    qs, ks, vs, kts, dos, bias, dq_t, dk, dv = scratch
    rows = q_ref.shape[0]
    total = bias.shape[0]
    kv_width = KV_HEADS * HEAD_DIM
    group = heads // KV_HEADS
    keys = g1 - g0
    fill_bias(bias, info, docs, short)
    for h in range(keys * group):
        lanes = slice((g0 * group + h) * HEAD_DIM, (g0 * group + h + 1) * HEAD_DIM)
        qs[h] = q_ref[:, lanes] * BF(HEAD_DIM**-0.5)
        dos[h] = do_ref[:, lanes]
    for g in range(keys):
        lo = (g0 + g) * HEAD_DIM
        for at, kv_ref in key_parts(kv_refs):
            ks[g, at] = kv_ref[:, lo : lo + HEAD_DIM]
            vs[g, at] = kv_ref[:, kv_width + lo : kv_width + lo + HEAD_DIM]
        kts[g] = jnp.transpose(ks[g].astype(F32)).astype(BF)
    dk[...] = jnp.zeros_like(dk)
    dv[...] = jnp.zeros_like(dv)

    def run(full):
        @pl.loop(0, keys * group)
        def _(h):
            g = h // group if keys > 1 else 0
            out_rows = pl.ds(pl.multiple_of(h * HEAD_DIM, HEAD_DIM), HEAD_DIM)
            for at in range(rows // block):
                start, stop = key_range(full, total, short, rows, block, at, causal)
                cols = slice(at * block, (at + 1) * block)
                q = qs[h, cols]
                do = dos[h, cols]
                s = times_back(ks[g, start:stop], q)
                p = jnp.exp(s + bias[start:stop, cols] - lse_ref[g0 * group + h, :, cols])
                dp = times_back(vs[g, start:stop], do)
                t = p * dp
                inner = jnp.sum(t, axis=0, keepdims=True)
                ds = (t - p * inner).astype(BF)
                dk[g, start:stop] += times(ds, q)
                dv[g, start:stop] += times(p.astype(BF), do)
                dq_t[out_rows, cols] = times(kts[g, :, start:stop], ds) * HEAD_DIM**-0.5

    pl.when(info[0] != 0)(lambda: run(True))
    pl.when(info[0] == 0)(lambda: run(False))
    outs[0][...] = jnp.transpose(dq_t[...])
    cut = total - outs[1].shape[0]
    for part, out in ((slice(cut, total), outs[1]),) + tuple((slice(0, cut), o) for o in outs[2:]):
        for g in range(keys):
            lo = g * HEAD_DIM
            out[:, lo : lo + HEAD_DIM] = dk[g, part].astype(out.dtype)
            lo += keys * HEAD_DIM
            out[:, lo : lo + HEAD_DIM] = dv[g, part].astype(out.dtype)


VM = pl.BlockSpec(memory_space=pltpu.VMEM)
SM = pl.BlockSpec(memory_space=pltpu.SMEM)


def attn_cost(rows, total, heads, products):
    return pl.CostEstimate(
        flops=8 * products * rows * total * heads * HEAD_DIM,
        bytes_accessed=4 * (rows + total) * heads * HEAD_DIM,
        transcendentals=rows * total * heads,
    )


def attention(q, kv, info, docs, short, causal):
    rows, width = q.shape
    total = sum(part.shape[0] for part in kv)
    heads = width // HEAD_DIM
    block = min(rows, 256)
    return pl.pallas_call(
        functools.partial(attn_fwd_kernel, heads, block, short, causal, docs),
        out_shape=(
            jax.ShapeDtypeStruct((rows, width), BF),
            jax.ShapeDtypeStruct((heads, 1, rows), F32),
        ),
        in_specs=[SM] + [VM] * (1 + len(kv)),
        out_specs=(VM, VM),
        scratch_shapes=[
            pltpu.VMEM((heads, rows, HEAD_DIM), BF),
            pltpu.VMEM((KV_HEADS, total, HEAD_DIM), BF),
            pltpu.VMEM((KV_HEADS * HEAD_DIM, total), BF),
            pltpu.VMEM((total, rows), F32),
            pltpu.VMEM((width, rows), F32),
        ],
        compiler_params=pltpu.CompilerParams(vmem_limit_bytes=20 * 2**20),
        cost_estimate=attn_cost(rows, total, heads, 2),
        name="attn_fwd",
    )(info, q, *kv)


def attention_back(q, kv, grad_out, lse, info, docs, short, causal, g0, g1):
    rows, width = q.shape
    total = sum(part.shape[0] for part in kv)
    heads = width // HEAD_DIM
    block = min(rows, 256)
    keys = g1 - g0
    mine = heads // KV_HEADS * keys
    outs = [jax.ShapeDtypeStruct((rows, mine * HEAD_DIM), F32)]
    if causal:
        outs.append(jax.ShapeDtypeStruct((rows, 2 * keys * HEAD_DIM), F32))
        outs.append(jax.ShapeDtypeStruct((total - rows, 2 * keys * HEAD_DIM), BF))
    else:
        outs.append(jax.ShapeDtypeStruct((total, 2 * keys * HEAD_DIM), F32))
    return pl.pallas_call(
        functools.partial(attn_bwd_kernel, heads, block, short, causal, docs, g0, g1, len(kv)),
        out_shape=outs,
        in_specs=[SM] + [VM] * (3 + len(kv)),
        out_specs=[VM] * len(outs),
        scratch_shapes=[
            pltpu.VMEM((mine, rows, HEAD_DIM), BF),
            pltpu.VMEM((keys, total, HEAD_DIM), BF),
            pltpu.VMEM((keys, total, HEAD_DIM), BF),
            pltpu.VMEM((keys, HEAD_DIM, total), BF),
            pltpu.VMEM((mine, rows, HEAD_DIM), BF),
            pltpu.VMEM((total, rows), F32),
            pltpu.VMEM((mine * HEAD_DIM, rows), F32),
            pltpu.VMEM((keys, total, HEAD_DIM), F32),
            pltpu.VMEM((keys, total, HEAD_DIM), F32),
        ],
        compiler_params=pltpu.CompilerParams(vmem_limit_bytes=20 * 2**20),
        cost_estimate=attn_cost(rows, total, mine, 5),
        name="attn_bwd",
    )(info, q, grad_out, lse, *kv)


TAIL = 2
MAIN = 16
PIECES = MAIN // TAIL


class Blocks:
    def __init__(self, dp_count, ctx_count):
        self.count = dp_count * ctx_count
        self.x = 1
        self.core = ctx_count
        self.y = 2 * ctx_count
        self.z = 4 * ctx_count
        self.zs = dp_count // 4
        self.masks = []
        for p in range(self.count):
            z, x = p % self.zs, p // self.zs % 2
            y, core = p // (2 * self.zs) % 2, p // (4 * self.zs)
            self.masks.append(x * self.x + y * self.y + core * self.core + z * self.z)

    def swap(self, values, mask):
        perm = [(i, i ^ mask) for i in range(self.count)]
        return lax.ppermute(values, AXES, perm)

    def along_z(self, mine):
        return jnp.stack([mine] + [self.swap(mine, d * self.z) for d in range(1, self.zs)])

    def add(self, keep, got):
        return (keep.astype(F32) + got.astype(F32)).astype(BF)

    def sum_z(self, held):
        got = [self.swap(held[d], d * self.z).astype(F32) for d in range(1, self.zs)]
        return functools.reduce(jnp.add, got, held[0].astype(F32))


class Sizes:
    def __init__(self, width, ff, dp, ctx, vec, kv_width):
        count = dp * ctx
        self.zs, self.ctx = dp // 4, ctx
        self.width, self.ff, self.count, self.vec = width, ff, count, vec
        self.rows = width // count
        self.f_rows = ff // count
        up = lambda n: (n + 127) // 128 * 128
        self.wide = up(width)
        self.qkv = width + 2 * kv_width
        self.a_width = up(self.qkv)
        self.tall = (self.rows + 1 + 7) // 8 * 8
        self.downs = self.f_rows // MAIN
        self.piece = 2 * ff // PIECES
        self.gate = 0
        self.tail = ff
        self.tail_o = self.tail + self.piece
        self.out = self.tail_o + 128
        self.down0 = self.out + self.wide
        self.first = self.down0 + self.wide
        self.second = ff + (self.downs - 1) * self.wide
        self.flat = self.a_width + 2 * self.wide

    def down_at(self, c):
        return (0, self.down0) if c == 0 else (1, self.ff + (c - 1) * self.wide)

    def fits(self):
        return (
            self.rows == MAIN + TAIL
            and self.f_rows % MAIN == 0
            and self.piece % 128 == 0
            and self.ff % 256 == 0
            and self.wide <= 128 * PIECES
            and self.vec <= 128
        )


def wire_kernel(
    size, g_ref, u_ref, o_ref, d_ref, xt_ref, cott_ref, out1, out2, x_any, cot_any,
    tail, tail_o, x_ref, cot_ref, sems,
):
    ff, width = size.ff, size.width
    x_ref[...] = jnp.transpose(xt_ref[...].astype(F32)).astype(BF)
    cot_ref[...] = jnp.transpose(cott_ref[...].astype(F32)).astype(BF)
    copies = fetch((x_ref, cot_ref), (x_any, cot_any), sems)
    out1[:, : ff] = g_ref[:MAIN]
    out2[:, : ff] = u_ref[:MAIN]
    out1[:, size.out : size.out + size.wide] = jnp.zeros((MAIN, size.wide), BF)
    out1[:, size.out : size.out + width] = o_ref[:MAIN]
    tail_o[...] = jnp.zeros_like(tail_o)
    odd = [ref[MAIN:].astype(F32) for ref in (g_ref, u_ref, o_ref)]
    for c in range(PIECES):
        src = odd[c * size.piece // ff]
        at = c * size.piece % ff
        tail[c * TAIL : (c + 1) * TAIL] = src[:, at : at + size.piece]
        used = min(128, width - c * 128)
        if used > 0:
            tail_o[c * TAIL : (c + 1) * TAIL, :used] = odd[2][:, c * 128 : c * 128 + used]
    out1[:, size.tail : size.tail + size.piece] = tail[...].astype(BF)
    out1[:, size.tail_o : size.tail_o + 128] = tail_o[...].astype(BF)
    for c in range(size.downs):
        which, at = size.down_at(c)
        out = (out1, out2)[which]
        out[:, at : at + size.wide] = jnp.zeros((MAIN, size.wide), BF)
        out[:, at : at + width] = d_ref[c * MAIN : (c + 1) * MAIN]
    for copy in copies:
        copy.wait()


def over(values, by):
    scale = 2**16 // by + 1
    whole = (values * scale) >> 16
    return whole, values - whole * by


def mask_of(size, p):
    z, rest = p % size.zs, p // size.zs
    x, y, core = rest % 2, rest // 2 % 2, rest // 4
    return x + core * size.ctx + y * (2 * size.ctx) + z * (4 * size.ctx)


def lanes(count):
    return lax.broadcasted_iota(jnp.int32, (1, count), 1)


def place_matrix(size, me, tall):
    if tall:
        p, inside = over(lanes(size.count * size.tall), size.tall)
        feature = jnp.where(inside < size.rows, size.rows * (me ^ mask_of(size, p)) + inside, -1)
    else:
        s = lanes(size.count * (MAIN + TAIL))
        tail = s - size.count * MAIN
        p = jnp.where(tail < 0, s // MAIN, tail // TAIL)
        inside = jnp.where(tail < 0, s % MAIN, MAIN + tail % TAIL)
        feature = size.rows * (me ^ mask_of(size, p)) + inside
    at = lax.broadcasted_iota(jnp.int32, (size.width, feature.shape[1]), 0)
    return jnp.where(at == feature, 1.0, 0.0).astype(BF)


def vector_places(size, me):
    at = lanes(size.flat)
    ends = (size.a_width, size.a_width + size.wide)
    part = jnp.where(at < ends[0], 0, jnp.where(at < ends[1], 1, 2))
    inside = at - jnp.where(part == 0, 0, jnp.where(part == 1, ends[0], ends[1]))
    start = jnp.where(part == 0, 0, jnp.where(part == 1, size.qkv, size.qkv + size.width))
    used = inside < jnp.where(part == 0, size.qkv, size.width)
    owner, lane = over(start + inside, size.vec)
    rows = lax.broadcasted_iota(jnp.int32, (128, size.flat), 0)
    spread = jnp.where((rows == lane) & used, 1.0, 0.0).astype(BF)
    p = lax.broadcasted_iota(jnp.int32, (size.count, 1), 0)
    return spread, (owner == (me ^ mask_of(size, p))) & used


def split_two(values):
    high = values.astype(BF)
    return high, (values - high.astype(F32)).astype(BF)


def swap_halves(u):
    rolled_back = pltpu.roll(u, 128 - HEAD_DIM // 2, 1)
    rolled = pltpu.roll(u, HEAD_DIM // 2, 1)
    lane = lax.broadcasted_iota(jnp.int32, u.shape, 1)
    return jnp.where(lane % HEAD_DIM < HEAD_DIM // 2, rolled_back, rolled)


def fetch(sources, targets, sems):
    copies = [
        pltpu.make_async_copy(src, dst, sems.at[i])
        for i, (src, dst) in enumerate(zip(sources, targets))
    ]
    for copy in copies:
        copy.start()
    return copies


def pre_kernel(
    size, me_ref, x_any, w00, w01, w10, w11, cos_any, sin_any,
    q_ref, kv_ref, n1t_any, flat_ref, w_any, x_ref, w, cos_ref, sin_ref, n1t, qkv, sems, out_sems,
):
    me = me_ref[0]
    quarter = w00.shape[0]
    parts = [w.at[pl.ds(i * quarter, quarter)] for i in range(4)]
    copies = fetch(
        (w00, w01, w10, w11, x_any, cos_any, sin_any), (*parts, x_ref, cos_ref, sin_ref), sems
    )
    place = place_matrix(size, me, True)
    spread, mine = vector_places(size, me)
    shape = (size.count, 4 * quarter)
    row = lax.broadcasted_iota(jnp.int32, shape, 0) * size.tall + size.rows
    row = jnp.where(lax.broadcasted_iota(jnp.int32, shape, 1) == row, 1.0, 0.0).astype(BF)
    for copy in copies:
        copy.wait()
    w_out = pltpu.make_async_copy(w, w_any, out_sems.at[0])
    w_out.start()
    packed = times(row, w[:, :128]).astype(BF)
    flat = jnp.sum(jnp.where(mine, times(packed, spread), 0.0), axis=0, keepdims=True)
    flat_ref[...] = flat
    gain = flat[:, size.a_width : size.a_width + size.width]
    x = x_ref[...].astype(F32)
    inv = lax.rsqrt(jnp.mean(x * x, axis=-1, keepdims=True) + EPS)
    n1 = (x * inv * gain).astype(BF)
    n1a = times(n1, place)
    n1t[...] = jnp.transpose(n1a).astype(BF)
    n1t_out = pltpu.make_async_copy(n1t, n1t_any, out_sems.at[1])
    n1t_out.start()
    qkv[...] = times(n1a.astype(BF), w[...]) + flat[:, : size.a_width]
    kv_width = kv_ref.shape[1] // 2
    for t in range((size.width + kv_width) // 128):
        u = qkv[:, t * 128 : (t + 1) * 128]
        qkv[:, t * 128 : (t + 1) * 128] = u * cos_ref[...] + swap_halves(u) * sin_ref[...]
    q_ref[...] = qkv[:, : size.width].astype(BF)
    kv_ref[...] = qkv[:, size.width : size.qkv].astype(BF)
    w_out.wait()
    n1t_out.wait()


def tail_place(size, c):
    shape = (size.count * TAIL, size.count * MAIN)
    q = lax.broadcasted_iota(jnp.int32, shape, 0)
    at = lax.broadcasted_iota(jnp.int32, shape, 1)
    want = (q // TAIL) * MAIN + c * TAIL + q % TAIL
    return jnp.where(at == want, 1.0, 0.0).astype(BF)


def tail_place_back(size, c):
    shape = (size.count * MAIN, size.count * TAIL)
    at = lax.broadcasted_iota(jnp.int32, shape, 0)
    q = lax.broadcasted_iota(jnp.int32, shape, 1)
    want = (q // TAIL) * MAIN + c * TAIL + q % TAIL
    return jnp.where(at == want, 1.0, 0.0).astype(BF)


def mlp_kernel(
    size, me_ref, attn_ref, x_ref, cot_ref, flat_ref,
    b1_00, b1_01, b1_10, b1_11, b2_00, b2_01, b2_10, b2_11,
    out_ref, keep1, give1, keep2, give2, gmid_ref, gattn_ref, ggain_ref,
    wg, wu, wo, wd, mid, n2s, n2t, place, acc, gacc, dwd, tails, tail_o, packed,
):
    me = me_ref[0]
    width, ff = size.width, size.ff
    part = b1_00.shape[0]
    half, main = 2 * part, 4 * part
    rows_z = part // 2
    place[...] = place_matrix(size, me, False)
    first = (b1_00, b1_01, b1_10, b1_11)
    second = (b2_00, b2_01, b2_10, b2_11)
    room = size.piece + 128
    for i, b1 in enumerate(first):
        rows = slice(i * part, (i + 1) * part)
        wg[rows] = b1[:, :ff]
        wo[rows] = b1[:, size.out : size.out + size.wide]
        packed[rows] = b1[:, size.tail : size.tail + room]
    for i, b2 in enumerate(second):
        for y in range(2):
            at = (i // 2) * half + y * part + (i % 2) * rows_z
            wu[at : at + rows_z] = b2[y * rows_z : (y + 1) * rows_z, :ff]
    for c in range(PIECES):
        sel = tail_place(size, c)
        target = wg if c * size.piece < ff else wu
        at = c * size.piece % ff
        got = times(sel, packed[:, : size.piece])
        target[main:, at : at + size.piece] = got.astype(BF)
        if c * 128 < size.wide:
            got = times(sel, packed[:, size.piece : room])
            wo[main:, c * 128 : (c + 1) * 128] = got.astype(BF)
    zs = rows_z // MAIN
    for p in range(size.count):
        z, x, y, core = p % zs, p // zs % 2, p // (2 * zs) % 2, p // (4 * zs)
        owner = me ^ mask_of(size, p)
        for c in range(size.downs):
            which, at = size.down_at(c)
            src, row = (second[2 * core + x], y * zs + z) if which else (
                first[2 * core + y], x * zs + z
            )
            to = pl.multiple_of(owner * size.f_rows + c * MAIN, MAIN)
            wd[pl.ds(to, MAIN), :] = src[row * MAIN : (row + 1) * MAIN, at : at + size.wide]
    attn_s = times(attn_ref[...], place[...])
    m = x_ref[...].astype(F32) + times(attn_s.astype(BF), wo[:, :width])
    mid[...] = m
    inv = lax.rsqrt(jnp.mean(m * m, axis=-1, keepdims=True) + EPS)
    lo = size.a_width + size.wide
    gain = flat_ref[:, lo : lo + width]
    n2 = (m * inv * gain).astype(BF)
    spread = times(n2, place[...])
    n2s[...] = spread.astype(BF)
    n2t[...] = jnp.transpose(spread).astype(BF)
    acc[...] = jnp.zeros_like(acc)
    gacc[...] = jnp.zeros_like(gacc)
    step = 512 if ff % 512 == 0 else 256

    @pl.loop(0, ff // step)
    def _(b):
        at = pl.multiple_of(b * step, step)
        cols = pl.ds(at, step)
        gate = times(n2s[...], wg[:, cols])
        up = times(n2s[...], wu[:, cols])
        sig = 1.0 / (1.0 + jnp.exp(-gate))
        act = gate * sig
        h = act * up
        gh = times_back(cot_ref[...], wd[cols, :width])
        gg = (gh * up * (sig * (1.0 + gate * (1.0 - sig)))).astype(BF)
        gu = (gh * act).astype(BF)
        acc[...] += times(h.astype(BF), wd[cols, :width])
        dwd[cols, :width] = times(jnp.transpose(h).astype(BF), cot_ref[...]).astype(BF)
        gacc[...] += times_back(gg, wg[:, cols]) + times_back(gu, wu[:, cols])
        for k, (grad, keep, give) in enumerate(((gg, keep1, give1), (gu, keep2, give2))):
            dw = times(n2t[...], grad).astype(BF)
            keep[:, cols] = dw[:half]
            give[:, cols] = dw[half:main]
            tails[:, pl.ds(pl.multiple_of(k * ff + at, 128), step)] = dw[main:]

    m = mid[...]
    inv = lax.rsqrt(jnp.mean(m * m, axis=-1, keepdims=True) + EPS)
    out_ref[...] = jnp.transpose(m + acc[...]).astype(BF)
    high, low = split_two(gacc[...])
    gn2 = times_back(high, place[...]) + times_back(low, place[...])
    scaled = gn2 * gain
    dot = jnp.mean(scaled * m, axis=-1, keepdims=True)
    ggain_ref[...] = jnp.sum(gn2 * m * inv, axis=0, keepdims=True)
    gmid = cot_ref[...].astype(F32) + inv * scaled - m * (inv * inv * inv * dot)
    gmid_ref[...] = gmid
    branch = gmid.astype(BF)
    gattn = times_back(branch, wo[:, :width]).astype(BF)
    gattn_ref[...] = times_back(gattn, place[...]).astype(BF)
    dwo = times(jnp.transpose(attn_s).astype(BF), branch).astype(BF)
    tail_o[...] = jnp.zeros_like(tail_o)
    tail_o[:, :width] = dwo[main:]
    terms = ((keep1, keep2), (give1, give2))
    for i, (term, _) in enumerate(terms):
        term[:, size.out : size.out + width] = dwo[i * half : (i + 1) * half]
    wire = jnp.zeros((main, size.piece), F32)
    wire_o = jnp.zeros((main, 128), F32)
    for c in range(PIECES):
        sel = tail_place_back(size, c)
        wire += times(sel, tails[:, c * size.piece : (c + 1) * size.piece])
        if c * 128 < size.wide:
            wire_o += times(sel, tail_o[:, c * 128 : (c + 1) * 128])
    for i, (term, _) in enumerate(terms):
        rows = slice(i * half, (i + 1) * half)
        term[:, size.tail : size.tail + size.piece] = wire[rows].astype(BF)
        term[:, size.tail_o : size.tail_o + 128] = wire_o[rows].astype(BF)
    for p in range(size.count):
        to = terms[p // (size.count // 2)]
        rows = slice(p * MAIN % half, p * MAIN % half + MAIN)
        owner = me ^ mask_of(size, p)
        for c in range(size.downs):
            which, at = size.down_at(c)
            src = pl.multiple_of(owner * size.f_rows + c * MAIN, MAIN)
            to[which][rows, at : at + size.wide] = dwd[pl.ds(src, MAIN), :]


def post_kernel(
    size, me_ref, dq0, dq1, dq2, own0, own1, own2, got0, got1, got2, cos_any, sin_any, n1t_any,
    w_any, x_any, gmid_any, flat_ref, ggain_ref,
    gx_ref, keep_ref, give_ref,
    cos_ref, sin_ref, n1t_ref, w_ref, x_ref, gmid_ref, turn_buf, grad, vec_row, sems,
):
    me = me_ref[0]
    width = size.width
    half = w_ref.shape[0] // 2
    copies = fetch(
        (cos_any, sin_any, n1t_any, w_any, x_any, gmid_any),
        (cos_ref, sin_ref, n1t_ref, w_ref, x_ref, gmid_ref), sems,
    )
    place = place_matrix(size, me, True)
    for copy in copies:
        copy.wait()
    kv_width = KV_HEADS * HEAD_DIM
    turned = width + kv_width
    third = width // KV_HEADS
    grad[...] = jnp.zeros_like(grad)
    parts = ((dq0, own0, got0), (dq1, own1, got1), (dq2, own2, got2))
    for g, (dq, own, got) in enumerate(parts):
        turn_buf[:, g * third : (g + 1) * third] = dq[...]
        dkv = own[...] + got[...].astype(F32)
        lo = width + g * HEAD_DIM
        turn_buf[:, lo : lo + HEAD_DIM] = dkv[:, :HEAD_DIM]
        lo += kv_width
        grad[:, lo : lo + HEAD_DIM] = dkv[:, HEAD_DIM:].astype(BF)
    for t in range(turned // 128):
        u = turn_buf[:, t * 128 : (t + 1) * 128]
        back = u * cos_ref[...] - swap_halves(u) * sin_ref[...]
        grad[:, t * 128 : (t + 1) * 128] = back.astype(BF)
    g = grad[...]
    high, low = split_two(times_back(g, w_ref[...]))
    gn1 = times_back(high, place) + times_back(low, place)
    x = x_ref[...].astype(F32)
    inv = lax.rsqrt(jnp.mean(x * x, axis=-1, keepdims=True) + EPS)
    gain = flat_ref[:, size.a_width : size.a_width + width]
    scaled = gn1 * gain
    dot = jnp.mean(scaled * x, axis=-1, keepdims=True)
    gx_ref[...] = jnp.transpose(gmid_ref[...] + inv * scaled - x * (inv * inv * inv * dot))
    vec_row[...] = jnp.zeros_like(vec_row)
    vec_row[:, : size.a_width] = jnp.sum(g.astype(F32), axis=0, keepdims=True)
    vec_row[:, size.a_width : size.a_width + width] = jnp.sum(gn1 * x * inv, axis=0, keepdims=True)
    lo = size.a_width + size.wide
    vec_row[:, lo : lo + width] = ggain_ref[...]
    spread, mine = vector_places(size, me)
    packed = times_back(jnp.where(mine, vec_row[...], 0.0).astype(BF), spread)
    shape = (half, size.count)
    for part, term in ((0, keep_ref), (1, give_ref)):
        rows = slice(part * half, (part + 1) * half)
        dw = times(n1t_ref[rows], g)
        term[...] = dw.astype(BF)
        want = lax.broadcasted_iota(jnp.int32, shape, 1) * size.tall + size.rows - part * half
        here = lax.broadcasted_iota(jnp.int32, shape, 0) == want
        extra = times(jnp.where(here, 1.0, 0.0).astype(BF), packed.astype(BF))
        term[:, :128] = (dw[:, :128] + extra).astype(BF)


def call(kernel, name, out_shape, scratch, flops, args, vmem, any_in=(), any_out=(), scalar=True):
    shapes = [jax.ShapeDtypeStruct(s, t) for s, t in out_shape]
    total = sum(int(np.prod(a.shape)) * a.dtype.itemsize for a in args)
    here = pl.BlockSpec(memory_space=pl.ANY)
    specs = [here if i in any_in else VM for i in range(len(args))]
    if scalar:
        specs[0] = SM
    return pl.pallas_call(
        kernel,
        out_shape=shapes,
        in_specs=specs,
        out_specs=[here if i in any_out else VM for i in range(len(shapes))],
        scratch_shapes=[
            pltpu.SemaphoreType.DMA(s) if t is None else pltpu.VMEM(s, t) for s, t in scratch
        ],
        compiler_params=pltpu.CompilerParams(vmem_limit_bytes=vmem * 2**20),
        cost_estimate=pl.CostEstimate(flops=flops, bytes_accessed=total, transcendentals=0),
        name=name,
    )(*args)


def pad_to(values, rows, columns):
    return jnp.pad(values, ((0, rows - values.shape[0]), (0, columns - values.shape[1])))


def tail_pack(rows, piece):
    rows = pad_to(rows, TAIL, PIECES * piece)
    return rows.reshape(TAIL, PIECES, piece).transpose(1, 0, 2).reshape(MAIN, piece)


def tail_unpack(wire, used):
    piece = wire.shape[1]
    rows = wire.reshape(PIECES, TAIL, piece).transpose(1, 0, 2).reshape(TAIL, PIECES * piece)
    return rows[:, :used]


def tie(*values):
    return lax.optimization_barrier(values)


def local_blocks(size, blocks, pos, args):
    (
        tokens, q_weight, k_weight, v_weight, o_weight, gate_weight, up_weight, down_weight,
        vectors, cotangent,
    ) = args
    tok_rows, width = tokens.shape
    ff, rows = size.ff, size.rows
    kv_width = KV_HEADS * HEAD_DIM
    ctx_index = lax.axis_index("ctx")
    me = (lax.axis_index("dp") * lax.axis_size("ctx") + ctx_index).astype(jnp.int32).reshape(1)
    half = size.count // 2
    info, docs, cos, sin = pos

    joined_w = jnp.concatenate(
        [w.reshape(rows, -1) for w in (q_weight, k_weight, v_weight)], axis=1
    )
    vec_row = pad_to(vectors.reshape(1, -1), size.tall - rows, size.a_width)
    wire_a = jnp.concatenate([pad_to(joined_w, rows, size.a_width), vec_row], axis=0)
    za = blocks.along_z(wire_a)
    xa = jnp.stack([za, blocks.swap(za, blocks.x)])
    _, flat_w = tie(za, (gate_weight, up_weight, o_weight, down_weight))
    w_rows = [w.reshape(rows, -1) for w in flat_w[:3]]
    wire_1, wire_2, tokens, cotangent = call(
        functools.partial(wire_kernel, size),
        "wire",
        [
            ((MAIN, size.first), BF), ((MAIN, size.second), BF), ((tok_rows, width), BF),
            ((tok_rows, width), BF),
        ],
        [
            ((MAIN, size.piece), F32), ((MAIN, 128), F32), ((tok_rows, width), BF),
            ((tok_rows, width), BF), ((2,), None),
        ],
        0,
        w_rows + [flat_w[3].reshape(size.f_rows, width), tokens.T, cotangent.T],
        10,
        any_out=(2, 3),
        scalar=False,
    )
    xa, wire_1, wire_2 = tie(xa, wire_1, wire_2)
    ya = blocks.swap(xa, blocks.y)
    z1 = blocks.along_z(wire_1)
    xa, ya, z1 = tie(xa, ya, z1)
    a_parts = [a.reshape(half // 2 * size.tall, size.a_width) for a in (xa, ya)]
    a_parts += [blocks.swap(a, blocks.core) for a in a_parts]
    wire_2, z1, *a_parts = tie(wire_2, z1, *a_parts)
    z2 = blocks.along_z(wire_2)
    x1 = jnp.stack([z1, blocks.swap(z1, blocks.x)])

    a_rows = size.count * size.tall
    q_rot, kv_mine, n1t, flat, w_a = call(
        functools.partial(pre_kernel, size),
        "norm_qkv",
        [
            ((tok_rows, width), BF), ((tok_rows, 2 * kv_width), BF), ((a_rows, tok_rows), BF),
            ((1, size.flat), F32), ((a_rows, size.a_width), BF),
        ],
        [
            ((tok_rows, width), BF), ((a_rows, size.a_width), BF), ((tok_rows, 128), F32),
            ((tok_rows, 128), F32), ((a_rows, tok_rows), BF), ((tok_rows, size.a_width), F32),
            ((7,), None), ((2,), None),
        ],
        4 * tok_rows * width * size.a_width,
        (me, tokens, *a_parts, cos, sin),
        20,
        any_in=range(1, 8),
        any_out=(2, 4),
    )
    kv_got = blocks.swap(kv_mine, blocks.x)
    z2 = tie(z2, kv_mine)[0]
    x1, kv_got = tie(x1, kv_got)
    y2 = jnp.stack([z2, blocks.swap(z2, blocks.y)])
    b1_parts = [b.reshape(half // 2 * MAIN, -1) for b in (x1, blocks.swap(x1, blocks.y))]
    b2_parts = [b.reshape(half // 2 * MAIN, -1) for b in (y2, blocks.swap(y2, blocks.x))]
    kv = (kv_got, kv_mine)
    attn, lse = attention(q_rot, kv, info, docs, tok_rows, True)

    b1_parts[1:] = [b1_parts[1], blocks.swap(b1_parts[0], blocks.core)]
    b2_parts[1:] = [b2_parts[1], blocks.swap(b2_parts[0], blocks.core)]
    attn, b2_parts[1] = tie(attn, b2_parts[1])
    attn, b1_parts[1] = tie(attn, b1_parts[1])
    b2_parts.append(blocks.swap(b2_parts[1], blocks.core))
    b1_parts.append(blocks.swap(b1_parts[1], blocks.core))
    main = size.count * MAIN
    slots = main + size.count * TAIL
    layer_out, keep1, give1, keep2, give2, grad_mid, grad_attn, grad_gain = call(
        functools.partial(mlp_kernel, size),
        "feed_forward",
        [
            ((width, tok_rows), BF),
            ((main // 2, size.first), BF), ((main // 2, size.first), BF),
            ((main // 2, size.second), BF), ((main // 2, size.second), BF),
            ((tok_rows, width), F32), ((tok_rows, width), BF), ((1, width), F32),
        ],
        [
            ((slots, ff), BF), ((slots, ff), BF), ((slots, size.wide), BF), ((ff, size.wide), BF),
            ((tok_rows, width), F32), ((tok_rows, slots), BF), ((slots, tok_rows), BF),
            ((width, slots), BF), ((tok_rows, width), F32), ((tok_rows, slots), F32),
            ((ff, size.wide), BF), ((size.count * TAIL, 2 * ff), BF),
            ((size.count * TAIL, size.wide), BF), ((main, size.piece + 128), BF),
        ],
        2 * tok_rows * width * (9 * ff + 5 * width),
        (
            me, attn, tokens, cotangent, flat, *b1_parts, *b2_parts,
        ),
        28,
    )

    got1 = blocks.swap(give1, blocks.core)
    got2 = blocks.swap(give2, blocks.core)
    shape = (2, 2, blocks.zs, MAIN, -1)
    h1 = blocks.add(keep1, got1).reshape(shape)
    h2 = blocks.add(keep2, got2).reshape(shape)
    grads, got_kv = [], []
    for g in range(KV_HEADS):
        if g == 1:
            grad_attn, h1, h2 = tie(grad_attn, h1, h2)
            h1 = blocks.add(h1[0], blocks.swap(h1[1], blocks.y))
            h2 = blocks.add(h2[:, 0], blocks.swap(h2[:, 1], blocks.x))
        dq, own, other = attention_back(
            q_rot, kv, grad_attn, lse, info, docs, tok_rows, True, g, g + 1
        )
        if g == KV_HEADS - 1:
            other, h1, h2 = tie(other, h1, h2)
        grads.append((dq, own))
        got_kv.append(blocks.swap(other, blocks.x))
    h1 = blocks.add(h1[0], blocks.swap(h1[1], blocks.x))
    h2 = blocks.add(h2[0], blocks.swap(h2[1], blocks.y))

    gx, keep_a, give_a = call(
        functools.partial(post_kernel, size),
        "norm_qkv_back",
        [
            ((width, tok_rows), F32), ((a_rows // 2, size.a_width), BF),
            ((a_rows // 2, size.a_width), BF),
        ],
        [
            ((tok_rows, 128), F32), ((tok_rows, 128), F32), ((a_rows, tok_rows), BF),
            ((a_rows, size.a_width), BF), ((tok_rows, width), BF), ((tok_rows, width), F32),
            ((tok_rows, width + kv_width), F32), ((tok_rows, size.a_width), BF),
            ((1, size.flat), F32), ((6,), None),
        ],
        6 * tok_rows * width * size.a_width,
        (
            me, *[g[0] for g in grads], *[g[1] for g in grads], *got_kv, cos, sin, n1t, w_a,
            tokens, grad_mid, flat, grad_gain,
        ),
        26,
        any_in=range(10, 16),
    )
    held = blocks.add(keep_a, blocks.swap(give_a, blocks.core))
    held = held.reshape(2, 2, blocks.zs, size.tall, size.a_width)
    give, h2 = tie(held[1], h2)
    got = blocks.swap(give, blocks.y)
    got, share2 = tie(got, blocks.sum_z(h2))
    held = blocks.add(held[0], got)
    give, h1 = tie(held[1], h1)
    got = blocks.swap(give, blocks.x)
    got, share1 = tie(got, blocks.sum_z(h1))
    held = blocks.add(held[0], got)
    share_a = blocks.sum_z(held)

    tails = tail_unpack(share1[:, size.tail : size.tail + size.piece], 2 * ff)
    tail_o = tail_unpack(share1[:, size.tail_o : size.tail_o + 128], width)
    share_out = jnp.concatenate([share1[:, size.out : size.out + width], tail_o], axis=0)
    share_gate = jnp.concatenate([share1[:, :ff], tails[:, :ff]], axis=0)
    share_up = jnp.concatenate([share2[:, :ff], tails[:, ff:]], axis=0)
    downs = [size.down_at(c) for c in range(size.downs)]
    share_down = jnp.concatenate(
        [(share1, share2)[which][:, at : at + width] for which, at in downs], axis=0
    )
    ends = (width, width + kv_width, size.qkv)
    return (
        layer_out.T, gx.T, share_a[:rows, : ends[0]].reshape(-1),
        share_a[:rows, ends[0] : ends[1]].reshape(-1),
        share_a[:rows, ends[1] : ends[2]].reshape(-1),
        share_out.reshape(-1), share_gate.reshape(-1), share_up.reshape(-1),
        share_down.reshape(-1), share_a[rows, : size.vec],
    )


def local(
    tokens, q_weight, k_weight, v_weight, o_weight, gate_weight, up_weight, down_weight,
    vectors, doc_lengths, cotangent,
):
    tok_rows, width = tokens.shape
    ctx_count = lax.axis_size("ctx")
    dp_count = lax.axis_size("dp")
    count = dp_count * ctx_count
    seq_tokens = tok_rows * ctx_count
    ctx_index = lax.axis_index("ctx")
    heads = width // HEAD_DIM
    kv_width = KV_HEADS * HEAD_DIM
    ff = gate_weight.shape[0] * count // width

    position_all = doc_layout(doc_lengths[0], seq_tokens)
    offset = ctx_index * tok_rows
    position_mine = lax.dynamic_slice_in_dim(position_all, offset, tok_rows)
    docs = doc_lengths.shape[1]
    others = (ctx_count - 1 - ctx_index) * tok_rows
    heads_of = jnp.stack([ctx_index, others, offset]).astype(jnp.int32)
    info = jnp.concatenate([heads_of, jnp.cumsum(doc_lengths[0])[:-1].astype(jnp.int32)])
    half = HEAD_DIM // 2
    freq = THETA ** (-jnp.arange(half, dtype=F32) * 2.0 / HEAD_DIM)
    position_f = position_mine.astype(F32)[:, None]

    whole_rows = width % count == 0 and ff % count == 0
    if whole_rows and ctx_count == 2 and dp_count % 4 == 0 and count & (count - 1) == 0:
        size = Sizes(width, ff, dp_count, ctx_count, vectors.shape[0], kv_width)
        if size.fits() and (width + kv_width) % 128 == 0:
            angle = position_f * jnp.tile(freq, 128 // half)[None, :]
            sign = np.where(np.arange(128) % HEAD_DIM < half, -1.0, 1.0).astype(np.float32)
            pos = (info, docs, jnp.cos(angle), jnp.sin(angle) * sign)
            args = (
                tokens, q_weight, k_weight, v_weight, o_weight, gate_weight, up_weight,
                down_weight, vectors, cotangent,
            )
            return local_blocks(size, Blocks(dp_count, ctx_count), pos, args)

    angle = position_f * freq[None, :]
    cosine = jnp.cos(angle)[:, None, :]
    sine = jnp.sin(angle)[:, None, :]
    inputs = tokens.astype(F32)
    inv_first = lax.rsqrt(jnp.mean(inputs * inputs, axis=-1, keepdims=True) + EPS)

    def whole(part):
        return lax.all_gather(part, AXES, axis=0, tiled=True)

    w_qkv = jnp.concatenate(
        [whole(w).reshape(width, -1) for w in (q_weight, k_weight, v_weight)], axis=1
    )
    w_out = whole(o_weight).reshape(width, width)
    w_gate = whole(gate_weight).reshape(width, ff)
    w_up = whole(up_weight).reshape(width, ff)
    w_down = whole(down_weight).reshape(ff, width)
    flat = whole(vectors).astype(F32)
    ends = [width, width + kv_width, width + 2 * kv_width, 2 * width + 2 * kv_width]
    gain_attn = flat[ends[2] : ends[3]]
    gain_mlp = flat[ends[3] : ends[3] + width]

    n_first = (inputs * inv_first * gain_attn).astype(BF)
    qkv = times(n_first, w_qkv) + flat[: ends[2]]
    q_rot = turn(qkv[:, :width].reshape(tok_rows, heads, HEAD_DIM), cosine, sine)
    q_rot = q_rot.astype(BF).reshape(tok_rows, width)
    k_rot = turn(qkv[:, width : ends[1]].reshape(tok_rows, KV_HEADS, HEAD_DIM), cosine, sine)
    k_rot = k_rot.astype(BF).reshape(tok_rows, kv_width)
    kv_mine = jnp.concatenate([k_rot, qkv[:, ends[1] :].astype(BF)], axis=1)
    kv = (lax.all_gather(kv_mine, "ctx", axis=0, tiled=True),)
    info = info.at[0].set(1)
    attn, lse = attention(q_rot, kv, info, docs, seq_tokens, False)
    mid = inputs + times(attn, w_out)
    inv_second = lax.rsqrt(jnp.mean(mid * mid, axis=-1, keepdims=True) + EPS)
    n_second = (mid * inv_second * gain_mlp).astype(BF)
    gate = times(n_second, w_gate)
    up_val = times(n_second, w_up)
    sig = jax.nn.sigmoid(gate)
    act = gate * sig
    hidden = (act * up_val).astype(BF)
    layer_out = (mid + times(hidden, w_down)).astype(BF)

    grad_wdown = inner_rows(hidden, cotangent)
    grad_hidden = times_back(cotangent, w_down)
    grad_gate = (grad_hidden * up_val * (sig * (1.0 + gate * (1.0 - sig)))).astype(BF)
    grad_up = (grad_hidden * act).astype(BF)
    grad_wgate = inner_rows(n_second, grad_gate)
    grad_wup = inner_rows(n_second, grad_up)
    grad_n2 = times_back(grad_gate, w_gate) + times_back(grad_up, w_up)
    grad_mid_norm, grad_gain_mlp = norm_back(mid, inv_second, gain_mlp, grad_n2)
    grad_mid = cotangent.astype(F32) + grad_mid_norm
    grad_branch = grad_mid.astype(BF)
    grad_wout = inner_rows(attn, grad_branch)
    grad_attn = times_back(grad_branch, w_out).astype(BF)
    grad_q_rot, grad_kv = attention_back(
        q_rot, kv, grad_attn, lse, info, docs, seq_tokens, False, 0, KV_HEADS
    )
    grad_kv_mine = lax.psum_scatter(
        grad_kv.astype(BF), "ctx", scatter_dimension=0, tiled=True
    ).astype(F32)
    grad_q = turn(grad_q_rot.reshape(tok_rows, heads, HEAD_DIM), cosine, -sine)
    grad_k = turn(
        grad_kv_mine[:, :kv_width].reshape(tok_rows, KV_HEADS, HEAD_DIM), cosine, -sine
    )
    grad_qkv = jnp.concatenate(
        [
            grad_q.reshape(tok_rows, width).astype(BF),
            grad_k.reshape(tok_rows, kv_width).astype(BF),
            grad_kv_mine[:, kv_width:].astype(BF),
        ],
        axis=1,
    )
    grad_wqkv = inner_rows(n_first, grad_qkv)
    grad_bias = jnp.sum(grad_qkv.astype(F32), axis=0)
    grad_n1 = times_back(grad_qkv, w_qkv)
    grad_x_norm, grad_gain_attn = norm_back(inputs, inv_first, gain_attn, grad_n1)
    input_grad = grad_mid + grad_x_norm
    used = 3 * width + 2 * kv_width
    padding = jnp.zeros((vectors.shape[0] * count - used,), F32)
    vector_term = jnp.concatenate([grad_bias, grad_gain_attn, grad_gain_mlp, padding])

    def shares(term):
        return lax.psum_scatter(term.reshape(-1), AXES, scatter_dimension=0, tiled=True)

    return (
        layer_out, input_grad, shares(grad_wqkv[:, :width]),
        shares(grad_wqkv[:, width : ends[1]]), shares(grad_wqkv[:, ends[1] :]),
        shares(grad_wout), shares(grad_wgate), shares(grad_wup), shares(grad_wdown),
        shares(vector_term),
    )


def solution(mesh):
    split = P(AXES)
    rows = P(AXES, None)
    in_specs = (rows,) + (split,) * 8 + (P("dp", None), rows)
    out_specs = (rows, rows) + (split,) * 8
    return jax.shard_map(local, mesh=mesh, in_specs=in_specs, out_specs=out_specs, check_vma=False)
```

```python
import functools

import jax
import jax.numpy as jnp
import numpy as np
from jax import lax
from jax.experimental import pallas as pl
from jax.experimental.pallas import tpu as pltpu
from jax.sharding import PartitionSpec as P

KV_HEADS = 3
HEAD_DIM = 64

EPS = 1e-06
THETA = 100000.0
NEG_FILL = -1e30
AXES = ("dp", "ctx")
BF = jnp.bfloat16
F32 = jnp.float32


def times(left, right):
    return jnp.dot(left, right, preferred_element_type=F32)


def inner_rows(left, right):
    return lax.dot_general(left, right, (((0,), (0,)), ((), ())), preferred_element_type=F32)


def times_back(left, right):
    return lax.dot_general(left, right, (((1,), (1,)), ((), ())), preferred_element_type=F32)


def norm_back(values, inv, gain, grad):
    scaled = grad * gain
    dot = jnp.mean(scaled * values, axis=-1, keepdims=True)
    grad_values = inv * scaled - values * (inv * inv * inv * dot)
    grad_gain = jnp.sum(grad * values * inv, axis=0)
    return grad_values, grad_gain


def turn(values, cosine, sine):
    half = values.shape[-1] // 2
    first = values[..., :half]
    second = values[..., half:]
    return jnp.concatenate(
        [first * cosine - second * sine, second * cosine + first * sine], axis=-1
    )


def doc_layout(lengths, count):
    ends = jnp.cumsum(lengths)
    place = jnp.arange(count, dtype=jnp.int32)
    segment = jnp.sum((place[:, None] >= ends[None, :-1]).astype(jnp.int32), axis=1)
    starts = ends - lengths
    picked = segment[:, None] == jnp.arange(lengths.shape[0], dtype=jnp.int32)[None, :]
    first = jnp.sum(jnp.where(picked, starts[None, :], 0), axis=1)
    return place - first


def fill_bias(bias, info, docs, short, own=None):
    total, rows = bias.shape
    row_q = lax.broadcasted_iota(jnp.int32, (1, rows), 1) + info[2]
    first = jnp.zeros_like(row_q)
    for j in range(docs - 1):
        first = jnp.where(row_q >= info[3 + j], info[3 + j], first)
    parts = ((0, total, 0),)
    if own is not None:
        parts = ((0, total, info[2] if own else info[1]),)
    elif short < total:
        parts = ((0, total - short, info[1]), (total - short, total, info[2]))
    for start, stop, base in parts:
        row_k = lax.broadcasted_iota(jnp.int32, (stop - start, rows), 0)
        allowed = (row_k >= first - base) & (row_k <= row_q - base)
        bias[start:stop] = jnp.where(allowed, 0.0, NEG_FILL)


def key_range(full, total, short, rows, block, at, causal):
    start = 0 if full else total - short
    stop = total - rows + (at + 1) * block if causal else total
    return start, stop


def key_parts(kv_refs):
    at = 0
    for kv_ref in kv_refs:
        yield slice(at, at + kv_ref.shape[0]), kv_ref
        at += kv_ref.shape[0]


def attn_fwd_kernel(
    heads, block, short, causal, docs, info, q_ref, *refs,
):
    kv_refs, (out_ref, lse_ref, qs, ks, vts, bias, out_t) = refs[:-7], refs[-7:]
    rows = q_ref.shape[0]
    total = bias.shape[0]
    kv_width = KV_HEADS * HEAD_DIM
    group = heads // KV_HEADS
    fill_bias(bias, info, docs, short)
    for h in range(heads):
        qs[h] = q_ref[:, h * HEAD_DIM : (h + 1) * HEAD_DIM] * BF(HEAD_DIM**-0.5)
    for at, kv_ref in key_parts(kv_refs):
        for g in range(KV_HEADS):
            ks[g, at] = kv_ref[:, g * HEAD_DIM : (g + 1) * HEAD_DIM]
        vts[:, at] = jnp.transpose(kv_ref[:, kv_width:].astype(F32)).astype(BF)

    def run(full):
        @pl.loop(0, KV_HEADS)
        def _(g):
            v_rows = pl.ds(pl.multiple_of(g * HEAD_DIM, HEAD_DIM), HEAD_DIM)
            for j in range(group):
                h = g * group + j
                out_rows = pl.ds(pl.multiple_of(h * HEAD_DIM, HEAD_DIM), HEAD_DIM)
                for at in range(rows // block):
                    start, stop = key_range(full, total, short, rows, block, at, causal)
                    cols = slice(at * block, (at + 1) * block)
                    s = times_back(ks[g, start:stop], qs[h, cols])
                    s = s + bias[start:stop, cols]
                    top = jnp.max(s, axis=0, keepdims=True)
                    p = jnp.exp(s - top)
                    total_p = jnp.sum(p, axis=0, keepdims=True)
                    o = times(vts[v_rows, start:stop], p.astype(BF))
                    out_t[out_rows, cols] = o / total_p
                    lse_ref[h, :, cols] = top + jnp.log(total_p)

    pl.when(info[0] != 0)(lambda: run(True))
    pl.when(info[0] == 0)(lambda: run(False))
    out_ref[...] = jnp.transpose(out_t[...]).astype(BF)


def attn_own_kernel(
    heads, block, docs, info, q_ref, kv_ref, acc, top_ref, sum_ref, qs, ks, vts, bias
):
    rows = q_ref.shape[0]
    kv_width = KV_HEADS * HEAD_DIM
    group = heads // KV_HEADS
    fill_bias(bias, info, docs, rows, own=True)
    for h in range(heads):
        qs[h] = q_ref[:, h * HEAD_DIM : (h + 1) * HEAD_DIM] * BF(HEAD_DIM**-0.5)
    for g in range(KV_HEADS):
        ks[g] = kv_ref[:, g * HEAD_DIM : (g + 1) * HEAD_DIM]
    vts[...] = jnp.transpose(kv_ref[:, kv_width:].astype(F32)).astype(BF)

    @pl.loop(0, KV_HEADS)
    def _(g):
        v_rows = pl.ds(pl.multiple_of(g * HEAD_DIM, HEAD_DIM), HEAD_DIM)
        for j in range(group):
            h = g * group + j
            out_rows = pl.ds(pl.multiple_of(h * HEAD_DIM, HEAD_DIM), HEAD_DIM)
            for at in range(rows // block):
                stop = (at + 1) * block
                cols = slice(at * block, stop)
                s = times_back(ks[g, :stop], qs[h, cols]) + bias[:stop, cols]
                top = jnp.max(s, axis=0, keepdims=True)
                p = jnp.exp(s - top)
                top_ref[h, :, cols] = top
                sum_ref[h, :, cols] = jnp.sum(p, axis=0, keepdims=True)
                acc[out_rows, cols] = times(vts[v_rows, :stop], p.astype(BF))


def attn_others_kernel(
    heads, block, docs, info, q_ref, kv_ref, acc, top_ref, sum_ref, out_ref, lse_ref,
    qs, ks, vts, bias, out_t,
):
    rows = q_ref.shape[0]
    kv_width = KV_HEADS * HEAD_DIM
    group = heads // KV_HEADS

    @pl.when(info[0] == 0)
    def _():
        for h in range(heads):
            at = slice(h * HEAD_DIM, (h + 1) * HEAD_DIM)
            out_t[at] = acc[at] / sum_ref[h]
            lse_ref[h] = top_ref[h] + jnp.log(sum_ref[h])

    @pl.when(info[0] != 0)
    def _():
        fill_bias(bias, info, docs, rows, own=False)
        for h in range(heads):
            qs[h] = q_ref[:, h * HEAD_DIM : (h + 1) * HEAD_DIM] * BF(HEAD_DIM**-0.5)
        for g in range(KV_HEADS):
            ks[g] = kv_ref[:, g * HEAD_DIM : (g + 1) * HEAD_DIM]
        vts[...] = jnp.transpose(kv_ref[:, kv_width:].astype(F32)).astype(BF)

        @pl.loop(0, KV_HEADS)
        def _(g):
            v_rows = pl.ds(pl.multiple_of(g * HEAD_DIM, HEAD_DIM), HEAD_DIM)
            for j in range(group):
                h = g * group + j
                out_rows = pl.ds(pl.multiple_of(h * HEAD_DIM, HEAD_DIM), HEAD_DIM)
                for at in range(rows // block):
                    cols = slice(at * block, (at + 1) * block)
                    s = times_back(ks[g], qs[h, cols]) + bias[:, cols]
                    own = top_ref[h, :, cols]
                    top = jnp.maximum(own, jnp.max(s, axis=0, keepdims=True))
                    scale = jnp.exp(own - top)
                    p = jnp.exp(s - top)
                    total_p = sum_ref[h, :, cols] * scale + jnp.sum(p, axis=0, keepdims=True)
                    o = acc[out_rows, cols] * scale + times(vts[v_rows], p.astype(BF))
                    out_t[out_rows, cols] = o / total_p
                    lse_ref[h, :, cols] = top + jnp.log(total_p)

    out_ref[...] = jnp.transpose(out_t[...]).astype(BF)


def attn_bwd_kernel(
    heads, block, short, causal, docs, g0, g1, parts, info, q_ref, do_ref, lse_ref, *refs,
):
    kv_refs, outs, scratch = refs[:parts], refs[parts:-9], refs[-9:]
    qs, ks, vs, kts, dos, bias, dq_t, dk, dv = scratch
    rows = q_ref.shape[0]
    total = bias.shape[0]
    kv_width = KV_HEADS * HEAD_DIM
    group = heads // KV_HEADS
    keys = g1 - g0
    fill_bias(bias, info, docs, short)
    for h in range(keys * group):
        lanes = slice((g0 * group + h) * HEAD_DIM, (g0 * group + h + 1) * HEAD_DIM)
        qs[h] = q_ref[:, lanes] * BF(HEAD_DIM**-0.5)
        dos[h] = do_ref[:, lanes]
    for g in range(keys):
        lo = (g0 + g) * HEAD_DIM
        for at, kv_ref in key_parts(kv_refs):
            ks[g, at] = kv_ref[:, lo : lo + HEAD_DIM]
            vs[g, at] = kv_ref[:, kv_width + lo : kv_width + lo + HEAD_DIM]
        kts[g] = jnp.transpose(ks[g].astype(F32)).astype(BF)
    dk[...] = jnp.zeros_like(dk)
    dv[...] = jnp.zeros_like(dv)

    def run(full):
        @pl.loop(0, keys * group)
        def _(h):
            g = h // group if keys > 1 else 0
            out_rows = pl.ds(pl.multiple_of(h * HEAD_DIM, HEAD_DIM), HEAD_DIM)
            for at in range(rows // block):
                start, stop = key_range(full, total, short, rows, block, at, causal)
                cols = slice(at * block, (at + 1) * block)
                q = qs[h, cols]
                do = dos[h, cols]
                s = times_back(ks[g, start:stop], q)
                p = jnp.exp(s + bias[start:stop, cols] - lse_ref[g0 * group + h, :, cols])
                dp = times_back(vs[g, start:stop], do)
                t = p * dp
                inner = jnp.sum(t, axis=0, keepdims=True)
                ds = (t - p * inner).astype(BF)
                dk[g, start:stop] += times(ds, q)
                dv[g, start:stop] += times(p.astype(BF), do)
                dq_t[out_rows, cols] = times(kts[g, :, start:stop], ds) * HEAD_DIM**-0.5

    pl.when(info[0] != 0)(lambda: run(True))
    pl.when(info[0] == 0)(lambda: run(False))
    outs[0][...] = jnp.transpose(dq_t[...])
    cut = total - outs[1].shape[0]
    for part, out in ((slice(cut, total), outs[1]),) + tuple((slice(0, cut), o) for o in outs[2:]):
        for g in range(keys):
            lo = g * HEAD_DIM
            out[:, lo : lo + HEAD_DIM] = dk[g, part].astype(out.dtype)
            lo += keys * HEAD_DIM
            out[:, lo : lo + HEAD_DIM] = dv[g, part].astype(out.dtype)


VM = pl.BlockSpec(memory_space=pltpu.VMEM)
SM = pl.BlockSpec(memory_space=pltpu.SMEM)


def attn_cost(rows, total, heads, products):
    return pl.CostEstimate(
        flops=8 * products * rows * total * heads * HEAD_DIM,
        bytes_accessed=4 * (rows + total) * heads * HEAD_DIM,
        transcendentals=rows * total * heads,
    )


def attention(q, kv, info, docs, short, causal):
    rows, width = q.shape
    total = sum(part.shape[0] for part in kv)
    heads = width // HEAD_DIM
    block = min(rows, 256)
    return pl.pallas_call(
        functools.partial(attn_fwd_kernel, heads, block, short, causal, docs),
        out_shape=(
            jax.ShapeDtypeStruct((rows, width), BF),
            jax.ShapeDtypeStruct((heads, 1, rows), F32),
        ),
        in_specs=[SM] + [VM] * (1 + len(kv)),
        out_specs=(VM, VM),
        scratch_shapes=[
            pltpu.VMEM((heads, rows, HEAD_DIM), BF),
            pltpu.VMEM((KV_HEADS, total, HEAD_DIM), BF),
            pltpu.VMEM((KV_HEADS * HEAD_DIM, total), BF),
            pltpu.VMEM((total, rows), F32),
            pltpu.VMEM((width, rows), F32),
        ],
        compiler_params=pltpu.CompilerParams(vmem_limit_bytes=20 * 2**20),
        cost_estimate=attn_cost(rows, total, heads, 2),
        name="attn_fwd",
    )(info, q, *kv)


def attention_own(q, kv, info, docs):
    rows, width = q.shape
    heads = width // HEAD_DIM
    stat = jax.ShapeDtypeStruct((heads, 1, rows), F32)
    return pl.pallas_call(
        functools.partial(attn_own_kernel, heads, min(rows, 256), docs),
        out_shape=(jax.ShapeDtypeStruct((width, rows), F32), stat, stat),
        in_specs=[SM, VM, VM],
        out_specs=(VM, VM, VM),
        scratch_shapes=attn_scratch(rows, heads),
        compiler_params=pltpu.CompilerParams(vmem_limit_bytes=16 * 2**20),
        cost_estimate=attn_cost(rows, rows, heads, 2),
        name="attn_own",
    )(info, q, kv)


def attn_scratch(rows, heads):
    return [
        pltpu.VMEM((heads, rows, HEAD_DIM), BF),
        pltpu.VMEM((KV_HEADS, rows, HEAD_DIM), BF),
        pltpu.VMEM((KV_HEADS * HEAD_DIM, rows), BF),
        pltpu.VMEM((rows, rows), F32),
    ]


def attention_others(q, kv, acc, top, total, info, docs):
    rows, width = q.shape
    heads = width // HEAD_DIM
    return pl.pallas_call(
        functools.partial(attn_others_kernel, heads, min(rows, 256), docs),
        out_shape=(
            jax.ShapeDtypeStruct((rows, width), BF),
            jax.ShapeDtypeStruct((heads, 1, rows), F32),
        ),
        in_specs=[SM] + [VM] * 5,
        out_specs=(VM, VM),
        scratch_shapes=attn_scratch(rows, heads) + [pltpu.VMEM((width, rows), F32)],
        compiler_params=pltpu.CompilerParams(vmem_limit_bytes=16 * 2**20),
        cost_estimate=attn_cost(rows, rows, heads, 2),
        name="attn_others",
    )(info, q, kv, acc, top, total)


def attention_back(q, kv, grad_out, lse, info, docs, short, causal, g0, g1):
    rows, width = q.shape
    total = sum(part.shape[0] for part in kv)
    heads = width // HEAD_DIM
    block = min(rows, 256)
    keys = g1 - g0
    mine = heads // KV_HEADS * keys
    outs = [jax.ShapeDtypeStruct((rows, mine * HEAD_DIM), F32)]
    if causal:
        outs.append(jax.ShapeDtypeStruct((rows, 2 * keys * HEAD_DIM), F32))
        outs.append(jax.ShapeDtypeStruct((total - rows, 2 * keys * HEAD_DIM), BF))
    else:
        outs.append(jax.ShapeDtypeStruct((total, 2 * keys * HEAD_DIM), F32))
    return pl.pallas_call(
        functools.partial(attn_bwd_kernel, heads, block, short, causal, docs, g0, g1, len(kv)),
        out_shape=outs,
        in_specs=[SM] + [VM] * (3 + len(kv)),
        out_specs=[VM] * len(outs),
        scratch_shapes=[
            pltpu.VMEM((mine, rows, HEAD_DIM), BF),
            pltpu.VMEM((keys, total, HEAD_DIM), BF),
            pltpu.VMEM((keys, total, HEAD_DIM), BF),
            pltpu.VMEM((keys, HEAD_DIM, total), BF),
            pltpu.VMEM((mine, rows, HEAD_DIM), BF),
            pltpu.VMEM((total, rows), F32),
            pltpu.VMEM((mine * HEAD_DIM, rows), F32),
            pltpu.VMEM((keys, total, HEAD_DIM), F32),
            pltpu.VMEM((keys, total, HEAD_DIM), F32),
        ],
        compiler_params=pltpu.CompilerParams(vmem_limit_bytes=20 * 2**20),
        cost_estimate=attn_cost(rows, total, mine, 5),
        name="attn_bwd",
    )(info, q, grad_out, lse, *kv)


TAIL = 2
MAIN = 16
PIECES = MAIN // TAIL


class Blocks:
    def __init__(self, dp_count, ctx_count):
        self.count = dp_count * ctx_count
        self.x = 1
        self.core = ctx_count
        self.y = 2 * ctx_count
        self.z = 4 * ctx_count
        self.zs = dp_count // 4
        self.masks = []
        for p in range(self.count):
            z, x = p % self.zs, p // self.zs % 2
            y, core = p // (2 * self.zs) % 2, p // (4 * self.zs)
            self.masks.append(x * self.x + y * self.y + core * self.core + z * self.z)

    def swap(self, values, mask):
        perm = [(i, i ^ mask) for i in range(self.count)]
        return lax.ppermute(values, AXES, perm)

    def along_z(self, mine):
        return jnp.stack([mine] + [self.swap(mine, d * self.z) for d in range(1, self.zs)])

    def add(self, keep, got):
        return (keep.astype(F32) + got.astype(F32)).astype(BF)

    def sum_z(self, held):
        got = [self.swap(held[d], d * self.z).astype(F32) for d in range(1, self.zs)]
        return functools.reduce(jnp.add, got, held[0].astype(F32))


class Sizes:
    def __init__(self, width, ff, dp, ctx, vec, kv_width):
        count = dp * ctx
        self.zs, self.ctx = dp // 4, ctx
        self.width, self.ff, self.count, self.vec = width, ff, count, vec
        self.rows = width // count
        self.f_rows = ff // count
        up = lambda n: (n + 127) // 128 * 128
        self.wide = up(width)
        self.qkv = width + 2 * kv_width
        self.a_width = up(self.qkv)
        self.tall = (self.rows + 1 + 7) // 8 * 8
        self.downs = self.f_rows // MAIN
        self.piece = 2 * ff // PIECES
        self.gate = 0
        self.tail = ff
        self.tail_o = self.tail + self.piece
        self.out = self.tail_o + 128
        self.down0 = self.out + self.wide
        self.first = self.down0 + self.wide
        self.second = ff + (self.downs - 1) * self.wide
        self.flat = self.a_width + 2 * self.wide

    def down_at(self, c):
        return (0, self.down0) if c == 0 else (1, self.ff + (c - 1) * self.wide)

    def fits(self):
        return (
            self.rows == MAIN + TAIL
            and self.f_rows % MAIN == 0
            and self.piece % 128 == 0
            and self.ff % 256 == 0
            and self.wide <= 128 * PIECES
            and self.vec <= 128
        )


def wire_kernel(
    size, g_ref, u_ref, o_ref, d_ref, xt_ref, cott_ref, out1, out2, x_any, cot_any,
    tail, tail_o, x_ref, cot_ref, sems,
):
    ff, width = size.ff, size.width
    x_ref[...] = jnp.transpose(xt_ref[...].astype(F32)).astype(BF)
    cot_ref[...] = jnp.transpose(cott_ref[...].astype(F32)).astype(BF)
    copies = fetch((x_ref, cot_ref), (x_any, cot_any), sems)
    out1[:, : ff] = g_ref[:MAIN]
    out2[:, : ff] = u_ref[:MAIN]
    out1[:, size.out : size.out + size.wide] = jnp.zeros((MAIN, size.wide), BF)
    out1[:, size.out : size.out + width] = o_ref[:MAIN]
    tail_o[...] = jnp.zeros_like(tail_o)
    odd = [ref[MAIN:].astype(F32) for ref in (g_ref, u_ref, o_ref)]
    for c in range(PIECES):
        src = odd[c * size.piece // ff]
        at = c * size.piece % ff
        tail[c * TAIL : (c + 1) * TAIL] = src[:, at : at + size.piece]
        used = min(128, width - c * 128)
        if used > 0:
            tail_o[c * TAIL : (c + 1) * TAIL, :used] = odd[2][:, c * 128 : c * 128 + used]
    out1[:, size.tail : size.tail + size.piece] = tail[...].astype(BF)
    out1[:, size.tail_o : size.tail_o + 128] = tail_o[...].astype(BF)
    for c in range(size.downs):
        which, at = size.down_at(c)
        out = (out1, out2)[which]
        out[:, at : at + size.wide] = jnp.zeros((MAIN, size.wide), BF)
        out[:, at : at + width] = d_ref[c * MAIN : (c + 1) * MAIN]
    for copy in copies:
        copy.wait()


def over(values, by):
    scale = 2**16 // by + 1
    whole = (values * scale) >> 16
    return whole, values - whole * by


def mask_of(size, p):
    z, rest = p % size.zs, p // size.zs
    x, y, core = rest % 2, rest // 2 % 2, rest // 4
    return x + core * size.ctx + y * (2 * size.ctx) + z * (4 * size.ctx)


def lanes(count):
    return lax.broadcasted_iota(jnp.int32, (1, count), 1)


def place_matrix(size, me, tall):
    if tall:
        p, inside = over(lanes(size.count * size.tall), size.tall)
        feature = jnp.where(inside < size.rows, size.rows * (me ^ mask_of(size, p)) + inside, -1)
    else:
        s = lanes(size.count * (MAIN + TAIL))
        tail = s - size.count * MAIN
        p = jnp.where(tail < 0, s // MAIN, tail // TAIL)
        inside = jnp.where(tail < 0, s % MAIN, MAIN + tail % TAIL)
        feature = size.rows * (me ^ mask_of(size, p)) + inside
    at = lax.broadcasted_iota(jnp.int32, (size.width, feature.shape[1]), 0)
    return jnp.where(at == feature, 1.0, 0.0).astype(BF)


def vector_places(size, me):
    at = lanes(size.flat)
    ends = (size.a_width, size.a_width + size.wide)
    part = jnp.where(at < ends[0], 0, jnp.where(at < ends[1], 1, 2))
    inside = at - jnp.where(part == 0, 0, jnp.where(part == 1, ends[0], ends[1]))
    start = jnp.where(part == 0, 0, jnp.where(part == 1, size.qkv, size.qkv + size.width))
    used = inside < jnp.where(part == 0, size.qkv, size.width)
    owner, lane = over(start + inside, size.vec)
    rows = lax.broadcasted_iota(jnp.int32, (128, size.flat), 0)
    spread = jnp.where((rows == lane) & used, 1.0, 0.0).astype(BF)
    p = lax.broadcasted_iota(jnp.int32, (size.count, 1), 0)
    return spread, (owner == (me ^ mask_of(size, p))) & used


def split_two(values):
    high = values.astype(BF)
    return high, (values - high.astype(F32)).astype(BF)


def swap_halves(u):
    rolled_back = pltpu.roll(u, 128 - HEAD_DIM // 2, 1)
    rolled = pltpu.roll(u, HEAD_DIM // 2, 1)
    lane = lax.broadcasted_iota(jnp.int32, u.shape, 1)
    return jnp.where(lane % HEAD_DIM < HEAD_DIM // 2, rolled_back, rolled)


def fetch(sources, targets, sems):
    copies = [
        pltpu.make_async_copy(src, dst, sems.at[i])
        for i, (src, dst) in enumerate(zip(sources, targets))
    ]
    for copy in copies:
        copy.start()
    return copies


def pre_kernel(
    size, me_ref, x_ref, wm_ref, wo_ref, cos_ref, sin_ref,
    q_ref, kv_ref, n1t_ref, flat_ref, w, qkv,
):
    me = me_ref[0]
    half = wm_ref.shape[0]
    w[:half] = wm_ref[...]
    w[half:] = wo_ref[...]
    place = place_matrix(size, me, True)
    spread, mine = vector_places(size, me)
    shape = (size.count, 2 * half)
    row = lax.broadcasted_iota(jnp.int32, shape, 0) * size.tall + size.rows
    row = jnp.where(lax.broadcasted_iota(jnp.int32, shape, 1) == row, 1.0, 0.0).astype(BF)
    packed = times(row, w[:, :128]).astype(BF)
    flat = jnp.sum(jnp.where(mine, times(packed, spread), 0.0), axis=0, keepdims=True)
    flat_ref[...] = flat
    gain = flat[:, size.a_width : size.a_width + size.width]
    x = x_ref[...].astype(F32)
    inv = lax.rsqrt(jnp.mean(x * x, axis=-1, keepdims=True) + EPS)
    n1 = (x * inv * gain).astype(BF)
    n1a = times(n1, place)
    n1t_ref[...] = jnp.transpose(n1a).astype(BF)
    qkv[...] = times(n1a.astype(BF), w[...]) + flat[:, : size.a_width]
    kv_width = kv_ref.shape[1] // 2
    for t in range((size.width + kv_width) // 128):
        u = qkv[:, t * 128 : (t + 1) * 128]
        qkv[:, t * 128 : (t + 1) * 128] = u * cos_ref[...] + swap_halves(u) * sin_ref[...]
    q_ref[...] = qkv[:, : size.width].astype(BF)
    kv_ref[...] = qkv[:, size.width : size.qkv].astype(BF)


def tail_place(size, c):
    shape = (size.count * TAIL, size.count * MAIN)
    q = lax.broadcasted_iota(jnp.int32, shape, 0)
    at = lax.broadcasted_iota(jnp.int32, shape, 1)
    want = (q // TAIL) * MAIN + c * TAIL + q % TAIL
    return jnp.where(at == want, 1.0, 0.0).astype(BF)


def tail_place_back(size, c):
    shape = (size.count * MAIN, size.count * TAIL)
    at = lax.broadcasted_iota(jnp.int32, shape, 0)
    q = lax.broadcasted_iota(jnp.int32, shape, 1)
    want = (q // TAIL) * MAIN + c * TAIL + q % TAIL
    return jnp.where(at == want, 1.0, 0.0).astype(BF)


def mlp_kernel(
    size, me_ref, attn_ref, x_ref, cot_ref, flat_ref,
    b1_00, b1_01, b1_10, b1_11, b2_00, b2_01, b2_10, b2_11,
    out_ref, keep1, give1, keep2, give2, gmid_ref, gattn_ref, ggain_ref,
    wg, wu, wo, wd, mid, n2s, n2t, place, acc, gacc, dwd, tails, tail_o, packed,
):
    me = me_ref[0]
    width, ff = size.width, size.ff
    part = b1_00.shape[0]
    half, main = 2 * part, 4 * part
    rows_z = part // 2
    place[...] = place_matrix(size, me, False)
    first = (b1_00, b1_01, b1_10, b1_11)
    second = (b2_00, b2_01, b2_10, b2_11)
    room = size.piece + 128
    for i, b1 in enumerate(first):
        rows = slice(i * part, (i + 1) * part)
        wg[rows] = b1[:, :ff]
        wo[rows] = b1[:, size.out : size.out + size.wide]
        packed[rows] = b1[:, size.tail : size.tail + room]
    for i, b2 in enumerate(second):
        for y in range(2):
            at = (i // 2) * half + y * part + (i % 2) * rows_z
            wu[at : at + rows_z] = b2[y * rows_z : (y + 1) * rows_z, :ff]
    for c in range(PIECES):
        sel = tail_place(size, c)
        target = wg if c * size.piece < ff else wu
        at = c * size.piece % ff
        got = times(sel, packed[:, : size.piece])
        target[main:, at : at + size.piece] = got.astype(BF)
        if c * 128 < size.wide:
            got = times(sel, packed[:, size.piece : room])
            wo[main:, c * 128 : (c + 1) * 128] = got.astype(BF)
    zs = rows_z // MAIN
    for p in range(size.count):
        z, x, y, core = p % zs, p // zs % 2, p // (2 * zs) % 2, p // (4 * zs)
        owner = me ^ mask_of(size, p)
        for c in range(size.downs):
            which, at = size.down_at(c)
            src, row = (second[2 * core + x], y * zs + z) if which else (
                first[2 * core + y], x * zs + z
            )
            to = pl.multiple_of(owner * size.f_rows + c * MAIN, MAIN)
            wd[pl.ds(to, MAIN), :] = src[row * MAIN : (row + 1) * MAIN, at : at + size.wide]
    attn_s = times(attn_ref[...], place[...])
    m = x_ref[...].astype(F32) + times(attn_s.astype(BF), wo[:, :width])
    mid[...] = m
    inv = lax.rsqrt(jnp.mean(m * m, axis=-1, keepdims=True) + EPS)
    lo = size.a_width + size.wide
    gain = flat_ref[:, lo : lo + width]
    n2 = (m * inv * gain).astype(BF)
    spread = times(n2, place[...])
    n2s[...] = spread.astype(BF)
    n2t[...] = jnp.transpose(spread).astype(BF)
    acc[...] = jnp.zeros_like(acc)
    gacc[...] = jnp.zeros_like(gacc)
    step = 512 if ff % 512 == 0 else 256

    @pl.loop(0, ff // step)
    def _(b):
        at = pl.multiple_of(b * step, step)
        cols = pl.ds(at, step)
        gate = times(n2s[...], wg[:, cols])
        up = times(n2s[...], wu[:, cols])
        sig = 1.0 / (1.0 + jnp.exp(-gate))
        act = gate * sig
        h = act * up
        gh = times_back(cot_ref[...], wd[cols, :width])
        gg = (gh * up * (sig * (1.0 + gate * (1.0 - sig)))).astype(BF)
        gu = (gh * act).astype(BF)
        acc[...] += times(h.astype(BF), wd[cols, :width])
        dwd[cols, :width] = times(jnp.transpose(h).astype(BF), cot_ref[...]).astype(BF)
        gacc[...] += times_back(gg, wg[:, cols]) + times_back(gu, wu[:, cols])
        for k, (grad, keep, give) in enumerate(((gg, keep1, give1), (gu, keep2, give2))):
            dw = times(n2t[...], grad).astype(BF)
            keep[:, cols] = dw[:half]
            give[:, cols] = dw[half:main]
            tails[:, pl.ds(pl.multiple_of(k * ff + at, 128), step)] = dw[main:]

    m = mid[...]
    inv = lax.rsqrt(jnp.mean(m * m, axis=-1, keepdims=True) + EPS)
    out_ref[...] = jnp.transpose(m + acc[...]).astype(BF)
    high, low = split_two(gacc[...])
    gn2 = times_back(high, place[...]) + times_back(low, place[...])
    scaled = gn2 * gain
    dot = jnp.mean(scaled * m, axis=-1, keepdims=True)
    ggain_ref[...] = jnp.sum(gn2 * m * inv, axis=0, keepdims=True)
    gmid = cot_ref[...].astype(F32) + inv * scaled - m * (inv * inv * inv * dot)
    gmid_ref[...] = gmid
    branch = gmid.astype(BF)
    gattn = times_back(branch, wo[:, :width]).astype(BF)
    gattn_ref[...] = times_back(gattn, place[...]).astype(BF)
    dwo = times(jnp.transpose(attn_s).astype(BF), branch).astype(BF)
    tail_o[...] = jnp.zeros_like(tail_o)
    tail_o[:, :width] = dwo[main:]
    terms = ((keep1, keep2), (give1, give2))
    for i, (term, _) in enumerate(terms):
        term[:, size.out : size.out + width] = dwo[i * half : (i + 1) * half]
    wire = jnp.zeros((main, size.piece), F32)
    wire_o = jnp.zeros((main, 128), F32)
    for c in range(PIECES):
        sel = tail_place_back(size, c)
        wire += times(sel, tails[:, c * size.piece : (c + 1) * size.piece])
        if c * 128 < size.wide:
            wire_o += times(sel, tail_o[:, c * 128 : (c + 1) * 128])
    for i, (term, _) in enumerate(terms):
        rows = slice(i * half, (i + 1) * half)
        term[:, size.tail : size.tail + size.piece] = wire[rows].astype(BF)
        term[:, size.tail_o : size.tail_o + 128] = wire_o[rows].astype(BF)
    for p in range(size.count):
        to = terms[p // (size.count // 2)]
        rows = slice(p * MAIN % half, p * MAIN % half + MAIN)
        owner = me ^ mask_of(size, p)
        for c in range(size.downs):
            which, at = size.down_at(c)
            src = pl.multiple_of(owner * size.f_rows + c * MAIN, MAIN)
            to[which][rows, at : at + size.wide] = dwd[pl.ds(src, MAIN), :]


def post_kernel(
    size, me_ref, dq0, dq1, dq2, own0, own1, own2, got0, got1, got2, cos_ref, sin_ref, n1t_ref,
    wm_ref, wo_ref, x_ref, gmid_ref, flat_ref, ggain_ref,
    gx_ref, keep_ref, give_ref, turn_buf, grad, vec_row,
):
    me = me_ref[0]
    width = size.width
    half = wm_ref.shape[0]
    place = place_matrix(size, me, True)
    kv_width = KV_HEADS * HEAD_DIM
    turned = width + kv_width
    third = width // KV_HEADS
    grad[...] = jnp.zeros_like(grad)
    parts = ((dq0, own0, got0), (dq1, own1, got1), (dq2, own2, got2))
    for g, (dq, own, got) in enumerate(parts):
        turn_buf[:, g * third : (g + 1) * third] = dq[...]
        dkv = own[...] + got[...].astype(F32)
        lo = width + g * HEAD_DIM
        turn_buf[:, lo : lo + HEAD_DIM] = dkv[:, :HEAD_DIM]
        lo += kv_width
        grad[:, lo : lo + HEAD_DIM] = dkv[:, HEAD_DIM:].astype(BF)
    for t in range(turned // 128):
        u = turn_buf[:, t * 128 : (t + 1) * 128]
        back = u * cos_ref[...] - swap_halves(u) * sin_ref[...]
        grad[:, t * 128 : (t + 1) * 128] = back.astype(BF)
    g = grad[...]
    gn1 = jnp.zeros((g.shape[0], width), F32)
    for part, w_ref in enumerate((wm_ref, wo_ref)):
        for values in split_two(times_back(g, w_ref[...])):
            gn1 += times_back(values, place[:, part * half : (part + 1) * half])
    x = x_ref[...].astype(F32)
    inv = lax.rsqrt(jnp.mean(x * x, axis=-1, keepdims=True) + EPS)
    gain = flat_ref[:, size.a_width : size.a_width + width]
    scaled = gn1 * gain
    dot = jnp.mean(scaled * x, axis=-1, keepdims=True)
    gx_ref[...] = jnp.transpose(gmid_ref[...] + inv * scaled - x * (inv * inv * inv * dot))
    vec_row[...] = jnp.zeros_like(vec_row)
    vec_row[:, : size.a_width] = jnp.sum(g.astype(F32), axis=0, keepdims=True)
    vec_row[:, size.a_width : size.a_width + width] = jnp.sum(gn1 * x * inv, axis=0, keepdims=True)
    lo = size.a_width + size.wide
    vec_row[:, lo : lo + width] = ggain_ref[...]
    spread, mine = vector_places(size, me)
    packed = times_back(jnp.where(mine, vec_row[...], 0.0).astype(BF), spread)
    shape = (half, size.count)
    for part, term in ((0, keep_ref), (1, give_ref)):
        rows = slice(part * half, (part + 1) * half)
        dw = times(n1t_ref[rows], g)
        term[...] = dw.astype(BF)
        want = lax.broadcasted_iota(jnp.int32, shape, 1) * size.tall + size.rows - part * half
        here = lax.broadcasted_iota(jnp.int32, shape, 0) == want
        extra = times(jnp.where(here, 1.0, 0.0).astype(BF), packed.astype(BF))
        term[:, :128] = (dw[:, :128] + extra).astype(BF)


def call(kernel, name, out_shape, scratch, flops, args, vmem, any_in=(), any_out=(), scalar=True):
    shapes = [jax.ShapeDtypeStruct(s, t) for s, t in out_shape]
    total = sum(int(np.prod(a.shape)) * a.dtype.itemsize for a in args)
    here = pl.BlockSpec(memory_space=pl.ANY)
    specs = [here if i in any_in else VM for i in range(len(args))]
    if scalar:
        specs[0] = SM
    return pl.pallas_call(
        kernel,
        out_shape=shapes,
        in_specs=specs,
        out_specs=[here if i in any_out else VM for i in range(len(shapes))],
        scratch_shapes=[
            pltpu.SemaphoreType.DMA(s) if t is None else pltpu.VMEM(s, t) for s, t in scratch
        ],
        compiler_params=pltpu.CompilerParams(vmem_limit_bytes=vmem * 2**20),
        cost_estimate=pl.CostEstimate(flops=flops, bytes_accessed=total, transcendentals=0),
        name=name,
    )(*args)


def pad_to(values, rows, columns):
    return jnp.pad(values, ((0, rows - values.shape[0]), (0, columns - values.shape[1])))


def tail_pack(rows, piece):
    rows = pad_to(rows, TAIL, PIECES * piece)
    return rows.reshape(TAIL, PIECES, piece).transpose(1, 0, 2).reshape(MAIN, piece)


def tail_unpack(wire, used):
    piece = wire.shape[1]
    rows = wire.reshape(PIECES, TAIL, piece).transpose(1, 0, 2).reshape(TAIL, PIECES * piece)
    return rows[:, :used]


def tie(*values):
    return lax.optimization_barrier(values)


def local_blocks(size, blocks, pos, args):
    (
        tokens, q_weight, k_weight, v_weight, o_weight, gate_weight, up_weight, down_weight,
        vectors, cotangent,
    ) = args
    tok_rows, width = tokens.shape
    ff, rows = size.ff, size.rows
    kv_width = KV_HEADS * HEAD_DIM
    ctx_index = lax.axis_index("ctx")
    me = (lax.axis_index("dp") * lax.axis_size("ctx") + ctx_index).astype(jnp.int32).reshape(1)
    half = size.count // 2
    info, docs, cos, sin = pos

    joined_w = jnp.concatenate(
        [w.reshape(rows, -1) for w in (q_weight, k_weight, v_weight)], axis=1
    )
    vec_row = pad_to(vectors.reshape(1, -1), size.tall - rows, size.a_width)
    wire_a = jnp.concatenate([pad_to(joined_w, rows, size.a_width), vec_row], axis=0)
    za = blocks.along_z(wire_a)
    xa = jnp.stack([za, blocks.swap(za, blocks.x)])
    flat_w = (gate_weight, up_weight, o_weight, down_weight)
    w_rows = [w.reshape(rows, -1) for w in flat_w[:3]]
    wire_1, wire_2, tokens, cotangent = call(
        functools.partial(wire_kernel, size),
        "wire",
        [
            ((MAIN, size.first), BF), ((MAIN, size.second), BF), ((tok_rows, width), BF),
            ((tok_rows, width), BF),
        ],
        [
            ((MAIN, size.piece), F32), ((MAIN, 128), F32), ((tok_rows, width), BF),
            ((tok_rows, width), BF), ((2,), None),
        ],
        0,
        w_rows + [flat_w[3].reshape(size.f_rows, width), tokens.T, cotangent.T],
        10,
        any_out=(2, 3),
        scalar=False,
    )
    z1 = blocks.along_z(wire_1)
    xa, z1, wire_2 = tie(xa, z1, wire_2)
    ya = blocks.swap(xa, blocks.y)
    z2 = blocks.along_z(wire_2)
    x1 = jnp.stack([z1, blocks.swap(z1, blocks.x)])
    ya, z2, x1 = tie(ya, z2, x1)
    a_mine = jnp.stack([xa, ya]).reshape(half * size.tall, size.a_width)
    a_other = blocks.swap(a_mine, blocks.core)

    a_rows = size.count * size.tall
    q_rot, kv_mine, n1t, flat = call(
        functools.partial(pre_kernel, size),
        "norm_qkv",
        [
            ((tok_rows, width), BF), ((tok_rows, 2 * kv_width), BF), ((a_rows, tok_rows), BF),
            ((1, size.flat), F32),
        ],
        [((a_rows, size.a_width), BF), ((tok_rows, size.a_width), F32)],
        4 * tok_rows * width * size.a_width,
        (me, tokens, a_mine, a_other, cos, sin),
        16,
    )
    kv_got = blocks.swap(kv_mine, blocks.x)
    own = attention_own(q_rot, kv_mine, info, docs)
    y2, x1 = tie(jnp.stack([z2, blocks.swap(z2, blocks.y)]), x1)
    b1_parts = [b.reshape(half // 2 * MAIN, -1) for b in (x1, blocks.swap(x1, blocks.y))]
    b2_parts = [b.reshape(half // 2 * MAIN, -1) for b in (y2, blocks.swap(y2, blocks.x))]
    kv = (kv_got, kv_mine)
    attn, lse = attention_others(q_rot, kv_got, *own, info, docs)

    b1_parts[1:] = [b1_parts[1], blocks.swap(b1_parts[0], blocks.core)]
    b2_parts[1:] = [b2_parts[1], blocks.swap(b2_parts[0], blocks.core)]
    attn, b2_parts[1] = tie(attn, b2_parts[1])
    attn, b1_parts[1] = tie(attn, b1_parts[1])
    b2_parts.append(blocks.swap(b2_parts[1], blocks.core))
    b1_parts.append(blocks.swap(b1_parts[1], blocks.core))
    main = size.count * MAIN
    slots = main + size.count * TAIL
    layer_out, keep1, give1, keep2, give2, grad_mid, grad_attn, grad_gain = call(
        functools.partial(mlp_kernel, size),
        "feed_forward",
        [
            ((width, tok_rows), BF),
            ((main // 2, size.first), BF), ((main // 2, size.first), BF),
            ((main // 2, size.second), BF), ((main // 2, size.second), BF),
            ((tok_rows, width), F32), ((tok_rows, width), BF), ((1, width), F32),
        ],
        [
            ((slots, ff), BF), ((slots, ff), BF), ((slots, size.wide), BF), ((ff, size.wide), BF),
            ((tok_rows, width), F32), ((tok_rows, slots), BF), ((slots, tok_rows), BF),
            ((width, slots), BF), ((tok_rows, width), F32), ((tok_rows, slots), F32),
            ((ff, size.wide), BF), ((size.count * TAIL, 2 * ff), BF),
            ((size.count * TAIL, size.wide), BF), ((main, size.piece + 128), BF),
        ],
        2 * tok_rows * width * (9 * ff + 5 * width),
        (
            me, attn, tokens, cotangent, flat, *b1_parts, *b2_parts,
        ),
        28,
    )

    got1 = blocks.swap(give1, blocks.core)
    got2 = blocks.swap(give2, blocks.core)
    shape = (2, 2, blocks.zs, MAIN, -1)
    h1 = blocks.add(keep1, got1).reshape(shape)
    h2 = blocks.add(keep2, got2).reshape(shape)
    grads, got_kv = [], []
    for g in range(KV_HEADS):
        if g == 1:
            grad_attn, h1, h2 = tie(grad_attn, h1, h2)
            h1 = blocks.add(h1[0], blocks.swap(h1[1], blocks.y))
            h2 = blocks.add(h2[:, 0], blocks.swap(h2[:, 1], blocks.x))
        dq, own, other = attention_back(
            q_rot, kv, grad_attn, lse, info, docs, tok_rows, True, g, g + 1
        )
        if g == KV_HEADS - 1:
            other, h1, h2 = tie(other, h1, h2)
        grads.append((dq, own))
        got_kv.append(blocks.swap(other, blocks.x))
    h1 = blocks.add(h1[0], blocks.swap(h1[1], blocks.x))
    h2 = blocks.add(h2[0], blocks.swap(h2[1], blocks.y))

    gx, keep_a, give_a = call(
        functools.partial(post_kernel, size),
        "norm_qkv_back",
        [
            ((width, tok_rows), F32), ((a_rows // 2, size.a_width), BF),
            ((a_rows // 2, size.a_width), BF),
        ],
        [
            ((tok_rows, width + kv_width), F32), ((tok_rows, size.a_width), BF),
            ((1, size.flat), F32),
        ],
        6 * tok_rows * width * size.a_width,
        (
            me, *[g[0] for g in grads], *[g[1] for g in grads], *got_kv, cos, sin, n1t, a_mine,
            a_other, tokens, grad_mid, flat, grad_gain,
        ),
        24,
    )
    held = blocks.add(keep_a, blocks.swap(give_a, blocks.core))
    held, h2 = tie(held, h2)
    held = held.reshape(2, 2, blocks.zs, size.tall, size.a_width)
    held = blocks.add(held[0], blocks.swap(held[1], blocks.y))
    held, share2, h1 = tie(held, blocks.sum_z(h2), h1)
    held = blocks.add(held[0], blocks.swap(held[1], blocks.x))
    held, share1 = tie(held, blocks.sum_z(h1))
    share_a = blocks.sum_z(held)

    tails = tail_unpack(share1[:, size.tail : size.tail + size.piece], 2 * ff)
    tail_o = tail_unpack(share1[:, size.tail_o : size.tail_o + 128], width)
    share_out = jnp.concatenate([share1[:, size.out : size.out + width], tail_o], axis=0)
    share_gate = jnp.concatenate([share1[:, :ff], tails[:, :ff]], axis=0)
    share_up = jnp.concatenate([share2[:, :ff], tails[:, ff:]], axis=0)
    downs = [size.down_at(c) for c in range(size.downs)]
    share_down = jnp.concatenate(
        [(share1, share2)[which][:, at : at + width] for which, at in downs], axis=0
    )
    ends = (width, width + kv_width, size.qkv)
    return (
        layer_out.T, gx.T, share_a[:rows, : ends[0]].reshape(-1),
        share_a[:rows, ends[0] : ends[1]].reshape(-1),
        share_a[:rows, ends[1] : ends[2]].reshape(-1),
        share_out.reshape(-1), share_gate.reshape(-1), share_up.reshape(-1),
        share_down.reshape(-1), share_a[rows, : size.vec],
    )


def local(
    tokens, q_weight, k_weight, v_weight, o_weight, gate_weight, up_weight, down_weight,
    vectors, doc_lengths, cotangent,
):
    tok_rows, width = tokens.shape
    ctx_count = lax.axis_size("ctx")
    dp_count = lax.axis_size("dp")
    count = dp_count * ctx_count
    seq_tokens = tok_rows * ctx_count
    ctx_index = lax.axis_index("ctx")
    heads = width // HEAD_DIM
    kv_width = KV_HEADS * HEAD_DIM
    ff = gate_weight.shape[0] * count // width

    position_all = doc_layout(doc_lengths[0], seq_tokens)
    offset = ctx_index * tok_rows
    position_mine = lax.dynamic_slice_in_dim(position_all, offset, tok_rows)
    docs = doc_lengths.shape[1]
    others = (ctx_count - 1 - ctx_index) * tok_rows
    heads_of = jnp.stack([ctx_index, others, offset]).astype(jnp.int32)
    info = jnp.concatenate([heads_of, jnp.cumsum(doc_lengths[0])[:-1].astype(jnp.int32)])
    half = HEAD_DIM // 2
    freq = THETA ** (-jnp.arange(half, dtype=F32) * 2.0 / HEAD_DIM)
    position_f = position_mine.astype(F32)[:, None]

    whole_rows = width % count == 0 and ff % count == 0
    if whole_rows and ctx_count == 2 and dp_count % 4 == 0 and count & (count - 1) == 0:
        size = Sizes(width, ff, dp_count, ctx_count, vectors.shape[0], kv_width)
        if size.fits() and (width + kv_width) % 128 == 0:
            angle = position_f * jnp.tile(freq, 128 // half)[None, :]
            sign = np.where(np.arange(128) % HEAD_DIM < half, -1.0, 1.0).astype(np.float32)
            pos = (info, docs, jnp.cos(angle), jnp.sin(angle) * sign)
            args = (
                tokens, q_weight, k_weight, v_weight, o_weight, gate_weight, up_weight,
                down_weight, vectors, cotangent,
            )
            return local_blocks(size, Blocks(dp_count, ctx_count), pos, args)

    angle = position_f * freq[None, :]
    cosine = jnp.cos(angle)[:, None, :]
    sine = jnp.sin(angle)[:, None, :]
    inputs = tokens.astype(F32)
    inv_first = lax.rsqrt(jnp.mean(inputs * inputs, axis=-1, keepdims=True) + EPS)

    def whole(part):
        return lax.all_gather(part, AXES, axis=0, tiled=True)

    w_qkv = jnp.concatenate(
        [whole(w).reshape(width, -1) for w in (q_weight, k_weight, v_weight)], axis=1
    )
    w_out = whole(o_weight).reshape(width, width)
    w_gate = whole(gate_weight).reshape(width, ff)
    w_up = whole(up_weight).reshape(width, ff)
    w_down = whole(down_weight).reshape(ff, width)
    flat = whole(vectors).astype(F32)
    ends = [width, width + kv_width, width + 2 * kv_width, 2 * width + 2 * kv_width]
    gain_attn = flat[ends[2] : ends[3]]
    gain_mlp = flat[ends[3] : ends[3] + width]

    n_first = (inputs * inv_first * gain_attn).astype(BF)
    qkv = times(n_first, w_qkv) + flat[: ends[2]]
    q_rot = turn(qkv[:, :width].reshape(tok_rows, heads, HEAD_DIM), cosine, sine)
    q_rot = q_rot.astype(BF).reshape(tok_rows, width)
    k_rot = turn(qkv[:, width : ends[1]].reshape(tok_rows, KV_HEADS, HEAD_DIM), cosine, sine)
    k_rot = k_rot.astype(BF).reshape(tok_rows, kv_width)
    kv_mine = jnp.concatenate([k_rot, qkv[:, ends[1] :].astype(BF)], axis=1)
    kv = (lax.all_gather(kv_mine, "ctx", axis=0, tiled=True),)
    info = info.at[0].set(1)
    attn, lse = attention(q_rot, kv, info, docs, seq_tokens, False)
    mid = inputs + times(attn, w_out)
    inv_second = lax.rsqrt(jnp.mean(mid * mid, axis=-1, keepdims=True) + EPS)
    n_second = (mid * inv_second * gain_mlp).astype(BF)
    gate = times(n_second, w_gate)
    up_val = times(n_second, w_up)
    sig = jax.nn.sigmoid(gate)
    act = gate * sig
    hidden = (act * up_val).astype(BF)
    layer_out = (mid + times(hidden, w_down)).astype(BF)

    grad_wdown = inner_rows(hidden, cotangent)
    grad_hidden = times_back(cotangent, w_down)
    grad_gate = (grad_hidden * up_val * (sig * (1.0 + gate * (1.0 - sig)))).astype(BF)
    grad_up = (grad_hidden * act).astype(BF)
    grad_wgate = inner_rows(n_second, grad_gate)
    grad_wup = inner_rows(n_second, grad_up)
    grad_n2 = times_back(grad_gate, w_gate) + times_back(grad_up, w_up)
    grad_mid_norm, grad_gain_mlp = norm_back(mid, inv_second, gain_mlp, grad_n2)
    grad_mid = cotangent.astype(F32) + grad_mid_norm
    grad_branch = grad_mid.astype(BF)
    grad_wout = inner_rows(attn, grad_branch)
    grad_attn = times_back(grad_branch, w_out).astype(BF)
    grad_q_rot, grad_kv = attention_back(
        q_rot, kv, grad_attn, lse, info, docs, seq_tokens, False, 0, KV_HEADS
    )
    grad_kv_mine = lax.psum_scatter(
        grad_kv.astype(BF), "ctx", scatter_dimension=0, tiled=True
    ).astype(F32)
    grad_q = turn(grad_q_rot.reshape(tok_rows, heads, HEAD_DIM), cosine, -sine)
    grad_k = turn(
        grad_kv_mine[:, :kv_width].reshape(tok_rows, KV_HEADS, HEAD_DIM), cosine, -sine
    )
    grad_qkv = jnp.concatenate(
        [
            grad_q.reshape(tok_rows, width).astype(BF),
            grad_k.reshape(tok_rows, kv_width).astype(BF),
            grad_kv_mine[:, kv_width:].astype(BF),
        ],
        axis=1,
    )
    grad_wqkv = inner_rows(n_first, grad_qkv)
    grad_bias = jnp.sum(grad_qkv.astype(F32), axis=0)
    grad_n1 = times_back(grad_qkv, w_qkv)
    grad_x_norm, grad_gain_attn = norm_back(inputs, inv_first, gain_attn, grad_n1)
    input_grad = grad_mid + grad_x_norm
    used = 3 * width + 2 * kv_width
    padding = jnp.zeros((vectors.shape[0] * count - used,), F32)
    vector_term = jnp.concatenate([grad_bias, grad_gain_attn, grad_gain_mlp, padding])

    def shares(term):
        return lax.psum_scatter(term.reshape(-1), AXES, scatter_dimension=0, tiled=True)

    return (
        layer_out, input_grad, shares(grad_wqkv[:, :width]),
        shares(grad_wqkv[:, width : ends[1]]), shares(grad_wqkv[:, ends[1] :]),
        shares(grad_wout), shares(grad_wgate), shares(grad_wup), shares(grad_wdown),
        shares(vector_term),
    )


def solution(mesh):
    split = P(AXES)
    rows = P(AXES, None)
    in_specs = (rows,) + (split,) * 8 + (P("dp", None), rows)
    out_specs = (rows, rows) + (split,) * 8
    return jax.shard_map(local, mesh=mesh, in_specs=in_specs, out_specs=out_specs, check_vma=False)
```

```python
import functools

import jax
import jax.numpy as jnp
import numpy as np
from jax import lax
from jax.experimental import pallas as pl
from jax.experimental.pallas import tpu as pltpu
from jax.sharding import PartitionSpec as P

KV_HEADS = 3
HEAD_DIM = 64

EPS = 1e-06
THETA = 100000.0
NEG_FILL = -1e30
AXES = ("dp", "ctx")
BF = jnp.bfloat16
F32 = jnp.float32


def times(left, right):
    return jnp.dot(left, right, preferred_element_type=F32)


def inner_rows(left, right):
    return lax.dot_general(left, right, (((0,), (0,)), ((), ())), preferred_element_type=F32)


def times_back(left, right):
    return lax.dot_general(left, right, (((1,), (1,)), ((), ())), preferred_element_type=F32)


def norm_back(values, inv, gain, grad):
    scaled = grad * gain
    dot = jnp.mean(scaled * values, axis=-1, keepdims=True)
    grad_values = inv * scaled - values * (inv * inv * inv * dot)
    grad_gain = jnp.sum(grad * values * inv, axis=0)
    return grad_values, grad_gain


def turn(values, cosine, sine):
    half = values.shape[-1] // 2
    first = values[..., :half]
    second = values[..., half:]
    return jnp.concatenate(
        [first * cosine - second * sine, second * cosine + first * sine], axis=-1
    )


def doc_layout(lengths, count):
    ends = jnp.cumsum(lengths)
    place = jnp.arange(count, dtype=jnp.int32)
    segment = jnp.sum((place[:, None] >= ends[None, :-1]).astype(jnp.int32), axis=1)
    starts = ends - lengths
    picked = segment[:, None] == jnp.arange(lengths.shape[0], dtype=jnp.int32)[None, :]
    first = jnp.sum(jnp.where(picked, starts[None, :], 0), axis=1)
    return place - first


def fill_bias(bias, info, docs, short, own=None):
    total, rows = bias.shape
    row_q = lax.broadcasted_iota(jnp.int32, (1, rows), 1) + info[2]
    first = jnp.zeros_like(row_q)
    for j in range(docs - 1):
        first = jnp.where(row_q >= info[3 + j], info[3 + j], first)
    parts = ((0, total, 0),)
    if own is not None:
        parts = ((0, total, info[2] if own else info[1]),)
    elif short < total:
        parts = ((0, total - short, info[1]), (total - short, total, info[2]))
    for start, stop, base in parts:
        row_k = lax.broadcasted_iota(jnp.int32, (stop - start, rows), 0)
        allowed = (row_k >= first - base) & (row_k <= row_q - base)
        bias[start:stop] = jnp.where(allowed, 0.0, NEG_FILL)


def key_range(full, total, short, rows, block, at, causal):
    start = 0 if full else total - short
    stop = total - rows + (at + 1) * block if causal else total
    return start, stop


def key_parts(kv_refs):
    at = 0
    for kv_ref in kv_refs:
        yield slice(at, at + kv_ref.shape[0]), kv_ref
        at += kv_ref.shape[0]


def attn_fwd_kernel(
    heads, block, short, causal, docs, info, q_ref, *refs,
):
    kv_refs, (out_ref, lse_ref, qs, ks, vts, bias, out_t) = refs[:-7], refs[-7:]
    rows = q_ref.shape[0]
    total = bias.shape[0]
    kv_width = KV_HEADS * HEAD_DIM
    group = heads // KV_HEADS
    fill_bias(bias, info, docs, short)
    for h in range(heads):
        qs[h] = q_ref[:, h * HEAD_DIM : (h + 1) * HEAD_DIM] * BF(HEAD_DIM**-0.5)
    for at, kv_ref in key_parts(kv_refs):
        for g in range(KV_HEADS):
            ks[g, at] = kv_ref[:, g * HEAD_DIM : (g + 1) * HEAD_DIM]
        vts[:, at] = jnp.transpose(kv_ref[:, kv_width:].astype(F32)).astype(BF)

    def run(full):
        @pl.loop(0, KV_HEADS)
        def _(g):
            v_rows = pl.ds(pl.multiple_of(g * HEAD_DIM, HEAD_DIM), HEAD_DIM)
            for j in range(group):
                h = g * group + j
                out_rows = pl.ds(pl.multiple_of(h * HEAD_DIM, HEAD_DIM), HEAD_DIM)
                for at in range(rows // block):
                    start, stop = key_range(full, total, short, rows, block, at, causal)
                    cols = slice(at * block, (at + 1) * block)
                    s = times_back(ks[g, start:stop], qs[h, cols])
                    s = s + bias[start:stop, cols]
                    top = jnp.max(s, axis=0, keepdims=True)
                    p = jnp.exp(s - top)
                    total_p = jnp.sum(p, axis=0, keepdims=True)
                    o = times(vts[v_rows, start:stop], p.astype(BF))
                    out_t[out_rows, cols] = o / total_p
                    lse_ref[h, :, cols] = top + jnp.log(total_p)

    pl.when(info[0] != 0)(lambda: run(True))
    pl.when(info[0] == 0)(lambda: run(False))
    out_ref[...] = jnp.transpose(out_t[...]).astype(BF)


def attn_own_kernel(
    heads, block, docs, info, q_ref, kv_ref, acc, top_ref, sum_ref, qs, ks, vts, bias
):
    rows = q_ref.shape[0]
    kv_width = KV_HEADS * HEAD_DIM
    group = heads // KV_HEADS
    fill_bias(bias, info, docs, rows, own=True)
    for h in range(heads):
        qs[h] = q_ref[:, h * HEAD_DIM : (h + 1) * HEAD_DIM] * BF(HEAD_DIM**-0.5)
    for g in range(KV_HEADS):
        ks[g] = kv_ref[:, g * HEAD_DIM : (g + 1) * HEAD_DIM]
    vts[...] = jnp.transpose(kv_ref[:, kv_width:].astype(F32)).astype(BF)

    @pl.loop(0, KV_HEADS)
    def _(g):
        v_rows = pl.ds(pl.multiple_of(g * HEAD_DIM, HEAD_DIM), HEAD_DIM)
        for j in range(group):
            h = g * group + j
            out_rows = pl.ds(pl.multiple_of(h * HEAD_DIM, HEAD_DIM), HEAD_DIM)
            for at in range(rows // block):
                stop = (at + 1) * block
                cols = slice(at * block, stop)
                s = times_back(ks[g, :stop], qs[h, cols]) + bias[:stop, cols]
                top = jnp.max(s, axis=0, keepdims=True)
                p = jnp.exp(s - top)
                top_ref[h, :, cols] = top
                sum_ref[h, :, cols] = jnp.sum(p, axis=0, keepdims=True)
                acc[out_rows, cols] = times(vts[v_rows, :stop], p.astype(BF))


def attn_others_kernel(
    heads, block, docs, info, q_ref, kv_ref, acc, top_ref, sum_ref, out_ref, lse_ref,
    qs, ks, vts, bias, out_t,
):
    rows = q_ref.shape[0]
    kv_width = KV_HEADS * HEAD_DIM
    group = heads // KV_HEADS

    @pl.when(info[0] == 0)
    def _():
        for h in range(heads):
            at = slice(h * HEAD_DIM, (h + 1) * HEAD_DIM)
            out_t[at] = acc[at] / sum_ref[h]
            lse_ref[h] = top_ref[h] + jnp.log(sum_ref[h])

    @pl.when(info[0] != 0)
    def _():
        fill_bias(bias, info, docs, rows, own=False)
        for h in range(heads):
            qs[h] = q_ref[:, h * HEAD_DIM : (h + 1) * HEAD_DIM] * BF(HEAD_DIM**-0.5)
        for g in range(KV_HEADS):
            ks[g] = kv_ref[:, g * HEAD_DIM : (g + 1) * HEAD_DIM]
        vts[...] = jnp.transpose(kv_ref[:, kv_width:].astype(F32)).astype(BF)

        @pl.loop(0, KV_HEADS)
        def _(g):
            v_rows = pl.ds(pl.multiple_of(g * HEAD_DIM, HEAD_DIM), HEAD_DIM)
            for j in range(group):
                h = g * group + j
                out_rows = pl.ds(pl.multiple_of(h * HEAD_DIM, HEAD_DIM), HEAD_DIM)
                for at in range(rows // block):
                    cols = slice(at * block, (at + 1) * block)
                    s = times_back(ks[g], qs[h, cols]) + bias[:, cols]
                    own = top_ref[h, :, cols]
                    top = jnp.maximum(own, jnp.max(s, axis=0, keepdims=True))
                    scale = jnp.exp(own - top)
                    p = jnp.exp(s - top)
                    total_p = sum_ref[h, :, cols] * scale + jnp.sum(p, axis=0, keepdims=True)
                    o = acc[out_rows, cols] * scale + times(vts[v_rows], p.astype(BF))
                    out_t[out_rows, cols] = o / total_p
                    lse_ref[h, :, cols] = top + jnp.log(total_p)

    out_ref[...] = jnp.transpose(out_t[...]).astype(BF)


def attn_grad_kernel(
    heads, block, docs, own, info, q_ref, kv_ref, do_ref, lse_ref, delta_ref, *refs
):
    refs, (qs, dos, ks, vs, kts, bias, dk, dv) = refs[:-8], refs[-8:]
    if own:
        before, dq_ref, dkv_ref, dq_t = refs
    else:
        dq_t, dkv_ref = refs
    rows = q_ref.shape[0]
    kv_width = KV_HEADS * HEAD_DIM
    group = heads // KV_HEADS
    dk[...] = jnp.zeros_like(dk)
    dv[...] = jnp.zeros_like(dv)

    def run():
        fill_bias(bias, info, docs, rows, own=own)
        for h in range(heads):
            at = slice(h * HEAD_DIM, (h + 1) * HEAD_DIM)
            qs[h] = q_ref[:, at] * BF(HEAD_DIM**-0.5)
            dos[h] = do_ref[:, at]
        for g in range(KV_HEADS):
            lo = g * HEAD_DIM
            ks[g] = kv_ref[:, lo : lo + HEAD_DIM]
            vs[g] = kv_ref[:, kv_width + lo : kv_width + lo + HEAD_DIM]
        kts[...] = jnp.transpose(kv_ref[:, :kv_width].astype(F32)).astype(BF)

        @pl.loop(0, KV_HEADS)
        def _(g):
            k_rows = pl.ds(pl.multiple_of(g * HEAD_DIM, HEAD_DIM), HEAD_DIM)
            for j in range(group):
                h = g * group + j
                out_rows = pl.ds(pl.multiple_of(h * HEAD_DIM, HEAD_DIM), HEAD_DIM)
                for at in range(rows // block):
                    stop = (at + 1) * block if own else rows
                    cols = slice(at * block, (at + 1) * block)
                    q = qs[h, cols]
                    do = dos[h, cols]
                    s = times_back(ks[g, :stop], q) + bias[:stop, cols]
                    p = jnp.exp(s - lse_ref[h, :, cols])
                    dp = times_back(vs[g, :stop], do)
                    ds = (p * (dp - delta_ref[h, :, cols])).astype(BF)
                    dk[g, :stop] += times(ds, q)
                    dv[g, :stop] += times(p.astype(BF), do)
                    dq = times(kts[k_rows, :stop], ds) * HEAD_DIM**-0.5
                    dq_t[out_rows, cols] = before[out_rows, cols] + dq if own else dq

    if own:
        run()
        dq_ref[...] = jnp.transpose(dq_t[...])
    else:
        pl.when(info[0] != 0)(run)

        @pl.when(info[0] == 0)
        def _():
            dq_t[...] = jnp.zeros_like(dq_t)

    for g in range(KV_HEADS):
        lo = g * HEAD_DIM
        dkv_ref[:, lo : lo + HEAD_DIM] = dk[g].astype(dkv_ref.dtype)
        dkv_ref[:, kv_width + lo : kv_width + lo + HEAD_DIM] = dv[g].astype(dkv_ref.dtype)


def attn_bwd_kernel(
    heads, block, short, causal, docs, g0, g1, parts, info, q_ref, do_ref, lse_ref, *refs,
):
    kv_refs, outs, scratch = refs[:parts], refs[parts:-9], refs[-9:]
    qs, ks, vs, kts, dos, bias, dq_t, dk, dv = scratch
    rows = q_ref.shape[0]
    total = bias.shape[0]
    kv_width = KV_HEADS * HEAD_DIM
    group = heads // KV_HEADS
    keys = g1 - g0
    fill_bias(bias, info, docs, short)
    for h in range(keys * group):
        lanes = slice((g0 * group + h) * HEAD_DIM, (g0 * group + h + 1) * HEAD_DIM)
        qs[h] = q_ref[:, lanes] * BF(HEAD_DIM**-0.5)
        dos[h] = do_ref[:, lanes]
    for g in range(keys):
        lo = (g0 + g) * HEAD_DIM
        for at, kv_ref in key_parts(kv_refs):
            ks[g, at] = kv_ref[:, lo : lo + HEAD_DIM]
            vs[g, at] = kv_ref[:, kv_width + lo : kv_width + lo + HEAD_DIM]
        kts[g] = jnp.transpose(ks[g].astype(F32)).astype(BF)
    dk[...] = jnp.zeros_like(dk)
    dv[...] = jnp.zeros_like(dv)

    def run(full):
        @pl.loop(0, keys * group)
        def _(h):
            g = h // group if keys > 1 else 0
            out_rows = pl.ds(pl.multiple_of(h * HEAD_DIM, HEAD_DIM), HEAD_DIM)
            for at in range(rows // block):
                start, stop = key_range(full, total, short, rows, block, at, causal)
                cols = slice(at * block, (at + 1) * block)
                q = qs[h, cols]
                do = dos[h, cols]
                s = times_back(ks[g, start:stop], q)
                p = jnp.exp(s + bias[start:stop, cols] - lse_ref[g0 * group + h, :, cols])
                dp = times_back(vs[g, start:stop], do)
                t = p * dp
                inner = jnp.sum(t, axis=0, keepdims=True)
                ds = (t - p * inner).astype(BF)
                dk[g, start:stop] += times(ds, q)
                dv[g, start:stop] += times(p.astype(BF), do)
                dq_t[out_rows, cols] = times(kts[g, :, start:stop], ds) * HEAD_DIM**-0.5

    pl.when(info[0] != 0)(lambda: run(True))
    pl.when(info[0] == 0)(lambda: run(False))
    outs[0][...] = jnp.transpose(dq_t[...])
    cut = total - outs[1].shape[0]
    for part, out in ((slice(cut, total), outs[1]),) + tuple((slice(0, cut), o) for o in outs[2:]):
        for g in range(keys):
            lo = g * HEAD_DIM
            out[:, lo : lo + HEAD_DIM] = dk[g, part].astype(out.dtype)
            lo += keys * HEAD_DIM
            out[:, lo : lo + HEAD_DIM] = dv[g, part].astype(out.dtype)


VM = pl.BlockSpec(memory_space=pltpu.VMEM)
SM = pl.BlockSpec(memory_space=pltpu.SMEM)


def cost_of(micros):
    return pl.CostEstimate(
        flops=int(micros * 1.1e9), bytes_accessed=2**20, transcendentals=0
    )


def attention(q, kv, info, docs, short, causal):
    rows, width = q.shape
    total = sum(part.shape[0] for part in kv)
    heads = width // HEAD_DIM
    block = min(rows, 256)
    return pl.pallas_call(
        functools.partial(attn_fwd_kernel, heads, block, short, causal, docs),
        out_shape=(
            jax.ShapeDtypeStruct((rows, width), BF),
            jax.ShapeDtypeStruct((heads, 1, rows), F32),
        ),
        in_specs=[SM] + [VM] * (1 + len(kv)),
        out_specs=(VM, VM),
        scratch_shapes=[
            pltpu.VMEM((heads, rows, HEAD_DIM), BF),
            pltpu.VMEM((KV_HEADS, total, HEAD_DIM), BF),
            pltpu.VMEM((KV_HEADS * HEAD_DIM, total), BF),
            pltpu.VMEM((total, rows), F32),
            pltpu.VMEM((width, rows), F32),
        ],
        compiler_params=pltpu.CompilerParams(vmem_limit_bytes=20 * 2**20),
        cost_estimate=cost_of(14),
        name="attn_fwd",
    )(info, q, *kv)


def attention_own(q, kv, info, docs):
    rows, width = q.shape
    heads = width // HEAD_DIM
    stat = jax.ShapeDtypeStruct((heads, 1, rows), F32)
    return pl.pallas_call(
        functools.partial(attn_own_kernel, heads, min(rows, 256), docs),
        out_shape=(jax.ShapeDtypeStruct((width, rows), F32), stat, stat),
        in_specs=[SM, VM, VM],
        out_specs=(VM, VM, VM),
        scratch_shapes=attn_scratch(rows, heads),
        compiler_params=pltpu.CompilerParams(vmem_limit_bytes=16 * 2**20),
        cost_estimate=cost_of(6),
        name="attn_own",
    )(info, q, kv)


def attn_scratch(rows, heads):
    return [
        pltpu.VMEM((heads, rows, HEAD_DIM), BF),
        pltpu.VMEM((KV_HEADS, rows, HEAD_DIM), BF),
        pltpu.VMEM((KV_HEADS * HEAD_DIM, rows), BF),
        pltpu.VMEM((rows, rows), F32),
    ]


def attention_grad(q, kv, grad_out, lse, delta, info, docs, before=None):
    rows, width = q.shape
    heads = width // HEAD_DIM
    own = before is not None
    turned = jax.ShapeDtypeStruct((width, rows), F32)
    if own:
        outs = [jax.ShapeDtypeStruct((rows, width), F32), jax.ShapeDtypeStruct(kv.shape, F32)]
    else:
        outs = [turned, jax.ShapeDtypeStruct(kv.shape, BF)]
    by_head = pltpu.VMEM((heads, rows, HEAD_DIM), BF)
    by_key = pltpu.VMEM((KV_HEADS, rows, HEAD_DIM), BF)
    sums = pltpu.VMEM((KV_HEADS, rows, HEAD_DIM), F32)
    return pl.pallas_call(
        functools.partial(attn_grad_kernel, heads, min(rows, 256), docs, own),
        out_shape=outs,
        in_specs=[SM] + [VM] * (6 if own else 5),
        out_specs=[VM] * 2,
        scratch_shapes=([pltpu.VMEM((width, rows), F32)] if own else []) + [
            by_head, by_head, by_key, by_key, pltpu.VMEM((KV_HEADS * HEAD_DIM, rows), BF),
            pltpu.VMEM((rows, rows), F32), sums, sums,
        ],
        compiler_params=pltpu.CompilerParams(vmem_limit_bytes=20 * 2**20),
        cost_estimate=cost_of(9 if own else 10),
        name="attn_grad_own" if own else "attn_grad_others",
    )(info, q, kv, grad_out, lse, delta, *([before] if own else []))


def attention_others(q, kv, acc, top, total, info, docs):
    rows, width = q.shape
    heads = width // HEAD_DIM
    return pl.pallas_call(
        functools.partial(attn_others_kernel, heads, min(rows, 256), docs),
        out_shape=(
            jax.ShapeDtypeStruct((rows, width), BF),
            jax.ShapeDtypeStruct((heads, 1, rows), F32),
        ),
        in_specs=[SM] + [VM] * 5,
        out_specs=(VM, VM),
        scratch_shapes=attn_scratch(rows, heads) + [pltpu.VMEM((width, rows), F32)],
        compiler_params=pltpu.CompilerParams(vmem_limit_bytes=16 * 2**20),
        cost_estimate=cost_of(10),
        name="attn_others",
    )(info, q, kv, acc, top, total)


def attention_back(q, kv, grad_out, lse, info, docs, short, causal, g0, g1):
    rows, width = q.shape
    total = sum(part.shape[0] for part in kv)
    heads = width // HEAD_DIM
    block = min(rows, 256)
    keys = g1 - g0
    mine = heads // KV_HEADS * keys
    outs = [jax.ShapeDtypeStruct((rows, mine * HEAD_DIM), F32)]
    if causal:
        outs.append(jax.ShapeDtypeStruct((rows, 2 * keys * HEAD_DIM), F32))
        outs.append(jax.ShapeDtypeStruct((total - rows, 2 * keys * HEAD_DIM), BF))
    else:
        outs.append(jax.ShapeDtypeStruct((total, 2 * keys * HEAD_DIM), F32))
    return pl.pallas_call(
        functools.partial(attn_bwd_kernel, heads, block, short, causal, docs, g0, g1, len(kv)),
        out_shape=outs,
        in_specs=[SM] + [VM] * (3 + len(kv)),
        out_specs=[VM] * len(outs),
        scratch_shapes=[
            pltpu.VMEM((mine, rows, HEAD_DIM), BF),
            pltpu.VMEM((keys, total, HEAD_DIM), BF),
            pltpu.VMEM((keys, total, HEAD_DIM), BF),
            pltpu.VMEM((keys, HEAD_DIM, total), BF),
            pltpu.VMEM((mine, rows, HEAD_DIM), BF),
            pltpu.VMEM((total, rows), F32),
            pltpu.VMEM((mine * HEAD_DIM, rows), F32),
            pltpu.VMEM((keys, total, HEAD_DIM), F32),
            pltpu.VMEM((keys, total, HEAD_DIM), F32),
        ],
        compiler_params=pltpu.CompilerParams(vmem_limit_bytes=20 * 2**20),
        cost_estimate=cost_of(20),
        name="attn_bwd",
    )(info, q, grad_out, lse, *kv)


TAIL = 2
MAIN = 16
PIECES = MAIN // TAIL


class Blocks:
    def __init__(self, dp_count, ctx_count):
        self.count = dp_count * ctx_count
        self.x = 1
        self.core = ctx_count
        self.y = 2 * ctx_count
        self.z = 4 * ctx_count
        self.zs = dp_count // 4
        self.masks = []
        for p in range(self.count):
            z, x = p % self.zs, p // self.zs % 2
            y, core = p // (2 * self.zs) % 2, p // (4 * self.zs)
            self.masks.append(x * self.x + y * self.y + core * self.core + z * self.z)

    def swap(self, values, mask):
        perm = [(i, i ^ mask) for i in range(self.count)]
        return lax.ppermute(values, AXES, perm)

    def along_z(self, mine):
        return jnp.stack([mine] + [self.swap(mine, d * self.z) for d in range(1, self.zs)])

    def add(self, keep, got):
        return (keep.astype(F32) + got.astype(F32)).astype(BF)

    def sum_z(self, held):
        got = [self.swap(held[d], d * self.z).astype(F32) for d in range(1, self.zs)]
        return functools.reduce(jnp.add, got, held[0].astype(F32))


class Sizes:
    def __init__(self, width, ff, dp, ctx, vec, kv_width):
        count = dp * ctx
        self.zs, self.ctx = dp // 4, ctx
        self.width, self.ff, self.count, self.vec = width, ff, count, vec
        self.rows = width // count
        self.f_rows = ff // count
        up = lambda n: (n + 127) // 128 * 128
        self.wide = up(width)
        self.qkv = width + 2 * kv_width
        self.a_width = up(self.qkv)
        self.tall = (self.rows + 1 + 7) // 8 * 8
        self.downs = self.f_rows // MAIN
        self.piece = 2 * ff // PIECES
        self.gate = 0
        self.tail = ff
        self.tail_o = self.tail + self.piece
        self.out = self.tail_o + 128
        self.down0 = self.out + self.wide
        self.first = self.down0 + self.wide
        self.second = ff + (self.downs - 1) * self.wide
        self.flat = self.a_width + 2 * self.wide

    def down_at(self, c):
        return (0, self.down0) if c == 0 else (1, self.ff + (c - 1) * self.wide)

    def fits(self):
        return (
            self.rows == MAIN + TAIL
            and self.f_rows % MAIN == 0
            and self.piece % 128 == 0
            and self.ff % 256 == 0
            and self.wide <= 128 * PIECES
            and self.vec <= 128
        )


def wire_kernel(
    size, g_ref, u_ref, o_ref, d_ref, xt_ref, cott_ref, out1, out2, x_any, cot_any,
    tail, tail_o, x_ref, cot_ref, sems,
):
    ff, width = size.ff, size.width
    x_ref[...] = jnp.transpose(xt_ref[...].astype(F32)).astype(BF)
    cot_ref[...] = jnp.transpose(cott_ref[...].astype(F32)).astype(BF)
    copies = fetch((x_ref, cot_ref), (x_any, cot_any), sems)
    out1[:, : ff] = g_ref[:MAIN]
    out2[:, : ff] = u_ref[:MAIN]
    out1[:, size.out : size.out + size.wide] = jnp.zeros((MAIN, size.wide), BF)
    out1[:, size.out : size.out + width] = o_ref[:MAIN]
    tail_o[...] = jnp.zeros_like(tail_o)
    odd = [ref[MAIN:].astype(F32) for ref in (g_ref, u_ref, o_ref)]
    for c in range(PIECES):
        src = odd[c * size.piece // ff]
        at = c * size.piece % ff
        tail[c * TAIL : (c + 1) * TAIL] = src[:, at : at + size.piece]
        used = min(128, width - c * 128)
        if used > 0:
            tail_o[c * TAIL : (c + 1) * TAIL, :used] = odd[2][:, c * 128 : c * 128 + used]
    out1[:, size.tail : size.tail + size.piece] = tail[...].astype(BF)
    out1[:, size.tail_o : size.tail_o + 128] = tail_o[...].astype(BF)
    for c in range(size.downs):
        which, at = size.down_at(c)
        out = (out1, out2)[which]
        out[:, at : at + size.wide] = jnp.zeros((MAIN, size.wide), BF)
        out[:, at : at + width] = d_ref[c * MAIN : (c + 1) * MAIN]
    for copy in copies:
        copy.wait()


def over(values, by):
    scale = 2**16 // by + 1
    whole = (values * scale) >> 16
    return whole, values - whole * by


def mask_of(size, p):
    z, rest = p % size.zs, p // size.zs
    x, y, core = rest % 2, rest // 2 % 2, rest // 4
    return x + core * size.ctx + y * (2 * size.ctx) + z * (4 * size.ctx)


def lanes(count):
    return lax.broadcasted_iota(jnp.int32, (1, count), 1)


def place_matrix(size, me, tall):
    if tall:
        p, inside = over(lanes(size.count * size.tall), size.tall)
        feature = jnp.where(inside < size.rows, size.rows * (me ^ mask_of(size, p)) + inside, -1)
    else:
        s = lanes(size.count * (MAIN + TAIL))
        tail = s - size.count * MAIN
        p = jnp.where(tail < 0, s // MAIN, tail // TAIL)
        inside = jnp.where(tail < 0, s % MAIN, MAIN + tail % TAIL)
        feature = size.rows * (me ^ mask_of(size, p)) + inside
    at = lax.broadcasted_iota(jnp.int32, (size.width, feature.shape[1]), 0)
    return jnp.where(at == feature, 1.0, 0.0).astype(BF)


def vector_places(size, me):
    at = lanes(size.flat)
    ends = (size.a_width, size.a_width + size.wide)
    part = jnp.where(at < ends[0], 0, jnp.where(at < ends[1], 1, 2))
    inside = at - jnp.where(part == 0, 0, jnp.where(part == 1, ends[0], ends[1]))
    start = jnp.where(part == 0, 0, jnp.where(part == 1, size.qkv, size.qkv + size.width))
    used = inside < jnp.where(part == 0, size.qkv, size.width)
    owner, lane = over(start + inside, size.vec)
    rows = lax.broadcasted_iota(jnp.int32, (128, size.flat), 0)
    spread = jnp.where((rows == lane) & used, 1.0, 0.0).astype(BF)
    p = lax.broadcasted_iota(jnp.int32, (size.count, 1), 0)
    return spread, (owner == (me ^ mask_of(size, p))) & used


def split_two(values):
    high = values.astype(BF)
    return high, (values - high.astype(F32)).astype(BF)


def swap_halves(u):
    rolled_back = pltpu.roll(u, 128 - HEAD_DIM // 2, 1)
    rolled = pltpu.roll(u, HEAD_DIM // 2, 1)
    lane = lax.broadcasted_iota(jnp.int32, u.shape, 1)
    return jnp.where(lane % HEAD_DIM < HEAD_DIM // 2, rolled_back, rolled)


def fetch(sources, targets, sems):
    copies = [
        pltpu.make_async_copy(src, dst, sems.at[i])
        for i, (src, dst) in enumerate(zip(sources, targets))
    ]
    for copy in copies:
        copy.start()
    return copies


def pre_kernel(
    size, me_ref, x_ref, wm_ref, wo_ref, cos_ref, sin_ref,
    q_ref, kv_ref, n1t_ref, flat_ref, w, qkv,
):
    me = me_ref[0]
    half = wm_ref.shape[0]
    w[:half] = wm_ref[...]
    w[half:] = wo_ref[...]
    place = place_matrix(size, me, True)
    spread, mine = vector_places(size, me)
    shape = (size.count, 2 * half)
    row = lax.broadcasted_iota(jnp.int32, shape, 0) * size.tall + size.rows
    row = jnp.where(lax.broadcasted_iota(jnp.int32, shape, 1) == row, 1.0, 0.0).astype(BF)
    packed = times(row, w[:, :128]).astype(BF)
    flat = jnp.sum(jnp.where(mine, times(packed, spread), 0.0), axis=0, keepdims=True)
    flat_ref[...] = flat
    gain = flat[:, size.a_width : size.a_width + size.width]
    x = x_ref[...].astype(F32)
    inv = lax.rsqrt(jnp.mean(x * x, axis=-1, keepdims=True) + EPS)
    n1 = (x * inv * gain).astype(BF)
    n1a = times(n1, place)
    n1t_ref[...] = jnp.transpose(n1a).astype(BF)
    qkv[...] = times(n1a.astype(BF), w[...]) + flat[:, : size.a_width]
    kv_width = kv_ref.shape[1] // 2
    for t in range((size.width + kv_width) // 128):
        u = qkv[:, t * 128 : (t + 1) * 128]
        qkv[:, t * 128 : (t + 1) * 128] = u * cos_ref[...] + swap_halves(u) * sin_ref[...]
    q_ref[...] = qkv[:, : size.width].astype(BF)
    kv_ref[...] = qkv[:, size.width : size.qkv].astype(BF)


def tail_place(size, c):
    shape = (size.count * TAIL, size.count * MAIN)
    q = lax.broadcasted_iota(jnp.int32, shape, 0)
    at = lax.broadcasted_iota(jnp.int32, shape, 1)
    want = (q // TAIL) * MAIN + c * TAIL + q % TAIL
    return jnp.where(at == want, 1.0, 0.0).astype(BF)


def tail_place_back(size, c):
    shape = (size.count * MAIN, size.count * TAIL)
    at = lax.broadcasted_iota(jnp.int32, shape, 0)
    q = lax.broadcasted_iota(jnp.int32, shape, 1)
    want = (q // TAIL) * MAIN + c * TAIL + q % TAIL
    return jnp.where(at == want, 1.0, 0.0).astype(BF)


def mlp_kernel(
    size, me_ref, attn_ref, x_ref, cot_ref, flat_ref,
    b1_00, b1_01, b1_10, b1_11, b2_00, b2_01, b2_10, b2_11,
    out_ref, keep1, give1, keep2, give2, gmid_ref, gattn_ref, ggain_ref, delta_ref,
    wg, wu, wo, wd, mid, n2s, n2t, place, acc, gacc, dwd, tails, tail_o, packed,
):
    me = me_ref[0]
    width, ff = size.width, size.ff
    part = b1_00.shape[0]
    half, main = 2 * part, 4 * part
    rows_z = part // 2
    place[...] = place_matrix(size, me, False)
    first = (b1_00, b1_01, b1_10, b1_11)
    second = (b2_00, b2_01, b2_10, b2_11)
    room = size.piece + 128
    for i, b1 in enumerate(first):
        rows = slice(i * part, (i + 1) * part)
        wg[rows] = b1[:, :ff]
        wo[rows] = b1[:, size.out : size.out + size.wide]
        packed[rows] = b1[:, size.tail : size.tail + room]
    for i, b2 in enumerate(second):
        for y in range(2):
            at = (i // 2) * half + y * part + (i % 2) * rows_z
            wu[at : at + rows_z] = b2[y * rows_z : (y + 1) * rows_z, :ff]
    for c in range(PIECES):
        sel = tail_place(size, c)
        target = wg if c * size.piece < ff else wu
        at = c * size.piece % ff
        got = times(sel, packed[:, : size.piece])
        target[main:, at : at + size.piece] = got.astype(BF)
        if c * 128 < size.wide:
            got = times(sel, packed[:, size.piece : room])
            wo[main:, c * 128 : (c + 1) * 128] = got.astype(BF)
    zs = rows_z // MAIN
    for p in range(size.count):
        z, x, y, core = p % zs, p // zs % 2, p // (2 * zs) % 2, p // (4 * zs)
        owner = me ^ mask_of(size, p)
        for c in range(size.downs):
            which, at = size.down_at(c)
            src, row = (second[2 * core + x], y * zs + z) if which else (
                first[2 * core + y], x * zs + z
            )
            to = pl.multiple_of(owner * size.f_rows + c * MAIN, MAIN)
            wd[pl.ds(to, MAIN), :] = src[row * MAIN : (row + 1) * MAIN, at : at + size.wide]
    attn_s = times(attn_ref[...], place[...])
    m = x_ref[...].astype(F32) + times(attn_s.astype(BF), wo[:, :width])
    mid[...] = m
    inv = lax.rsqrt(jnp.mean(m * m, axis=-1, keepdims=True) + EPS)
    lo = size.a_width + size.wide
    gain = flat_ref[:, lo : lo + width]
    n2 = (m * inv * gain).astype(BF)
    spread = times(n2, place[...])
    n2s[...] = spread.astype(BF)
    n2t[...] = jnp.transpose(spread).astype(BF)
    acc[...] = jnp.zeros_like(acc)
    gacc[...] = jnp.zeros_like(gacc)
    step = 512 if ff % 512 == 0 else 256

    @pl.loop(0, ff // step)
    def _(b):
        at = pl.multiple_of(b * step, step)
        cols = pl.ds(at, step)
        gate = times(n2s[...], wg[:, cols])
        up = times(n2s[...], wu[:, cols])
        sig = 1.0 / (1.0 + jnp.exp(-gate))
        act = gate * sig
        h = act * up
        gh = times_back(cot_ref[...], wd[cols, :width])
        gg = (gh * up * (sig * (1.0 + gate * (1.0 - sig)))).astype(BF)
        gu = (gh * act).astype(BF)
        acc[...] += times(h.astype(BF), wd[cols, :width])
        dwd[cols, :width] = times(jnp.transpose(h).astype(BF), cot_ref[...]).astype(BF)
        gacc[...] += times_back(gg, wg[:, cols]) + times_back(gu, wu[:, cols])
        for k, (grad, keep, give) in enumerate(((gg, keep1, give1), (gu, keep2, give2))):
            dw = times(n2t[...], grad).astype(BF)
            keep[:, cols] = dw[:half]
            give[:, cols] = dw[half:main]
            tails[:, pl.ds(pl.multiple_of(k * ff + at, 128), step)] = dw[main:]

    m = mid[...]
    inv = lax.rsqrt(jnp.mean(m * m, axis=-1, keepdims=True) + EPS)
    out_ref[...] = jnp.transpose(m + acc[...]).astype(BF)
    high, low = split_two(gacc[...])
    gn2 = times_back(high, place[...]) + times_back(low, place[...])
    scaled = gn2 * gain
    dot = jnp.mean(scaled * m, axis=-1, keepdims=True)
    ggain_ref[...] = jnp.sum(gn2 * m * inv, axis=0, keepdims=True)
    gmid = cot_ref[...].astype(F32) + inv * scaled - m * (inv * inv * inv * dot)
    gmid_ref[...] = gmid
    branch = gmid.astype(BF)
    gattn = times_back(branch, wo[:, :width]).astype(BF)
    gattn = times_back(gattn, place[...]).astype(BF)
    gattn_ref[...] = gattn
    both = jnp.transpose(gattn.astype(F32) * attn_ref[...].astype(F32))
    for h in range(width // HEAD_DIM):
        at = slice(h * HEAD_DIM, (h + 1) * HEAD_DIM)
        delta_ref[h] = jnp.sum(both[at], axis=0, keepdims=True)
    dwo = times(jnp.transpose(attn_s).astype(BF), branch).astype(BF)
    tail_o[...] = jnp.zeros_like(tail_o)
    tail_o[:, :width] = dwo[main:]
    terms = ((keep1, keep2), (give1, give2))
    for i, (term, _) in enumerate(terms):
        term[:, size.out : size.out + width] = dwo[i * half : (i + 1) * half]
    wire = jnp.zeros((main, size.piece), F32)
    wire_o = jnp.zeros((main, 128), F32)
    for c in range(PIECES):
        sel = tail_place_back(size, c)
        wire += times(sel, tails[:, c * size.piece : (c + 1) * size.piece])
        if c * 128 < size.wide:
            wire_o += times(sel, tail_o[:, c * 128 : (c + 1) * 128])
    for i, (term, _) in enumerate(terms):
        rows = slice(i * half, (i + 1) * half)
        term[:, size.tail : size.tail + size.piece] = wire[rows].astype(BF)
        term[:, size.tail_o : size.tail_o + 128] = wire_o[rows].astype(BF)
    for p in range(size.count):
        to = terms[p // (size.count // 2)]
        rows = slice(p * MAIN % half, p * MAIN % half + MAIN)
        owner = me ^ mask_of(size, p)
        for c in range(size.downs):
            which, at = size.down_at(c)
            src = pl.multiple_of(owner * size.f_rows + c * MAIN, MAIN)
            to[which][rows, at : at + size.wide] = dwd[pl.ds(src, MAIN), :]


def post_kernel(
    size, me_ref, dq_ref, dkv_ref, got_ref, cos_ref, sin_ref, n1t_ref,
    wm_ref, wo_ref, x_ref, gmid_ref, flat_ref, ggain_ref,
    gx_ref, keep_ref, give_ref, turn_buf, grad, vec_row,
):
    me = me_ref[0]
    width = size.width
    half = wm_ref.shape[0]
    place = place_matrix(size, me, True)
    kv_width = KV_HEADS * HEAD_DIM
    turned = width + kv_width
    dkv = dkv_ref[...] + got_ref[...].astype(F32)
    turn_buf[:, :width] = dq_ref[...]
    turn_buf[:, width:] = dkv[:, :kv_width]
    grad[...] = jnp.zeros_like(grad)
    grad[:, turned : turned + kv_width] = dkv[:, kv_width:].astype(BF)
    for t in range(turned // 128):
        u = turn_buf[:, t * 128 : (t + 1) * 128]
        back = u * cos_ref[...] - swap_halves(u) * sin_ref[...]
        grad[:, t * 128 : (t + 1) * 128] = back.astype(BF)
    g = grad[...]
    gn1 = jnp.zeros((g.shape[0], width), F32)
    for part, w_ref in enumerate((wm_ref, wo_ref)):
        for values in split_two(times_back(g, w_ref[...])):
            gn1 += times_back(values, place[:, part * half : (part + 1) * half])
    x = x_ref[...].astype(F32)
    inv = lax.rsqrt(jnp.mean(x * x, axis=-1, keepdims=True) + EPS)
    gain = flat_ref[:, size.a_width : size.a_width + width]
    scaled = gn1 * gain
    dot = jnp.mean(scaled * x, axis=-1, keepdims=True)
    gx_ref[...] = jnp.transpose(gmid_ref[...] + inv * scaled - x * (inv * inv * inv * dot))
    vec_row[...] = jnp.zeros_like(vec_row)
    vec_row[:, : size.a_width] = jnp.sum(g.astype(F32), axis=0, keepdims=True)
    vec_row[:, size.a_width : size.a_width + width] = jnp.sum(gn1 * x * inv, axis=0, keepdims=True)
    lo = size.a_width + size.wide
    vec_row[:, lo : lo + width] = ggain_ref[...]
    spread, mine = vector_places(size, me)
    packed = times_back(jnp.where(mine, vec_row[...], 0.0).astype(BF), spread)
    shape = (half, size.count)
    for part, term in ((0, keep_ref), (1, give_ref)):
        rows = slice(part * half, (part + 1) * half)
        dw = times(n1t_ref[rows], g)
        term[...] = dw.astype(BF)
        want = lax.broadcasted_iota(jnp.int32, shape, 1) * size.tall + size.rows - part * half
        here = lax.broadcasted_iota(jnp.int32, shape, 0) == want
        extra = times(jnp.where(here, 1.0, 0.0).astype(BF), packed.astype(BF))
        term[:, :128] = (dw[:, :128] + extra).astype(BF)


def call(kernel, name, out_shape, scratch, micros, args, vmem, any_in=(), any_out=(), scalar=True):
    shapes = [jax.ShapeDtypeStruct(s, t) for s, t in out_shape]
    here = pl.BlockSpec(memory_space=pl.ANY)
    specs = [here if i in any_in else VM for i in range(len(args))]
    if scalar:
        specs[0] = SM
    return pl.pallas_call(
        kernel,
        out_shape=shapes,
        in_specs=specs,
        out_specs=[here if i in any_out else VM for i in range(len(shapes))],
        scratch_shapes=[
            pltpu.SemaphoreType.DMA(s) if t is None else pltpu.VMEM(s, t) for s, t in scratch
        ],
        compiler_params=pltpu.CompilerParams(vmem_limit_bytes=vmem * 2**20),
        cost_estimate=cost_of(micros),
        name=name,
    )(*args)


def pad_to(values, rows, columns):
    return jnp.pad(values, ((0, rows - values.shape[0]), (0, columns - values.shape[1])))


def tail_pack(rows, piece):
    rows = pad_to(rows, TAIL, PIECES * piece)
    return rows.reshape(TAIL, PIECES, piece).transpose(1, 0, 2).reshape(MAIN, piece)


def tail_unpack(wire, used):
    piece = wire.shape[1]
    rows = wire.reshape(PIECES, TAIL, piece).transpose(1, 0, 2).reshape(TAIL, PIECES * piece)
    return rows[:, :used]


def tie(*values):
    return lax.optimization_barrier(values)


def local_blocks(size, blocks, pos, args):
    (
        tokens, q_weight, k_weight, v_weight, o_weight, gate_weight, up_weight, down_weight,
        vectors, cotangent,
    ) = args
    tok_rows, width = tokens.shape
    ff, rows = size.ff, size.rows
    kv_width = KV_HEADS * HEAD_DIM
    ctx_index = lax.axis_index("ctx")
    me = (lax.axis_index("dp") * lax.axis_size("ctx") + ctx_index).astype(jnp.int32).reshape(1)
    half = size.count // 2
    info, docs, cos, sin = pos

    joined_w = jnp.concatenate(
        [w.reshape(rows, -1) for w in (q_weight, k_weight, v_weight)], axis=1
    )
    vec_row = pad_to(vectors.reshape(1, -1), size.tall - rows, size.a_width)
    wire_a = jnp.concatenate([pad_to(joined_w, rows, size.a_width), vec_row], axis=0)
    za = blocks.along_z(wire_a)
    xa = jnp.stack([za, blocks.swap(za, blocks.x)])
    _, flat_w = tie(za, (gate_weight, up_weight, o_weight, down_weight))
    w_rows = [w.reshape(rows, -1) for w in flat_w[:3]]
    wire_1, wire_2, tokens, cotangent = call(
        functools.partial(wire_kernel, size),
        "wire",
        [
            ((MAIN, size.first), BF), ((MAIN, size.second), BF), ((tok_rows, width), BF),
            ((tok_rows, width), BF),
        ],
        [
            ((MAIN, size.piece), F32), ((MAIN, 128), F32), ((tok_rows, width), BF),
            ((tok_rows, width), BF), ((2,), None),
        ],
        1,
        w_rows + [flat_w[3].reshape(size.f_rows, width), tokens.T, cotangent.T],
        10,
        any_out=(2, 3),
        scalar=False,
    )
    xa, wire_1, wire_2 = tie(xa, wire_1, wire_2)
    ya = blocks.swap(xa, blocks.y)
    z1 = blocks.along_z(wire_1)
    z1, wire_2, ya = tie(z1, wire_2, ya)
    z2 = blocks.along_z(wire_2)
    x1 = jnp.stack([z1, blocks.swap(z1, blocks.x)])
    a_mine = jnp.stack([xa, ya]).reshape(half * size.tall, size.a_width)
    a_other = blocks.swap(a_mine, blocks.core)

    a_rows = size.count * size.tall
    q_rot, kv_mine, n1t, flat = call(
        functools.partial(pre_kernel, size),
        "norm_qkv",
        [
            ((tok_rows, width), BF), ((tok_rows, 2 * kv_width), BF), ((a_rows, tok_rows), BF),
            ((1, size.flat), F32),
        ],
        [((a_rows, size.a_width), BF), ((tok_rows, size.a_width), F32)],
        3,
        (me, tokens, a_mine, a_other, cos, sin),
        16,
    )
    kv_got = blocks.swap(kv_mine, blocks.x)
    own = attention_own(q_rot, kv_mine, info, docs)
    z2, x1 = tie(z2, x1, kv_mine)[:2]
    y2 = jnp.stack([z2, blocks.swap(z2, blocks.y)])
    b1_parts = [b.reshape(half // 2 * MAIN, -1) for b in (x1, blocks.swap(x1, blocks.y))]
    b2_parts = [b.reshape(half // 2 * MAIN, -1) for b in (y2, blocks.swap(y2, blocks.x))]
    attn, lse = attention_others(q_rot, kv_got, *own, info, docs)

    b1_parts[1:] = [b1_parts[1], blocks.swap(b1_parts[0], blocks.core)]
    b2_parts[1:] = [b2_parts[1], blocks.swap(b2_parts[0], blocks.core)]
    attn, b2_parts[1] = tie(attn, b2_parts[1])
    attn, b1_parts[1] = tie(attn, b1_parts[1])
    b2_parts.append(blocks.swap(b2_parts[1], blocks.core))
    b1_parts.append(blocks.swap(b1_parts[1], blocks.core))
    main = size.count * MAIN
    slots = main + size.count * TAIL
    layer_out, keep1, give1, keep2, give2, grad_mid, grad_attn, grad_gain, delta = call(
        functools.partial(mlp_kernel, size),
        "feed_forward",
        [
            ((width, tok_rows), BF),
            ((main // 2, size.first), BF), ((main // 2, size.first), BF),
            ((main // 2, size.second), BF), ((main // 2, size.second), BF),
            ((tok_rows, width), F32), ((tok_rows, width), BF), ((1, width), F32),
            ((width // HEAD_DIM, 1, tok_rows), F32),
        ],
        [
            ((slots, ff), BF), ((slots, ff), BF), ((slots, size.wide), BF), ((ff, size.wide), BF),
            ((tok_rows, width), F32), ((tok_rows, slots), BF), ((slots, tok_rows), BF),
            ((width, slots), BF), ((tok_rows, width), F32), ((tok_rows, slots), F32),
            ((ff, size.wide), BF), ((size.count * TAIL, 2 * ff), BF),
            ((size.count * TAIL, size.wide), BF), ((main, size.piece + 128), BF),
        ],
        21,
        (
            me, attn, tokens, cotangent, flat, *b1_parts, *b2_parts,
        ),
        28,
    )

    got1 = blocks.swap(give1, blocks.core)
    got2 = blocks.swap(give2, blocks.core)
    shape = (2, 2, blocks.zs, MAIN, -1)
    h1 = blocks.add(keep1, got1).reshape(shape)
    h2 = blocks.add(keep2, got2).reshape(shape)
    dq_others, give_kv = attention_grad(q_rot, kv_got, grad_attn, lse, delta, info, docs)
    got_kv = blocks.swap(give_kv, blocks.x)
    dq_others, h1, h2 = tie(dq_others, h1, h2)
    h1 = blocks.add(h1[0], blocks.swap(h1[1], blocks.y))
    h2 = blocks.add(h2[:, 0], blocks.swap(h2[:, 1], blocks.x))
    grad_q_rot, own_kv = attention_grad(
        q_rot, kv_mine, grad_attn, lse, delta, info, docs, dq_others
    )
    got_kv, h1, h2 = tie(got_kv, h1, h2)
    h1 = blocks.add(h1[0], blocks.swap(h1[1], blocks.x))
    h2 = blocks.add(h2[0], blocks.swap(h2[1], blocks.y))

    gx, keep_a, give_a = call(
        functools.partial(post_kernel, size),
        "norm_qkv_back",
        [
            ((width, tok_rows), F32), ((a_rows // 2, size.a_width), BF),
            ((a_rows // 2, size.a_width), BF),
        ],
        [
            ((tok_rows, width + kv_width), F32), ((tok_rows, size.a_width), BF),
            ((1, size.flat), F32),
        ],
        6,
        (
            me, grad_q_rot, own_kv, got_kv, cos, sin, n1t, a_mine,
            a_other, tokens, grad_mid, flat, grad_gain,
        ),
        24,
    )
    held = blocks.add(keep_a, blocks.swap(give_a, blocks.core))
    held, h2 = tie(held, h2)
    held = held.reshape(2, 2, blocks.zs, size.tall, size.a_width)
    held = blocks.add(held[0], blocks.swap(held[1], blocks.y))
    held, share2, h1 = tie(held, blocks.sum_z(h2), h1)
    held = blocks.add(held[0], blocks.swap(held[1], blocks.x))
    held, share1 = tie(held, blocks.sum_z(h1))
    share_a = blocks.sum_z(held)

    tails = tail_unpack(share1[:, size.tail : size.tail + size.piece], 2 * ff)
    tail_o = tail_unpack(share1[:, size.tail_o : size.tail_o + 128], width)
    share_out = jnp.concatenate([share1[:, size.out : size.out + width], tail_o], axis=0)
    share_gate = jnp.concatenate([share1[:, :ff], tails[:, :ff]], axis=0)
    share_up = jnp.concatenate([share2[:, :ff], tails[:, ff:]], axis=0)
    downs = [size.down_at(c) for c in range(size.downs)]
    share_down = jnp.concatenate(
        [(share1, share2)[which][:, at : at + width] for which, at in downs], axis=0
    )
    ends = (width, width + kv_width, size.qkv)
    return (
        layer_out.T, gx.T, share_a[:rows, : ends[0]].reshape(-1),
        share_a[:rows, ends[0] : ends[1]].reshape(-1),
        share_a[:rows, ends[1] : ends[2]].reshape(-1),
        share_out.reshape(-1), share_gate.reshape(-1), share_up.reshape(-1),
        share_down.reshape(-1), share_a[rows, : size.vec],
    )


def local(
    tokens, q_weight, k_weight, v_weight, o_weight, gate_weight, up_weight, down_weight,
    vectors, doc_lengths, cotangent,
):
    tok_rows, width = tokens.shape
    ctx_count = lax.axis_size("ctx")
    dp_count = lax.axis_size("dp")
    count = dp_count * ctx_count
    seq_tokens = tok_rows * ctx_count
    ctx_index = lax.axis_index("ctx")
    heads = width // HEAD_DIM
    kv_width = KV_HEADS * HEAD_DIM
    ff = gate_weight.shape[0] * count // width

    position_all = doc_layout(doc_lengths[0], seq_tokens)
    offset = ctx_index * tok_rows
    position_mine = lax.dynamic_slice_in_dim(position_all, offset, tok_rows)
    docs = doc_lengths.shape[1]
    others = (ctx_count - 1 - ctx_index) * tok_rows
    heads_of = jnp.stack([ctx_index, others, offset]).astype(jnp.int32)
    info = jnp.concatenate([heads_of, jnp.cumsum(doc_lengths[0])[:-1].astype(jnp.int32)])
    half = HEAD_DIM // 2
    freq = THETA ** (-jnp.arange(half, dtype=F32) * 2.0 / HEAD_DIM)
    position_f = position_mine.astype(F32)[:, None]

    whole_rows = width % count == 0 and ff % count == 0
    if whole_rows and ctx_count == 2 and dp_count % 4 == 0 and count & (count - 1) == 0:
        size = Sizes(width, ff, dp_count, ctx_count, vectors.shape[0], kv_width)
        if size.fits() and (width + kv_width) % 128 == 0:
            angle = position_f * jnp.tile(freq, 128 // half)[None, :]
            sign = np.where(np.arange(128) % HEAD_DIM < half, -1.0, 1.0).astype(np.float32)
            pos = (info, docs, jnp.cos(angle), jnp.sin(angle) * sign)
            args = (
                tokens, q_weight, k_weight, v_weight, o_weight, gate_weight, up_weight,
                down_weight, vectors, cotangent,
            )
            return local_blocks(size, Blocks(dp_count, ctx_count), pos, args)

    angle = position_f * freq[None, :]
    cosine = jnp.cos(angle)[:, None, :]
    sine = jnp.sin(angle)[:, None, :]
    inputs = tokens.astype(F32)
    inv_first = lax.rsqrt(jnp.mean(inputs * inputs, axis=-1, keepdims=True) + EPS)

    def whole(part):
        return lax.all_gather(part, AXES, axis=0, tiled=True)

    w_qkv = jnp.concatenate(
        [whole(w).reshape(width, -1) for w in (q_weight, k_weight, v_weight)], axis=1
    )
    w_out = whole(o_weight).reshape(width, width)
    w_gate = whole(gate_weight).reshape(width, ff)
    w_up = whole(up_weight).reshape(width, ff)
    w_down = whole(down_weight).reshape(ff, width)
    flat = whole(vectors).astype(F32)
    ends = [width, width + kv_width, width + 2 * kv_width, 2 * width + 2 * kv_width]
    gain_attn = flat[ends[2] : ends[3]]
    gain_mlp = flat[ends[3] : ends[3] + width]

    n_first = (inputs * inv_first * gain_attn).astype(BF)
    qkv = times(n_first, w_qkv) + flat[: ends[2]]
    q_rot = turn(qkv[:, :width].reshape(tok_rows, heads, HEAD_DIM), cosine, sine)
    q_rot = q_rot.astype(BF).reshape(tok_rows, width)
    k_rot = turn(qkv[:, width : ends[1]].reshape(tok_rows, KV_HEADS, HEAD_DIM), cosine, sine)
    k_rot = k_rot.astype(BF).reshape(tok_rows, kv_width)
    kv_mine = jnp.concatenate([k_rot, qkv[:, ends[1] :].astype(BF)], axis=1)
    kv = (lax.all_gather(kv_mine, "ctx", axis=0, tiled=True),)
    info = info.at[0].set(1)
    attn, lse = attention(q_rot, kv, info, docs, seq_tokens, False)
    mid = inputs + times(attn, w_out)
    inv_second = lax.rsqrt(jnp.mean(mid * mid, axis=-1, keepdims=True) + EPS)
    n_second = (mid * inv_second * gain_mlp).astype(BF)
    gate = times(n_second, w_gate)
    up_val = times(n_second, w_up)
    sig = jax.nn.sigmoid(gate)
    act = gate * sig
    hidden = (act * up_val).astype(BF)
    layer_out = (mid + times(hidden, w_down)).astype(BF)

    grad_wdown = inner_rows(hidden, cotangent)
    grad_hidden = times_back(cotangent, w_down)
    grad_gate = (grad_hidden * up_val * (sig * (1.0 + gate * (1.0 - sig)))).astype(BF)
    grad_up = (grad_hidden * act).astype(BF)
    grad_wgate = inner_rows(n_second, grad_gate)
    grad_wup = inner_rows(n_second, grad_up)
    grad_n2 = times_back(grad_gate, w_gate) + times_back(grad_up, w_up)
    grad_mid_norm, grad_gain_mlp = norm_back(mid, inv_second, gain_mlp, grad_n2)
    grad_mid = cotangent.astype(F32) + grad_mid_norm
    grad_branch = grad_mid.astype(BF)
    grad_wout = inner_rows(attn, grad_branch)
    grad_attn = times_back(grad_branch, w_out).astype(BF)
    grad_q_rot, grad_kv = attention_back(
        q_rot, kv, grad_attn, lse, info, docs, seq_tokens, False, 0, KV_HEADS
    )
    grad_kv_mine = lax.psum_scatter(
        grad_kv.astype(BF), "ctx", scatter_dimension=0, tiled=True
    ).astype(F32)
    grad_q = turn(grad_q_rot.reshape(tok_rows, heads, HEAD_DIM), cosine, -sine)
    grad_k = turn(
        grad_kv_mine[:, :kv_width].reshape(tok_rows, KV_HEADS, HEAD_DIM), cosine, -sine
    )
    grad_qkv = jnp.concatenate(
        [
            grad_q.reshape(tok_rows, width).astype(BF),
            grad_k.reshape(tok_rows, kv_width).astype(BF),
            grad_kv_mine[:, kv_width:].astype(BF),
        ],
        axis=1,
    )
    grad_wqkv = inner_rows(n_first, grad_qkv)
    grad_bias = jnp.sum(grad_qkv.astype(F32), axis=0)
    grad_n1 = times_back(grad_qkv, w_qkv)
    grad_x_norm, grad_gain_attn = norm_back(inputs, inv_first, gain_attn, grad_n1)
    input_grad = grad_mid + grad_x_norm
    used = 3 * width + 2 * kv_width
    padding = jnp.zeros((vectors.shape[0] * count - used,), F32)
    vector_term = jnp.concatenate([grad_bias, grad_gain_attn, grad_gain_mlp, padding])

    def shares(term):
        return lax.psum_scatter(term.reshape(-1), AXES, scatter_dimension=0, tiled=True)

    return (
        layer_out, input_grad, shares(grad_wqkv[:, :width]),
        shares(grad_wqkv[:, width : ends[1]]), shares(grad_wqkv[:, ends[1] :]),
        shares(grad_wout), shares(grad_wgate), shares(grad_wup), shares(grad_wdown),
        shares(vector_term),
    )


def solution(mesh):
    split = P(AXES)
    rows = P(AXES, None)
    in_specs = (rows,) + (split,) * 8 + (P("dp", None), rows)
    out_specs = (rows, rows) + (split,) * 8
    return jax.shard_map(local, mesh=mesh, in_specs=in_specs, out_specs=out_specs, check_vma=False)
```

```python
import functools

import jax
import jax.numpy as jnp
import numpy as np
from jax import lax
from jax.experimental import pallas as pl
from jax.experimental.pallas import tpu as pltpu
from jax.sharding import PartitionSpec as P

KV_HEADS = 3
HEAD_DIM = 64

EPS = 1e-06
THETA = 100000.0
NEG_FILL = -1e30
AXES = ("dp", "ctx")
BF = jnp.bfloat16
F32 = jnp.float32


def times(left, right):
    return jnp.dot(left, right, preferred_element_type=F32)


def inner_rows(left, right):
    return lax.dot_general(left, right, (((0,), (0,)), ((), ())), preferred_element_type=F32)


def times_back(left, right):
    return lax.dot_general(left, right, (((1,), (1,)), ((), ())), preferred_element_type=F32)


def norm_back(values, inv, gain, grad):
    scaled = grad * gain
    dot = jnp.mean(scaled * values, axis=-1, keepdims=True)
    grad_values = inv * scaled - values * (inv * inv * inv * dot)
    grad_gain = jnp.sum(grad * values * inv, axis=0)
    return grad_values, grad_gain


def turn(values, cosine, sine):
    half = values.shape[-1] // 2
    first = values[..., :half]
    second = values[..., half:]
    return jnp.concatenate(
        [first * cosine - second * sine, second * cosine + first * sine], axis=-1
    )


def doc_layout(lengths, count):
    ends = jnp.cumsum(lengths)
    place = jnp.arange(count, dtype=jnp.int32)
    segment = jnp.sum((place[:, None] >= ends[None, :-1]).astype(jnp.int32), axis=1)
    starts = ends - lengths
    picked = segment[:, None] == jnp.arange(lengths.shape[0], dtype=jnp.int32)[None, :]
    first = jnp.sum(jnp.where(picked, starts[None, :], 0), axis=1)
    return place - first


def fill_bias(bias, info, docs, short, own=None):
    total, rows = bias.shape
    row_q = lax.broadcasted_iota(jnp.int32, (1, rows), 1) + info[2]
    first = jnp.zeros_like(row_q)
    for j in range(docs - 1):
        first = jnp.where(row_q >= info[3 + j], info[3 + j], first)
    parts = ((0, total, 0),)
    if own is not None:
        parts = ((0, total, info[2] if own else info[1]),)
    elif short < total:
        parts = ((0, total - short, info[1]), (total - short, total, info[2]))
    for start, stop, base in parts:
        row_k = lax.broadcasted_iota(jnp.int32, (stop - start, rows), 0)
        allowed = (row_k >= first - base) & (row_k <= row_q - base)
        bias[start:stop] = jnp.where(allowed, 0.0, NEG_FILL)


def key_range(full, total, short, rows, block, at, causal):
    start = 0 if full else total - short
    stop = total - rows + (at + 1) * block if causal else total
    return start, stop


def key_parts(kv_refs):
    at = 0
    for kv_ref in kv_refs:
        yield slice(at, at + kv_ref.shape[0]), kv_ref
        at += kv_ref.shape[0]


def attn_fwd_kernel(
    heads, block, short, causal, docs, info, q_ref, *refs,
):
    kv_refs, (out_ref, lse_ref, qs, ks, vts, bias, out_t) = refs[:-7], refs[-7:]
    rows = q_ref.shape[0]
    total = bias.shape[0]
    kv_width = KV_HEADS * HEAD_DIM
    group = heads // KV_HEADS
    fill_bias(bias, info, docs, short)
    for h in range(heads):
        qs[h] = q_ref[:, h * HEAD_DIM : (h + 1) * HEAD_DIM] * BF(HEAD_DIM**-0.5)
    for at, kv_ref in key_parts(kv_refs):
        for g in range(KV_HEADS):
            ks[g, at] = kv_ref[:, g * HEAD_DIM : (g + 1) * HEAD_DIM]
        vts[:, at] = jnp.transpose(kv_ref[:, kv_width:].astype(F32)).astype(BF)

    def run(full):
        @pl.loop(0, KV_HEADS)
        def _(g):
            v_rows = pl.ds(pl.multiple_of(g * HEAD_DIM, HEAD_DIM), HEAD_DIM)
            for j in range(group):
                h = g * group + j
                out_rows = pl.ds(pl.multiple_of(h * HEAD_DIM, HEAD_DIM), HEAD_DIM)
                for at in range(rows // block):
                    start, stop = key_range(full, total, short, rows, block, at, causal)
                    cols = slice(at * block, (at + 1) * block)
                    s = times_back(ks[g, start:stop], qs[h, cols])
                    s = s + bias[start:stop, cols]
                    top = jnp.max(s, axis=0, keepdims=True)
                    p = jnp.exp(s - top)
                    total_p = jnp.sum(p, axis=0, keepdims=True)
                    o = times(vts[v_rows, start:stop], p.astype(BF))
                    out_t[out_rows, cols] = o / total_p
                    lse_ref[h, :, cols] = top + jnp.log(total_p)

    pl.when(info[0] != 0)(lambda: run(True))
    pl.when(info[0] == 0)(lambda: run(False))
    out_ref[...] = jnp.transpose(out_t[...]).astype(BF)


def attn_own_kernel(
    heads, block, docs, info, q_ref, kv_ref, acc, top_ref, sum_ref, qs, ks, vts, bias
):
    rows = q_ref.shape[0]
    kv_width = KV_HEADS * HEAD_DIM
    group = heads // KV_HEADS
    fill_bias(bias, info, docs, rows, own=True)
    for h in range(heads):
        qs[h] = q_ref[:, h * HEAD_DIM : (h + 1) * HEAD_DIM] * BF(HEAD_DIM**-0.5)
    for g in range(KV_HEADS):
        ks[g] = kv_ref[:, g * HEAD_DIM : (g + 1) * HEAD_DIM]
    vts[...] = jnp.transpose(kv_ref[:, kv_width:].astype(F32)).astype(BF)

    @pl.loop(0, KV_HEADS)
    def _(g):
        v_rows = pl.ds(pl.multiple_of(g * HEAD_DIM, HEAD_DIM), HEAD_DIM)
        for j in range(group):
            h = g * group + j
            out_rows = pl.ds(pl.multiple_of(h * HEAD_DIM, HEAD_DIM), HEAD_DIM)
            for at in range(rows // block):
                stop = (at + 1) * block
                cols = slice(at * block, stop)
                s = times_back(ks[g, :stop], qs[h, cols]) + bias[:stop, cols]
                top = jnp.max(s, axis=0, keepdims=True)
                p = jnp.exp(s - top)
                top_ref[h, :, cols] = top
                sum_ref[h, :, cols] = jnp.sum(p, axis=0, keepdims=True)
                acc[out_rows, cols] = times(vts[v_rows, :stop], p.astype(BF))


def attn_others_kernel(
    heads, block, docs, info, q_ref, kv_ref, acc, top_ref, sum_ref, out_ref, lse_ref,
    qs, ks, vts, bias, out_t,
):
    rows = q_ref.shape[0]
    kv_width = KV_HEADS * HEAD_DIM
    group = heads // KV_HEADS

    @pl.when(info[0] == 0)
    def _():
        for h in range(heads):
            at = slice(h * HEAD_DIM, (h + 1) * HEAD_DIM)
            out_t[at] = acc[at] / sum_ref[h]
            lse_ref[h] = top_ref[h] + jnp.log(sum_ref[h])

    @pl.when(info[0] != 0)
    def _():
        fill_bias(bias, info, docs, rows, own=False)
        for h in range(heads):
            qs[h] = q_ref[:, h * HEAD_DIM : (h + 1) * HEAD_DIM] * BF(HEAD_DIM**-0.5)
        for g in range(KV_HEADS):
            ks[g] = kv_ref[:, g * HEAD_DIM : (g + 1) * HEAD_DIM]
        vts[...] = jnp.transpose(kv_ref[:, kv_width:].astype(F32)).astype(BF)

        @pl.loop(0, KV_HEADS)
        def _(g):
            v_rows = pl.ds(pl.multiple_of(g * HEAD_DIM, HEAD_DIM), HEAD_DIM)
            for j in range(group):
                h = g * group + j
                out_rows = pl.ds(pl.multiple_of(h * HEAD_DIM, HEAD_DIM), HEAD_DIM)
                for at in range(rows // block):
                    cols = slice(at * block, (at + 1) * block)
                    s = times_back(ks[g], qs[h, cols]) + bias[:, cols]
                    own = top_ref[h, :, cols]
                    top = jnp.maximum(own, jnp.max(s, axis=0, keepdims=True))
                    scale = jnp.exp(own - top)
                    p = jnp.exp(s - top)
                    total_p = sum_ref[h, :, cols] * scale + jnp.sum(p, axis=0, keepdims=True)
                    o = acc[out_rows, cols] * scale + times(vts[v_rows], p.astype(BF))
                    out_t[out_rows, cols] = o / total_p
                    lse_ref[h, :, cols] = top + jnp.log(total_p)

    out_ref[...] = jnp.transpose(out_t[...]).astype(BF)


def attn_grad_kernel(
    heads, block, docs, own, info, q_ref, kv_ref, do_ref, lse_ref, delta_ref, *refs
):
    refs, (qs, dos, ks, vs, kts, bias, dk, dv) = refs[:-8], refs[-8:]
    if own:
        before, dq_ref, dkv_ref, dq_t = refs
    else:
        dq_t, dkv_ref = refs
    rows = q_ref.shape[0]
    kv_width = KV_HEADS * HEAD_DIM
    group = heads // KV_HEADS
    dk[...] = jnp.zeros_like(dk)
    dv[...] = jnp.zeros_like(dv)

    def run():
        fill_bias(bias, info, docs, rows, own=own)
        for h in range(heads):
            at = slice(h * HEAD_DIM, (h + 1) * HEAD_DIM)
            qs[h] = q_ref[:, at] * BF(HEAD_DIM**-0.5)
            dos[h] = do_ref[:, at]
        for g in range(KV_HEADS):
            lo = g * HEAD_DIM
            ks[g] = kv_ref[:, lo : lo + HEAD_DIM]
            vs[g] = kv_ref[:, kv_width + lo : kv_width + lo + HEAD_DIM]
        kts[...] = jnp.transpose(kv_ref[:, :kv_width].astype(F32)).astype(BF)

        @pl.loop(0, KV_HEADS)
        def _(g):
            k_rows = pl.ds(pl.multiple_of(g * HEAD_DIM, HEAD_DIM), HEAD_DIM)
            for j in range(group):
                h = g * group + j
                out_rows = pl.ds(pl.multiple_of(h * HEAD_DIM, HEAD_DIM), HEAD_DIM)
                for at in range(rows // block):
                    stop = (at + 1) * block if own else rows
                    cols = slice(at * block, (at + 1) * block)
                    q = qs[h, cols]
                    do = dos[h, cols]
                    s = times_back(ks[g, :stop], q) + bias[:stop, cols]
                    p = jnp.exp(s - lse_ref[h, :, cols])
                    dp = times_back(vs[g, :stop], do)
                    ds = (p * (dp - delta_ref[h, :, cols])).astype(BF)
                    dk[g, :stop] += times(ds, q)
                    dv[g, :stop] += times(p.astype(BF), do)
                    dq = times(kts[k_rows, :stop], ds) * HEAD_DIM**-0.5
                    dq_t[out_rows, cols] = before[out_rows, cols] + dq if own else dq

    if own:
        run()
        dq_ref[...] = jnp.transpose(dq_t[...])
    else:
        pl.when(info[0] != 0)(run)

        @pl.when(info[0] == 0)
        def _():
            dq_t[...] = jnp.zeros_like(dq_t)

    for g in range(KV_HEADS):
        lo = g * HEAD_DIM
        dkv_ref[:, lo : lo + HEAD_DIM] = dk[g].astype(dkv_ref.dtype)
        dkv_ref[:, kv_width + lo : kv_width + lo + HEAD_DIM] = dv[g].astype(dkv_ref.dtype)


def attn_bwd_kernel(
    heads, block, short, causal, docs, g0, g1, parts, info, q_ref, do_ref, lse_ref, *refs,
):
    kv_refs, outs, scratch = refs[:parts], refs[parts:-9], refs[-9:]
    qs, ks, vs, kts, dos, bias, dq_t, dk, dv = scratch
    rows = q_ref.shape[0]
    total = bias.shape[0]
    kv_width = KV_HEADS * HEAD_DIM
    group = heads // KV_HEADS
    keys = g1 - g0
    fill_bias(bias, info, docs, short)
    for h in range(keys * group):
        lanes = slice((g0 * group + h) * HEAD_DIM, (g0 * group + h + 1) * HEAD_DIM)
        qs[h] = q_ref[:, lanes] * BF(HEAD_DIM**-0.5)
        dos[h] = do_ref[:, lanes]
    for g in range(keys):
        lo = (g0 + g) * HEAD_DIM
        for at, kv_ref in key_parts(kv_refs):
            ks[g, at] = kv_ref[:, lo : lo + HEAD_DIM]
            vs[g, at] = kv_ref[:, kv_width + lo : kv_width + lo + HEAD_DIM]
        kts[g] = jnp.transpose(ks[g].astype(F32)).astype(BF)
    dk[...] = jnp.zeros_like(dk)
    dv[...] = jnp.zeros_like(dv)

    def run(full):
        @pl.loop(0, keys * group)
        def _(h):
            g = h // group if keys > 1 else 0
            out_rows = pl.ds(pl.multiple_of(h * HEAD_DIM, HEAD_DIM), HEAD_DIM)
            for at in range(rows // block):
                start, stop = key_range(full, total, short, rows, block, at, causal)
                cols = slice(at * block, (at + 1) * block)
                q = qs[h, cols]
                do = dos[h, cols]
                s = times_back(ks[g, start:stop], q)
                p = jnp.exp(s + bias[start:stop, cols] - lse_ref[g0 * group + h, :, cols])
                dp = times_back(vs[g, start:stop], do)
                t = p * dp
                inner = jnp.sum(t, axis=0, keepdims=True)
                ds = (t - p * inner).astype(BF)
                dk[g, start:stop] += times(ds, q)
                dv[g, start:stop] += times(p.astype(BF), do)
                dq_t[out_rows, cols] = times(kts[g, :, start:stop], ds) * HEAD_DIM**-0.5

    pl.when(info[0] != 0)(lambda: run(True))
    pl.when(info[0] == 0)(lambda: run(False))
    outs[0][...] = jnp.transpose(dq_t[...])
    cut = total - outs[1].shape[0]
    for part, out in ((slice(cut, total), outs[1]),) + tuple((slice(0, cut), o) for o in outs[2:]):
        for g in range(keys):
            lo = g * HEAD_DIM
            out[:, lo : lo + HEAD_DIM] = dk[g, part].astype(out.dtype)
            lo += keys * HEAD_DIM
            out[:, lo : lo + HEAD_DIM] = dv[g, part].astype(out.dtype)


VM = pl.BlockSpec(memory_space=pltpu.VMEM)
SM = pl.BlockSpec(memory_space=pltpu.SMEM)


def cost_of(micros):
    return pl.CostEstimate(
        flops=int(micros * 1.1e9), bytes_accessed=2**20, transcendentals=0
    )


def attention(q, kv, info, docs, short, causal):
    rows, width = q.shape
    total = sum(part.shape[0] for part in kv)
    heads = width // HEAD_DIM
    block = min(rows, 256)
    return pl.pallas_call(
        functools.partial(attn_fwd_kernel, heads, block, short, causal, docs),
        out_shape=(
            jax.ShapeDtypeStruct((rows, width), BF),
            jax.ShapeDtypeStruct((heads, 1, rows), F32),
        ),
        in_specs=[SM] + [VM] * (1 + len(kv)),
        out_specs=(VM, VM),
        scratch_shapes=[
            pltpu.VMEM((heads, rows, HEAD_DIM), BF),
            pltpu.VMEM((KV_HEADS, total, HEAD_DIM), BF),
            pltpu.VMEM((KV_HEADS * HEAD_DIM, total), BF),
            pltpu.VMEM((total, rows), F32),
            pltpu.VMEM((width, rows), F32),
        ],
        compiler_params=pltpu.CompilerParams(vmem_limit_bytes=20 * 2**20),
        cost_estimate=cost_of(14),
        name="attn_fwd",
    )(info, q, *kv)


def attention_own(q, kv, info, docs):
    rows, width = q.shape
    heads = width // HEAD_DIM
    stat = jax.ShapeDtypeStruct((heads, 1, rows), F32)
    return pl.pallas_call(
        functools.partial(attn_own_kernel, heads, min(rows, 256), docs),
        out_shape=(jax.ShapeDtypeStruct((width, rows), F32), stat, stat),
        in_specs=[SM, VM, VM],
        out_specs=(VM, VM, VM),
        scratch_shapes=attn_scratch(rows, heads),
        compiler_params=pltpu.CompilerParams(vmem_limit_bytes=16 * 2**20),
        cost_estimate=cost_of(6),
        name="attn_own",
    )(info, q, kv)


def attn_scratch(rows, heads):
    return [
        pltpu.VMEM((heads, rows, HEAD_DIM), BF),
        pltpu.VMEM((KV_HEADS, rows, HEAD_DIM), BF),
        pltpu.VMEM((KV_HEADS * HEAD_DIM, rows), BF),
        pltpu.VMEM((rows, rows), F32),
    ]


def attention_grad(q, kv, grad_out, lse, delta, info, docs, before=None):
    rows, width = q.shape
    heads = width // HEAD_DIM
    own = before is not None
    turned = jax.ShapeDtypeStruct((width, rows), F32)
    if own:
        outs = [jax.ShapeDtypeStruct((rows, width), F32), jax.ShapeDtypeStruct(kv.shape, F32)]
    else:
        outs = [turned, jax.ShapeDtypeStruct(kv.shape, BF)]
    by_head = pltpu.VMEM((heads, rows, HEAD_DIM), BF)
    by_key = pltpu.VMEM((KV_HEADS, rows, HEAD_DIM), BF)
    sums = pltpu.VMEM((KV_HEADS, rows, HEAD_DIM), F32)
    return pl.pallas_call(
        functools.partial(attn_grad_kernel, heads, min(rows, 256), docs, own),
        out_shape=outs,
        in_specs=[SM] + [VM] * (6 if own else 5),
        out_specs=[VM] * 2,
        scratch_shapes=([pltpu.VMEM((width, rows), F32)] if own else []) + [
            by_head, by_head, by_key, by_key, pltpu.VMEM((KV_HEADS * HEAD_DIM, rows), BF),
            pltpu.VMEM((rows, rows), F32), sums, sums,
        ],
        compiler_params=pltpu.CompilerParams(vmem_limit_bytes=20 * 2**20),
        cost_estimate=cost_of(2.5),
        name="attn_grad_own" if own else "attn_grad_others",
    )(info, q, kv, grad_out, lse, delta, *([before] if own else []))


def attention_others(q, kv, acc, top, total, info, docs):
    rows, width = q.shape
    heads = width // HEAD_DIM
    return pl.pallas_call(
        functools.partial(attn_others_kernel, heads, min(rows, 256), docs),
        out_shape=(
            jax.ShapeDtypeStruct((rows, width), BF),
            jax.ShapeDtypeStruct((heads, 1, rows), F32),
        ),
        in_specs=[SM] + [VM] * 5,
        out_specs=(VM, VM),
        scratch_shapes=attn_scratch(rows, heads) + [pltpu.VMEM((width, rows), F32)],
        compiler_params=pltpu.CompilerParams(vmem_limit_bytes=16 * 2**20),
        cost_estimate=cost_of(10),
        name="attn_others",
    )(info, q, kv, acc, top, total)


def attention_back(q, kv, grad_out, lse, info, docs, short, causal, g0, g1):
    rows, width = q.shape
    total = sum(part.shape[0] for part in kv)
    heads = width // HEAD_DIM
    block = min(rows, 256)
    keys = g1 - g0
    mine = heads // KV_HEADS * keys
    outs = [jax.ShapeDtypeStruct((rows, mine * HEAD_DIM), F32)]
    if causal:
        outs.append(jax.ShapeDtypeStruct((rows, 2 * keys * HEAD_DIM), F32))
        outs.append(jax.ShapeDtypeStruct((total - rows, 2 * keys * HEAD_DIM), BF))
    else:
        outs.append(jax.ShapeDtypeStruct((total, 2 * keys * HEAD_DIM), F32))
    return pl.pallas_call(
        functools.partial(attn_bwd_kernel, heads, block, short, causal, docs, g0, g1, len(kv)),
        out_shape=outs,
        in_specs=[SM] + [VM] * (3 + len(kv)),
        out_specs=[VM] * len(outs),
        scratch_shapes=[
            pltpu.VMEM((mine, rows, HEAD_DIM), BF),
            pltpu.VMEM((keys, total, HEAD_DIM), BF),
            pltpu.VMEM((keys, total, HEAD_DIM), BF),
            pltpu.VMEM((keys, HEAD_DIM, total), BF),
            pltpu.VMEM((mine, rows, HEAD_DIM), BF),
            pltpu.VMEM((total, rows), F32),
            pltpu.VMEM((mine * HEAD_DIM, rows), F32),
            pltpu.VMEM((keys, total, HEAD_DIM), F32),
            pltpu.VMEM((keys, total, HEAD_DIM), F32),
        ],
        compiler_params=pltpu.CompilerParams(vmem_limit_bytes=20 * 2**20),
        cost_estimate=cost_of(20),
        name="attn_bwd",
    )(info, q, grad_out, lse, *kv)


TAIL = 2
MAIN = 16
PIECES = MAIN // TAIL


class Blocks:
    def __init__(self, dp_count, ctx_count):
        self.count = dp_count * ctx_count
        self.x = 1
        self.core = ctx_count
        self.y = 2 * ctx_count
        self.z = 4 * ctx_count
        self.zs = dp_count // 4
        self.masks = []
        for p in range(self.count):
            z, x = p % self.zs, p // self.zs % 2
            y, core = p // (2 * self.zs) % 2, p // (4 * self.zs)
            self.masks.append(x * self.x + y * self.y + core * self.core + z * self.z)

    def swap(self, values, mask):
        perm = [(i, i ^ mask) for i in range(self.count)]
        return lax.ppermute(values, AXES, perm)

    def along_z(self, mine):
        return jnp.stack([mine] + [self.swap(mine, d * self.z) for d in range(1, self.zs)])

    def add(self, keep, got):
        return (keep.astype(F32) + got.astype(F32)).astype(BF)

    def sum_z(self, held):
        got = [self.swap(held[d], d * self.z).astype(F32) for d in range(1, self.zs)]
        return functools.reduce(jnp.add, got, held[0].astype(F32))


class Sizes:
    def __init__(self, width, ff, dp, ctx, vec, kv_width):
        count = dp * ctx
        self.zs, self.ctx = dp // 4, ctx
        self.width, self.ff, self.count, self.vec = width, ff, count, vec
        self.rows = width // count
        self.f_rows = ff // count
        up = lambda n: (n + 127) // 128 * 128
        self.wide = up(width)
        self.qkv = width + 2 * kv_width
        self.a_width = up(self.qkv)
        self.tall = (self.rows + 1 + 7) // 8 * 8
        self.downs = self.f_rows // MAIN
        self.piece = 2 * ff // PIECES
        self.gate = 0
        self.tail = ff
        self.tail_o = self.tail + self.piece
        self.out = self.tail_o + 128
        self.down0 = self.out + self.wide
        self.first = self.down0 + (self.downs - 1) * self.wide
        self.second = ff + self.wide
        self.flat = self.a_width + 2 * self.wide

    def down_at(self, c):
        return (0, self.down0 + c * self.wide) if c < self.downs - 1 else (1, self.ff)

    def fits(self):
        return (
            self.rows == MAIN + TAIL
            and self.f_rows % MAIN == 0
            and self.piece % 128 == 0
            and self.ff % 256 == 0
            and self.wide <= 128 * PIECES
            and self.vec <= 128
        )


def wire_kernel(
    size, g_ref, u_ref, o_ref, d_ref, xt_ref, cott_ref, out1, out2, x_any, cot_any,
    tail, tail_o, x_ref, cot_ref, sems,
):
    ff, width = size.ff, size.width
    x_ref[...] = jnp.transpose(xt_ref[...].astype(F32)).astype(BF)
    cot_ref[...] = jnp.transpose(cott_ref[...].astype(F32)).astype(BF)
    copies = fetch((x_ref, cot_ref), (x_any, cot_any), sems)
    out1[:, : ff] = g_ref[:MAIN]
    out2[:, : ff] = u_ref[:MAIN]
    out1[:, size.out : size.out + size.wide] = jnp.zeros((MAIN, size.wide), BF)
    out1[:, size.out : size.out + width] = o_ref[:MAIN]
    tail_o[...] = jnp.zeros_like(tail_o)
    odd = [ref[MAIN:].astype(F32) for ref in (g_ref, u_ref, o_ref)]
    for c in range(PIECES):
        src = odd[c * size.piece // ff]
        at = c * size.piece % ff
        tail[c * TAIL : (c + 1) * TAIL] = src[:, at : at + size.piece]
        used = min(128, width - c * 128)
        if used > 0:
            tail_o[c * TAIL : (c + 1) * TAIL, :used] = odd[2][:, c * 128 : c * 128 + used]
    out1[:, size.tail : size.tail + size.piece] = tail[...].astype(BF)
    out1[:, size.tail_o : size.tail_o + 128] = tail_o[...].astype(BF)
    for c in range(size.downs):
        which, at = size.down_at(c)
        out = (out1, out2)[which]
        out[:, at : at + size.wide] = jnp.zeros((MAIN, size.wide), BF)
        out[:, at : at + width] = d_ref[c * MAIN : (c + 1) * MAIN]
    for copy in copies:
        copy.wait()


def over(values, by):
    scale = 2**16 // by + 1
    whole = (values * scale) >> 16
    return whole, values - whole * by


def mask_of(size, p):
    z, rest = p % size.zs, p // size.zs
    x, y, core = rest % 2, rest // 2 % 2, rest // 4
    return x + core * size.ctx + y * (2 * size.ctx) + z * (4 * size.ctx)


def lanes(count):
    return lax.broadcasted_iota(jnp.int32, (1, count), 1)


def place_matrix(size, me, tall):
    if tall:
        p, inside = over(lanes(size.count * size.tall), size.tall)
        feature = jnp.where(inside < size.rows, size.rows * (me ^ mask_of(size, p)) + inside, -1)
    else:
        s = lanes(size.count * (MAIN + TAIL))
        tail = s - size.count * MAIN
        p = jnp.where(tail < 0, s // MAIN, tail // TAIL)
        inside = jnp.where(tail < 0, s % MAIN, MAIN + tail % TAIL)
        feature = size.rows * (me ^ mask_of(size, p)) + inside
    at = lax.broadcasted_iota(jnp.int32, (size.width, feature.shape[1]), 0)
    return jnp.where(at == feature, 1.0, 0.0).astype(BF)


def vector_places(size, me):
    at = lanes(size.flat)
    ends = (size.a_width, size.a_width + size.wide)
    part = jnp.where(at < ends[0], 0, jnp.where(at < ends[1], 1, 2))
    inside = at - jnp.where(part == 0, 0, jnp.where(part == 1, ends[0], ends[1]))
    start = jnp.where(part == 0, 0, jnp.where(part == 1, size.qkv, size.qkv + size.width))
    used = inside < jnp.where(part == 0, size.qkv, size.width)
    owner, lane = over(start + inside, size.vec)
    rows = lax.broadcasted_iota(jnp.int32, (128, size.flat), 0)
    spread = jnp.where((rows == lane) & used, 1.0, 0.0).astype(BF)
    p = lax.broadcasted_iota(jnp.int32, (size.count, 1), 0)
    return spread, (owner == (me ^ mask_of(size, p))) & used


def split_two(values):
    high = values.astype(BF)
    return high, (values - high.astype(F32)).astype(BF)


def swap_halves(u):
    rolled_back = pltpu.roll(u, 128 - HEAD_DIM // 2, 1)
    rolled = pltpu.roll(u, HEAD_DIM // 2, 1)
    lane = lax.broadcasted_iota(jnp.int32, u.shape, 1)
    return jnp.where(lane % HEAD_DIM < HEAD_DIM // 2, rolled_back, rolled)


def fetch(sources, targets, sems):
    copies = [
        pltpu.make_async_copy(src, dst, sems.at[i])
        for i, (src, dst) in enumerate(zip(sources, targets))
    ]
    for copy in copies:
        copy.start()
    return copies


def pre_kernel(
    size, me_ref, x_ref, wm_ref, wo_ref, cos_ref, sin_ref,
    q_ref, kv_ref, n1t_ref, flat_ref, w, qkv,
):
    me = me_ref[0]
    half = wm_ref.shape[0]
    w[:half] = wm_ref[...]
    w[half:] = wo_ref[...]
    place = place_matrix(size, me, True)
    spread, mine = vector_places(size, me)
    shape = (size.count, 2 * half)
    row = lax.broadcasted_iota(jnp.int32, shape, 0) * size.tall + size.rows
    row = jnp.where(lax.broadcasted_iota(jnp.int32, shape, 1) == row, 1.0, 0.0).astype(BF)
    packed = times(row, w[:, :128]).astype(BF)
    flat = jnp.sum(jnp.where(mine, times(packed, spread), 0.0), axis=0, keepdims=True)
    flat_ref[...] = flat
    gain = flat[:, size.a_width : size.a_width + size.width]
    x = x_ref[...].astype(F32)
    inv = lax.rsqrt(jnp.mean(x * x, axis=-1, keepdims=True) + EPS)
    n1 = (x * inv * gain).astype(BF)
    n1a = times(n1, place)
    n1t_ref[...] = jnp.transpose(n1a).astype(BF)
    qkv[...] = times(n1a.astype(BF), w[...]) + flat[:, : size.a_width]
    kv_width = kv_ref.shape[1] // 2
    for t in range((size.width + kv_width) // 128):
        u = qkv[:, t * 128 : (t + 1) * 128]
        qkv[:, t * 128 : (t + 1) * 128] = u * cos_ref[...] + swap_halves(u) * sin_ref[...]
    q_ref[...] = qkv[:, : size.width].astype(BF)
    kv_ref[...] = qkv[:, size.width : size.qkv].astype(BF)


def tail_place(size, c):
    shape = (size.count * TAIL, size.count * MAIN)
    q = lax.broadcasted_iota(jnp.int32, shape, 0)
    at = lax.broadcasted_iota(jnp.int32, shape, 1)
    want = (q // TAIL) * MAIN + c * TAIL + q % TAIL
    return jnp.where(at == want, 1.0, 0.0).astype(BF)


def tail_place_back(size, c):
    shape = (size.count * MAIN, size.count * TAIL)
    at = lax.broadcasted_iota(jnp.int32, shape, 0)
    q = lax.broadcasted_iota(jnp.int32, shape, 1)
    want = (q // TAIL) * MAIN + c * TAIL + q % TAIL
    return jnp.where(at == want, 1.0, 0.0).astype(BF)


def mlp_kernel(
    size, me_ref, attn_ref, x_ref, cot_ref, flat_ref,
    b1_00, b1_01, b1_10, b1_11, b2_00, b2_01, b2_10, b2_11,
    out_ref, keep1, give1, keep2, give2, gmid_ref, gattn_ref, ggain_ref, delta_ref,
    wg, wu, wo, wd, mid, n2s, n2t, place, acc, gacc, dwd, tails, tail_o, packed,
):
    me = me_ref[0]
    width, ff = size.width, size.ff
    part = b1_00.shape[0]
    half, main = 2 * part, 4 * part
    rows_z = part // 2
    place[...] = place_matrix(size, me, False)
    first = (b1_00, b1_01, b1_10, b1_11)
    second = (b2_00, b2_01, b2_10, b2_11)
    room = size.piece + 128
    for i, b1 in enumerate(first):
        rows = slice(i * part, (i + 1) * part)
        wg[rows] = b1[:, :ff]
        wo[rows] = b1[:, size.out : size.out + size.wide]
        packed[rows] = b1[:, size.tail : size.tail + room]
    for i, b2 in enumerate(second):
        for y in range(2):
            at = (i // 2) * half + y * part + (i % 2) * rows_z
            wu[at : at + rows_z] = b2[y * rows_z : (y + 1) * rows_z, :ff]
    for c in range(PIECES):
        sel = tail_place(size, c)
        target = wg if c * size.piece < ff else wu
        at = c * size.piece % ff
        got = times(sel, packed[:, : size.piece])
        target[main:, at : at + size.piece] = got.astype(BF)
        if c * 128 < size.wide:
            got = times(sel, packed[:, size.piece : room])
            wo[main:, c * 128 : (c + 1) * 128] = got.astype(BF)
    zs = rows_z // MAIN
    for p in range(size.count):
        z, x, y, core = p % zs, p // zs % 2, p // (2 * zs) % 2, p // (4 * zs)
        owner = me ^ mask_of(size, p)
        for c in range(size.downs):
            which, at = size.down_at(c)
            src, row = (second[2 * core + x], y * zs + z) if which else (
                first[2 * core + y], x * zs + z
            )
            to = pl.multiple_of(owner * size.f_rows + c * MAIN, MAIN)
            wd[pl.ds(to, MAIN), :] = src[row * MAIN : (row + 1) * MAIN, at : at + size.wide]
    attn_s = times(attn_ref[...], place[...])
    m = x_ref[...].astype(F32) + times(attn_s.astype(BF), wo[:, :width])
    mid[...] = m
    inv = lax.rsqrt(jnp.mean(m * m, axis=-1, keepdims=True) + EPS)
    lo = size.a_width + size.wide
    gain = flat_ref[:, lo : lo + width]
    n2 = (m * inv * gain).astype(BF)
    spread = times(n2, place[...])
    n2s[...] = spread.astype(BF)
    n2t[...] = jnp.transpose(spread).astype(BF)
    acc[...] = jnp.zeros_like(acc)
    gacc[...] = jnp.zeros_like(gacc)
    step = 512 if ff % 512 == 0 else 256

    @pl.loop(0, ff // step)
    def _(b):
        at = pl.multiple_of(b * step, step)
        cols = pl.ds(at, step)
        gate = times(n2s[...], wg[:, cols])
        up = times(n2s[...], wu[:, cols])
        sig = 1.0 / (1.0 + jnp.exp(-gate))
        act = gate * sig
        h = act * up
        gh = times_back(cot_ref[...], wd[cols, :width])
        gg = (gh * up * (sig * (1.0 + gate * (1.0 - sig)))).astype(BF)
        gu = (gh * act).astype(BF)
        acc[...] += times(h.astype(BF), wd[cols, :width])
        dwd[cols, :width] = times(jnp.transpose(h).astype(BF), cot_ref[...]).astype(BF)
        gacc[...] += times_back(gg, wg[:, cols]) + times_back(gu, wu[:, cols])
        for k, (grad, keep, give) in enumerate(((gg, keep1, give1), (gu, keep2, give2))):
            dw = times(n2t[...], grad).astype(BF)
            keep[:, cols] = dw[:half]
            give[:, cols] = dw[half:main]
            tails[:, pl.ds(pl.multiple_of(k * ff + at, 128), step)] = dw[main:]

    m = mid[...]
    inv = lax.rsqrt(jnp.mean(m * m, axis=-1, keepdims=True) + EPS)
    out_ref[...] = jnp.transpose(m + acc[...]).astype(BF)
    high, low = split_two(gacc[...])
    gn2 = times_back(high, place[...]) + times_back(low, place[...])
    scaled = gn2 * gain
    dot = jnp.mean(scaled * m, axis=-1, keepdims=True)
    ggain_ref[...] = jnp.sum(gn2 * m * inv, axis=0, keepdims=True)
    gmid = cot_ref[...].astype(F32) + inv * scaled - m * (inv * inv * inv * dot)
    gmid_ref[...] = gmid
    branch = gmid.astype(BF)
    gattn = times_back(branch, wo[:, :width]).astype(BF)
    gattn = times_back(gattn, place[...]).astype(BF)
    gattn_ref[...] = gattn
    both = jnp.transpose(gattn.astype(F32) * attn_ref[...].astype(F32))
    for h in range(width // HEAD_DIM):
        at = slice(h * HEAD_DIM, (h + 1) * HEAD_DIM)
        delta_ref[h] = jnp.sum(both[at], axis=0, keepdims=True)
    dwo = times(jnp.transpose(attn_s).astype(BF), branch).astype(BF)
    tail_o[...] = jnp.zeros_like(tail_o)
    tail_o[:, :width] = dwo[main:]
    terms = ((keep1, keep2), (give1, give2))
    for i, (term, _) in enumerate(terms):
        term[:, size.out : size.out + width] = dwo[i * half : (i + 1) * half]
    wire = jnp.zeros((main, size.piece), F32)
    wire_o = jnp.zeros((main, 128), F32)
    for c in range(PIECES):
        sel = tail_place_back(size, c)
        wire += times(sel, tails[:, c * size.piece : (c + 1) * size.piece])
        if c * 128 < size.wide:
            wire_o += times(sel, tail_o[:, c * 128 : (c + 1) * 128])
    for i, (term, _) in enumerate(terms):
        rows = slice(i * half, (i + 1) * half)
        term[:, size.tail : size.tail + size.piece] = wire[rows].astype(BF)
        term[:, size.tail_o : size.tail_o + 128] = wire_o[rows].astype(BF)
    for p in range(size.count):
        to = terms[p // (size.count // 2)]
        rows = slice(p * MAIN % half, p * MAIN % half + MAIN)
        owner = me ^ mask_of(size, p)
        for c in range(size.downs):
            which, at = size.down_at(c)
            src = pl.multiple_of(owner * size.f_rows + c * MAIN, MAIN)
            to[which][rows, at : at + size.wide] = dwd[pl.ds(src, MAIN), :]


def post_kernel(
    size, me_ref, dq_ref, dkv_ref, got_ref, cos_ref, sin_ref, n1t_ref,
    wm_ref, wo_ref, x_ref, gmid_ref, flat_ref, ggain_ref,
    gx_ref, keep_ref, give_ref, turn_buf, grad, vec_row,
):
    me = me_ref[0]
    width = size.width
    half = wm_ref.shape[0]
    place = place_matrix(size, me, True)
    kv_width = KV_HEADS * HEAD_DIM
    turned = width + kv_width
    dkv = dkv_ref[...] + got_ref[...].astype(F32)
    turn_buf[:, :width] = dq_ref[...]
    turn_buf[:, width:] = dkv[:, :kv_width]
    grad[...] = jnp.zeros_like(grad)
    grad[:, turned : turned + kv_width] = dkv[:, kv_width:].astype(BF)
    for t in range(turned // 128):
        u = turn_buf[:, t * 128 : (t + 1) * 128]
        back = u * cos_ref[...] - swap_halves(u) * sin_ref[...]
        grad[:, t * 128 : (t + 1) * 128] = back.astype(BF)
    g = grad[...]
    gn1 = jnp.zeros((g.shape[0], width), F32)
    for part, w_ref in enumerate((wm_ref, wo_ref)):
        for values in split_two(times_back(g, w_ref[...])):
            gn1 += times_back(values, place[:, part * half : (part + 1) * half])
    x = x_ref[...].astype(F32)
    inv = lax.rsqrt(jnp.mean(x * x, axis=-1, keepdims=True) + EPS)
    gain = flat_ref[:, size.a_width : size.a_width + width]
    scaled = gn1 * gain
    dot = jnp.mean(scaled * x, axis=-1, keepdims=True)
    gx_ref[...] = jnp.transpose(gmid_ref[...] + inv * scaled - x * (inv * inv * inv * dot))
    vec_row[...] = jnp.zeros_like(vec_row)
    vec_row[:, : size.a_width] = jnp.sum(g.astype(F32), axis=0, keepdims=True)
    vec_row[:, size.a_width : size.a_width + width] = jnp.sum(gn1 * x * inv, axis=0, keepdims=True)
    lo = size.a_width + size.wide
    vec_row[:, lo : lo + width] = ggain_ref[...]
    spread, mine = vector_places(size, me)
    packed = times_back(jnp.where(mine, vec_row[...], 0.0).astype(BF), spread)
    shape = (half, size.count)
    for part, term in ((0, keep_ref), (1, give_ref)):
        rows = slice(part * half, (part + 1) * half)
        dw = times(n1t_ref[rows], g)
        term[...] = dw.astype(BF)
        want = lax.broadcasted_iota(jnp.int32, shape, 1) * size.tall + size.rows - part * half
        here = lax.broadcasted_iota(jnp.int32, shape, 0) == want
        extra = times(jnp.where(here, 1.0, 0.0).astype(BF), packed.astype(BF))
        term[:, :128] = (dw[:, :128] + extra).astype(BF)


def call(kernel, name, out_shape, scratch, micros, args, vmem, any_in=(), any_out=(), scalar=True):
    shapes = [jax.ShapeDtypeStruct(s, t) for s, t in out_shape]
    here = pl.BlockSpec(memory_space=pl.ANY)
    specs = [here if i in any_in else VM for i in range(len(args))]
    if scalar:
        specs[0] = SM
    return pl.pallas_call(
        kernel,
        out_shape=shapes,
        in_specs=specs,
        out_specs=[here if i in any_out else VM for i in range(len(shapes))],
        scratch_shapes=[
            pltpu.SemaphoreType.DMA(s) if t is None else pltpu.VMEM(s, t) for s, t in scratch
        ],
        compiler_params=pltpu.CompilerParams(vmem_limit_bytes=vmem * 2**20),
        cost_estimate=cost_of(micros),
        name=name,
    )(*args)


def pad_to(values, rows, columns):
    return jnp.pad(values, ((0, rows - values.shape[0]), (0, columns - values.shape[1])))


def tail_pack(rows, piece):
    rows = pad_to(rows, TAIL, PIECES * piece)
    return rows.reshape(TAIL, PIECES, piece).transpose(1, 0, 2).reshape(MAIN, piece)


def tail_unpack(wire, used):
    piece = wire.shape[1]
    rows = wire.reshape(PIECES, TAIL, piece).transpose(1, 0, 2).reshape(TAIL, PIECES * piece)
    return rows[:, :used]


def tie(*values):
    return lax.optimization_barrier(values)


def local_blocks(size, blocks, pos, args):
    (
        tokens, q_weight, k_weight, v_weight, o_weight, gate_weight, up_weight, down_weight,
        vectors, cotangent,
    ) = args
    tok_rows, width = tokens.shape
    ff, rows = size.ff, size.rows
    kv_width = KV_HEADS * HEAD_DIM
    ctx_index = lax.axis_index("ctx")
    me = (lax.axis_index("dp") * lax.axis_size("ctx") + ctx_index).astype(jnp.int32).reshape(1)
    half = size.count // 2
    info, docs, cos, sin = pos

    joined_w = jnp.concatenate(
        [w.reshape(rows, -1) for w in (q_weight, k_weight, v_weight)], axis=1
    )
    vec_row = pad_to(vectors.reshape(1, -1), size.tall - rows, size.a_width)
    wire_a = jnp.concatenate([pad_to(joined_w, rows, size.a_width), vec_row], axis=0)
    za = blocks.along_z(wire_a)
    xa = jnp.stack([za, blocks.swap(za, blocks.x)])
    _, flat_w = tie(za, (gate_weight, up_weight, o_weight, down_weight))
    w_rows = [w.reshape(rows, -1) for w in flat_w[:3]]
    wire_1, wire_2, tokens, cotangent = call(
        functools.partial(wire_kernel, size),
        "wire",
        [
            ((MAIN, size.first), BF), ((MAIN, size.second), BF), ((tok_rows, width), BF),
            ((tok_rows, width), BF),
        ],
        [
            ((MAIN, size.piece), F32), ((MAIN, 128), F32), ((tok_rows, width), BF),
            ((tok_rows, width), BF), ((2,), None),
        ],
        1,
        w_rows + [flat_w[3].reshape(size.f_rows, width), tokens.T, cotangent.T],
        10,
        any_out=(2, 3),
        scalar=False,
    )
    xa, wire_1, wire_2 = tie(xa, wire_1, wire_2)
    ya = blocks.swap(xa, blocks.y)
    z1 = blocks.along_z(wire_1)
    z1, wire_2, ya = tie(z1, wire_2, ya)
    z2 = blocks.along_z(wire_2)
    x1 = jnp.stack([z1, blocks.swap(z1, blocks.x)])
    a_mine = jnp.stack([xa, ya]).reshape(half * size.tall, size.a_width)
    a_other = blocks.swap(a_mine, blocks.core)

    a_rows = size.count * size.tall
    q_rot, kv_mine, n1t, flat = call(
        functools.partial(pre_kernel, size),
        "norm_qkv",
        [
            ((tok_rows, width), BF), ((tok_rows, 2 * kv_width), BF), ((a_rows, tok_rows), BF),
            ((1, size.flat), F32),
        ],
        [((a_rows, size.a_width), BF), ((tok_rows, size.a_width), F32)],
        3,
        (me, tokens, a_mine, a_other, cos, sin),
        16,
    )
    kv_got = blocks.swap(kv_mine, blocks.x)
    own = attention_own(q_rot, kv_mine, info, docs)
    z2, x1 = tie(z2, x1, kv_mine)[:2]
    y2 = jnp.stack([z2, blocks.swap(z2, blocks.y)])
    b1_parts = [b.reshape(half // 2 * MAIN, -1) for b in (x1, blocks.swap(x1, blocks.y))]
    b2_parts = [b.reshape(half // 2 * MAIN, -1) for b in (y2, blocks.swap(y2, blocks.x))]
    attn, lse = attention_others(q_rot, kv_got, *own, info, docs)

    b1_parts[1:] = [b1_parts[1], blocks.swap(b1_parts[0], blocks.core)]
    b2_parts[1:] = [b2_parts[1], blocks.swap(b2_parts[0], blocks.core)]
    attn, b2_parts[1] = tie(attn, b2_parts[1])
    attn, b1_parts[1] = tie(attn, b1_parts[1])
    b2_parts.append(blocks.swap(b2_parts[1], blocks.core))
    b1_parts.append(blocks.swap(b1_parts[1], blocks.core))
    main = size.count * MAIN
    slots = main + size.count * TAIL
    layer_out, keep1, give1, keep2, give2, grad_mid, grad_attn, grad_gain, delta = call(
        functools.partial(mlp_kernel, size),
        "feed_forward",
        [
            ((width, tok_rows), BF),
            ((main // 2, size.first), BF), ((main // 2, size.first), BF),
            ((main // 2, size.second), BF), ((main // 2, size.second), BF),
            ((tok_rows, width), F32), ((tok_rows, width), BF), ((1, width), F32),
            ((width // HEAD_DIM, 1, tok_rows), F32),
        ],
        [
            ((slots, ff), BF), ((slots, ff), BF), ((slots, size.wide), BF), ((ff, size.wide), BF),
            ((tok_rows, width), F32), ((tok_rows, slots), BF), ((slots, tok_rows), BF),
            ((width, slots), BF), ((tok_rows, width), F32), ((tok_rows, slots), F32),
            ((ff, size.wide), BF), ((size.count * TAIL, 2 * ff), BF),
            ((size.count * TAIL, size.wide), BF), ((main, size.piece + 128), BF),
        ],
        21,
        (
            me, attn, tokens, cotangent, flat, *b1_parts, *b2_parts,
        ),
        28,
    )

    got1 = blocks.swap(give1, blocks.core)
    got2 = blocks.swap(give2, blocks.core)
    shape = (2, 2, blocks.zs, MAIN, -1)
    h1 = blocks.add(keep1, got1).reshape(shape)
    h2 = blocks.add(keep2, got2).reshape(shape)
    dq_others, give_kv = attention_grad(q_rot, kv_got, grad_attn, lse, delta, info, docs)
    got_kv = blocks.swap(give_kv, blocks.x)
    dq_others, h1, h2 = tie(dq_others, h1, h2)
    h1 = blocks.add(h1[0], blocks.swap(h1[1], blocks.y))
    h2 = blocks.add(h2[:, 0], blocks.swap(h2[:, 1], blocks.x))
    grad_q_rot, own_kv = attention_grad(
        q_rot, kv_mine, grad_attn, lse, delta, info, docs, dq_others
    )
    gx, keep_a, give_a = call(
        functools.partial(post_kernel, size),
        "norm_qkv_back",
        [
            ((width, tok_rows), F32), ((a_rows // 2, size.a_width), BF),
            ((a_rows // 2, size.a_width), BF),
        ],
        [
            ((tok_rows, width + kv_width), F32), ((tok_rows, size.a_width), BF),
            ((1, size.flat), F32),
        ],
        1.5,
        (
            me, grad_q_rot, own_kv, got_kv, cos, sin, n1t, a_mine,
            a_other, tokens, grad_mid, flat, grad_gain,
        ),
        24,
    )
    give_a, h1, h2 = tie(give_a, h1, h2)
    held = blocks.add(keep_a, blocks.swap(give_a, blocks.core))
    held = held.reshape(2, 2, blocks.zs, size.tall, size.a_width)
    h1 = blocks.add(h1[0], blocks.swap(h1[1], blocks.x))
    h2 = blocks.add(h2[0], blocks.swap(h2[1], blocks.y))
    held = blocks.add(held[0], blocks.swap(held[1], blocks.y))
    held, share2 = tie(held, blocks.sum_z(h2))
    held = blocks.add(held[0], blocks.swap(held[1], blocks.x))
    held, share1 = tie(held, blocks.sum_z(h1))
    share_a = blocks.sum_z(held)

    tails = tail_unpack(share1[:, size.tail : size.tail + size.piece], 2 * ff)
    tail_o = tail_unpack(share1[:, size.tail_o : size.tail_o + 128], width)
    share_out = jnp.concatenate([share1[:, size.out : size.out + width], tail_o], axis=0)
    share_gate = jnp.concatenate([share1[:, :ff], tails[:, :ff]], axis=0)
    share_up = jnp.concatenate([share2[:, :ff], tails[:, ff:]], axis=0)
    downs = [size.down_at(c) for c in range(size.downs)]
    share_down = jnp.concatenate(
        [(share1, share2)[which][:, at : at + width] for which, at in downs], axis=0
    )
    ends = (width, width + kv_width, size.qkv)
    return (
        layer_out.T, gx.T, share_a[:rows, : ends[0]].reshape(-1),
        share_a[:rows, ends[0] : ends[1]].reshape(-1),
        share_a[:rows, ends[1] : ends[2]].reshape(-1),
        share_out.reshape(-1), share_gate.reshape(-1), share_up.reshape(-1),
        share_down.reshape(-1), share_a[rows, : size.vec],
    )


def local(
    tokens, q_weight, k_weight, v_weight, o_weight, gate_weight, up_weight, down_weight,
    vectors, doc_lengths, cotangent,
):
    tok_rows, width = tokens.shape
    ctx_count = lax.axis_size("ctx")
    dp_count = lax.axis_size("dp")
    count = dp_count * ctx_count
    seq_tokens = tok_rows * ctx_count
    ctx_index = lax.axis_index("ctx")
    heads = width // HEAD_DIM
    kv_width = KV_HEADS * HEAD_DIM
    ff = gate_weight.shape[0] * count // width

    position_all = doc_layout(doc_lengths[0], seq_tokens)
    offset = ctx_index * tok_rows
    position_mine = lax.dynamic_slice_in_dim(position_all, offset, tok_rows)
    docs = doc_lengths.shape[1]
    others = (ctx_count - 1 - ctx_index) * tok_rows
    heads_of = jnp.stack([ctx_index, others, offset]).astype(jnp.int32)
    info = jnp.concatenate([heads_of, jnp.cumsum(doc_lengths[0])[:-1].astype(jnp.int32)])
    half = HEAD_DIM // 2
    freq = THETA ** (-jnp.arange(half, dtype=F32) * 2.0 / HEAD_DIM)
    position_f = position_mine.astype(F32)[:, None]

    whole_rows = width % count == 0 and ff % count == 0
    if whole_rows and ctx_count == 2 and dp_count % 4 == 0 and count & (count - 1) == 0:
        size = Sizes(width, ff, dp_count, ctx_count, vectors.shape[0], kv_width)
        if size.fits() and (width + kv_width) % 128 == 0:
            angle = position_f * jnp.tile(freq, 128 // half)[None, :]
            sign = np.where(np.arange(128) % HEAD_DIM < half, -1.0, 1.0).astype(np.float32)
            pos = (info, docs, jnp.cos(angle), jnp.sin(angle) * sign)
            args = (
                tokens, q_weight, k_weight, v_weight, o_weight, gate_weight, up_weight,
                down_weight, vectors, cotangent,
            )
            return local_blocks(size, Blocks(dp_count, ctx_count), pos, args)

    angle = position_f * freq[None, :]
    cosine = jnp.cos(angle)[:, None, :]
    sine = jnp.sin(angle)[:, None, :]
    inputs = tokens.astype(F32)
    inv_first = lax.rsqrt(jnp.mean(inputs * inputs, axis=-1, keepdims=True) + EPS)

    def whole(part):
        return lax.all_gather(part, AXES, axis=0, tiled=True)

    w_qkv = jnp.concatenate(
        [whole(w).reshape(width, -1) for w in (q_weight, k_weight, v_weight)], axis=1
    )
    w_out = whole(o_weight).reshape(width, width)
    w_gate = whole(gate_weight).reshape(width, ff)
    w_up = whole(up_weight).reshape(width, ff)
    w_down = whole(down_weight).reshape(ff, width)
    flat = whole(vectors).astype(F32)
    ends = [width, width + kv_width, width + 2 * kv_width, 2 * width + 2 * kv_width]
    gain_attn = flat[ends[2] : ends[3]]
    gain_mlp = flat[ends[3] : ends[3] + width]

    n_first = (inputs * inv_first * gain_attn).astype(BF)
    qkv = times(n_first, w_qkv) + flat[: ends[2]]
    q_rot = turn(qkv[:, :width].reshape(tok_rows, heads, HEAD_DIM), cosine, sine)
    q_rot = q_rot.astype(BF).reshape(tok_rows, width)
    k_rot = turn(qkv[:, width : ends[1]].reshape(tok_rows, KV_HEADS, HEAD_DIM), cosine, sine)
    k_rot = k_rot.astype(BF).reshape(tok_rows, kv_width)
    kv_mine = jnp.concatenate([k_rot, qkv[:, ends[1] :].astype(BF)], axis=1)
    kv = (lax.all_gather(kv_mine, "ctx", axis=0, tiled=True),)
    info = info.at[0].set(1)
    attn, lse = attention(q_rot, kv, info, docs, seq_tokens, False)
    mid = inputs + times(attn, w_out)
    inv_second = lax.rsqrt(jnp.mean(mid * mid, axis=-1, keepdims=True) + EPS)
    n_second = (mid * inv_second * gain_mlp).astype(BF)
    gate = times(n_second, w_gate)
    up_val = times(n_second, w_up)
    sig = jax.nn.sigmoid(gate)
    act = gate * sig
    hidden = (act * up_val).astype(BF)
    layer_out = (mid + times(hidden, w_down)).astype(BF)

    grad_wdown = inner_rows(hidden, cotangent)
    grad_hidden = times_back(cotangent, w_down)
    grad_gate = (grad_hidden * up_val * (sig * (1.0 + gate * (1.0 - sig)))).astype(BF)
    grad_up = (grad_hidden * act).astype(BF)
    grad_wgate = inner_rows(n_second, grad_gate)
    grad_wup = inner_rows(n_second, grad_up)
    grad_n2 = times_back(grad_gate, w_gate) + times_back(grad_up, w_up)
    grad_mid_norm, grad_gain_mlp = norm_back(mid, inv_second, gain_mlp, grad_n2)
    grad_mid = cotangent.astype(F32) + grad_mid_norm
    grad_branch = grad_mid.astype(BF)
    grad_wout = inner_rows(attn, grad_branch)
    grad_attn = times_back(grad_branch, w_out).astype(BF)
    grad_q_rot, grad_kv = attention_back(
        q_rot, kv, grad_attn, lse, info, docs, seq_tokens, False, 0, KV_HEADS
    )
    grad_kv_mine = lax.psum_scatter(
        grad_kv.astype(BF), "ctx", scatter_dimension=0, tiled=True
    ).astype(F32)
    grad_q = turn(grad_q_rot.reshape(tok_rows, heads, HEAD_DIM), cosine, -sine)
    grad_k = turn(
        grad_kv_mine[:, :kv_width].reshape(tok_rows, KV_HEADS, HEAD_DIM), cosine, -sine
    )
    grad_qkv = jnp.concatenate(
        [
            grad_q.reshape(tok_rows, width).astype(BF),
            grad_k.reshape(tok_rows, kv_width).astype(BF),
            grad_kv_mine[:, kv_width:].astype(BF),
        ],
        axis=1,
    )
    grad_wqkv = inner_rows(n_first, grad_qkv)
    grad_bias = jnp.sum(grad_qkv.astype(F32), axis=0)
    grad_n1 = times_back(grad_qkv, w_qkv)
    grad_x_norm, grad_gain_attn = norm_back(inputs, inv_first, gain_attn, grad_n1)
    input_grad = grad_mid + grad_x_norm
    used = 3 * width + 2 * kv_width
    padding = jnp.zeros((vectors.shape[0] * count - used,), F32)
    vector_term = jnp.concatenate([grad_bias, grad_gain_attn, grad_gain_mlp, padding])

    def shares(term):
        return lax.psum_scatter(term.reshape(-1), AXES, scatter_dimension=0, tiled=True)

    return (
        layer_out, input_grad, shares(grad_wqkv[:, :width]),
        shares(grad_wqkv[:, width : ends[1]]), shares(grad_wqkv[:, ends[1] :]),
        shares(grad_wout), shares(grad_wgate), shares(grad_wup), shares(grad_wdown),
        shares(vector_term),
    )


def solution(mesh):
    split = P(AXES)
    rows = P(AXES, None)
    in_specs = (rows,) + (split,) * 8 + (P("dp", None), rows)
    out_specs = (rows, rows) + (split,) * 8
    return jax.shard_map(local, mesh=mesh, in_specs=in_specs, out_specs=out_specs, check_vma=False)
```

```python
import functools

import jax
import jax.numpy as jnp
import numpy as np
from jax import lax
from jax.experimental import pallas as pl
from jax.experimental.pallas import tpu as pltpu
from jax.sharding import PartitionSpec as P

KV_HEADS = 3
HEAD_DIM = 64

EPS = 1e-06
THETA = 100000.0
NEG_FILL = -1e30
AXES = ("dp", "ctx")
BF = jnp.bfloat16
F32 = jnp.float32


def times(left, right):
    return jnp.dot(left, right, preferred_element_type=F32)


def inner_rows(left, right):
    return lax.dot_general(left, right, (((0,), (0,)), ((), ())), preferred_element_type=F32)


def times_back(left, right):
    return lax.dot_general(left, right, (((1,), (1,)), ((), ())), preferred_element_type=F32)


def norm_back(values, inv, gain, grad):
    scaled = grad * gain
    dot = jnp.mean(scaled * values, axis=-1, keepdims=True)
    grad_values = inv * scaled - values * (inv * inv * inv * dot)
    grad_gain = jnp.sum(grad * values * inv, axis=0)
    return grad_values, grad_gain


def turn(values, cosine, sine):
    half = values.shape[-1] // 2
    first = values[..., :half]
    second = values[..., half:]
    return jnp.concatenate(
        [first * cosine - second * sine, second * cosine + first * sine], axis=-1
    )


def doc_layout(lengths, count):
    ends = jnp.cumsum(lengths)
    place = jnp.arange(count, dtype=jnp.int32)
    segment = jnp.sum((place[:, None] >= ends[None, :-1]).astype(jnp.int32), axis=1)
    starts = ends - lengths
    picked = segment[:, None] == jnp.arange(lengths.shape[0], dtype=jnp.int32)[None, :]
    first = jnp.sum(jnp.where(picked, starts[None, :], 0), axis=1)
    return place - first


def fill_bias(bias, info, docs, short, own=None):
    total, rows = bias.shape
    row_q = lax.broadcasted_iota(jnp.int32, (1, rows), 1) + info[2]
    first = jnp.zeros_like(row_q)
    for j in range(docs - 1):
        first = jnp.where(row_q >= info[3 + j], info[3 + j], first)
    parts = ((0, total, 0),)
    if own is not None:
        parts = ((0, total, info[2] if own else info[1]),)
    elif short < total:
        parts = ((0, total - short, info[1]), (total - short, total, info[2]))
    for start, stop, base in parts:
        row_k = lax.broadcasted_iota(jnp.int32, (stop - start, rows), 0)
        allowed = (row_k >= first - base) & (row_k <= row_q - base)
        bias[start:stop] = jnp.where(allowed, 0.0, NEG_FILL)


def key_range(full, total, short, rows, block, at, causal):
    start = 0 if full else total - short
    stop = total - rows + (at + 1) * block if causal else total
    return start, stop


def key_parts(kv_refs):
    at = 0
    for kv_ref in kv_refs:
        yield slice(at, at + kv_ref.shape[0]), kv_ref
        at += kv_ref.shape[0]


def attn_fwd_kernel(
    heads, block, short, causal, docs, info, q_ref, *refs,
):
    kv_refs, (out_ref, lse_ref, qs, ks, vts, bias, out_t) = refs[:-7], refs[-7:]
    rows = q_ref.shape[0]
    total = bias.shape[0]
    kv_width = KV_HEADS * HEAD_DIM
    group = heads // KV_HEADS
    fill_bias(bias, info, docs, short)
    for h in range(heads):
        qs[h] = q_ref[:, h * HEAD_DIM : (h + 1) * HEAD_DIM] * BF(HEAD_DIM**-0.5)
    for at, kv_ref in key_parts(kv_refs):
        for g in range(KV_HEADS):
            ks[g, at] = kv_ref[:, g * HEAD_DIM : (g + 1) * HEAD_DIM]
        vts[:, at] = jnp.transpose(kv_ref[:, kv_width:].astype(F32)).astype(BF)

    def run(full):
        @pl.loop(0, KV_HEADS)
        def _(g):
            v_rows = pl.ds(pl.multiple_of(g * HEAD_DIM, HEAD_DIM), HEAD_DIM)
            for j in range(group):
                h = g * group + j
                out_rows = pl.ds(pl.multiple_of(h * HEAD_DIM, HEAD_DIM), HEAD_DIM)
                for at in range(rows // block):
                    start, stop = key_range(full, total, short, rows, block, at, causal)
                    cols = slice(at * block, (at + 1) * block)
                    s = times_back(ks[g, start:stop], qs[h, cols])
                    s = s + bias[start:stop, cols]
                    top = jnp.max(s, axis=0, keepdims=True)
                    p = jnp.exp(s - top)
                    total_p = jnp.sum(p, axis=0, keepdims=True)
                    o = times(vts[v_rows, start:stop], p.astype(BF))
                    out_t[out_rows, cols] = o / total_p
                    lse_ref[h, :, cols] = top + jnp.log(total_p)

    pl.when(info[0] != 0)(lambda: run(True))
    pl.when(info[0] == 0)(lambda: run(False))
    out_ref[...] = jnp.transpose(out_t[...]).astype(BF)


def attn_own_kernel(
    heads, block, docs, info, q_ref, kv_ref, acc, top_ref, sum_ref, qs, ks, vts, bias
):
    rows = q_ref.shape[0]
    kv_width = KV_HEADS * HEAD_DIM
    group = heads // KV_HEADS
    fill_bias(bias, info, docs, rows, own=True)
    for h in range(heads):
        qs[h] = q_ref[:, h * HEAD_DIM : (h + 1) * HEAD_DIM] * BF(HEAD_DIM**-0.5)
    for g in range(KV_HEADS):
        ks[g] = kv_ref[:, g * HEAD_DIM : (g + 1) * HEAD_DIM]
    vts[...] = jnp.transpose(kv_ref[:, kv_width:].astype(F32)).astype(BF)

    @pl.loop(0, KV_HEADS)
    def _(g):
        v_rows = pl.ds(pl.multiple_of(g * HEAD_DIM, HEAD_DIM), HEAD_DIM)
        for j in range(group):
            h = g * group + j
            out_rows = pl.ds(pl.multiple_of(h * HEAD_DIM, HEAD_DIM), HEAD_DIM)
            for at in range(rows // block):
                stop = (at + 1) * block
                cols = slice(at * block, stop)
                s = times_back(ks[g, :stop], qs[h, cols]) + bias[:stop, cols]
                top = jnp.max(s, axis=0, keepdims=True)
                p = jnp.exp(s - top)
                top_ref[h, :, cols] = top
                sum_ref[h, :, cols] = jnp.sum(p, axis=0, keepdims=True)
                acc[out_rows, cols] = times(vts[v_rows, :stop], p.astype(BF))


def attn_others_kernel(
    heads, block, docs, info, q_ref, kv_ref, acc, top_ref, sum_ref, out_ref, lse_ref,
    qs, ks, vts, bias, out_t,
):
    rows = q_ref.shape[0]
    kv_width = KV_HEADS * HEAD_DIM
    group = heads // KV_HEADS

    @pl.when(info[0] == 0)
    def _():
        for h in range(heads):
            at = slice(h * HEAD_DIM, (h + 1) * HEAD_DIM)
            out_t[at] = acc[at] / sum_ref[h]
            lse_ref[h] = top_ref[h] + jnp.log(sum_ref[h])

    @pl.when(info[0] != 0)
    def _():
        fill_bias(bias, info, docs, rows, own=False)
        for h in range(heads):
            qs[h] = q_ref[:, h * HEAD_DIM : (h + 1) * HEAD_DIM] * BF(HEAD_DIM**-0.5)
        for g in range(KV_HEADS):
            ks[g] = kv_ref[:, g * HEAD_DIM : (g + 1) * HEAD_DIM]
        vts[...] = jnp.transpose(kv_ref[:, kv_width:].astype(F32)).astype(BF)

        @pl.loop(0, KV_HEADS)
        def _(g):
            v_rows = pl.ds(pl.multiple_of(g * HEAD_DIM, HEAD_DIM), HEAD_DIM)
            for j in range(group):
                h = g * group + j
                out_rows = pl.ds(pl.multiple_of(h * HEAD_DIM, HEAD_DIM), HEAD_DIM)
                for at in range(rows // block):
                    cols = slice(at * block, (at + 1) * block)
                    s = times_back(ks[g], qs[h, cols]) + bias[:, cols]
                    own = top_ref[h, :, cols]
                    top = jnp.maximum(own, jnp.max(s, axis=0, keepdims=True))
                    scale = jnp.exp(own - top)
                    p = jnp.exp(s - top)
                    total_p = sum_ref[h, :, cols] * scale + jnp.sum(p, axis=0, keepdims=True)
                    o = acc[out_rows, cols] * scale + times(vts[v_rows], p.astype(BF))
                    out_t[out_rows, cols] = o / total_p
                    lse_ref[h, :, cols] = top + jnp.log(total_p)

    out_ref[...] = jnp.transpose(out_t[...]).astype(BF)


def attn_grad_kernel(
    heads, block, docs, own, info, q_ref, kv_ref, do_ref, lse_ref, delta_ref, *refs
):
    refs, (qs, dos, ks, vs, kts, bias, dk, dv) = refs[:-8], refs[-8:]
    if own:
        before, dq_ref, dkv_ref, dq_t = refs
    else:
        dq_t, dkv_ref = refs
    rows = q_ref.shape[0]
    kv_width = KV_HEADS * HEAD_DIM
    group = heads // KV_HEADS
    dk[...] = jnp.zeros_like(dk)
    dv[...] = jnp.zeros_like(dv)

    def run():
        fill_bias(bias, info, docs, rows, own=own)
        for h in range(heads):
            at = slice(h * HEAD_DIM, (h + 1) * HEAD_DIM)
            qs[h] = q_ref[:, at] * BF(HEAD_DIM**-0.5)
            dos[h] = do_ref[:, at]
        for g in range(KV_HEADS):
            lo = g * HEAD_DIM
            ks[g] = kv_ref[:, lo : lo + HEAD_DIM]
            vs[g] = kv_ref[:, kv_width + lo : kv_width + lo + HEAD_DIM]
        kts[...] = jnp.transpose(kv_ref[:, :kv_width].astype(F32)).astype(BF)

        @pl.loop(0, KV_HEADS)
        def _(g):
            k_rows = pl.ds(pl.multiple_of(g * HEAD_DIM, HEAD_DIM), HEAD_DIM)
            for j in range(group):
                h = g * group + j
                out_rows = pl.ds(pl.multiple_of(h * HEAD_DIM, HEAD_DIM), HEAD_DIM)
                for at in range(rows // block):
                    stop = (at + 1) * block if own else rows
                    cols = slice(at * block, (at + 1) * block)
                    q = qs[h, cols]
                    do = dos[h, cols]
                    s = times_back(ks[g, :stop], q) + bias[:stop, cols]
                    p = jnp.exp(s - lse_ref[h, :, cols])
                    dp = times_back(vs[g, :stop], do)
                    ds = (p * (dp - delta_ref[h, :, cols])).astype(BF)
                    dk[g, :stop] += times(ds, q)
                    dv[g, :stop] += times(p.astype(BF), do)
                    dq = times(kts[k_rows, :stop], ds) * HEAD_DIM**-0.5
                    dq_t[out_rows, cols] = before[out_rows, cols] + dq if own else dq

    if own:
        run()
        dq_ref[...] = jnp.transpose(dq_t[...])
    else:
        pl.when(info[0] != 0)(run)

        @pl.when(info[0] == 0)
        def _():
            dq_t[...] = jnp.zeros_like(dq_t)

    for g in range(KV_HEADS):
        lo = g * HEAD_DIM
        dkv_ref[:, lo : lo + HEAD_DIM] = dk[g].astype(dkv_ref.dtype)
        dkv_ref[:, kv_width + lo : kv_width + lo + HEAD_DIM] = dv[g].astype(dkv_ref.dtype)


def attn_bwd_kernel(
    heads, block, short, causal, docs, g0, g1, parts, info, q_ref, do_ref, lse_ref, *refs,
):
    kv_refs, outs, scratch = refs[:parts], refs[parts:-9], refs[-9:]
    qs, ks, vs, kts, dos, bias, dq_t, dk, dv = scratch
    rows = q_ref.shape[0]
    total = bias.shape[0]
    kv_width = KV_HEADS * HEAD_DIM
    group = heads // KV_HEADS
    keys = g1 - g0
    fill_bias(bias, info, docs, short)
    for h in range(keys * group):
        lanes = slice((g0 * group + h) * HEAD_DIM, (g0 * group + h + 1) * HEAD_DIM)
        qs[h] = q_ref[:, lanes] * BF(HEAD_DIM**-0.5)
        dos[h] = do_ref[:, lanes]
    for g in range(keys):
        lo = (g0 + g) * HEAD_DIM
        for at, kv_ref in key_parts(kv_refs):
            ks[g, at] = kv_ref[:, lo : lo + HEAD_DIM]
            vs[g, at] = kv_ref[:, kv_width + lo : kv_width + lo + HEAD_DIM]
        kts[g] = jnp.transpose(ks[g].astype(F32)).astype(BF)
    dk[...] = jnp.zeros_like(dk)
    dv[...] = jnp.zeros_like(dv)

    def run(full):
        @pl.loop(0, keys * group)
        def _(h):
            g = h // group if keys > 1 else 0
            out_rows = pl.ds(pl.multiple_of(h * HEAD_DIM, HEAD_DIM), HEAD_DIM)
            for at in range(rows // block):
                start, stop = key_range(full, total, short, rows, block, at, causal)
                cols = slice(at * block, (at + 1) * block)
                q = qs[h, cols]
                do = dos[h, cols]
                s = times_back(ks[g, start:stop], q)
                p = jnp.exp(s + bias[start:stop, cols] - lse_ref[g0 * group + h, :, cols])
                dp = times_back(vs[g, start:stop], do)
                t = p * dp
                inner = jnp.sum(t, axis=0, keepdims=True)
                ds = (t - p * inner).astype(BF)
                dk[g, start:stop] += times(ds, q)
                dv[g, start:stop] += times(p.astype(BF), do)
                dq_t[out_rows, cols] = times(kts[g, :, start:stop], ds) * HEAD_DIM**-0.5

    pl.when(info[0] != 0)(lambda: run(True))
    pl.when(info[0] == 0)(lambda: run(False))
    outs[0][...] = jnp.transpose(dq_t[...])
    cut = total - outs[1].shape[0]
    for part, out in ((slice(cut, total), outs[1]),) + tuple((slice(0, cut), o) for o in outs[2:]):
        for g in range(keys):
            lo = g * HEAD_DIM
            out[:, lo : lo + HEAD_DIM] = dk[g, part].astype(out.dtype)
            lo += keys * HEAD_DIM
            out[:, lo : lo + HEAD_DIM] = dv[g, part].astype(out.dtype)


VM = pl.BlockSpec(memory_space=pltpu.VMEM)
SM = pl.BlockSpec(memory_space=pltpu.SMEM)


def cost_of(micros):
    return pl.CostEstimate(
        flops=int(micros * 1.1e9), bytes_accessed=2**20, transcendentals=0
    )


def attention(q, kv, info, docs, short, causal):
    rows, width = q.shape
    total = sum(part.shape[0] for part in kv)
    heads = width // HEAD_DIM
    block = min(rows, 256)
    return pl.pallas_call(
        functools.partial(attn_fwd_kernel, heads, block, short, causal, docs),
        out_shape=(
            jax.ShapeDtypeStruct((rows, width), BF),
            jax.ShapeDtypeStruct((heads, 1, rows), F32),
        ),
        in_specs=[SM] + [VM] * (1 + len(kv)),
        out_specs=(VM, VM),
        scratch_shapes=[
            pltpu.VMEM((heads, rows, HEAD_DIM), BF),
            pltpu.VMEM((KV_HEADS, total, HEAD_DIM), BF),
            pltpu.VMEM((KV_HEADS * HEAD_DIM, total), BF),
            pltpu.VMEM((total, rows), F32),
            pltpu.VMEM((width, rows), F32),
        ],
        compiler_params=pltpu.CompilerParams(vmem_limit_bytes=20 * 2**20),
        cost_estimate=cost_of(14),
        name="attn_fwd",
    )(info, q, *kv)


def attention_own(q, kv, info, docs):
    rows, width = q.shape
    heads = width // HEAD_DIM
    stat = jax.ShapeDtypeStruct((heads, 1, rows), F32)
    return pl.pallas_call(
        functools.partial(attn_own_kernel, heads, min(rows, 256), docs),
        out_shape=(jax.ShapeDtypeStruct((width, rows), F32), stat, stat),
        in_specs=[SM, VM, VM],
        out_specs=(VM, VM, VM),
        scratch_shapes=attn_scratch(rows, heads),
        compiler_params=pltpu.CompilerParams(vmem_limit_bytes=16 * 2**20),
        cost_estimate=cost_of(6),
        name="attn_own",
    )(info, q, kv)


def attn_scratch(rows, heads):
    return [
        pltpu.VMEM((heads, rows, HEAD_DIM), BF),
        pltpu.VMEM((KV_HEADS, rows, HEAD_DIM), BF),
        pltpu.VMEM((KV_HEADS * HEAD_DIM, rows), BF),
        pltpu.VMEM((rows, rows), F32),
    ]


def attention_grad(q, kv, grad_out, lse, delta, info, docs, before=None):
    rows, width = q.shape
    heads = width // HEAD_DIM
    own = before is not None
    turned = jax.ShapeDtypeStruct((width, rows), F32)
    if own:
        outs = [jax.ShapeDtypeStruct((rows, width), F32), jax.ShapeDtypeStruct(kv.shape, F32)]
    else:
        outs = [turned, jax.ShapeDtypeStruct(kv.shape, BF)]
    by_head = pltpu.VMEM((heads, rows, HEAD_DIM), BF)
    by_key = pltpu.VMEM((KV_HEADS, rows, HEAD_DIM), BF)
    sums = pltpu.VMEM((KV_HEADS, rows, HEAD_DIM), F32)
    return pl.pallas_call(
        functools.partial(attn_grad_kernel, heads, min(rows, 256), docs, own),
        out_shape=outs,
        in_specs=[SM] + [VM] * (6 if own else 5),
        out_specs=[VM] * 2,
        scratch_shapes=([pltpu.VMEM((width, rows), F32)] if own else []) + [
            by_head, by_head, by_key, by_key, pltpu.VMEM((KV_HEADS * HEAD_DIM, rows), BF),
            pltpu.VMEM((rows, rows), F32), sums, sums,
        ],
        compiler_params=pltpu.CompilerParams(vmem_limit_bytes=20 * 2**20),
        cost_estimate=cost_of(9 if own else 10),
        name="attn_grad_own" if own else "attn_grad_others",
    )(info, q, kv, grad_out, lse, delta, *([before] if own else []))


def attention_others(q, kv, acc, top, total, info, docs):
    rows, width = q.shape
    heads = width // HEAD_DIM
    return pl.pallas_call(
        functools.partial(attn_others_kernel, heads, min(rows, 256), docs),
        out_shape=(
            jax.ShapeDtypeStruct((rows, width), BF),
            jax.ShapeDtypeStruct((heads, 1, rows), F32),
        ),
        in_specs=[SM] + [VM] * 5,
        out_specs=(VM, VM),
        scratch_shapes=attn_scratch(rows, heads) + [pltpu.VMEM((width, rows), F32)],
        compiler_params=pltpu.CompilerParams(vmem_limit_bytes=16 * 2**20),
        cost_estimate=cost_of(10),
        name="attn_others",
    )(info, q, kv, acc, top, total)


def attention_back(q, kv, grad_out, lse, info, docs, short, causal, g0, g1):
    rows, width = q.shape
    total = sum(part.shape[0] for part in kv)
    heads = width // HEAD_DIM
    block = min(rows, 256)
    keys = g1 - g0
    mine = heads // KV_HEADS * keys
    outs = [jax.ShapeDtypeStruct((rows, mine * HEAD_DIM), F32)]
    if causal:
        outs.append(jax.ShapeDtypeStruct((rows, 2 * keys * HEAD_DIM), F32))
        outs.append(jax.ShapeDtypeStruct((total - rows, 2 * keys * HEAD_DIM), BF))
    else:
        outs.append(jax.ShapeDtypeStruct((total, 2 * keys * HEAD_DIM), F32))
    return pl.pallas_call(
        functools.partial(attn_bwd_kernel, heads, block, short, causal, docs, g0, g1, len(kv)),
        out_shape=outs,
        in_specs=[SM] + [VM] * (3 + len(kv)),
        out_specs=[VM] * len(outs),
        scratch_shapes=[
            pltpu.VMEM((mine, rows, HEAD_DIM), BF),
            pltpu.VMEM((keys, total, HEAD_DIM), BF),
            pltpu.VMEM((keys, total, HEAD_DIM), BF),
            pltpu.VMEM((keys, HEAD_DIM, total), BF),
            pltpu.VMEM((mine, rows, HEAD_DIM), BF),
            pltpu.VMEM((total, rows), F32),
            pltpu.VMEM((mine * HEAD_DIM, rows), F32),
            pltpu.VMEM((keys, total, HEAD_DIM), F32),
            pltpu.VMEM((keys, total, HEAD_DIM), F32),
        ],
        compiler_params=pltpu.CompilerParams(vmem_limit_bytes=20 * 2**20),
        cost_estimate=cost_of(20),
        name="attn_bwd",
    )(info, q, grad_out, lse, *kv)


TAIL = 2
MAIN = 16
PIECES = MAIN // TAIL


class Blocks:
    def __init__(self, dp_count, ctx_count):
        self.count = dp_count * ctx_count
        self.x = 1
        self.core = ctx_count
        self.y = 2 * ctx_count
        self.z = 4 * ctx_count
        self.zs = dp_count // 4
        self.masks = []
        for p in range(self.count):
            z, x = p % self.zs, p // self.zs % 2
            y, core = p // (2 * self.zs) % 2, p // (4 * self.zs)
            self.masks.append(x * self.x + y * self.y + core * self.core + z * self.z)

    def swap(self, values, mask):
        perm = [(i, i ^ mask) for i in range(self.count)]
        return lax.ppermute(values, AXES, perm)

    def along_z(self, mine):
        return jnp.stack([mine] + [self.swap(mine, d * self.z) for d in range(1, self.zs)])

    def add(self, keep, got):
        return (keep.astype(F32) + got.astype(F32)).astype(BF)

    def sum_z(self, held):
        got = [self.swap(held[d], d * self.z).astype(F32) for d in range(1, self.zs)]
        return functools.reduce(jnp.add, got, held[0].astype(F32))


class Sizes:
    def __init__(self, width, ff, dp, ctx, vec, kv_width):
        count = dp * ctx
        self.zs, self.ctx = dp // 4, ctx
        self.width, self.ff, self.count, self.vec = width, ff, count, vec
        self.rows = width // count
        self.f_rows = ff // count
        up = lambda n: (n + 127) // 128 * 128
        self.wide = up(width)
        self.qkv = width + 2 * kv_width
        self.a_width = up(self.qkv)
        self.tall = (self.rows + 1 + 7) // 8 * 8
        self.downs = self.f_rows // MAIN
        self.piece = 2 * ff // PIECES
        self.gate = 0
        self.tail = ff
        self.tail_o = self.tail + self.piece
        self.out = self.tail_o + 128
        self.down0 = self.out + self.wide
        self.first = self.down0 + self.wide
        self.second = ff + (self.downs - 1) * self.wide
        self.back_first = self.down0 + (self.downs - 1) * self.wide
        self.back_second = ff + self.wide
        self.flat = self.a_width + 2 * self.wide

    def down_at(self, c):
        return (0, self.down0) if c == 0 else (1, self.ff + (c - 1) * self.wide)

    def down_back_at(self, c):
        return (0, self.down0 + c * self.wide) if c < self.downs - 1 else (1, self.ff)

    def fits(self):
        return (
            self.rows == MAIN + TAIL
            and self.f_rows % MAIN == 0
            and self.piece % 128 == 0
            and self.ff % 256 == 0
            and self.wide <= 128 * PIECES
            and self.vec <= 128
        )


def wire_kernel(
    size, g_ref, u_ref, o_ref, d_ref, xt_ref, cott_ref, out1, out2, x_any, cot_any,
    tail, tail_o, x_ref, cot_ref, sems,
):
    ff, width = size.ff, size.width
    x_ref[...] = jnp.transpose(xt_ref[...].astype(F32)).astype(BF)
    cot_ref[...] = jnp.transpose(cott_ref[...].astype(F32)).astype(BF)
    copies = fetch((x_ref, cot_ref), (x_any, cot_any), sems)
    out1[:, : ff] = g_ref[:MAIN]
    out2[:, : ff] = u_ref[:MAIN]
    out1[:, size.out : size.out + size.wide] = jnp.zeros((MAIN, size.wide), BF)
    out1[:, size.out : size.out + width] = o_ref[:MAIN]
    tail_o[...] = jnp.zeros_like(tail_o)
    odd = [ref[MAIN:].astype(F32) for ref in (g_ref, u_ref, o_ref)]
    for c in range(PIECES):
        src = odd[c * size.piece // ff]
        at = c * size.piece % ff
        tail[c * TAIL : (c + 1) * TAIL] = src[:, at : at + size.piece]
        used = min(128, width - c * 128)
        if used > 0:
            tail_o[c * TAIL : (c + 1) * TAIL, :used] = odd[2][:, c * 128 : c * 128 + used]
    out1[:, size.tail : size.tail + size.piece] = tail[...].astype(BF)
    out1[:, size.tail_o : size.tail_o + 128] = tail_o[...].astype(BF)
    for c in range(size.downs):
        which, at = size.down_at(c)
        out = (out1, out2)[which]
        out[:, at : at + size.wide] = jnp.zeros((MAIN, size.wide), BF)
        out[:, at : at + width] = d_ref[c * MAIN : (c + 1) * MAIN]
    for copy in copies:
        copy.wait()


def over(values, by):
    scale = 2**16 // by + 1
    whole = (values * scale) >> 16
    return whole, values - whole * by


def mask_of(size, p):
    z, rest = p % size.zs, p // size.zs
    x, y, core = rest % 2, rest // 2 % 2, rest // 4
    return x + core * size.ctx + y * (2 * size.ctx) + z * (4 * size.ctx)


def lanes(count):
    return lax.broadcasted_iota(jnp.int32, (1, count), 1)


def place_matrix(size, me, tall):
    if tall:
        p, inside = over(lanes(size.count * size.tall), size.tall)
        feature = jnp.where(inside < size.rows, size.rows * (me ^ mask_of(size, p)) + inside, -1)
    else:
        s = lanes(size.count * (MAIN + TAIL))
        tail = s - size.count * MAIN
        p = jnp.where(tail < 0, s // MAIN, tail // TAIL)
        inside = jnp.where(tail < 0, s % MAIN, MAIN + tail % TAIL)
        feature = size.rows * (me ^ mask_of(size, p)) + inside
    at = lax.broadcasted_iota(jnp.int32, (size.width, feature.shape[1]), 0)
    return jnp.where(at == feature, 1.0, 0.0).astype(BF)


def vector_places(size, me):
    at = lanes(size.flat)
    ends = (size.a_width, size.a_width + size.wide)
    part = jnp.where(at < ends[0], 0, jnp.where(at < ends[1], 1, 2))
    inside = at - jnp.where(part == 0, 0, jnp.where(part == 1, ends[0], ends[1]))
    start = jnp.where(part == 0, 0, jnp.where(part == 1, size.qkv, size.qkv + size.width))
    used = inside < jnp.where(part == 0, size.qkv, size.width)
    owner, lane = over(start + inside, size.vec)
    rows = lax.broadcasted_iota(jnp.int32, (128, size.flat), 0)
    spread = jnp.where((rows == lane) & used, 1.0, 0.0).astype(BF)
    p = lax.broadcasted_iota(jnp.int32, (size.count, 1), 0)
    return spread, (owner == (me ^ mask_of(size, p))) & used


def swap_halves(u):
    rolled_back = pltpu.roll(u, 128 - HEAD_DIM // 2, 1)
    rolled = pltpu.roll(u, HEAD_DIM // 2, 1)
    lane = lax.broadcasted_iota(jnp.int32, u.shape, 1)
    return jnp.where(lane % HEAD_DIM < HEAD_DIM // 2, rolled_back, rolled)


def fetch(sources, targets, sems):
    copies = [
        pltpu.make_async_copy(src, dst, sems.at[i])
        for i, (src, dst) in enumerate(zip(sources, targets))
    ]
    for copy in copies:
        copy.start()
    return copies


def pre_kernel(
    size, me_ref, x_ref, wm_ref, wo_ref, cos_ref, sin_ref,
    q_ref, kv_ref, n1t_ref, flat_ref, w, qkv,
):
    me = me_ref[0]
    half = wm_ref.shape[0]
    w[:half] = wm_ref[...]
    w[half:] = wo_ref[...]
    place = place_matrix(size, me, True)
    spread, mine = vector_places(size, me)
    shape = (size.count, 2 * half)
    row = lax.broadcasted_iota(jnp.int32, shape, 0) * size.tall + size.rows
    row = jnp.where(lax.broadcasted_iota(jnp.int32, shape, 1) == row, 1.0, 0.0).astype(BF)
    packed = times(row, w[:, :128]).astype(BF)
    flat = jnp.sum(jnp.where(mine, times(packed, spread), 0.0), axis=0, keepdims=True)
    flat_ref[...] = flat
    gain = flat[:, size.a_width : size.a_width + size.width]
    x = x_ref[...].astype(F32)
    inv = lax.rsqrt(jnp.mean(x * x, axis=-1, keepdims=True) + EPS)
    n1 = (x * inv * gain).astype(BF)
    n1a = times(n1, place)
    n1t_ref[...] = jnp.transpose(n1a).astype(BF)
    qkv[...] = times(n1a.astype(BF), w[...]) + flat[:, : size.a_width]
    kv_width = kv_ref.shape[1] // 2
    for t in range((size.width + kv_width) // 128):
        u = qkv[:, t * 128 : (t + 1) * 128]
        qkv[:, t * 128 : (t + 1) * 128] = u * cos_ref[...] + swap_halves(u) * sin_ref[...]
    q_ref[...] = qkv[:, : size.width].astype(BF)
    kv_ref[...] = qkv[:, size.width : size.qkv].astype(BF)


def tail_place(size, back):
    odd, count = size.count * TAIL, size.count * MAIN
    row = lax.broadcasted_iota(jnp.int32, (count, count), 1 if back else 0)
    at = lax.broadcasted_iota(jnp.int32, (count, count), 0 if back else 1)
    c, q = row // odd, row % odd
    want = (q // TAIL) * MAIN + c * TAIL + q % TAIL
    return jnp.where(at == want, 1.0, 0.0).astype(BF)


def mlp_kernel(
    size, me_ref, attn_ref, x_ref, cot_ref, flat_ref,
    b1_00, b1_01, b1_10, b1_11, b2_00, b2_01, b2_10, b2_11,
    out_ref, keep1, give1, keep2, give2, gmid_ref, gattn_ref, ggain_ref, delta_ref,
    wg, wu, wo, wd, mid, n2s, n2t, place, acc, gacc, dwd, tails, tail_o, packed,
):
    me = me_ref[0]
    width, ff = size.width, size.ff
    part = b1_00.shape[0]
    half, main = 2 * part, 4 * part
    rows_z = part // 2
    place[...] = place_matrix(size, me, False)
    first = (b1_00, b1_01, b1_10, b1_11)
    second = (b2_00, b2_01, b2_10, b2_11)
    room = size.piece + 128
    for i, b1 in enumerate(first):
        rows = slice(i * part, (i + 1) * part)
        wg[rows] = b1[:, :ff]
        wo[rows] = b1[:, size.out : size.out + size.wide]
        packed[rows] = b1[:, size.tail : size.tail + room]
    for i, b2 in enumerate(second):
        for y in range(2):
            at = (i // 2) * half + y * part + (i % 2) * rows_z
            wu[at : at + rows_z] = b2[y * rows_z : (y + 1) * rows_z, :ff]
    odd = size.count * TAIL
    got = times(tail_place(size, False), packed[...]).astype(BF)
    for c in range(PIECES):
        rows = slice(c * odd, (c + 1) * odd)
        target = wg if c * size.piece < ff else wu
        at = c * size.piece % ff
        target[main:, at : at + size.piece] = got[rows, : size.piece]
        if c * 128 < size.wide:
            wo[main:, c * 128 : (c + 1) * 128] = got[rows, size.piece :]
    zs = rows_z // MAIN
    for p in range(size.count):
        z, x, y, core = p % zs, p // zs % 2, p // (2 * zs) % 2, p // (4 * zs)
        owner = me ^ mask_of(size, p)
        for c in range(size.downs):
            which, at = size.down_at(c)
            src, row = (second[2 * core + x], y * zs + z) if which else (
                first[2 * core + y], x * zs + z
            )
            to = pl.multiple_of(owner * size.f_rows + c * MAIN, MAIN)
            wd[pl.ds(to, MAIN), :] = src[row * MAIN : (row + 1) * MAIN, at : at + size.wide]
    attn_s = times(attn_ref[...], place[...])
    m = x_ref[...].astype(F32) + times(attn_s.astype(BF), wo[:, :width])
    mid[...] = m
    inv = lax.rsqrt(jnp.mean(m * m, axis=-1, keepdims=True) + EPS)
    lo = size.a_width + size.wide
    gain = flat_ref[:, lo : lo + width]
    n2 = (m * inv * gain).astype(BF)
    spread = times(n2, place[...])
    n2s[...] = spread.astype(BF)
    n2t[...] = jnp.transpose(spread).astype(BF)
    acc[...] = jnp.zeros_like(acc)
    gacc[...] = jnp.zeros_like(gacc)
    step = 512 if ff % 512 == 0 else 256

    @pl.loop(0, ff // step)
    def _(b):
        at = pl.multiple_of(b * step, step)
        cols = pl.ds(at, step)
        gate = times(n2s[...], wg[:, cols])
        up = times(n2s[...], wu[:, cols])
        sig = 1.0 / (1.0 + jnp.exp(-gate))
        act = gate * sig
        h = act * up
        gh = times_back(cot_ref[...], wd[cols, :width])
        gg = (gh * up * (sig * (1.0 + gate * (1.0 - sig)))).astype(BF)
        gu = (gh * act).astype(BF)
        acc[...] += times(h.astype(BF), wd[cols, :width])
        dwd[cols, :width] = times(jnp.transpose(h).astype(BF), cot_ref[...]).astype(BF)
        gacc[...] += times_back(gg, wg[:, cols]) + times_back(gu, wu[:, cols])
        for k, (grad, keep, give) in enumerate(((gg, keep1, give1), (gu, keep2, give2))):
            dw = times(n2t[...], grad).astype(BF)
            keep[:, cols] = dw[:half]
            give[:, cols] = dw[half:main]
            tails[:, pl.ds(pl.multiple_of(k * ff + at, 128), step)] = dw[main:]

    m = mid[...]
    inv = lax.rsqrt(jnp.mean(m * m, axis=-1, keepdims=True) + EPS)
    out_ref[...] = jnp.transpose(m + acc[...]).astype(BF)
    gn2 = times_back(gacc[...].astype(BF), place[...])
    scaled = gn2 * gain
    dot = jnp.mean(scaled * m, axis=-1, keepdims=True)
    ggain_ref[...] = jnp.sum(gn2 * m * inv, axis=0, keepdims=True)
    gmid = cot_ref[...].astype(F32) + inv * scaled - m * (inv * inv * inv * dot)
    gmid_ref[...] = gmid
    branch = gmid.astype(BF)
    gattn = times_back(branch, wo[:, :width]).astype(BF)
    gattn = times_back(gattn, place[...]).astype(BF)
    gattn_ref[...] = gattn
    both = jnp.transpose(gattn.astype(F32) * attn_ref[...].astype(F32))
    for h in range(width // HEAD_DIM):
        at = slice(h * HEAD_DIM, (h + 1) * HEAD_DIM)
        delta_ref[h] = jnp.sum(both[at], axis=0, keepdims=True)
    dwo = times(jnp.transpose(attn_s).astype(BF), branch).astype(BF)
    tail_o[...] = jnp.zeros_like(tail_o)
    tail_o[:, :width] = dwo[main:]
    terms = ((keep1, keep2), (give1, give2))
    for i, (term, _) in enumerate(terms):
        term[:, size.out : size.out + width] = dwo[i * half : (i + 1) * half]
    packed[...] = jnp.zeros_like(packed)
    for c in range(PIECES):
        rows = slice(c * odd, (c + 1) * odd)
        packed[rows, : size.piece] = tails[:, c * size.piece : (c + 1) * size.piece]
        if c * 128 < size.wide:
            packed[rows, size.piece :] = tail_o[:, c * 128 : (c + 1) * 128]
    wire = times(tail_place(size, True), packed[...]).astype(BF)
    for i, (term, _) in enumerate(terms):
        rows = slice(i * half, (i + 1) * half)
        term[:, size.tail : size.tail + room] = wire[rows]
    for p in range(size.count):
        to = terms[p // (size.count // 2)]
        rows = slice(p * MAIN % half, p * MAIN % half + MAIN)
        owner = me ^ mask_of(size, p)
        for c in range(size.downs):
            which, at = size.down_back_at(c)
            src = pl.multiple_of(owner * size.f_rows + c * MAIN, MAIN)
            to[which][rows, at : at + size.wide] = dwd[pl.ds(src, MAIN), :]


def post_kernel(
    size, me_ref, dq_ref, dkv_ref, got_ref, cos_ref, sin_ref, n1t_ref,
    wm_ref, wo_ref, x_ref, gmid_ref, flat_ref, ggain_ref,
    gx_ref, keep_ref, give_ref, turn_buf, grad, vec_row,
):
    me = me_ref[0]
    width = size.width
    half = wm_ref.shape[0]
    place = place_matrix(size, me, True)
    kv_width = KV_HEADS * HEAD_DIM
    turned = width + kv_width
    dkv = dkv_ref[...] + got_ref[...].astype(F32)
    turn_buf[:, :width] = dq_ref[...]
    turn_buf[:, width:] = dkv[:, :kv_width]
    grad[...] = jnp.zeros_like(grad)
    grad[:, turned : turned + kv_width] = dkv[:, kv_width:].astype(BF)
    for t in range(turned // 128):
        u = turn_buf[:, t * 128 : (t + 1) * 128]
        back = u * cos_ref[...] - swap_halves(u) * sin_ref[...]
        grad[:, t * 128 : (t + 1) * 128] = back.astype(BF)
    g = grad[...]
    gn1 = jnp.zeros((g.shape[0], width), F32)
    for part, w_ref in enumerate((wm_ref, wo_ref)):
        values = times_back(g, w_ref[...]).astype(BF)
        gn1 += times_back(values, place[:, part * half : (part + 1) * half])
    x = x_ref[...].astype(F32)
    inv = lax.rsqrt(jnp.mean(x * x, axis=-1, keepdims=True) + EPS)
    gain = flat_ref[:, size.a_width : size.a_width + width]
    scaled = gn1 * gain
    dot = jnp.mean(scaled * x, axis=-1, keepdims=True)
    gx_ref[...] = jnp.transpose(gmid_ref[...] + inv * scaled - x * (inv * inv * inv * dot))
    vec_row[...] = jnp.zeros_like(vec_row)
    vec_row[:, : size.a_width] = jnp.sum(g.astype(F32), axis=0, keepdims=True)
    vec_row[:, size.a_width : size.a_width + width] = jnp.sum(gn1 * x * inv, axis=0, keepdims=True)
    lo = size.a_width + size.wide
    vec_row[:, lo : lo + width] = ggain_ref[...]
    spread, mine = vector_places(size, me)
    packed = times_back(jnp.where(mine, vec_row[...], 0.0).astype(BF), spread)
    shape = (half, size.count)
    for part, term in ((0, keep_ref), (1, give_ref)):
        rows = slice(part * half, (part + 1) * half)
        dw = times(n1t_ref[rows], g)
        term[...] = dw.astype(BF)
        want = lax.broadcasted_iota(jnp.int32, shape, 1) * size.tall + size.rows - part * half
        here = lax.broadcasted_iota(jnp.int32, shape, 0) == want
        extra = times(jnp.where(here, 1.0, 0.0).astype(BF), packed.astype(BF))
        term[:, :128] = (dw[:, :128] + extra).astype(BF)


def call(kernel, name, out_shape, scratch, micros, args, vmem, any_in=(), any_out=(), scalar=True):
    shapes = [jax.ShapeDtypeStruct(s, t) for s, t in out_shape]
    here = pl.BlockSpec(memory_space=pl.ANY)
    specs = [here if i in any_in else VM for i in range(len(args))]
    if scalar:
        specs[0] = SM
    return pl.pallas_call(
        kernel,
        out_shape=shapes,
        in_specs=specs,
        out_specs=[here if i in any_out else VM for i in range(len(shapes))],
        scratch_shapes=[
            pltpu.SemaphoreType.DMA(s) if t is None else pltpu.VMEM(s, t) for s, t in scratch
        ],
        compiler_params=pltpu.CompilerParams(vmem_limit_bytes=vmem * 2**20),
        cost_estimate=cost_of(micros),
        name=name,
    )(*args)


def pad_to(values, rows, columns):
    return jnp.pad(values, ((0, rows - values.shape[0]), (0, columns - values.shape[1])))


def tail_pack(rows, piece):
    rows = pad_to(rows, TAIL, PIECES * piece)
    return rows.reshape(TAIL, PIECES, piece).transpose(1, 0, 2).reshape(MAIN, piece)


def tail_unpack(wire, used):
    piece = wire.shape[1]
    rows = wire.reshape(PIECES, TAIL, piece).transpose(1, 0, 2).reshape(TAIL, PIECES * piece)
    return rows[:, :used]


def tie(*values):
    return lax.optimization_barrier(values)


def local_blocks(size, blocks, pos, args):
    (
        tokens, q_weight, k_weight, v_weight, o_weight, gate_weight, up_weight, down_weight,
        vectors, cotangent,
    ) = args
    tok_rows, width = tokens.shape
    ff, rows = size.ff, size.rows
    kv_width = KV_HEADS * HEAD_DIM
    ctx_index = lax.axis_index("ctx")
    me = (lax.axis_index("dp") * lax.axis_size("ctx") + ctx_index).astype(jnp.int32).reshape(1)
    half = size.count // 2
    info, docs, cos, sin = pos

    joined_w = jnp.concatenate(
        [w.reshape(rows, -1) for w in (q_weight, k_weight, v_weight)], axis=1
    )
    vec_row = pad_to(vectors.reshape(1, -1), size.tall - rows, size.a_width)
    wire_a = jnp.concatenate([pad_to(joined_w, rows, size.a_width), vec_row], axis=0)
    za = blocks.along_z(wire_a)
    xa = jnp.stack([za, blocks.swap(za, blocks.x)])
    _, flat_w = tie(za, (gate_weight, up_weight, o_weight, down_weight))
    w_rows = [w.reshape(rows, -1) for w in flat_w[:3]]
    wire_1, wire_2, tokens, cotangent = call(
        functools.partial(wire_kernel, size),
        "wire",
        [
            ((MAIN, size.first), BF), ((MAIN, size.second), BF), ((tok_rows, width), BF),
            ((tok_rows, width), BF),
        ],
        [
            ((MAIN, size.piece), F32), ((MAIN, 128), F32), ((tok_rows, width), BF),
            ((tok_rows, width), BF), ((2,), None),
        ],
        1,
        w_rows + [flat_w[3].reshape(size.f_rows, width), tokens.T, cotangent.T],
        10,
        any_out=(2, 3),
        scalar=False,
    )
    xa, wire_1, wire_2 = tie(xa, wire_1, wire_2)
    ya = blocks.swap(xa, blocks.y)
    z1 = blocks.along_z(wire_1)
    z1, wire_2, ya = tie(z1, wire_2, ya)
    z2 = blocks.along_z(wire_2)
    x1 = jnp.stack([z1, blocks.swap(z1, blocks.x)])
    a_mine = jnp.stack([xa, ya]).reshape(half * size.tall, size.a_width)
    a_other = blocks.swap(a_mine, blocks.core)

    a_rows = size.count * size.tall
    q_rot, kv_mine, n1t, flat = call(
        functools.partial(pre_kernel, size),
        "norm_qkv",
        [
            ((tok_rows, width), BF), ((tok_rows, 2 * kv_width), BF), ((a_rows, tok_rows), BF),
            ((1, size.flat), F32),
        ],
        [((a_rows, size.a_width), BF), ((tok_rows, size.a_width), F32)],
        3,
        (me, tokens, a_mine, a_other, cos, sin),
        16,
    )
    kv_got = blocks.swap(kv_mine, blocks.x)
    own = attention_own(q_rot, kv_mine, info, docs)
    z2, x1 = tie(z2, x1, kv_mine)[:2]
    y2 = jnp.stack([z2, blocks.swap(z2, blocks.y)])
    b1_parts = [b.reshape(half // 2 * MAIN, -1) for b in (x1, blocks.swap(x1, blocks.y))]
    b2_parts = [b.reshape(half // 2 * MAIN, -1) for b in (y2, blocks.swap(y2, blocks.x))]
    attn, lse = attention_others(q_rot, kv_got, *own, info, docs)

    b1_parts[1:] = [b1_parts[1], blocks.swap(b1_parts[0], blocks.core)]
    b2_parts[1:] = [b2_parts[1], blocks.swap(b2_parts[0], blocks.core)]
    attn, b2_parts[1] = tie(attn, b2_parts[1])
    attn, b1_parts[1] = tie(attn, b1_parts[1])
    b2_parts.append(blocks.swap(b2_parts[1], blocks.core))
    b1_parts.append(blocks.swap(b1_parts[1], blocks.core))
    main = size.count * MAIN
    slots = main + size.count * TAIL
    layer_out, keep1, give1, keep2, give2, grad_mid, grad_attn, grad_gain, delta = call(
        functools.partial(mlp_kernel, size),
        "feed_forward",
        [
            ((width, tok_rows), BF),
            ((main // 2, size.back_first), BF), ((main // 2, size.back_first), BF),
            ((main // 2, size.back_second), BF), ((main // 2, size.back_second), BF),
            ((tok_rows, width), F32), ((tok_rows, width), BF), ((1, width), F32),
            ((width // HEAD_DIM, 1, tok_rows), F32),
        ],
        [
            ((slots, ff), BF), ((slots, ff), BF), ((slots, size.wide), BF), ((ff, size.wide), BF),
            ((tok_rows, width), F32), ((tok_rows, slots), BF), ((slots, tok_rows), BF),
            ((width, slots), BF), ((tok_rows, width), F32), ((tok_rows, slots), F32),
            ((ff, size.wide), BF), ((size.count * TAIL, 2 * ff), BF),
            ((size.count * TAIL, size.wide), BF), ((main, size.piece + 128), BF),
        ],
        21,
        (
            me, attn, tokens, cotangent, flat, *b1_parts, *b2_parts,
        ),
        28,
    )

    got1 = blocks.swap(give1, blocks.core)
    got2 = blocks.swap(give2, blocks.core)
    shape = (2, 2, blocks.zs, MAIN, -1)
    h1 = blocks.add(keep1, got1).reshape(shape)
    h2 = blocks.add(keep2, got2).reshape(shape)
    dq_others, give_kv = attention_grad(q_rot, kv_got, grad_attn, lse, delta, info, docs)
    got_kv = blocks.swap(give_kv, blocks.x)
    dq_others, h1, h2 = tie(dq_others, h1, h2)
    h1 = blocks.add(h1[0], blocks.swap(h1[1], blocks.y))
    h2 = blocks.add(h2[:, 0], blocks.swap(h2[:, 1], blocks.x))
    grad_q_rot, own_kv = attention_grad(
        q_rot, kv_mine, grad_attn, lse, delta, info, docs, dq_others
    )
    got_kv, h1, h2 = tie(got_kv, h1, h2)
    h1 = blocks.add(h1[0], blocks.swap(h1[1], blocks.x))
    h2 = blocks.add(h2[0], blocks.swap(h2[1], blocks.y))

    gx, keep_a, give_a = call(
        functools.partial(post_kernel, size),
        "norm_qkv_back",
        [
            ((width, tok_rows), F32), ((a_rows // 2, size.a_width), BF),
            ((a_rows // 2, size.a_width), BF),
        ],
        [
            ((tok_rows, width + kv_width), F32), ((tok_rows, size.a_width), BF),
            ((1, size.flat), F32),
        ],
        6,
        (
            me, grad_q_rot, own_kv, got_kv, cos, sin, n1t, a_mine,
            a_other, tokens, grad_mid, flat, grad_gain,
        ),
        24,
    )
    held = blocks.add(keep_a, blocks.swap(give_a, blocks.core))
    held, h2 = tie(held, h2)
    held = held.reshape(2, 2, blocks.zs, size.tall, size.a_width)
    held = blocks.add(held[0], blocks.swap(held[1], blocks.y))
    held, share2, h1 = tie(held, blocks.sum_z(h2), h1)
    held = blocks.add(held[0], blocks.swap(held[1], blocks.x))
    held, share1 = tie(held, blocks.sum_z(h1))
    share_a = blocks.sum_z(held)

    tails = tail_unpack(share1[:, size.tail : size.tail + size.piece], 2 * ff)
    tail_o = tail_unpack(share1[:, size.tail_o : size.tail_o + 128], width)
    share_out = jnp.concatenate([share1[:, size.out : size.out + width], tail_o], axis=0)
    share_gate = jnp.concatenate([share1[:, :ff], tails[:, :ff]], axis=0)
    share_up = jnp.concatenate([share2[:, :ff], tails[:, ff:]], axis=0)
    downs = [size.down_back_at(c) for c in range(size.downs)]
    share_down = jnp.concatenate(
        [(share1, share2)[which][:, at : at + width] for which, at in downs], axis=0
    )
    ends = (width, width + kv_width, size.qkv)
    return (
        layer_out.T, gx.T, share_a[:rows, : ends[0]].reshape(-1),
        share_a[:rows, ends[0] : ends[1]].reshape(-1),
        share_a[:rows, ends[1] : ends[2]].reshape(-1),
        share_out.reshape(-1), share_gate.reshape(-1), share_up.reshape(-1),
        share_down.reshape(-1), share_a[rows, : size.vec],
    )


def local(
    tokens, q_weight, k_weight, v_weight, o_weight, gate_weight, up_weight, down_weight,
    vectors, doc_lengths, cotangent,
):
    tok_rows, width = tokens.shape
    ctx_count = lax.axis_size("ctx")
    dp_count = lax.axis_size("dp")
    count = dp_count * ctx_count
    seq_tokens = tok_rows * ctx_count
    ctx_index = lax.axis_index("ctx")
    heads = width // HEAD_DIM
    kv_width = KV_HEADS * HEAD_DIM
    ff = gate_weight.shape[0] * count // width

    position_all = doc_layout(doc_lengths[0], seq_tokens)
    offset = ctx_index * tok_rows
    position_mine = lax.dynamic_slice_in_dim(position_all, offset, tok_rows)
    docs = doc_lengths.shape[1]
    others = (ctx_count - 1 - ctx_index) * tok_rows
    heads_of = jnp.stack([ctx_index, others, offset]).astype(jnp.int32)
    info = jnp.concatenate([heads_of, jnp.cumsum(doc_lengths[0])[:-1].astype(jnp.int32)])
    half = HEAD_DIM // 2
    freq = THETA ** (-jnp.arange(half, dtype=F32) * 2.0 / HEAD_DIM)
    position_f = position_mine.astype(F32)[:, None]

    whole_rows = width % count == 0 and ff % count == 0
    if whole_rows and ctx_count == 2 and dp_count % 4 == 0 and count & (count - 1) == 0:
        size = Sizes(width, ff, dp_count, ctx_count, vectors.shape[0], kv_width)
        if size.fits() and (width + kv_width) % 128 == 0:
            angle = position_f * jnp.tile(freq, 128 // half)[None, :]
            sign = np.where(np.arange(128) % HEAD_DIM < half, -1.0, 1.0).astype(np.float32)
            pos = (info, docs, jnp.cos(angle), jnp.sin(angle) * sign)
            args = (
                tokens, q_weight, k_weight, v_weight, o_weight, gate_weight, up_weight,
                down_weight, vectors, cotangent,
            )
            return local_blocks(size, Blocks(dp_count, ctx_count), pos, args)

    angle = position_f * freq[None, :]
    cosine = jnp.cos(angle)[:, None, :]
    sine = jnp.sin(angle)[:, None, :]
    inputs = tokens.astype(F32)
    inv_first = lax.rsqrt(jnp.mean(inputs * inputs, axis=-1, keepdims=True) + EPS)

    def whole(part):
        return lax.all_gather(part, AXES, axis=0, tiled=True)

    w_qkv = jnp.concatenate(
        [whole(w).reshape(width, -1) for w in (q_weight, k_weight, v_weight)], axis=1
    )
    w_out = whole(o_weight).reshape(width, width)
    w_gate = whole(gate_weight).reshape(width, ff)
    w_up = whole(up_weight).reshape(width, ff)
    w_down = whole(down_weight).reshape(ff, width)
    flat = whole(vectors).astype(F32)
    ends = [width, width + kv_width, width + 2 * kv_width, 2 * width + 2 * kv_width]
    gain_attn = flat[ends[2] : ends[3]]
    gain_mlp = flat[ends[3] : ends[3] + width]

    n_first = (inputs * inv_first * gain_attn).astype(BF)
    qkv = times(n_first, w_qkv) + flat[: ends[2]]
    q_rot = turn(qkv[:, :width].reshape(tok_rows, heads, HEAD_DIM), cosine, sine)
    q_rot = q_rot.astype(BF).reshape(tok_rows, width)
    k_rot = turn(qkv[:, width : ends[1]].reshape(tok_rows, KV_HEADS, HEAD_DIM), cosine, sine)
    k_rot = k_rot.astype(BF).reshape(tok_rows, kv_width)
    kv_mine = jnp.concatenate([k_rot, qkv[:, ends[1] :].astype(BF)], axis=1)
    kv = (lax.all_gather(kv_mine, "ctx", axis=0, tiled=True),)
    info = info.at[0].set(1)
    attn, lse = attention(q_rot, kv, info, docs, seq_tokens, False)
    mid = inputs + times(attn, w_out)
    inv_second = lax.rsqrt(jnp.mean(mid * mid, axis=-1, keepdims=True) + EPS)
    n_second = (mid * inv_second * gain_mlp).astype(BF)
    gate = times(n_second, w_gate)
    up_val = times(n_second, w_up)
    sig = jax.nn.sigmoid(gate)
    act = gate * sig
    hidden = (act * up_val).astype(BF)
    layer_out = (mid + times(hidden, w_down)).astype(BF)

    grad_wdown = inner_rows(hidden, cotangent)
    grad_hidden = times_back(cotangent, w_down)
    grad_gate = (grad_hidden * up_val * (sig * (1.0 + gate * (1.0 - sig)))).astype(BF)
    grad_up = (grad_hidden * act).astype(BF)
    grad_wgate = inner_rows(n_second, grad_gate)
    grad_wup = inner_rows(n_second, grad_up)
    grad_n2 = times_back(grad_gate, w_gate) + times_back(grad_up, w_up)
    grad_mid_norm, grad_gain_mlp = norm_back(mid, inv_second, gain_mlp, grad_n2)
    grad_mid = cotangent.astype(F32) + grad_mid_norm
    grad_branch = grad_mid.astype(BF)
    grad_wout = inner_rows(attn, grad_branch)
    grad_attn = times_back(grad_branch, w_out).astype(BF)
    grad_q_rot, grad_kv = attention_back(
        q_rot, kv, grad_attn, lse, info, docs, seq_tokens, False, 0, KV_HEADS
    )
    grad_kv_mine = lax.psum_scatter(
        grad_kv.astype(BF), "ctx", scatter_dimension=0, tiled=True
    ).astype(F32)
    grad_q = turn(grad_q_rot.reshape(tok_rows, heads, HEAD_DIM), cosine, -sine)
    grad_k = turn(
        grad_kv_mine[:, :kv_width].reshape(tok_rows, KV_HEADS, HEAD_DIM), cosine, -sine
    )
    grad_qkv = jnp.concatenate(
        [
            grad_q.reshape(tok_rows, width).astype(BF),
            grad_k.reshape(tok_rows, kv_width).astype(BF),
            grad_kv_mine[:, kv_width:].astype(BF),
        ],
        axis=1,
    )
    grad_wqkv = inner_rows(n_first, grad_qkv)
    grad_bias = jnp.sum(grad_qkv.astype(F32), axis=0)
    grad_n1 = times_back(grad_qkv, w_qkv)
    grad_x_norm, grad_gain_attn = norm_back(inputs, inv_first, gain_attn, grad_n1)
    input_grad = grad_mid + grad_x_norm
    used = 3 * width + 2 * kv_width
    padding = jnp.zeros((vectors.shape[0] * count - used,), F32)
    vector_term = jnp.concatenate([grad_bias, grad_gain_attn, grad_gain_mlp, padding])

    def shares(term):
        return lax.psum_scatter(term.reshape(-1), AXES, scatter_dimension=0, tiled=True)

    return (
        layer_out, input_grad, shares(grad_wqkv[:, :width]),
        shares(grad_wqkv[:, width : ends[1]]), shares(grad_wqkv[:, ends[1] :]),
        shares(grad_wout), shares(grad_wgate), shares(grad_wup), shares(grad_wdown),
        shares(vector_term),
    )


def solution(mesh):
    split = P(AXES)
    rows = P(AXES, None)
    in_specs = (rows,) + (split,) * 8 + (P("dp", None), rows)
    out_specs = (rows, rows) + (split,) * 8
    return jax.shard_map(local, mesh=mesh, in_specs=in_specs, out_specs=out_specs, check_vma=False)
```

```python
import functools

import jax
import jax.numpy as jnp
import numpy as np
from jax import lax
from jax.experimental import pallas as pl
from jax.experimental.pallas import tpu as pltpu
from jax.sharding import PartitionSpec as P

KV_HEADS = 3
HEAD_DIM = 64

EPS = 1e-06
THETA = 100000.0
NEG_FILL = -1e30
AXES = ("dp", "ctx")
BF = jnp.bfloat16
F32 = jnp.float32


def times(left, right):
    return jnp.dot(left, right, preferred_element_type=F32)


def inner_rows(left, right):
    return lax.dot_general(left, right, (((0,), (0,)), ((), ())), preferred_element_type=F32)


def times_back(left, right):
    return lax.dot_general(left, right, (((1,), (1,)), ((), ())), preferred_element_type=F32)


def norm_back(values, inv, gain, grad):
    scaled = grad * gain
    dot = jnp.mean(scaled * values, axis=-1, keepdims=True)
    grad_values = inv * scaled - values * (inv * inv * inv * dot)
    grad_gain = jnp.sum(grad * values * inv, axis=0)
    return grad_values, grad_gain


def turn(values, cosine, sine):
    half = values.shape[-1] // 2
    first = values[..., :half]
    second = values[..., half:]
    return jnp.concatenate(
        [first * cosine - second * sine, second * cosine + first * sine], axis=-1
    )


def doc_layout(lengths, count):
    ends = jnp.cumsum(lengths)
    place = jnp.arange(count, dtype=jnp.int32)
    segment = jnp.sum((place[:, None] >= ends[None, :-1]).astype(jnp.int32), axis=1)
    starts = ends - lengths
    picked = segment[:, None] == jnp.arange(lengths.shape[0], dtype=jnp.int32)[None, :]
    first = jnp.sum(jnp.where(picked, starts[None, :], 0), axis=1)
    return place - first


def fill_bias(bias, info, docs, short, own=None):
    total, rows = bias.shape
    row_q = lax.broadcasted_iota(jnp.int32, (1, rows), 1) + info[2]
    first = jnp.zeros_like(row_q)
    for j in range(docs - 1):
        first = jnp.where(row_q >= info[3 + j], info[3 + j], first)
    parts = ((0, total, 0),)
    if own is not None:
        parts = ((0, total, info[2] if own else info[1]),)
    elif short < total:
        parts = ((0, total - short, info[1]), (total - short, total, info[2]))
    for start, stop, base in parts:
        row_k = lax.broadcasted_iota(jnp.int32, (stop - start, rows), 0)
        allowed = (row_k >= first - base) & (row_k <= row_q - base)
        bias[start:stop] = jnp.where(allowed, 0.0, NEG_FILL)


def key_range(full, total, short, rows, block, at, causal):
    start = 0 if full else total - short
    stop = total - rows + (at + 1) * block if causal else total
    return start, stop


def key_parts(kv_refs):
    at = 0
    for kv_ref in kv_refs:
        yield slice(at, at + kv_ref.shape[0]), kv_ref
        at += kv_ref.shape[0]


def attn_fwd_kernel(
    heads, block, short, causal, docs, info, q_ref, *refs,
):
    kv_refs, (out_ref, lse_ref, qs, ks, vts, bias, out_t) = refs[:-7], refs[-7:]
    rows = q_ref.shape[0]
    total = bias.shape[0]
    kv_width = KV_HEADS * HEAD_DIM
    group = heads // KV_HEADS
    fill_bias(bias, info, docs, short)
    for h in range(heads):
        qs[h] = q_ref[:, h * HEAD_DIM : (h + 1) * HEAD_DIM] * BF(HEAD_DIM**-0.5)
    for at, kv_ref in key_parts(kv_refs):
        for g in range(KV_HEADS):
            ks[g, at] = kv_ref[:, g * HEAD_DIM : (g + 1) * HEAD_DIM]
        vts[:, at] = jnp.transpose(kv_ref[:, kv_width:].astype(F32)).astype(BF)

    def run(full):
        @pl.loop(0, KV_HEADS)
        def _(g):
            v_rows = pl.ds(pl.multiple_of(g * HEAD_DIM, HEAD_DIM), HEAD_DIM)
            for j in range(group):
                h = g * group + j
                out_rows = pl.ds(pl.multiple_of(h * HEAD_DIM, HEAD_DIM), HEAD_DIM)
                for at in range(rows // block):
                    start, stop = key_range(full, total, short, rows, block, at, causal)
                    cols = slice(at * block, (at + 1) * block)
                    s = times_back(ks[g, start:stop], qs[h, cols])
                    s = s + bias[start:stop, cols]
                    top = jnp.max(s, axis=0, keepdims=True)
                    p = jnp.exp(s - top)
                    total_p = jnp.sum(p, axis=0, keepdims=True)
                    o = times(vts[v_rows, start:stop], p.astype(BF))
                    out_t[out_rows, cols] = o / total_p
                    lse_ref[h, :, cols] = top + jnp.log(total_p)

    pl.when(info[0] != 0)(lambda: run(True))
    pl.when(info[0] == 0)(lambda: run(False))
    out_ref[...] = jnp.transpose(out_t[...]).astype(BF)


def attn_own_kernel(
    heads, block, docs, info, q_ref, kv_ref, acc, top_ref, sum_ref, qs, ks, vts, bias
):
    rows = q_ref.shape[0]
    kv_width = KV_HEADS * HEAD_DIM
    group = heads // KV_HEADS
    fill_bias(bias, info, docs, rows, own=True)
    for h in range(heads):
        qs[h] = q_ref[:, h * HEAD_DIM : (h + 1) * HEAD_DIM] * BF(HEAD_DIM**-0.5)
    for g in range(KV_HEADS):
        ks[g] = kv_ref[:, g * HEAD_DIM : (g + 1) * HEAD_DIM]
    vts[...] = jnp.transpose(kv_ref[:, kv_width:].astype(F32)).astype(BF)

    @pl.loop(0, heads)
    def _(h):
        g = h // group
        v_rows = pl.ds(pl.multiple_of(g * HEAD_DIM, HEAD_DIM), HEAD_DIM)
        out_rows = pl.ds(pl.multiple_of(h * HEAD_DIM, HEAD_DIM), HEAD_DIM)
        for at in range(rows // block):
            stop = (at + 1) * block
            cols = slice(at * block, stop)
            s = times_back(ks[g, :stop], qs[h, cols]) + bias[:stop, cols]
            top = jnp.max(s, axis=0, keepdims=True)
            p = jnp.exp(s - top)
            top_ref[h, :, cols] = top
            sum_ref[h, :, cols] = jnp.sum(p, axis=0, keepdims=True)
            acc[out_rows, cols] = times(vts[v_rows, :stop], p.astype(BF))


def attn_others_kernel(
    heads, block, docs, info, q_ref, kv_ref, acc, top_ref, sum_ref, out_ref, lse_ref,
    qs, ks, vts, bias, out_t,
):
    rows = q_ref.shape[0]
    kv_width = KV_HEADS * HEAD_DIM
    group = heads // KV_HEADS

    @pl.when(info[0] == 0)
    def _():
        for h in range(heads):
            at = slice(h * HEAD_DIM, (h + 1) * HEAD_DIM)
            out_t[at] = acc[at] / sum_ref[h]
            lse_ref[h] = top_ref[h] + jnp.log(sum_ref[h])

    @pl.when(info[0] != 0)
    def _():
        fill_bias(bias, info, docs, rows, own=False)
        for h in range(heads):
            qs[h] = q_ref[:, h * HEAD_DIM : (h + 1) * HEAD_DIM] * BF(HEAD_DIM**-0.5)
        for g in range(KV_HEADS):
            ks[g] = kv_ref[:, g * HEAD_DIM : (g + 1) * HEAD_DIM]
        vts[...] = jnp.transpose(kv_ref[:, kv_width:].astype(F32)).astype(BF)

        @pl.loop(0, heads)
        def _(h):
            g = h // group
            v_rows = pl.ds(pl.multiple_of(g * HEAD_DIM, HEAD_DIM), HEAD_DIM)
            out_rows = pl.ds(pl.multiple_of(h * HEAD_DIM, HEAD_DIM), HEAD_DIM)
            for at in range(rows // block):
                cols = slice(at * block, (at + 1) * block)
                s = times_back(ks[g], qs[h, cols]) + bias[:, cols]
                own = top_ref[h, :, cols]
                top = jnp.maximum(own, jnp.max(s, axis=0, keepdims=True))
                scale = jnp.exp(own - top)
                p = jnp.exp(s - top)
                total_p = sum_ref[h, :, cols] * scale + jnp.sum(p, axis=0, keepdims=True)
                o = acc[out_rows, cols] * scale + times(vts[v_rows], p.astype(BF))
                out_t[out_rows, cols] = o / total_p
                lse_ref[h, :, cols] = top + jnp.log(total_p)

    out_ref[...] = jnp.transpose(out_t[...]).astype(BF)


def attn_grad_kernel(
    heads, block, docs, own, info, q_ref, kv_ref, do_ref, lse_ref, delta_ref, *refs
):
    refs, (qs, dos, ks, vs, kts, bias, dk, dv) = refs[:-8], refs[-8:]
    if own:
        before, dq_ref, dkv_ref, dq_t = refs
    else:
        dq_t, dkv_ref = refs
    rows = q_ref.shape[0]
    kv_width = KV_HEADS * HEAD_DIM
    group = heads // KV_HEADS
    dk[...] = jnp.zeros_like(dk)
    dv[...] = jnp.zeros_like(dv)

    def run():
        fill_bias(bias, info, docs, rows, own=own)
        for h in range(heads):
            at = slice(h * HEAD_DIM, (h + 1) * HEAD_DIM)
            qs[h] = q_ref[:, at] * BF(HEAD_DIM**-0.5)
            dos[h] = do_ref[:, at]
        for g in range(KV_HEADS):
            lo = g * HEAD_DIM
            ks[g] = kv_ref[:, lo : lo + HEAD_DIM]
            vs[g] = kv_ref[:, kv_width + lo : kv_width + lo + HEAD_DIM]
        kts[...] = jnp.transpose(kv_ref[:, :kv_width].astype(F32)).astype(BF)

        @pl.loop(0, heads)
        def _(h):
            g = h // group
            k_rows = pl.ds(pl.multiple_of(g * HEAD_DIM, HEAD_DIM), HEAD_DIM)
            out_rows = pl.ds(pl.multiple_of(h * HEAD_DIM, HEAD_DIM), HEAD_DIM)
            for at in range(rows // block):
                stop = (at + 1) * block if own else rows
                cols = slice(at * block, (at + 1) * block)
                q = qs[h, cols]
                do = dos[h, cols]
                s = times_back(ks[g, :stop], q) + bias[:stop, cols]
                p = jnp.exp(s - lse_ref[h, :, cols])
                dp = times_back(vs[g, :stop], do)
                ds = (p * (dp - delta_ref[h, :, cols])).astype(BF)
                dk[g, :stop] += times(ds, q)
                dv[g, :stop] += times(p.astype(BF), do)
                dq = times(kts[k_rows, :stop], ds) * HEAD_DIM**-0.5
                dq_t[out_rows, cols] = before[out_rows, cols] + dq if own else dq

    if own:
        run()
        dq_ref[...] = jnp.transpose(dq_t[...])
    else:
        pl.when(info[0] != 0)(run)

        @pl.when(info[0] == 0)
        def _():
            dq_t[...] = jnp.zeros_like(dq_t)

    for g in range(KV_HEADS):
        lo = g * HEAD_DIM
        dkv_ref[:, lo : lo + HEAD_DIM] = dk[g].astype(dkv_ref.dtype)
        dkv_ref[:, kv_width + lo : kv_width + lo + HEAD_DIM] = dv[g].astype(dkv_ref.dtype)


def attn_bwd_kernel(
    heads, block, short, causal, docs, g0, g1, parts, info, q_ref, do_ref, lse_ref, *refs,
):
    kv_refs, outs, scratch = refs[:parts], refs[parts:-9], refs[-9:]
    qs, ks, vs, kts, dos, bias, dq_t, dk, dv = scratch
    rows = q_ref.shape[0]
    total = bias.shape[0]
    kv_width = KV_HEADS * HEAD_DIM
    group = heads // KV_HEADS
    keys = g1 - g0
    fill_bias(bias, info, docs, short)
    for h in range(keys * group):
        lanes = slice((g0 * group + h) * HEAD_DIM, (g0 * group + h + 1) * HEAD_DIM)
        qs[h] = q_ref[:, lanes] * BF(HEAD_DIM**-0.5)
        dos[h] = do_ref[:, lanes]
    for g in range(keys):
        lo = (g0 + g) * HEAD_DIM
        for at, kv_ref in key_parts(kv_refs):
            ks[g, at] = kv_ref[:, lo : lo + HEAD_DIM]
            vs[g, at] = kv_ref[:, kv_width + lo : kv_width + lo + HEAD_DIM]
        kts[g] = jnp.transpose(ks[g].astype(F32)).astype(BF)
    dk[...] = jnp.zeros_like(dk)
    dv[...] = jnp.zeros_like(dv)

    def run(full):
        @pl.loop(0, keys * group)
        def _(h):
            g = h // group if keys > 1 else 0
            out_rows = pl.ds(pl.multiple_of(h * HEAD_DIM, HEAD_DIM), HEAD_DIM)
            for at in range(rows // block):
                start, stop = key_range(full, total, short, rows, block, at, causal)
                cols = slice(at * block, (at + 1) * block)
                q = qs[h, cols]
                do = dos[h, cols]
                s = times_back(ks[g, start:stop], q)
                p = jnp.exp(s + bias[start:stop, cols] - lse_ref[g0 * group + h, :, cols])
                dp = times_back(vs[g, start:stop], do)
                t = p * dp
                inner = jnp.sum(t, axis=0, keepdims=True)
                ds = (t - p * inner).astype(BF)
                dk[g, start:stop] += times(ds, q)
                dv[g, start:stop] += times(p.astype(BF), do)
                dq_t[out_rows, cols] = times(kts[g, :, start:stop], ds) * HEAD_DIM**-0.5

    pl.when(info[0] != 0)(lambda: run(True))
    pl.when(info[0] == 0)(lambda: run(False))
    outs[0][...] = jnp.transpose(dq_t[...])
    cut = total - outs[1].shape[0]
    for part, out in ((slice(cut, total), outs[1]),) + tuple((slice(0, cut), o) for o in outs[2:]):
        for g in range(keys):
            lo = g * HEAD_DIM
            out[:, lo : lo + HEAD_DIM] = dk[g, part].astype(out.dtype)
            lo += keys * HEAD_DIM
            out[:, lo : lo + HEAD_DIM] = dv[g, part].astype(out.dtype)


VM = pl.BlockSpec(memory_space=pltpu.VMEM)
SM = pl.BlockSpec(memory_space=pltpu.SMEM)


def cost_of(micros):
    return pl.CostEstimate(
        flops=int(micros * 1.1e9), bytes_accessed=2**20, transcendentals=0
    )


def attention(q, kv, info, docs, short, causal):
    rows, width = q.shape
    total = sum(part.shape[0] for part in kv)
    heads = width // HEAD_DIM
    block = min(rows, 256)
    return pl.pallas_call(
        functools.partial(attn_fwd_kernel, heads, block, short, causal, docs),
        out_shape=(
            jax.ShapeDtypeStruct((rows, width), BF),
            jax.ShapeDtypeStruct((heads, 1, rows), F32),
        ),
        in_specs=[SM] + [VM] * (1 + len(kv)),
        out_specs=(VM, VM),
        scratch_shapes=[
            pltpu.VMEM((heads, rows, HEAD_DIM), BF),
            pltpu.VMEM((KV_HEADS, total, HEAD_DIM), BF),
            pltpu.VMEM((KV_HEADS * HEAD_DIM, total), BF),
            pltpu.VMEM((total, rows), F32),
            pltpu.VMEM((width, rows), F32),
        ],
        compiler_params=pltpu.CompilerParams(vmem_limit_bytes=20 * 2**20),
        cost_estimate=cost_of(14),
        name="attn_fwd",
    )(info, q, *kv)


def attention_own(q, kv, info, docs):
    rows, width = q.shape
    heads = width // HEAD_DIM
    stat = jax.ShapeDtypeStruct((heads, 1, rows), F32)
    return pl.pallas_call(
        functools.partial(attn_own_kernel, heads, min(rows, 256), docs),
        out_shape=(jax.ShapeDtypeStruct((width, rows), F32), stat, stat),
        in_specs=[SM, VM, VM],
        out_specs=(VM, VM, VM),
        scratch_shapes=attn_scratch(rows, heads),
        compiler_params=pltpu.CompilerParams(vmem_limit_bytes=16 * 2**20),
        cost_estimate=cost_of(6),
        name="attn_own",
    )(info, q, kv)


def attn_scratch(rows, heads):
    return [
        pltpu.VMEM((heads, rows, HEAD_DIM), BF),
        pltpu.VMEM((KV_HEADS, rows, HEAD_DIM), BF),
        pltpu.VMEM((KV_HEADS * HEAD_DIM, rows), BF),
        pltpu.VMEM((rows, rows), F32),
    ]


def attention_grad(q, kv, grad_out, lse, delta, info, docs, before=None):
    rows, width = q.shape
    heads = width // HEAD_DIM
    own = before is not None
    turned = jax.ShapeDtypeStruct((width, rows), F32)
    if own:
        outs = [jax.ShapeDtypeStruct((rows, width), F32), jax.ShapeDtypeStruct(kv.shape, F32)]
    else:
        outs = [turned, jax.ShapeDtypeStruct(kv.shape, BF)]
    by_head = pltpu.VMEM((heads, rows, HEAD_DIM), BF)
    by_key = pltpu.VMEM((KV_HEADS, rows, HEAD_DIM), BF)
    sums = pltpu.VMEM((KV_HEADS, rows, HEAD_DIM), F32)
    return pl.pallas_call(
        functools.partial(attn_grad_kernel, heads, min(rows, 256), docs, own),
        out_shape=outs,
        in_specs=[SM] + [VM] * (6 if own else 5),
        out_specs=[VM] * 2,
        scratch_shapes=([pltpu.VMEM((width, rows), F32)] if own else []) + [
            by_head, by_head, by_key, by_key, pltpu.VMEM((KV_HEADS * HEAD_DIM, rows), BF),
            pltpu.VMEM((rows, rows), F32), sums, sums,
        ],
        compiler_params=pltpu.CompilerParams(vmem_limit_bytes=20 * 2**20),
        cost_estimate=cost_of(9 if own else 10),
        name="attn_grad_own" if own else "attn_grad_others",
    )(info, q, kv, grad_out, lse, delta, *([before] if own else []))


def attention_others(q, kv, acc, top, total, info, docs):
    rows, width = q.shape
    heads = width // HEAD_DIM
    return pl.pallas_call(
        functools.partial(attn_others_kernel, heads, min(rows, 256), docs),
        out_shape=(
            jax.ShapeDtypeStruct((rows, width), BF),
            jax.ShapeDtypeStruct((heads, 1, rows), F32),
        ),
        in_specs=[SM] + [VM] * 5,
        out_specs=(VM, VM),
        scratch_shapes=attn_scratch(rows, heads) + [pltpu.VMEM((width, rows), F32)],
        compiler_params=pltpu.CompilerParams(vmem_limit_bytes=16 * 2**20),
        cost_estimate=cost_of(10),
        name="attn_others",
    )(info, q, kv, acc, top, total)


def attention_back(q, kv, grad_out, lse, info, docs, short, causal, g0, g1):
    rows, width = q.shape
    total = sum(part.shape[0] for part in kv)
    heads = width // HEAD_DIM
    block = min(rows, 256)
    keys = g1 - g0
    mine = heads // KV_HEADS * keys
    outs = [jax.ShapeDtypeStruct((rows, mine * HEAD_DIM), F32)]
    if causal:
        outs.append(jax.ShapeDtypeStruct((rows, 2 * keys * HEAD_DIM), F32))
        outs.append(jax.ShapeDtypeStruct((total - rows, 2 * keys * HEAD_DIM), BF))
    else:
        outs.append(jax.ShapeDtypeStruct((total, 2 * keys * HEAD_DIM), F32))
    return pl.pallas_call(
        functools.partial(attn_bwd_kernel, heads, block, short, causal, docs, g0, g1, len(kv)),
        out_shape=outs,
        in_specs=[SM] + [VM] * (3 + len(kv)),
        out_specs=[VM] * len(outs),
        scratch_shapes=[
            pltpu.VMEM((mine, rows, HEAD_DIM), BF),
            pltpu.VMEM((keys, total, HEAD_DIM), BF),
            pltpu.VMEM((keys, total, HEAD_DIM), BF),
            pltpu.VMEM((keys, HEAD_DIM, total), BF),
            pltpu.VMEM((mine, rows, HEAD_DIM), BF),
            pltpu.VMEM((total, rows), F32),
            pltpu.VMEM((mine * HEAD_DIM, rows), F32),
            pltpu.VMEM((keys, total, HEAD_DIM), F32),
            pltpu.VMEM((keys, total, HEAD_DIM), F32),
        ],
        compiler_params=pltpu.CompilerParams(vmem_limit_bytes=20 * 2**20),
        cost_estimate=cost_of(20),
        name="attn_bwd",
    )(info, q, grad_out, lse, *kv)


TAIL = 2
MAIN = 16
PIECES = MAIN // TAIL


class Blocks:
    def __init__(self, dp_count, ctx_count):
        self.count = dp_count * ctx_count
        self.x = 1
        self.core = ctx_count
        self.y = 2 * ctx_count
        self.z = 4 * ctx_count
        self.zs = dp_count // 4
        self.masks = []
        for p in range(self.count):
            z, x = p % self.zs, p // self.zs % 2
            y, core = p // (2 * self.zs) % 2, p // (4 * self.zs)
            self.masks.append(x * self.x + y * self.y + core * self.core + z * self.z)

    def swap(self, values, mask):
        perm = [(i, i ^ mask) for i in range(self.count)]
        return lax.ppermute(values, AXES, perm)

    def along_z(self, mine):
        return jnp.stack([mine] + [self.swap(mine, d * self.z) for d in range(1, self.zs)])

    def add(self, keep, got):
        return (keep.astype(F32) + got.astype(F32)).astype(BF)

    def sum_z(self, held):
        got = [self.swap(held[d], d * self.z).astype(F32) for d in range(1, self.zs)]
        return functools.reduce(jnp.add, got, held[0].astype(F32))


class Sizes:
    def __init__(self, width, ff, dp, ctx, vec, kv_width):
        count = dp * ctx
        self.zs, self.ctx = dp // 4, ctx
        self.width, self.ff, self.count, self.vec = width, ff, count, vec
        self.rows = width // count
        self.f_rows = ff // count
        up = lambda n: (n + 127) // 128 * 128
        self.wide = up(width)
        self.qkv = width + 2 * kv_width
        self.a_width = up(self.qkv)
        self.tall = (self.rows + 1 + 7) // 8 * 8
        self.downs = self.f_rows // MAIN
        self.piece = 2 * ff // PIECES
        self.gate = 0
        self.tail = ff
        self.tail_o = self.tail + self.piece
        self.out = self.tail_o + 128
        self.down0 = self.out + self.wide
        self.first = self.down0 + self.wide
        self.second = ff + (self.downs - 1) * self.wide
        self.back_first = self.down0 + (self.downs - 1) * self.wide
        self.back_second = ff + self.wide
        self.flat = self.a_width + 2 * self.wide

    def down_at(self, c):
        return (0, self.down0) if c == 0 else (1, self.ff + (c - 1) * self.wide)

    def down_back_at(self, c):
        return (0, self.down0 + c * self.wide) if c < self.downs - 1 else (1, self.ff)

    def fits(self):
        return (
            self.rows == MAIN + TAIL
            and self.f_rows % MAIN == 0
            and self.piece % 128 == 0
            and self.ff % 256 == 0
            and self.wide <= 128 * PIECES
            and self.vec <= 128
        )


def wire_kernel(
    size, g_ref, u_ref, o_ref, d_ref, xt_ref, cott_ref, out1, out2, x_any, cot_any,
    tail, tail_o, x_ref, cot_ref, sems,
):
    ff, width = size.ff, size.width
    x_ref[...] = jnp.transpose(xt_ref[...].astype(F32)).astype(BF)
    cot_ref[...] = jnp.transpose(cott_ref[...].astype(F32)).astype(BF)
    copies = fetch((x_ref, cot_ref), (x_any, cot_any), sems)
    out1[:, : ff] = g_ref[:MAIN]
    out2[:, : ff] = u_ref[:MAIN]
    out1[:, size.out : size.out + size.wide] = jnp.zeros((MAIN, size.wide), BF)
    out1[:, size.out : size.out + width] = o_ref[:MAIN]
    tail_o[...] = jnp.zeros_like(tail_o)
    odd = [ref[MAIN:].astype(F32) for ref in (g_ref, u_ref, o_ref)]
    for c in range(PIECES):
        src = odd[c * size.piece // ff]
        at = c * size.piece % ff
        tail[c * TAIL : (c + 1) * TAIL] = src[:, at : at + size.piece]
        used = min(128, width - c * 128)
        if used > 0:
            tail_o[c * TAIL : (c + 1) * TAIL, :used] = odd[2][:, c * 128 : c * 128 + used]
    out1[:, size.tail : size.tail + size.piece] = tail[...].astype(BF)
    out1[:, size.tail_o : size.tail_o + 128] = tail_o[...].astype(BF)
    for c in range(size.downs):
        which, at = size.down_at(c)
        out = (out1, out2)[which]
        out[:, at : at + size.wide] = jnp.zeros((MAIN, size.wide), BF)
        out[:, at : at + width] = d_ref[c * MAIN : (c + 1) * MAIN]
    for copy in copies:
        copy.wait()


def over(values, by):
    scale = 2**16 // by + 1
    whole = (values * scale) >> 16
    return whole, values - whole * by


def mask_of(size, p):
    z, rest = p % size.zs, p // size.zs
    x, y, core = rest % 2, rest // 2 % 2, rest // 4
    return x + core * size.ctx + y * (2 * size.ctx) + z * (4 * size.ctx)


def lanes(count):
    return lax.broadcasted_iota(jnp.int32, (1, count), 1)


def place_matrix(size, me, tall):
    if tall:
        p, inside = over(lanes(size.count * size.tall), size.tall)
        feature = jnp.where(inside < size.rows, size.rows * (me ^ mask_of(size, p)) + inside, -1)
    else:
        s = lanes(size.count * (MAIN + TAIL))
        tail = s - size.count * MAIN
        p = jnp.where(tail < 0, s // MAIN, tail // TAIL)
        inside = jnp.where(tail < 0, s % MAIN, MAIN + tail % TAIL)
        feature = size.rows * (me ^ mask_of(size, p)) + inside
    at = lax.broadcasted_iota(jnp.int32, (size.width, feature.shape[1]), 0)
    return jnp.where(at == feature, 1.0, 0.0).astype(BF)


def vector_places(size, me):
    at = lanes(size.flat)
    ends = (size.a_width, size.a_width + size.wide)
    part = jnp.where(at < ends[0], 0, jnp.where(at < ends[1], 1, 2))
    inside = at - jnp.where(part == 0, 0, jnp.where(part == 1, ends[0], ends[1]))
    start = jnp.where(part == 0, 0, jnp.where(part == 1, size.qkv, size.qkv + size.width))
    used = inside < jnp.where(part == 0, size.qkv, size.width)
    owner, lane = over(start + inside, size.vec)
    rows = lax.broadcasted_iota(jnp.int32, (128, size.flat), 0)
    spread = jnp.where((rows == lane) & used, 1.0, 0.0).astype(BF)
    p = lax.broadcasted_iota(jnp.int32, (size.count, 1), 0)
    return spread, (owner == (me ^ mask_of(size, p))) & used


def swap_halves(u):
    rolled_back = pltpu.roll(u, 128 - HEAD_DIM // 2, 1)
    rolled = pltpu.roll(u, HEAD_DIM // 2, 1)
    lane = lax.broadcasted_iota(jnp.int32, u.shape, 1)
    return jnp.where(lane % HEAD_DIM < HEAD_DIM // 2, rolled_back, rolled)


def fetch(sources, targets, sems):
    copies = [
        pltpu.make_async_copy(src, dst, sems.at[i])
        for i, (src, dst) in enumerate(zip(sources, targets))
    ]
    for copy in copies:
        copy.start()
    return copies


def pre_kernel(
    size, me_ref, x_ref, wm_ref, wo_ref, cos_ref, sin_ref,
    q_ref, kv_ref, n1t_ref, flat_ref, w, qkv,
):
    me = me_ref[0]
    half = wm_ref.shape[0]
    w[:half] = wm_ref[...]
    w[half:] = wo_ref[...]
    place = place_matrix(size, me, True)
    spread, mine = vector_places(size, me)
    shape = (size.count, 2 * half)
    row = lax.broadcasted_iota(jnp.int32, shape, 0) * size.tall + size.rows
    row = jnp.where(lax.broadcasted_iota(jnp.int32, shape, 1) == row, 1.0, 0.0).astype(BF)
    packed = times(row, w[:, :128]).astype(BF)
    flat = jnp.sum(jnp.where(mine, times(packed, spread), 0.0), axis=0, keepdims=True)
    flat_ref[...] = flat
    gain = flat[:, size.a_width : size.a_width + size.width]
    x = x_ref[...].astype(F32)
    inv = lax.rsqrt(jnp.mean(x * x, axis=-1, keepdims=True) + EPS)
    n1 = (x * inv * gain).astype(BF)
    n1a = times(n1, place)
    n1t_ref[...] = jnp.transpose(n1a).astype(BF)
    qkv[...] = times(n1a.astype(BF), w[...]) + flat[:, : size.a_width]
    kv_width = kv_ref.shape[1] // 2
    for t in range((size.width + kv_width) // 128):
        u = qkv[:, t * 128 : (t + 1) * 128]
        qkv[:, t * 128 : (t + 1) * 128] = u * cos_ref[...] + swap_halves(u) * sin_ref[...]
    q_ref[...] = qkv[:, : size.width].astype(BF)
    kv_ref[...] = qkv[:, size.width : size.qkv].astype(BF)


def tail_place(size, back):
    odd, count = size.count * TAIL, size.count * MAIN
    row = lax.broadcasted_iota(jnp.int32, (count, count), 1 if back else 0)
    at = lax.broadcasted_iota(jnp.int32, (count, count), 0 if back else 1)
    c, q = row // odd, row % odd
    want = (q // TAIL) * MAIN + c * TAIL + q % TAIL
    return jnp.where(at == want, 1.0, 0.0).astype(BF)


def mlp_kernel(
    size, me_ref, attn_ref, x_ref, cot_ref, flat_ref,
    b1_00, b1_01, b1_10, b1_11, b2_00, b2_01, b2_10, b2_11,
    out_ref, keep1, give1, keep2, give2, gmid_ref, gattn_ref, ggain_ref, delta_ref,
    wg, wu, wo, wd, mid, n2s, n2t, place, acc, gacc, dwd, tails, tail_o, packed,
):
    me = me_ref[0]
    width, ff = size.width, size.ff
    part = b1_00.shape[0]
    half, main = 2 * part, 4 * part
    rows_z = part // 2
    place[...] = place_matrix(size, me, False)
    first = (b1_00, b1_01, b1_10, b1_11)
    second = (b2_00, b2_01, b2_10, b2_11)
    room = size.piece + 128
    for i, b1 in enumerate(first):
        rows = slice(i * part, (i + 1) * part)
        wg[rows] = b1[:, :ff]
        wo[rows] = b1[:, size.out : size.out + size.wide]
        packed[rows] = b1[:, size.tail : size.tail + room]
    for i, b2 in enumerate(second):
        for y in range(2):
            at = (i // 2) * half + y * part + (i % 2) * rows_z
            wu[at : at + rows_z] = b2[y * rows_z : (y + 1) * rows_z, :ff]
    odd = size.count * TAIL
    got = times(tail_place(size, False), packed[...]).astype(BF)
    for c in range(PIECES):
        rows = slice(c * odd, (c + 1) * odd)
        target = wg if c * size.piece < ff else wu
        at = c * size.piece % ff
        target[main:, at : at + size.piece] = got[rows, : size.piece]
        if c * 128 < size.wide:
            wo[main:, c * 128 : (c + 1) * 128] = got[rows, size.piece :]
    zs = rows_z // MAIN
    for p in range(size.count):
        z, x, y, core = p % zs, p // zs % 2, p // (2 * zs) % 2, p // (4 * zs)
        owner = me ^ mask_of(size, p)
        for c in range(size.downs):
            which, at = size.down_at(c)
            src, row = (second[2 * core + x], y * zs + z) if which else (
                first[2 * core + y], x * zs + z
            )
            to = pl.multiple_of(owner * size.f_rows + c * MAIN, MAIN)
            wd[pl.ds(to, MAIN), :] = src[row * MAIN : (row + 1) * MAIN, at : at + size.wide]
    attn_s = times(attn_ref[...], place[...])
    m = x_ref[...].astype(F32) + times(attn_s.astype(BF), wo[:, :width])
    mid[...] = m
    inv = lax.rsqrt(jnp.mean(m * m, axis=-1, keepdims=True) + EPS)
    lo = size.a_width + size.wide
    gain = flat_ref[:, lo : lo + width]
    n2 = (m * inv * gain).astype(BF)
    spread = times(n2, place[...])
    n2s[...] = spread.astype(BF)
    n2t[...] = jnp.transpose(spread).astype(BF)
    acc[...] = jnp.zeros_like(acc)
    gacc[...] = jnp.zeros_like(gacc)
    step = 512 if ff % 512 == 0 else 256

    @pl.loop(0, ff // step)
    def _(b):
        at = pl.multiple_of(b * step, step)
        cols = pl.ds(at, step)
        gate = times(n2s[...], wg[:, cols])
        up = times(n2s[...], wu[:, cols])
        sig = 1.0 / (1.0 + jnp.exp(-gate))
        act = gate * sig
        h = act * up
        gh = times_back(cot_ref[...], wd[cols, :width])
        gg = (gh * up * (sig * (1.0 + gate * (1.0 - sig)))).astype(BF)
        gu = (gh * act).astype(BF)
        acc[...] += times(h.astype(BF), wd[cols, :width])
        dwd[cols, :width] = times(jnp.transpose(h).astype(BF), cot_ref[...]).astype(BF)
        gacc[...] += times_back(gg, wg[:, cols]) + times_back(gu, wu[:, cols])
        for k, (grad, keep, give) in enumerate(((gg, keep1, give1), (gu, keep2, give2))):
            dw = times(n2t[...], grad).astype(BF)
            keep[:, cols] = dw[:half]
            give[:, cols] = dw[half:main]
            tails[:, pl.ds(pl.multiple_of(k * ff + at, 128), step)] = dw[main:]

    m = mid[...]
    inv = lax.rsqrt(jnp.mean(m * m, axis=-1, keepdims=True) + EPS)
    out_ref[...] = jnp.transpose(m + acc[...]).astype(BF)
    gn2 = times_back(gacc[...].astype(BF), place[...])
    scaled = gn2 * gain
    dot = jnp.mean(scaled * m, axis=-1, keepdims=True)
    ggain_ref[...] = jnp.sum(gn2 * m * inv, axis=0, keepdims=True)
    gmid = cot_ref[...].astype(F32) + inv * scaled - m * (inv * inv * inv * dot)
    gmid_ref[...] = gmid
    branch = gmid.astype(BF)
    gattn = times_back(branch, wo[:, :width]).astype(BF)
    gattn = times_back(gattn, place[...]).astype(BF)
    gattn_ref[...] = gattn
    both = jnp.transpose(gattn.astype(F32) * attn_ref[...].astype(F32))
    for h in range(width // HEAD_DIM):
        at = slice(h * HEAD_DIM, (h + 1) * HEAD_DIM)
        delta_ref[h] = jnp.sum(both[at], axis=0, keepdims=True)
    dwo = times(jnp.transpose(attn_s).astype(BF), branch).astype(BF)
    tail_o[...] = jnp.zeros_like(tail_o)
    tail_o[:, :width] = dwo[main:]
    terms = ((keep1, keep2), (give1, give2))
    for i, (term, _) in enumerate(terms):
        term[:, size.out : size.out + width] = dwo[i * half : (i + 1) * half]
    packed[...] = jnp.zeros_like(packed)
    for c in range(PIECES):
        rows = slice(c * odd, (c + 1) * odd)
        packed[rows, : size.piece] = tails[:, c * size.piece : (c + 1) * size.piece]
        if c * 128 < size.wide:
            packed[rows, size.piece :] = tail_o[:, c * 128 : (c + 1) * 128]
    wire = times(tail_place(size, True), packed[...]).astype(BF)
    for i, (term, _) in enumerate(terms):
        rows = slice(i * half, (i + 1) * half)
        term[:, size.tail : size.tail + room] = wire[rows]
    for p in range(size.count):
        to = terms[p // (size.count // 2)]
        rows = slice(p * MAIN % half, p * MAIN % half + MAIN)
        owner = me ^ mask_of(size, p)
        for c in range(size.downs):
            which, at = size.down_back_at(c)
            src = pl.multiple_of(owner * size.f_rows + c * MAIN, MAIN)
            to[which][rows, at : at + size.wide] = dwd[pl.ds(src, MAIN), :]


def post_kernel(
    size, me_ref, dq_ref, dkv_ref, got_ref, cos_ref, sin_ref, n1t_ref,
    wm_ref, wo_ref, x_ref, gmid_ref, flat_ref, ggain_ref,
    gx_ref, keep_ref, give_ref, turn_buf, grad, vec_row,
):
    me = me_ref[0]
    width = size.width
    half = wm_ref.shape[0]
    place = place_matrix(size, me, True)
    kv_width = KV_HEADS * HEAD_DIM
    turned = width + kv_width
    dkv = dkv_ref[...] + got_ref[...].astype(F32)
    turn_buf[:, :width] = dq_ref[...]
    turn_buf[:, width:] = dkv[:, :kv_width]
    grad[...] = jnp.zeros_like(grad)
    grad[:, turned : turned + kv_width] = dkv[:, kv_width:].astype(BF)
    for t in range(turned // 128):
        u = turn_buf[:, t * 128 : (t + 1) * 128]
        back = u * cos_ref[...] - swap_halves(u) * sin_ref[...]
        grad[:, t * 128 : (t + 1) * 128] = back.astype(BF)
    g = grad[...]
    gn1 = jnp.zeros((g.shape[0], width), F32)
    for part, w_ref in enumerate((wm_ref, wo_ref)):
        values = times_back(g, w_ref[...]).astype(BF)
        gn1 += times_back(values, place[:, part * half : (part + 1) * half])
    x = x_ref[...].astype(F32)
    inv = lax.rsqrt(jnp.mean(x * x, axis=-1, keepdims=True) + EPS)
    gain = flat_ref[:, size.a_width : size.a_width + width]
    scaled = gn1 * gain
    dot = jnp.mean(scaled * x, axis=-1, keepdims=True)
    gx_ref[...] = jnp.transpose(gmid_ref[...] + inv * scaled - x * (inv * inv * inv * dot))
    vec_row[...] = jnp.zeros_like(vec_row)
    vec_row[:, : size.a_width] = jnp.sum(g.astype(F32), axis=0, keepdims=True)
    vec_row[:, size.a_width : size.a_width + width] = jnp.sum(gn1 * x * inv, axis=0, keepdims=True)
    lo = size.a_width + size.wide
    vec_row[:, lo : lo + width] = ggain_ref[...]
    spread, mine = vector_places(size, me)
    packed = times_back(jnp.where(mine, vec_row[...], 0.0).astype(BF), spread)
    shape = (half, size.count)
    for part, term in ((0, keep_ref), (1, give_ref)):
        rows = slice(part * half, (part + 1) * half)
        dw = times(n1t_ref[rows], g)
        term[...] = dw.astype(BF)
        want = lax.broadcasted_iota(jnp.int32, shape, 1) * size.tall + size.rows - part * half
        here = lax.broadcasted_iota(jnp.int32, shape, 0) == want
        extra = times(jnp.where(here, 1.0, 0.0).astype(BF), packed.astype(BF))
        term[:, :128] = (dw[:, :128] + extra).astype(BF)


def call(kernel, name, out_shape, scratch, micros, args, vmem, any_in=(), any_out=(), scalar=True):
    shapes = [jax.ShapeDtypeStruct(s, t) for s, t in out_shape]
    here = pl.BlockSpec(memory_space=pl.ANY)
    specs = [here if i in any_in else VM for i in range(len(args))]
    if scalar:
        specs[0] = SM
    return pl.pallas_call(
        kernel,
        out_shape=shapes,
        in_specs=specs,
        out_specs=[here if i in any_out else VM for i in range(len(shapes))],
        scratch_shapes=[
            pltpu.SemaphoreType.DMA(s) if t is None else pltpu.VMEM(s, t) for s, t in scratch
        ],
        compiler_params=pltpu.CompilerParams(vmem_limit_bytes=vmem * 2**20),
        cost_estimate=cost_of(micros),
        name=name,
    )(*args)


def pad_to(values, rows, columns):
    return jnp.pad(values, ((0, rows - values.shape[0]), (0, columns - values.shape[1])))


def tail_pack(rows, piece):
    rows = pad_to(rows, TAIL, PIECES * piece)
    return rows.reshape(TAIL, PIECES, piece).transpose(1, 0, 2).reshape(MAIN, piece)


def tail_unpack(wire, used):
    piece = wire.shape[1]
    rows = wire.reshape(PIECES, TAIL, piece).transpose(1, 0, 2).reshape(TAIL, PIECES * piece)
    return rows[:, :used]


def tie(*values):
    return lax.optimization_barrier(values)


def local_blocks(size, blocks, pos, args):
    (
        tokens, q_weight, k_weight, v_weight, o_weight, gate_weight, up_weight, down_weight,
        vectors, cotangent,
    ) = args
    tok_rows, width = tokens.shape
    ff, rows = size.ff, size.rows
    kv_width = KV_HEADS * HEAD_DIM
    ctx_index = lax.axis_index("ctx")
    me = (lax.axis_index("dp") * lax.axis_size("ctx") + ctx_index).astype(jnp.int32).reshape(1)
    half = size.count // 2
    info, docs, cos, sin = pos

    joined_w = jnp.concatenate(
        [w.reshape(rows, -1) for w in (q_weight, k_weight, v_weight)], axis=1
    )
    vec_row = pad_to(vectors.reshape(1, -1), size.tall - rows, size.a_width)
    wire_a = jnp.concatenate([pad_to(joined_w, rows, size.a_width), vec_row], axis=0)
    za = blocks.along_z(wire_a)
    xa = jnp.stack([za, blocks.swap(za, blocks.x)])
    _, flat_w = tie(za, (gate_weight, up_weight, o_weight, down_weight))
    w_rows = [w.reshape(rows, -1) for w in flat_w[:3]]
    wire_1, wire_2, tokens, cotangent = call(
        functools.partial(wire_kernel, size),
        "wire",
        [
            ((MAIN, size.first), BF), ((MAIN, size.second), BF), ((tok_rows, width), BF),
            ((tok_rows, width), BF),
        ],
        [
            ((MAIN, size.piece), F32), ((MAIN, 128), F32), ((tok_rows, width), BF),
            ((tok_rows, width), BF), ((2,), None),
        ],
        1,
        w_rows + [flat_w[3].reshape(size.f_rows, width), tokens.T, cotangent.T],
        10,
        any_out=(2, 3),
        scalar=False,
    )
    xa, wire_1, wire_2 = tie(xa, wire_1, wire_2)
    ya = blocks.swap(xa, blocks.y)
    z1 = blocks.along_z(wire_1)
    z1, wire_2, ya = tie(z1, wire_2, ya)
    z2 = blocks.along_z(wire_2)
    x1 = jnp.stack([z1, blocks.swap(z1, blocks.x)])
    a_mine = jnp.stack([xa, ya]).reshape(half * size.tall, size.a_width)
    a_other = blocks.swap(a_mine, blocks.core)

    a_rows = size.count * size.tall
    q_rot, kv_mine, n1t, flat = call(
        functools.partial(pre_kernel, size),
        "norm_qkv",
        [
            ((tok_rows, width), BF), ((tok_rows, 2 * kv_width), BF), ((a_rows, tok_rows), BF),
            ((1, size.flat), F32),
        ],
        [((a_rows, size.a_width), BF), ((tok_rows, size.a_width), F32)],
        3,
        (me, tokens, a_mine, a_other, cos, sin),
        16,
    )
    kv_got = blocks.swap(kv_mine, blocks.x)
    own = attention_own(q_rot, kv_mine, info, docs)
    z2, x1 = tie(z2, x1, kv_mine)[:2]
    y2 = jnp.stack([z2, blocks.swap(z2, blocks.y)])
    b1_parts = [b.reshape(half // 2 * MAIN, -1) for b in (x1, blocks.swap(x1, blocks.y))]
    b2_parts = [b.reshape(half // 2 * MAIN, -1) for b in (y2, blocks.swap(y2, blocks.x))]
    attn, lse = attention_others(q_rot, kv_got, *own, info, docs)

    b1_parts[1:] = [b1_parts[1], blocks.swap(b1_parts[0], blocks.core)]
    b2_parts[1:] = [b2_parts[1], blocks.swap(b2_parts[0], blocks.core)]
    attn, b2_parts[1] = tie(attn, b2_parts[1])
    attn, b1_parts[1] = tie(attn, b1_parts[1])
    b2_parts.append(blocks.swap(b2_parts[1], blocks.core))
    b1_parts.append(blocks.swap(b1_parts[1], blocks.core))
    main = size.count * MAIN
    slots = main + size.count * TAIL
    layer_out, keep1, give1, keep2, give2, grad_mid, grad_attn, grad_gain, delta = call(
        functools.partial(mlp_kernel, size),
        "feed_forward",
        [
            ((width, tok_rows), BF),
            ((main // 2, size.back_first), BF), ((main // 2, size.back_first), BF),
            ((main // 2, size.back_second), BF), ((main // 2, size.back_second), BF),
            ((tok_rows, width), F32), ((tok_rows, width), BF), ((1, width), F32),
            ((width // HEAD_DIM, 1, tok_rows), F32),
        ],
        [
            ((slots, ff), BF), ((slots, ff), BF), ((slots, size.wide), BF), ((ff, size.wide), BF),
            ((tok_rows, width), F32), ((tok_rows, slots), BF), ((slots, tok_rows), BF),
            ((width, slots), BF), ((tok_rows, width), F32), ((tok_rows, slots), F32),
            ((ff, size.wide), BF), ((size.count * TAIL, 2 * ff), BF),
            ((size.count * TAIL, size.wide), BF), ((main, size.piece + 128), BF),
        ],
        21,
        (
            me, attn, tokens, cotangent, flat, *b1_parts, *b2_parts,
        ),
        28,
    )

    got1 = blocks.swap(give1, blocks.core)
    got2 = blocks.swap(give2, blocks.core)
    shape = (2, 2, blocks.zs, MAIN, -1)
    h1 = blocks.add(keep1, got1).reshape(shape)
    h2 = blocks.add(keep2, got2).reshape(shape)
    dq_others, give_kv = attention_grad(q_rot, kv_got, grad_attn, lse, delta, info, docs)
    got_kv = blocks.swap(give_kv, blocks.x)
    dq_others, h1, h2 = tie(dq_others, h1, h2)
    h1 = blocks.add(h1[0], blocks.swap(h1[1], blocks.y))
    h2 = blocks.add(h2[:, 0], blocks.swap(h2[:, 1], blocks.x))
    grad_q_rot, own_kv = attention_grad(
        q_rot, kv_mine, grad_attn, lse, delta, info, docs, dq_others
    )
    got_kv, h1, h2 = tie(got_kv, h1, h2)
    h1 = blocks.add(h1[0], blocks.swap(h1[1], blocks.x))
    h2 = blocks.add(h2[0], blocks.swap(h2[1], blocks.y))

    gx, keep_a, give_a = call(
        functools.partial(post_kernel, size),
        "norm_qkv_back",
        [
            ((width, tok_rows), F32), ((a_rows // 2, size.a_width), BF),
            ((a_rows // 2, size.a_width), BF),
        ],
        [
            ((tok_rows, width + kv_width), F32), ((tok_rows, size.a_width), BF),
            ((1, size.flat), F32),
        ],
        6,
        (
            me, grad_q_rot, own_kv, got_kv, cos, sin, n1t, a_mine,
            a_other, tokens, grad_mid, flat, grad_gain,
        ),
        24,
    )
    held = blocks.add(keep_a, blocks.swap(give_a, blocks.core))
    held, h2 = tie(held, h2)
    held = held.reshape(2, 2, blocks.zs, size.tall, size.a_width)
    held = blocks.add(held[0], blocks.swap(held[1], blocks.y))
    held, share2, h1 = tie(held, blocks.sum_z(h2), h1)
    held = blocks.add(held[0], blocks.swap(held[1], blocks.x))
    held, share1 = tie(held, blocks.sum_z(h1))
    share_a = blocks.sum_z(held)

    tails = tail_unpack(share1[:, size.tail : size.tail + size.piece], 2 * ff)
    tail_o = tail_unpack(share1[:, size.tail_o : size.tail_o + 128], width)
    share_out = jnp.concatenate([share1[:, size.out : size.out + width], tail_o], axis=0)
    share_gate = jnp.concatenate([share1[:, :ff], tails[:, :ff]], axis=0)
    share_up = jnp.concatenate([share2[:, :ff], tails[:, ff:]], axis=0)
    downs = [size.down_back_at(c) for c in range(size.downs)]
    share_down = jnp.concatenate(
        [(share1, share2)[which][:, at : at + width] for which, at in downs], axis=0
    )
    ends = (width, width + kv_width, size.qkv)
    return (
        layer_out.T, gx.T, share_a[:rows, : ends[0]].reshape(-1),
        share_a[:rows, ends[0] : ends[1]].reshape(-1),
        share_a[:rows, ends[1] : ends[2]].reshape(-1),
        share_out.reshape(-1), share_gate.reshape(-1), share_up.reshape(-1),
        share_down.reshape(-1), share_a[rows, : size.vec],
    )


def local(
    tokens, q_weight, k_weight, v_weight, o_weight, gate_weight, up_weight, down_weight,
    vectors, doc_lengths, cotangent,
):
    tok_rows, width = tokens.shape
    ctx_count = lax.axis_size("ctx")
    dp_count = lax.axis_size("dp")
    count = dp_count * ctx_count
    seq_tokens = tok_rows * ctx_count
    ctx_index = lax.axis_index("ctx")
    heads = width // HEAD_DIM
    kv_width = KV_HEADS * HEAD_DIM
    ff = gate_weight.shape[0] * count // width

    position_all = doc_layout(doc_lengths[0], seq_tokens)
    offset = ctx_index * tok_rows
    position_mine = lax.dynamic_slice_in_dim(position_all, offset, tok_rows)
    docs = doc_lengths.shape[1]
    others = (ctx_count - 1 - ctx_index) * tok_rows
    heads_of = jnp.stack([ctx_index, others, offset]).astype(jnp.int32)
    info = jnp.concatenate([heads_of, jnp.cumsum(doc_lengths[0])[:-1].astype(jnp.int32)])
    half = HEAD_DIM // 2
    freq = THETA ** (-jnp.arange(half, dtype=F32) * 2.0 / HEAD_DIM)
    position_f = position_mine.astype(F32)[:, None]

    whole_rows = width % count == 0 and ff % count == 0
    if whole_rows and ctx_count == 2 and dp_count % 4 == 0 and count & (count - 1) == 0:
        size = Sizes(width, ff, dp_count, ctx_count, vectors.shape[0], kv_width)
        if size.fits() and (width + kv_width) % 128 == 0:
            angle = position_f * jnp.tile(freq, 128 // half)[None, :]
            sign = np.where(np.arange(128) % HEAD_DIM < half, -1.0, 1.0).astype(np.float32)
            pos = (info, docs, jnp.cos(angle), jnp.sin(angle) * sign)
            args = (
                tokens, q_weight, k_weight, v_weight, o_weight, gate_weight, up_weight,
                down_weight, vectors, cotangent,
            )
            return local_blocks(size, Blocks(dp_count, ctx_count), pos, args)

    angle = position_f * freq[None, :]
    cosine = jnp.cos(angle)[:, None, :]
    sine = jnp.sin(angle)[:, None, :]
    inputs = tokens.astype(F32)
    inv_first = lax.rsqrt(jnp.mean(inputs * inputs, axis=-1, keepdims=True) + EPS)

    def whole(part):
        return lax.all_gather(part, AXES, axis=0, tiled=True)

    w_qkv = jnp.concatenate(
        [whole(w).reshape(width, -1) for w in (q_weight, k_weight, v_weight)], axis=1
    )
    w_out = whole(o_weight).reshape(width, width)
    w_gate = whole(gate_weight).reshape(width, ff)
    w_up = whole(up_weight).reshape(width, ff)
    w_down = whole(down_weight).reshape(ff, width)
    flat = whole(vectors).astype(F32)
    ends = [width, width + kv_width, width + 2 * kv_width, 2 * width + 2 * kv_width]
    gain_attn = flat[ends[2] : ends[3]]
    gain_mlp = flat[ends[3] : ends[3] + width]

    n_first = (inputs * inv_first * gain_attn).astype(BF)
    qkv = times(n_first, w_qkv) + flat[: ends[2]]
    q_rot = turn(qkv[:, :width].reshape(tok_rows, heads, HEAD_DIM), cosine, sine)
    q_rot = q_rot.astype(BF).reshape(tok_rows, width)
    k_rot = turn(qkv[:, width : ends[1]].reshape(tok_rows, KV_HEADS, HEAD_DIM), cosine, sine)
    k_rot = k_rot.astype(BF).reshape(tok_rows, kv_width)
    kv_mine = jnp.concatenate([k_rot, qkv[:, ends[1] :].astype(BF)], axis=1)
    kv = (lax.all_gather(kv_mine, "ctx", axis=0, tiled=True),)
    info = info.at[0].set(1)
    attn, lse = attention(q_rot, kv, info, docs, seq_tokens, False)
    mid = inputs + times(attn, w_out)
    inv_second = lax.rsqrt(jnp.mean(mid * mid, axis=-1, keepdims=True) + EPS)
    n_second = (mid * inv_second * gain_mlp).astype(BF)
    gate = times(n_second, w_gate)
    up_val = times(n_second, w_up)
    sig = jax.nn.sigmoid(gate)
    act = gate * sig
    hidden = (act * up_val).astype(BF)
    layer_out = (mid + times(hidden, w_down)).astype(BF)

    grad_wdown = inner_rows(hidden, cotangent)
    grad_hidden = times_back(cotangent, w_down)
    grad_gate = (grad_hidden * up_val * (sig * (1.0 + gate * (1.0 - sig)))).astype(BF)
    grad_up = (grad_hidden * act).astype(BF)
    grad_wgate = inner_rows(n_second, grad_gate)
    grad_wup = inner_rows(n_second, grad_up)
    grad_n2 = times_back(grad_gate, w_gate) + times_back(grad_up, w_up)
    grad_mid_norm, grad_gain_mlp = norm_back(mid, inv_second, gain_mlp, grad_n2)
    grad_mid = cotangent.astype(F32) + grad_mid_norm
    grad_branch = grad_mid.astype(BF)
    grad_wout = inner_rows(attn, grad_branch)
    grad_attn = times_back(grad_branch, w_out).astype(BF)
    grad_q_rot, grad_kv = attention_back(
        q_rot, kv, grad_attn, lse, info, docs, seq_tokens, False, 0, KV_HEADS
    )
    grad_kv_mine = lax.psum_scatter(
        grad_kv.astype(BF), "ctx", scatter_dimension=0, tiled=True
    ).astype(F32)
    grad_q = turn(grad_q_rot.reshape(tok_rows, heads, HEAD_DIM), cosine, -sine)
    grad_k = turn(
        grad_kv_mine[:, :kv_width].reshape(tok_rows, KV_HEADS, HEAD_DIM), cosine, -sine
    )
    grad_qkv = jnp.concatenate(
        [
            grad_q.reshape(tok_rows, width).astype(BF),
            grad_k.reshape(tok_rows, kv_width).astype(BF),
            grad_kv_mine[:, kv_width:].astype(BF),
        ],
        axis=1,
    )
    grad_wqkv = inner_rows(n_first, grad_qkv)
    grad_bias = jnp.sum(grad_qkv.astype(F32), axis=0)
    grad_n1 = times_back(grad_qkv, w_qkv)
    grad_x_norm, grad_gain_attn = norm_back(inputs, inv_first, gain_attn, grad_n1)
    input_grad = grad_mid + grad_x_norm
    used = 3 * width + 2 * kv_width
    padding = jnp.zeros((vectors.shape[0] * count - used,), F32)
    vector_term = jnp.concatenate([grad_bias, grad_gain_attn, grad_gain_mlp, padding])

    def shares(term):
        return lax.psum_scatter(term.reshape(-1), AXES, scatter_dimension=0, tiled=True)

    return (
        layer_out, input_grad, shares(grad_wqkv[:, :width]),
        shares(grad_wqkv[:, width : ends[1]]), shares(grad_wqkv[:, ends[1] :]),
        shares(grad_wout), shares(grad_wgate), shares(grad_wup), shares(grad_wdown),
        shares(vector_term),
    )


def solution(mesh):
    split = P(AXES)
    rows = P(AXES, None)
    in_specs = (rows,) + (split,) * 8 + (P("dp", None), rows)
    out_specs = (rows, rows) + (split,) * 8
    return jax.shard_map(local, mesh=mesh, in_specs=in_specs, out_specs=out_specs, check_vma=False)
```

```python
import functools

import jax
import jax.numpy as jnp
import numpy as np
from jax import lax
from jax.experimental import pallas as pl
from jax.experimental.pallas import tpu as pltpu
from jax.sharding import PartitionSpec as P

KV_HEADS = 3
HEAD_DIM = 64

EPS = 1e-06
THETA = 100000.0
NEG_FILL = -1e30
AXES = ("dp", "ctx")
BF = jnp.bfloat16
F32 = jnp.float32


def times(left, right):
    return jnp.dot(left, right, preferred_element_type=F32)


def inner_rows(left, right):
    return lax.dot_general(left, right, (((0,), (0,)), ((), ())), preferred_element_type=F32)


def times_back(left, right):
    return lax.dot_general(left, right, (((1,), (1,)), ((), ())), preferred_element_type=F32)


def norm_back(values, inv, gain, grad):
    scaled = grad * gain
    dot = jnp.mean(scaled * values, axis=-1, keepdims=True)
    grad_values = inv * scaled - values * (inv * inv * inv * dot)
    grad_gain = jnp.sum(grad * values * inv, axis=0)
    return grad_values, grad_gain


def turn(values, cosine, sine):
    half = values.shape[-1] // 2
    first = values[..., :half]
    second = values[..., half:]
    return jnp.concatenate(
        [first * cosine - second * sine, second * cosine + first * sine], axis=-1
    )


def doc_layout(lengths, count):
    ends = jnp.cumsum(lengths)
    place = jnp.arange(count, dtype=jnp.int32)
    segment = jnp.sum((place[:, None] >= ends[None, :-1]).astype(jnp.int32), axis=1)
    starts = ends - lengths
    picked = segment[:, None] == jnp.arange(lengths.shape[0], dtype=jnp.int32)[None, :]
    first = jnp.sum(jnp.where(picked, starts[None, :], 0), axis=1)
    return place - first


def fill_bias(bias, info, docs, short, own=None):
    total, rows = bias.shape
    row_q = lax.broadcasted_iota(jnp.int32, (1, rows), 1) + info[2]
    first = jnp.zeros_like(row_q)
    for j in range(docs - 1):
        first = jnp.where(row_q >= info[3 + j], info[3 + j], first)
    parts = ((0, total, 0),)
    if own is not None:
        parts = ((0, total, info[2] if own else info[1]),)
    elif short < total:
        parts = ((0, total - short, info[1]), (total - short, total, info[2]))
    for start, stop, base in parts:
        row_k = lax.broadcasted_iota(jnp.int32, (stop - start, rows), 0)
        allowed = (row_k >= first - base) & (row_k <= row_q - base)
        bias[start:stop] = jnp.where(allowed, 0.0, NEG_FILL)


def key_range(full, total, short, rows, block, at, causal):
    start = 0 if full else total - short
    stop = total - rows + (at + 1) * block if causal else total
    return start, stop


def key_parts(kv_refs):
    at = 0
    for kv_ref in kv_refs:
        yield slice(at, at + kv_ref.shape[0]), kv_ref
        at += kv_ref.shape[0]


def attn_fwd_kernel(
    heads, block, short, causal, docs, info, q_ref, *refs,
):
    kv_refs, (out_ref, lse_ref, qs, ks, vts, bias, out_t) = refs[:-7], refs[-7:]
    rows = q_ref.shape[0]
    total = bias.shape[0]
    kv_width = KV_HEADS * HEAD_DIM
    group = heads // KV_HEADS
    fill_bias(bias, info, docs, short)
    for h in range(heads):
        qs[h] = q_ref[:, h * HEAD_DIM : (h + 1) * HEAD_DIM] * BF(HEAD_DIM**-0.5)
    for at, kv_ref in key_parts(kv_refs):
        for g in range(KV_HEADS):
            ks[g, at] = kv_ref[:, g * HEAD_DIM : (g + 1) * HEAD_DIM]
        vts[:, at] = jnp.transpose(kv_ref[:, kv_width:].astype(F32)).astype(BF)

    def run(full):
        @pl.loop(0, KV_HEADS)
        def _(g):
            v_rows = pl.ds(pl.multiple_of(g * HEAD_DIM, HEAD_DIM), HEAD_DIM)
            for j in range(group):
                h = g * group + j
                out_rows = pl.ds(pl.multiple_of(h * HEAD_DIM, HEAD_DIM), HEAD_DIM)
                for at in range(rows // block):
                    start, stop = key_range(full, total, short, rows, block, at, causal)
                    cols = slice(at * block, (at + 1) * block)
                    s = times_back(ks[g, start:stop], qs[h, cols])
                    s = s + bias[start:stop, cols]
                    top = jnp.max(s, axis=0, keepdims=True)
                    p = jnp.exp(s - top)
                    total_p = jnp.sum(p, axis=0, keepdims=True)
                    o = times(vts[v_rows, start:stop], p.astype(BF))
                    out_t[out_rows, cols] = o / total_p
                    lse_ref[h, :, cols] = top + jnp.log(total_p)

    pl.when(info[0] != 0)(lambda: run(True))
    pl.when(info[0] == 0)(lambda: run(False))
    out_ref[...] = jnp.transpose(out_t[...]).astype(BF)


def attn_own_kernel(
    heads, block, docs, info, q_ref, kv_ref, acc, top_ref, sum_ref, qs, ks, vts, bias
):
    rows = q_ref.shape[0]
    kv_width = KV_HEADS * HEAD_DIM
    group = heads // KV_HEADS
    fill_bias(bias, info, docs, rows, own=True)
    for h in range(heads):
        qs[h] = q_ref[:, h * HEAD_DIM : (h + 1) * HEAD_DIM] * BF(HEAD_DIM**-0.5)
    for g in range(KV_HEADS):
        ks[g] = kv_ref[:, g * HEAD_DIM : (g + 1) * HEAD_DIM]
    vts[...] = jnp.transpose(kv_ref[:, kv_width:].astype(F32)).astype(BF)

    @pl.loop(0, heads)
    def _(h):
        g = h // group
        v_rows = pl.ds(pl.multiple_of(g * HEAD_DIM, HEAD_DIM), HEAD_DIM)
        out_rows = pl.ds(pl.multiple_of(h * HEAD_DIM, HEAD_DIM), HEAD_DIM)
        for at in range(rows // block):
            stop = (at + 1) * block
            cols = slice(at * block, stop)
            s = times_back(ks[g, :stop], qs[h, cols]) + bias[:stop, cols]
            top = jnp.max(s, axis=0, keepdims=True)
            p = jnp.exp(s - top)
            top_ref[h, :, cols] = top
            sum_ref[h, :, cols] = jnp.sum(p, axis=0, keepdims=True)
            acc[out_rows, cols] = times(vts[v_rows, :stop], p.astype(BF))


def attn_others_kernel(
    heads, block, docs, info, q_ref, kv_ref, acc, top_ref, sum_ref, out_ref, lse_ref,
    qs, ks, vts, bias, out_t,
):
    rows = q_ref.shape[0]
    kv_width = KV_HEADS * HEAD_DIM
    group = heads // KV_HEADS

    @pl.when(info[0] == 0)
    def _():
        for h in range(heads):
            at = slice(h * HEAD_DIM, (h + 1) * HEAD_DIM)
            out_t[at] = acc[at] / sum_ref[h]
            lse_ref[h] = top_ref[h] + jnp.log(sum_ref[h])

    @pl.when(info[0] != 0)
    def _():
        fill_bias(bias, info, docs, rows, own=False)
        for h in range(heads):
            qs[h] = q_ref[:, h * HEAD_DIM : (h + 1) * HEAD_DIM] * BF(HEAD_DIM**-0.5)
        for g in range(KV_HEADS):
            ks[g] = kv_ref[:, g * HEAD_DIM : (g + 1) * HEAD_DIM]
        vts[...] = jnp.transpose(kv_ref[:, kv_width:].astype(F32)).astype(BF)

        @pl.loop(0, heads)
        def _(h):
            g = h // group
            v_rows = pl.ds(pl.multiple_of(g * HEAD_DIM, HEAD_DIM), HEAD_DIM)
            out_rows = pl.ds(pl.multiple_of(h * HEAD_DIM, HEAD_DIM), HEAD_DIM)
            for at in range(rows // block):
                cols = slice(at * block, (at + 1) * block)
                s = times_back(ks[g], qs[h, cols]) + bias[:, cols]
                own = top_ref[h, :, cols]
                top = jnp.maximum(own, jnp.max(s, axis=0, keepdims=True))
                scale = jnp.exp(own - top)
                p = jnp.exp(s - top)
                total_p = sum_ref[h, :, cols] * scale + jnp.sum(p, axis=0, keepdims=True)
                o = acc[out_rows, cols] * scale + times(vts[v_rows], p.astype(BF))
                out_t[out_rows, cols] = o / total_p
                lse_ref[h, :, cols] = top + jnp.log(total_p)

    out_ref[...] = jnp.transpose(out_t[...]).astype(BF)


def attn_grad_kernel(
    heads, block, docs, own, info, q_ref, kv_ref, do_ref, lse_ref, delta_ref, *refs
):
    refs, (qs, dos, ks, vs, kts, bias, dk, dv) = refs[:-8], refs[-8:]
    if own:
        before, dq_ref, dkv_ref, dq_t = refs
    else:
        dq_t, dkv_ref = refs
    rows = q_ref.shape[0]
    kv_width = KV_HEADS * HEAD_DIM
    group = heads // KV_HEADS
    dk[...] = jnp.zeros_like(dk)
    dv[...] = jnp.zeros_like(dv)

    def run():
        fill_bias(bias, info, docs, rows, own=own)
        for h in range(heads):
            at = slice(h * HEAD_DIM, (h + 1) * HEAD_DIM)
            qs[h] = q_ref[:, at] * BF(HEAD_DIM**-0.5)
            dos[h] = do_ref[:, at]
        for g in range(KV_HEADS):
            lo = g * HEAD_DIM
            ks[g] = kv_ref[:, lo : lo + HEAD_DIM]
            vs[g] = kv_ref[:, kv_width + lo : kv_width + lo + HEAD_DIM]
        kts[...] = jnp.transpose(kv_ref[:, :kv_width].astype(F32)).astype(BF)

        @pl.loop(0, heads)
        def _(h):
            g = h // group
            k_rows = pl.ds(pl.multiple_of(g * HEAD_DIM, HEAD_DIM), HEAD_DIM)
            out_rows = pl.ds(pl.multiple_of(h * HEAD_DIM, HEAD_DIM), HEAD_DIM)
            for at in range(rows // block):
                stop = (at + 1) * block if own else rows
                cols = slice(at * block, (at + 1) * block)
                q = qs[h, cols]
                do = dos[h, cols]
                s = times_back(ks[g, :stop], q) + bias[:stop, cols]
                p = jnp.exp(s - lse_ref[h, :, cols])
                dp = times_back(vs[g, :stop], do)
                ds = (p * (dp - delta_ref[h, :, cols])).astype(BF)
                dk[g, :stop] += times(ds, q)
                dv[g, :stop] += times(p.astype(BF), do)
                dq = times(kts[k_rows, :stop], ds) * HEAD_DIM**-0.5
                dq_t[out_rows, cols] = before[out_rows, cols] + dq if own else dq

    if own:
        run()
        dq_ref[...] = jnp.transpose(dq_t[...])
    else:
        pl.when(info[0] != 0)(run)

        @pl.when(info[0] == 0)
        def _():
            dq_t[...] = jnp.zeros_like(dq_t)

    for g in range(KV_HEADS):
        lo = g * HEAD_DIM
        dkv_ref[:, lo : lo + HEAD_DIM] = dk[g].astype(dkv_ref.dtype)
        dkv_ref[:, kv_width + lo : kv_width + lo + HEAD_DIM] = dv[g].astype(dkv_ref.dtype)


def attn_bwd_kernel(
    heads, block, short, causal, docs, g0, g1, parts, info, q_ref, do_ref, lse_ref, *refs,
):
    kv_refs, outs, scratch = refs[:parts], refs[parts:-9], refs[-9:]
    qs, ks, vs, kts, dos, bias, dq_t, dk, dv = scratch
    rows = q_ref.shape[0]
    total = bias.shape[0]
    kv_width = KV_HEADS * HEAD_DIM
    group = heads // KV_HEADS
    keys = g1 - g0
    fill_bias(bias, info, docs, short)
    for h in range(keys * group):
        lanes = slice((g0 * group + h) * HEAD_DIM, (g0 * group + h + 1) * HEAD_DIM)
        qs[h] = q_ref[:, lanes] * BF(HEAD_DIM**-0.5)
        dos[h] = do_ref[:, lanes]
    for g in range(keys):
        lo = (g0 + g) * HEAD_DIM
        for at, kv_ref in key_parts(kv_refs):
            ks[g, at] = kv_ref[:, lo : lo + HEAD_DIM]
            vs[g, at] = kv_ref[:, kv_width + lo : kv_width + lo + HEAD_DIM]
        kts[g] = jnp.transpose(ks[g].astype(F32)).astype(BF)
    dk[...] = jnp.zeros_like(dk)
    dv[...] = jnp.zeros_like(dv)

    def run(full):
        @pl.loop(0, keys * group)
        def _(h):
            g = h // group if keys > 1 else 0
            out_rows = pl.ds(pl.multiple_of(h * HEAD_DIM, HEAD_DIM), HEAD_DIM)
            for at in range(rows // block):
                start, stop = key_range(full, total, short, rows, block, at, causal)
                cols = slice(at * block, (at + 1) * block)
                q = qs[h, cols]
                do = dos[h, cols]
                s = times_back(ks[g, start:stop], q)
                p = jnp.exp(s + bias[start:stop, cols] - lse_ref[g0 * group + h, :, cols])
                dp = times_back(vs[g, start:stop], do)
                t = p * dp
                inner = jnp.sum(t, axis=0, keepdims=True)
                ds = (t - p * inner).astype(BF)
                dk[g, start:stop] += times(ds, q)
                dv[g, start:stop] += times(p.astype(BF), do)
                dq_t[out_rows, cols] = times(kts[g, :, start:stop], ds) * HEAD_DIM**-0.5

    pl.when(info[0] != 0)(lambda: run(True))
    pl.when(info[0] == 0)(lambda: run(False))
    outs[0][...] = jnp.transpose(dq_t[...])
    cut = total - outs[1].shape[0]
    for part, out in ((slice(cut, total), outs[1]),) + tuple((slice(0, cut), o) for o in outs[2:]):
        for g in range(keys):
            lo = g * HEAD_DIM
            out[:, lo : lo + HEAD_DIM] = dk[g, part].astype(out.dtype)
            lo += keys * HEAD_DIM
            out[:, lo : lo + HEAD_DIM] = dv[g, part].astype(out.dtype)


VM = pl.BlockSpec(memory_space=pltpu.VMEM)
SM = pl.BlockSpec(memory_space=pltpu.SMEM)


def cost_of(micros):
    return pl.CostEstimate(
        flops=int(micros * 1.1e9), bytes_accessed=2**20, transcendentals=0
    )


def attention(q, kv, info, docs, short, causal):
    rows, width = q.shape
    total = sum(part.shape[0] for part in kv)
    heads = width // HEAD_DIM
    block = min(rows, 256)
    return pl.pallas_call(
        functools.partial(attn_fwd_kernel, heads, block, short, causal, docs),
        out_shape=(
            jax.ShapeDtypeStruct((rows, width), BF),
            jax.ShapeDtypeStruct((heads, 1, rows), F32),
        ),
        in_specs=[SM] + [VM] * (1 + len(kv)),
        out_specs=(VM, VM),
        scratch_shapes=[
            pltpu.VMEM((heads, rows, HEAD_DIM), BF),
            pltpu.VMEM((KV_HEADS, total, HEAD_DIM), BF),
            pltpu.VMEM((KV_HEADS * HEAD_DIM, total), BF),
            pltpu.VMEM((total, rows), F32),
            pltpu.VMEM((width, rows), F32),
        ],
        compiler_params=pltpu.CompilerParams(vmem_limit_bytes=20 * 2**20),
        cost_estimate=cost_of(14),
        name="attn_fwd",
    )(info, q, *kv)


def attention_own(q, kv, info, docs):
    rows, width = q.shape
    heads = width // HEAD_DIM
    stat = jax.ShapeDtypeStruct((heads, 1, rows), F32)
    return pl.pallas_call(
        functools.partial(attn_own_kernel, heads, min(rows, 256), docs),
        out_shape=(jax.ShapeDtypeStruct((width, rows), F32), stat, stat),
        in_specs=[SM, VM, VM],
        out_specs=(VM, VM, VM),
        scratch_shapes=attn_scratch(rows, heads),
        compiler_params=pltpu.CompilerParams(vmem_limit_bytes=16 * 2**20),
        cost_estimate=cost_of(6),
        name="attn_own",
    )(info, q, kv)


def attn_scratch(rows, heads):
    return [
        pltpu.VMEM((heads, rows, HEAD_DIM), BF),
        pltpu.VMEM((KV_HEADS, rows, HEAD_DIM), BF),
        pltpu.VMEM((KV_HEADS * HEAD_DIM, rows), BF),
        pltpu.VMEM((rows, rows), F32),
    ]


def attention_grad(q, kv, grad_out, lse, delta, info, docs, before=None):
    rows, width = q.shape
    heads = width // HEAD_DIM
    own = before is not None
    turned = jax.ShapeDtypeStruct((width, rows), F32)
    if own:
        outs = [jax.ShapeDtypeStruct((rows, width), F32), jax.ShapeDtypeStruct(kv.shape, F32)]
    else:
        outs = [turned, jax.ShapeDtypeStruct(kv.shape, BF)]
    by_head = pltpu.VMEM((heads, rows, HEAD_DIM), BF)
    by_key = pltpu.VMEM((KV_HEADS, rows, HEAD_DIM), BF)
    sums = pltpu.VMEM((KV_HEADS, rows, HEAD_DIM), F32)
    return pl.pallas_call(
        functools.partial(attn_grad_kernel, heads, min(rows, 256), docs, own),
        out_shape=outs,
        in_specs=[SM] + [VM] * (6 if own else 5),
        out_specs=[VM] * 2,
        scratch_shapes=([pltpu.VMEM((width, rows), F32)] if own else []) + [
            by_head, by_head, by_key, by_key, pltpu.VMEM((KV_HEADS * HEAD_DIM, rows), BF),
            pltpu.VMEM((rows, rows), F32), sums, sums,
        ],
        compiler_params=pltpu.CompilerParams(vmem_limit_bytes=20 * 2**20),
        cost_estimate=cost_of(2.5),
        name="attn_grad_own" if own else "attn_grad_others",
    )(info, q, kv, grad_out, lse, delta, *([before] if own else []))


def attention_others(q, kv, acc, top, total, info, docs):
    rows, width = q.shape
    heads = width // HEAD_DIM
    return pl.pallas_call(
        functools.partial(attn_others_kernel, heads, min(rows, 256), docs),
        out_shape=(
            jax.ShapeDtypeStruct((rows, width), BF),
            jax.ShapeDtypeStruct((heads, 1, rows), F32),
        ),
        in_specs=[SM] + [VM] * 5,
        out_specs=(VM, VM),
        scratch_shapes=attn_scratch(rows, heads) + [pltpu.VMEM((width, rows), F32)],
        compiler_params=pltpu.CompilerParams(vmem_limit_bytes=16 * 2**20),
        cost_estimate=cost_of(10),
        name="attn_others",
    )(info, q, kv, acc, top, total)


def attention_back(q, kv, grad_out, lse, info, docs, short, causal, g0, g1):
    rows, width = q.shape
    total = sum(part.shape[0] for part in kv)
    heads = width // HEAD_DIM
    block = min(rows, 256)
    keys = g1 - g0
    mine = heads // KV_HEADS * keys
    outs = [jax.ShapeDtypeStruct((rows, mine * HEAD_DIM), F32)]
    if causal:
        outs.append(jax.ShapeDtypeStruct((rows, 2 * keys * HEAD_DIM), F32))
        outs.append(jax.ShapeDtypeStruct((total - rows, 2 * keys * HEAD_DIM), BF))
    else:
        outs.append(jax.ShapeDtypeStruct((total, 2 * keys * HEAD_DIM), F32))
    return pl.pallas_call(
        functools.partial(attn_bwd_kernel, heads, block, short, causal, docs, g0, g1, len(kv)),
        out_shape=outs,
        in_specs=[SM] + [VM] * (3 + len(kv)),
        out_specs=[VM] * len(outs),
        scratch_shapes=[
            pltpu.VMEM((mine, rows, HEAD_DIM), BF),
            pltpu.VMEM((keys, total, HEAD_DIM), BF),
            pltpu.VMEM((keys, total, HEAD_DIM), BF),
            pltpu.VMEM((keys, HEAD_DIM, total), BF),
            pltpu.VMEM((mine, rows, HEAD_DIM), BF),
            pltpu.VMEM((total, rows), F32),
            pltpu.VMEM((mine * HEAD_DIM, rows), F32),
            pltpu.VMEM((keys, total, HEAD_DIM), F32),
            pltpu.VMEM((keys, total, HEAD_DIM), F32),
        ],
        compiler_params=pltpu.CompilerParams(vmem_limit_bytes=20 * 2**20),
        cost_estimate=cost_of(20),
        name="attn_bwd",
    )(info, q, grad_out, lse, *kv)


TAIL = 2
MAIN = 16
PIECES = MAIN // TAIL


class Blocks:
    def __init__(self, dp_count, ctx_count):
        self.count = dp_count * ctx_count
        self.x = 1
        self.core = ctx_count
        self.y = 2 * ctx_count
        self.z = 4 * ctx_count
        self.zs = dp_count // 4
        self.masks = []
        for p in range(self.count):
            z, x = p % self.zs, p // self.zs % 2
            y, core = p // (2 * self.zs) % 2, p // (4 * self.zs)
            self.masks.append(x * self.x + y * self.y + core * self.core + z * self.z)

    def swap(self, values, mask):
        perm = [(i, i ^ mask) for i in range(self.count)]
        return lax.ppermute(values, AXES, perm)

    def along_z(self, mine):
        return jnp.stack([mine] + [self.swap(mine, d * self.z) for d in range(1, self.zs)])

    def add(self, keep, got):
        return (keep.astype(F32) + got.astype(F32)).astype(BF)

    def sum_z(self, held):
        got = [self.swap(held[d], d * self.z).astype(F32) for d in range(1, self.zs)]
        return functools.reduce(jnp.add, got, held[0].astype(F32))


class Sizes:
    def __init__(self, width, ff, dp, ctx, vec, kv_width):
        count = dp * ctx
        self.zs, self.ctx = dp // 4, ctx
        self.width, self.ff, self.count, self.vec = width, ff, count, vec
        self.rows = width // count
        self.f_rows = ff // count
        up = lambda n: (n + 127) // 128 * 128
        self.wide = up(width)
        self.qkv = width + 2 * kv_width
        self.a_width = up(self.qkv)
        self.tall = (self.rows + 1 + 7) // 8 * 8
        self.downs = self.f_rows // MAIN
        self.piece = 2 * ff // PIECES
        self.gate = 0
        self.tail = ff
        self.tail_o = self.tail + self.piece
        self.out = self.tail_o + 128
        self.down0 = self.out + self.wide
        self.first = self.down0 + self.wide
        self.second = ff + (self.downs - 1) * self.wide
        self.back_first = self.down0 + (self.downs - 1) * self.wide
        self.back_second = ff + self.wide
        self.flat = self.a_width + 2 * self.wide

    def down_at(self, c):
        return (0, self.down0) if c == 0 else (1, self.ff + (c - 1) * self.wide)

    def down_back_at(self, c):
        return (0, self.down0 + c * self.wide) if c < self.downs - 1 else (1, self.ff)

    def fits(self):
        return (
            self.rows == MAIN + TAIL
            and self.f_rows % MAIN == 0
            and self.piece % 128 == 0
            and self.ff % 256 == 0
            and self.wide <= 128 * PIECES
            and self.vec <= 128
        )


def wire_kernel(
    size, g_ref, u_ref, o_ref, d_ref, xt_ref, cott_ref, out1, out2, x_any, cot_any,
    tail, tail_o, x_ref, cot_ref, sems,
):
    ff, width = size.ff, size.width
    x_ref[...] = jnp.transpose(xt_ref[...].astype(F32)).astype(BF)
    cot_ref[...] = jnp.transpose(cott_ref[...].astype(F32)).astype(BF)
    copies = fetch((x_ref, cot_ref), (x_any, cot_any), sems)
    out1[:, : ff] = g_ref[:MAIN]
    out2[:, : ff] = u_ref[:MAIN]
    out1[:, size.out : size.out + size.wide] = jnp.zeros((MAIN, size.wide), BF)
    out1[:, size.out : size.out + width] = o_ref[:MAIN]
    tail_o[...] = jnp.zeros_like(tail_o)
    odd = [ref[MAIN:].astype(F32) for ref in (g_ref, u_ref, o_ref)]
    for c in range(PIECES):
        src = odd[c * size.piece // ff]
        at = c * size.piece % ff
        tail[c * TAIL : (c + 1) * TAIL] = src[:, at : at + size.piece]
        used = min(128, width - c * 128)
        if used > 0:
            tail_o[c * TAIL : (c + 1) * TAIL, :used] = odd[2][:, c * 128 : c * 128 + used]
    out1[:, size.tail : size.tail + size.piece] = tail[...].astype(BF)
    out1[:, size.tail_o : size.tail_o + 128] = tail_o[...].astype(BF)
    for c in range(size.downs):
        which, at = size.down_at(c)
        out = (out1, out2)[which]
        out[:, at : at + size.wide] = jnp.zeros((MAIN, size.wide), BF)
        out[:, at : at + width] = d_ref[c * MAIN : (c + 1) * MAIN]
    for copy in copies:
        copy.wait()


def over(values, by):
    scale = 2**16 // by + 1
    whole = (values * scale) >> 16
    return whole, values - whole * by


def mask_of(size, p):
    z, rest = p % size.zs, p // size.zs
    x, y, core = rest % 2, rest // 2 % 2, rest // 4
    return x + core * size.ctx + y * (2 * size.ctx) + z * (4 * size.ctx)


def lanes(count):
    return lax.broadcasted_iota(jnp.int32, (1, count), 1)


def place_matrix(size, me, tall):
    if tall:
        p, inside = over(lanes(size.count * size.tall), size.tall)
        feature = jnp.where(inside < size.rows, size.rows * (me ^ mask_of(size, p)) + inside, -1)
    else:
        s = lanes(size.count * (MAIN + TAIL))
        tail = s - size.count * MAIN
        p = jnp.where(tail < 0, s // MAIN, tail // TAIL)
        inside = jnp.where(tail < 0, s % MAIN, MAIN + tail % TAIL)
        feature = size.rows * (me ^ mask_of(size, p)) + inside
    at = lax.broadcasted_iota(jnp.int32, (size.width, feature.shape[1]), 0)
    return jnp.where(at == feature, 1.0, 0.0).astype(BF)


def vector_places(size, me):
    at = lanes(size.flat)
    ends = (size.a_width, size.a_width + size.wide)
    part = jnp.where(at < ends[0], 0, jnp.where(at < ends[1], 1, 2))
    inside = at - jnp.where(part == 0, 0, jnp.where(part == 1, ends[0], ends[1]))
    start = jnp.where(part == 0, 0, jnp.where(part == 1, size.qkv, size.qkv + size.width))
    used = inside < jnp.where(part == 0, size.qkv, size.width)
    owner, lane = over(start + inside, size.vec)
    rows = lax.broadcasted_iota(jnp.int32, (128, size.flat), 0)
    spread = jnp.where((rows == lane) & used, 1.0, 0.0).astype(BF)
    p = lax.broadcasted_iota(jnp.int32, (size.count, 1), 0)
    return spread, (owner == (me ^ mask_of(size, p))) & used


def swap_halves(u):
    rolled_back = pltpu.roll(u, 128 - HEAD_DIM // 2, 1)
    rolled = pltpu.roll(u, HEAD_DIM // 2, 1)
    lane = lax.broadcasted_iota(jnp.int32, u.shape, 1)
    return jnp.where(lane % HEAD_DIM < HEAD_DIM // 2, rolled_back, rolled)


def fetch(sources, targets, sems):
    copies = [
        pltpu.make_async_copy(src, dst, sems.at[i])
        for i, (src, dst) in enumerate(zip(sources, targets))
    ]
    for copy in copies:
        copy.start()
    return copies


def pre_kernel(
    size, me_ref, x_ref, wm_ref, wo_ref, cos_ref, sin_ref,
    q_ref, kv_ref, n1t_ref, flat_ref, w, qkv,
):
    me = me_ref[0]
    half = wm_ref.shape[0]
    w[:half] = wm_ref[...]
    w[half:] = wo_ref[...]
    place = place_matrix(size, me, True)
    spread, mine = vector_places(size, me)
    shape = (size.count, 2 * half)
    row = lax.broadcasted_iota(jnp.int32, shape, 0) * size.tall + size.rows
    row = jnp.where(lax.broadcasted_iota(jnp.int32, shape, 1) == row, 1.0, 0.0).astype(BF)
    packed = times(row, w[:, :128]).astype(BF)
    flat = jnp.sum(jnp.where(mine, times(packed, spread), 0.0), axis=0, keepdims=True)
    flat_ref[...] = flat
    gain = flat[:, size.a_width : size.a_width + size.width]
    x = x_ref[...].astype(F32)
    inv = lax.rsqrt(jnp.mean(x * x, axis=-1, keepdims=True) + EPS)
    n1 = (x * inv * gain).astype(BF)
    n1a = times(n1, place)
    n1t_ref[...] = jnp.transpose(n1a).astype(BF)
    qkv[...] = times(n1a.astype(BF), w[...]) + flat[:, : size.a_width]
    kv_width = kv_ref.shape[1] // 2
    for t in range((size.width + kv_width) // 128):
        u = qkv[:, t * 128 : (t + 1) * 128]
        qkv[:, t * 128 : (t + 1) * 128] = u * cos_ref[...] + swap_halves(u) * sin_ref[...]
    q_ref[...] = qkv[:, : size.width].astype(BF)
    kv_ref[...] = qkv[:, size.width : size.qkv].astype(BF)


def tail_place(size, back):
    odd, count = size.count * TAIL, size.count * MAIN
    row = lax.broadcasted_iota(jnp.int32, (count, count), 1 if back else 0)
    at = lax.broadcasted_iota(jnp.int32, (count, count), 0 if back else 1)
    c, q = row // odd, row % odd
    want = (q // TAIL) * MAIN + c * TAIL + q % TAIL
    return jnp.where(at == want, 1.0, 0.0).astype(BF)


def mlp_kernel(
    size, me_ref, attn_ref, x_ref, cot_ref, flat_ref,
    b1_00, b1_01, b1_10, b1_11, b2_00, b2_01, b2_10, b2_11,
    out_ref, keep1, give1, keep2, give2, gmid_ref, gattn_ref, ggain_ref, delta_ref,
    wg, wu, wo, wd, mid, n2s, n2t, place, acc, gacc, dwd, tails, tail_o, packed,
):
    me = me_ref[0]
    width, ff = size.width, size.ff
    part = b1_00.shape[0]
    half, main = 2 * part, 4 * part
    rows_z = part // 2
    place[...] = place_matrix(size, me, False)
    first = (b1_00, b1_01, b1_10, b1_11)
    second = (b2_00, b2_01, b2_10, b2_11)
    room = size.piece + 128
    for i, b1 in enumerate(first):
        rows = slice(i * part, (i + 1) * part)
        wg[rows] = b1[:, :ff]
        wo[rows] = b1[:, size.out : size.out + size.wide]
        packed[rows] = b1[:, size.tail : size.tail + room]
    for i, b2 in enumerate(second):
        for y in range(2):
            at = (i // 2) * half + y * part + (i % 2) * rows_z
            wu[at : at + rows_z] = b2[y * rows_z : (y + 1) * rows_z, :ff]
    odd = size.count * TAIL
    got = times(tail_place(size, False), packed[...]).astype(BF)
    for c in range(PIECES):
        rows = slice(c * odd, (c + 1) * odd)
        target = wg if c * size.piece < ff else wu
        at = c * size.piece % ff
        target[main:, at : at + size.piece] = got[rows, : size.piece]
        if c * 128 < size.wide:
            wo[main:, c * 128 : (c + 1) * 128] = got[rows, size.piece :]
    zs = rows_z // MAIN
    for p in range(size.count):
        z, x, y, core = p % zs, p // zs % 2, p // (2 * zs) % 2, p // (4 * zs)
        owner = me ^ mask_of(size, p)
        for c in range(size.downs):
            which, at = size.down_at(c)
            src, row = (second[2 * core + x], y * zs + z) if which else (
                first[2 * core + y], x * zs + z
            )
            to = pl.multiple_of(owner * size.f_rows + c * MAIN, MAIN)
            wd[pl.ds(to, MAIN), :] = src[row * MAIN : (row + 1) * MAIN, at : at + size.wide]
    attn_s = times(attn_ref[...], place[...])
    m = x_ref[...].astype(F32) + times(attn_s.astype(BF), wo[:, :width])
    mid[...] = m
    inv = lax.rsqrt(jnp.mean(m * m, axis=-1, keepdims=True) + EPS)
    lo = size.a_width + size.wide
    gain = flat_ref[:, lo : lo + width]
    n2 = (m * inv * gain).astype(BF)
    spread = times(n2, place[...])
    n2s[...] = spread.astype(BF)
    n2t[...] = jnp.transpose(spread).astype(BF)
    acc[...] = jnp.zeros_like(acc)
    gacc[...] = jnp.zeros_like(gacc)
    step = 512 if ff % 512 == 0 else 256

    @pl.loop(0, ff // step)
    def _(b):
        at = pl.multiple_of(b * step, step)
        cols = pl.ds(at, step)
        gate = times(n2s[...], wg[:, cols])
        up = times(n2s[...], wu[:, cols])
        sig = 1.0 / (1.0 + jnp.exp(-gate))
        act = gate * sig
        h = act * up
        gh = times_back(cot_ref[...], wd[cols, :width])
        gg = (gh * up * (sig * (1.0 + gate * (1.0 - sig)))).astype(BF)
        gu = (gh * act).astype(BF)
        acc[...] += times(h.astype(BF), wd[cols, :width])
        dwd[cols, :width] = times(jnp.transpose(h).astype(BF), cot_ref[...]).astype(BF)
        gacc[...] += times_back(gg, wg[:, cols]) + times_back(gu, wu[:, cols])
        for k, (grad, keep, give) in enumerate(((gg, keep1, give1), (gu, keep2, give2))):
            dw = times(n2t[...], grad).astype(BF)
            keep[:, cols] = dw[:half]
            give[:, cols] = dw[half:main]
            tails[:, pl.ds(pl.multiple_of(k * ff + at, 128), step)] = dw[main:]

    m = mid[...]
    inv = lax.rsqrt(jnp.mean(m * m, axis=-1, keepdims=True) + EPS)
    out_ref[...] = jnp.transpose(m + acc[...]).astype(BF)
    gn2 = times_back(gacc[...].astype(BF), place[...])
    scaled = gn2 * gain
    dot = jnp.mean(scaled * m, axis=-1, keepdims=True)
    ggain_ref[...] = jnp.sum(gn2 * m * inv, axis=0, keepdims=True)
    gmid = cot_ref[...].astype(F32) + inv * scaled - m * (inv * inv * inv * dot)
    gmid_ref[...] = gmid
    branch = gmid.astype(BF)
    gattn = times_back(branch, wo[:, :width]).astype(BF)
    gattn = times_back(gattn, place[...]).astype(BF)
    gattn_ref[...] = gattn
    both = jnp.transpose(gattn.astype(F32) * attn_ref[...].astype(F32))
    for h in range(width // HEAD_DIM):
        at = slice(h * HEAD_DIM, (h + 1) * HEAD_DIM)
        delta_ref[h] = jnp.sum(both[at], axis=0, keepdims=True)
    dwo = times(jnp.transpose(attn_s).astype(BF), branch).astype(BF)
    tail_o[...] = jnp.zeros_like(tail_o)
    tail_o[:, :width] = dwo[main:]
    terms = ((keep1, keep2), (give1, give2))
    for i, (term, _) in enumerate(terms):
        term[:, size.out : size.out + width] = dwo[i * half : (i + 1) * half]
    packed[...] = jnp.zeros_like(packed)
    for c in range(PIECES):
        rows = slice(c * odd, (c + 1) * odd)
        packed[rows, : size.piece] = tails[:, c * size.piece : (c + 1) * size.piece]
        if c * 128 < size.wide:
            packed[rows, size.piece :] = tail_o[:, c * 128 : (c + 1) * 128]
    wire = times(tail_place(size, True), packed[...]).astype(BF)
    for i, (term, _) in enumerate(terms):
        rows = slice(i * half, (i + 1) * half)
        term[:, size.tail : size.tail + room] = wire[rows]
    for p in range(size.count):
        to = terms[p // (size.count // 2)]
        rows = slice(p * MAIN % half, p * MAIN % half + MAIN)
        owner = me ^ mask_of(size, p)
        for c in range(size.downs):
            which, at = size.down_back_at(c)
            src = pl.multiple_of(owner * size.f_rows + c * MAIN, MAIN)
            to[which][rows, at : at + size.wide] = dwd[pl.ds(src, MAIN), :]


def post_kernel(
    size, me_ref, dq_ref, dkv_ref, got_ref, cos_ref, sin_ref, n1t_ref,
    wm_ref, wo_ref, x_ref, gmid_ref, flat_ref, ggain_ref,
    gx_ref, keep_ref, give_ref, turn_buf, grad, vec_row,
):
    me = me_ref[0]
    width = size.width
    half = wm_ref.shape[0]
    place = place_matrix(size, me, True)
    kv_width = KV_HEADS * HEAD_DIM
    turned = width + kv_width
    dkv = dkv_ref[...] + got_ref[...].astype(F32)
    turn_buf[:, :width] = dq_ref[...]
    turn_buf[:, width:] = dkv[:, :kv_width]
    grad[...] = jnp.zeros_like(grad)
    grad[:, turned : turned + kv_width] = dkv[:, kv_width:].astype(BF)
    for t in range(turned // 128):
        u = turn_buf[:, t * 128 : (t + 1) * 128]
        back = u * cos_ref[...] - swap_halves(u) * sin_ref[...]
        grad[:, t * 128 : (t + 1) * 128] = back.astype(BF)
    g = grad[...]
    gn1 = jnp.zeros((g.shape[0], width), F32)
    for part, w_ref in enumerate((wm_ref, wo_ref)):
        values = times_back(g, w_ref[...]).astype(BF)
        gn1 += times_back(values, place[:, part * half : (part + 1) * half])
    x = x_ref[...].astype(F32)
    inv = lax.rsqrt(jnp.mean(x * x, axis=-1, keepdims=True) + EPS)
    gain = flat_ref[:, size.a_width : size.a_width + width]
    scaled = gn1 * gain
    dot = jnp.mean(scaled * x, axis=-1, keepdims=True)
    gx_ref[...] = jnp.transpose(gmid_ref[...] + inv * scaled - x * (inv * inv * inv * dot))
    vec_row[...] = jnp.zeros_like(vec_row)
    vec_row[:, : size.a_width] = jnp.sum(g.astype(F32), axis=0, keepdims=True)
    vec_row[:, size.a_width : size.a_width + width] = jnp.sum(gn1 * x * inv, axis=0, keepdims=True)
    lo = size.a_width + size.wide
    vec_row[:, lo : lo + width] = ggain_ref[...]
    spread, mine = vector_places(size, me)
    packed = times_back(jnp.where(mine, vec_row[...], 0.0).astype(BF), spread)
    shape = (half, size.count)
    for part, term in ((0, keep_ref), (1, give_ref)):
        rows = slice(part * half, (part + 1) * half)
        dw = times(n1t_ref[rows], g)
        term[...] = dw.astype(BF)
        want = lax.broadcasted_iota(jnp.int32, shape, 1) * size.tall + size.rows - part * half
        here = lax.broadcasted_iota(jnp.int32, shape, 0) == want
        extra = times(jnp.where(here, 1.0, 0.0).astype(BF), packed.astype(BF))
        term[:, :128] = (dw[:, :128] + extra).astype(BF)


def call(kernel, name, out_shape, scratch, micros, args, vmem, any_in=(), any_out=(), scalar=True):
    shapes = [jax.ShapeDtypeStruct(s, t) for s, t in out_shape]
    here = pl.BlockSpec(memory_space=pl.ANY)
    specs = [here if i in any_in else VM for i in range(len(args))]
    if scalar:
        specs[0] = SM
    return pl.pallas_call(
        kernel,
        out_shape=shapes,
        in_specs=specs,
        out_specs=[here if i in any_out else VM for i in range(len(shapes))],
        scratch_shapes=[
            pltpu.SemaphoreType.DMA(s) if t is None else pltpu.VMEM(s, t) for s, t in scratch
        ],
        compiler_params=pltpu.CompilerParams(vmem_limit_bytes=vmem * 2**20),
        cost_estimate=cost_of(micros),
        name=name,
    )(*args)


def pad_to(values, rows, columns):
    return jnp.pad(values, ((0, rows - values.shape[0]), (0, columns - values.shape[1])))


def tail_pack(rows, piece):
    rows = pad_to(rows, TAIL, PIECES * piece)
    return rows.reshape(TAIL, PIECES, piece).transpose(1, 0, 2).reshape(MAIN, piece)


def tail_unpack(wire, used):
    piece = wire.shape[1]
    rows = wire.reshape(PIECES, TAIL, piece).transpose(1, 0, 2).reshape(TAIL, PIECES * piece)
    return rows[:, :used]


def tie(*values):
    return lax.optimization_barrier(values)


def local_blocks(size, blocks, pos, args):
    (
        tokens, q_weight, k_weight, v_weight, o_weight, gate_weight, up_weight, down_weight,
        vectors, cotangent,
    ) = args
    tok_rows, width = tokens.shape
    ff, rows = size.ff, size.rows
    kv_width = KV_HEADS * HEAD_DIM
    ctx_index = lax.axis_index("ctx")
    me = (lax.axis_index("dp") * lax.axis_size("ctx") + ctx_index).astype(jnp.int32).reshape(1)
    half = size.count // 2
    info, docs, cos, sin = pos

    joined_w = jnp.concatenate(
        [w.reshape(rows, -1) for w in (q_weight, k_weight, v_weight)], axis=1
    )
    vec_row = pad_to(vectors.reshape(1, -1), size.tall - rows, size.a_width)
    wire_a = jnp.concatenate([pad_to(joined_w, rows, size.a_width), vec_row], axis=0)
    za = blocks.along_z(wire_a)
    xa = jnp.stack([za, blocks.swap(za, blocks.x)])
    _, flat_w = tie(za, (gate_weight, up_weight, o_weight, down_weight))
    w_rows = [w.reshape(rows, -1) for w in flat_w[:3]]
    wire_1, wire_2, tokens, cotangent = call(
        functools.partial(wire_kernel, size),
        "wire",
        [
            ((MAIN, size.first), BF), ((MAIN, size.second), BF), ((tok_rows, width), BF),
            ((tok_rows, width), BF),
        ],
        [
            ((MAIN, size.piece), F32), ((MAIN, 128), F32), ((tok_rows, width), BF),
            ((tok_rows, width), BF), ((2,), None),
        ],
        1,
        w_rows + [flat_w[3].reshape(size.f_rows, width), tokens.T, cotangent.T],
        10,
        any_out=(2, 3),
        scalar=False,
    )
    xa, wire_1, wire_2 = tie(xa, wire_1, wire_2)
    ya = blocks.swap(xa, blocks.y)
    z1 = blocks.along_z(wire_1)
    z1, wire_2, ya = tie(z1, wire_2, ya)
    z2 = blocks.along_z(wire_2)
    x1 = jnp.stack([z1, blocks.swap(z1, blocks.x)])
    a_mine = jnp.stack([xa, ya]).reshape(half * size.tall, size.a_width)
    a_other = blocks.swap(a_mine, blocks.core)

    a_rows = size.count * size.tall
    q_rot, kv_mine, n1t, flat = call(
        functools.partial(pre_kernel, size),
        "norm_qkv",
        [
            ((tok_rows, width), BF), ((tok_rows, 2 * kv_width), BF), ((a_rows, tok_rows), BF),
            ((1, size.flat), F32),
        ],
        [((a_rows, size.a_width), BF), ((tok_rows, size.a_width), F32)],
        3,
        (me, tokens, a_mine, a_other, cos, sin),
        16,
    )
    kv_got = blocks.swap(kv_mine, blocks.x)
    own = attention_own(q_rot, kv_mine, info, docs)
    z2, x1 = tie(z2, x1, kv_mine)[:2]
    y2 = jnp.stack([z2, blocks.swap(z2, blocks.y)])
    b1_parts = [b.reshape(half // 2 * MAIN, -1) for b in (x1, blocks.swap(x1, blocks.y))]
    b2_parts = [b.reshape(half // 2 * MAIN, -1) for b in (y2, blocks.swap(y2, blocks.x))]
    attn, lse = attention_others(q_rot, kv_got, *own, info, docs)

    b1_parts[1:] = [b1_parts[1], blocks.swap(b1_parts[0], blocks.core)]
    b2_parts[1:] = [b2_parts[1], blocks.swap(b2_parts[0], blocks.core)]
    attn, b2_parts[1] = tie(attn, b2_parts[1])
    attn, b1_parts[1] = tie(attn, b1_parts[1])
    b2_parts.append(blocks.swap(b2_parts[1], blocks.core))
    b1_parts.append(blocks.swap(b1_parts[1], blocks.core))
    main = size.count * MAIN
    slots = main + size.count * TAIL
    layer_out, keep1, give1, keep2, give2, grad_mid, grad_attn, grad_gain, delta = call(
        functools.partial(mlp_kernel, size),
        "feed_forward",
        [
            ((width, tok_rows), BF),
            ((main // 2, size.back_first), BF), ((main // 2, size.back_first), BF),
            ((main // 2, size.back_second), BF), ((main // 2, size.back_second), BF),
            ((tok_rows, width), F32), ((tok_rows, width), BF), ((1, width), F32),
            ((width // HEAD_DIM, 1, tok_rows), F32),
        ],
        [
            ((slots, ff), BF), ((slots, ff), BF), ((slots, size.wide), BF), ((ff, size.wide), BF),
            ((tok_rows, width), F32), ((tok_rows, slots), BF), ((slots, tok_rows), BF),
            ((width, slots), BF), ((tok_rows, width), F32), ((tok_rows, slots), F32),
            ((ff, size.wide), BF), ((size.count * TAIL, 2 * ff), BF),
            ((size.count * TAIL, size.wide), BF), ((main, size.piece + 128), BF),
        ],
        21,
        (
            me, attn, tokens, cotangent, flat, *b1_parts, *b2_parts,
        ),
        28,
    )

    got1 = blocks.swap(give1, blocks.core)
    got2 = blocks.swap(give2, blocks.core)
    shape = (2, 2, blocks.zs, MAIN, -1)
    h1 = blocks.add(keep1, got1).reshape(shape)
    h2 = blocks.add(keep2, got2).reshape(shape)
    dq_others, give_kv = attention_grad(q_rot, kv_got, grad_attn, lse, delta, info, docs)
    got_kv = blocks.swap(give_kv, blocks.x)
    dq_others, h1, h2 = tie(dq_others, h1, h2)
    h1 = blocks.add(h1[0], blocks.swap(h1[1], blocks.y))
    h2 = blocks.add(h2[:, 0], blocks.swap(h2[:, 1], blocks.x))
    grad_q_rot, own_kv = attention_grad(
        q_rot, kv_mine, grad_attn, lse, delta, info, docs, dq_others
    )

    gx, keep_a, give_a = call(
        functools.partial(post_kernel, size),
        "norm_qkv_back",
        [
            ((width, tok_rows), F32), ((a_rows // 2, size.a_width), BF),
            ((a_rows // 2, size.a_width), BF),
        ],
        [
            ((tok_rows, width + kv_width), F32), ((tok_rows, size.a_width), BF),
            ((1, size.flat), F32),
        ],
        1.5,
        (
            me, grad_q_rot, own_kv, got_kv, cos, sin, n1t, a_mine,
            a_other, tokens, grad_mid, flat, grad_gain,
        ),
        24,
    )
    got_a = blocks.swap(give_a, blocks.core)
    got_a, h1, h2 = tie(got_a, h1, h2)
    held = blocks.add(keep_a, got_a)
    h1 = blocks.add(h1[0], blocks.swap(h1[1], blocks.x))
    h2 = blocks.add(h2[0], blocks.swap(h2[1], blocks.y))
    held, h2 = tie(held, h2)
    held = held.reshape(2, 2, blocks.zs, size.tall, size.a_width)
    held = blocks.add(held[0], blocks.swap(held[1], blocks.y))
    held, share2, h1 = tie(held, blocks.sum_z(h2), h1)
    held = blocks.add(held[0], blocks.swap(held[1], blocks.x))
    held, share1 = tie(held, blocks.sum_z(h1))
    share_a = blocks.sum_z(held)

    tails = tail_unpack(share1[:, size.tail : size.tail + size.piece], 2 * ff)
    tail_o = tail_unpack(share1[:, size.tail_o : size.tail_o + 128], width)
    share_out = jnp.concatenate([share1[:, size.out : size.out + width], tail_o], axis=0)
    share_gate = jnp.concatenate([share1[:, :ff], tails[:, :ff]], axis=0)
    share_up = jnp.concatenate([share2[:, :ff], tails[:, ff:]], axis=0)
    downs = [size.down_back_at(c) for c in range(size.downs)]
    share_down = jnp.concatenate(
        [(share1, share2)[which][:, at : at + width] for which, at in downs], axis=0
    )
    ends = (width, width + kv_width, size.qkv)
    return (
        layer_out.T, gx.T, share_a[:rows, : ends[0]].reshape(-1),
        share_a[:rows, ends[0] : ends[1]].reshape(-1),
        share_a[:rows, ends[1] : ends[2]].reshape(-1),
        share_out.reshape(-1), share_gate.reshape(-1), share_up.reshape(-1),
        share_down.reshape(-1), share_a[rows, : size.vec],
    )


def local(
    tokens, q_weight, k_weight, v_weight, o_weight, gate_weight, up_weight, down_weight,
    vectors, doc_lengths, cotangent,
):
    tok_rows, width = tokens.shape
    ctx_count = lax.axis_size("ctx")
    dp_count = lax.axis_size("dp")
    count = dp_count * ctx_count
    seq_tokens = tok_rows * ctx_count
    ctx_index = lax.axis_index("ctx")
    heads = width // HEAD_DIM
    kv_width = KV_HEADS * HEAD_DIM
    ff = gate_weight.shape[0] * count // width

    position_all = doc_layout(doc_lengths[0], seq_tokens)
    offset = ctx_index * tok_rows
    position_mine = lax.dynamic_slice_in_dim(position_all, offset, tok_rows)
    docs = doc_lengths.shape[1]
    others = (ctx_count - 1 - ctx_index) * tok_rows
    heads_of = jnp.stack([ctx_index, others, offset]).astype(jnp.int32)
    info = jnp.concatenate([heads_of, jnp.cumsum(doc_lengths[0])[:-1].astype(jnp.int32)])
    half = HEAD_DIM // 2
    freq = THETA ** (-jnp.arange(half, dtype=F32) * 2.0 / HEAD_DIM)
    position_f = position_mine.astype(F32)[:, None]

    whole_rows = width % count == 0 and ff % count == 0
    if whole_rows and ctx_count == 2 and dp_count % 4 == 0 and count & (count - 1) == 0:
        size = Sizes(width, ff, dp_count, ctx_count, vectors.shape[0], kv_width)
        if size.fits() and (width + kv_width) % 128 == 0:
            angle = position_f * jnp.tile(freq, 128 // half)[None, :]
            sign = np.where(np.arange(128) % HEAD_DIM < half, -1.0, 1.0).astype(np.float32)
            pos = (info, docs, jnp.cos(angle), jnp.sin(angle) * sign)
            args = (
                tokens, q_weight, k_weight, v_weight, o_weight, gate_weight, up_weight,
                down_weight, vectors, cotangent,
            )
            return local_blocks(size, Blocks(dp_count, ctx_count), pos, args)

    angle = position_f * freq[None, :]
    cosine = jnp.cos(angle)[:, None, :]
    sine = jnp.sin(angle)[:, None, :]
    inputs = tokens.astype(F32)
    inv_first = lax.rsqrt(jnp.mean(inputs * inputs, axis=-1, keepdims=True) + EPS)

    def whole(part):
        return lax.all_gather(part, AXES, axis=0, tiled=True)

    w_qkv = jnp.concatenate(
        [whole(w).reshape(width, -1) for w in (q_weight, k_weight, v_weight)], axis=1
    )
    w_out = whole(o_weight).reshape(width, width)
    w_gate = whole(gate_weight).reshape(width, ff)
    w_up = whole(up_weight).reshape(width, ff)
    w_down = whole(down_weight).reshape(ff, width)
    flat = whole(vectors).astype(F32)
    ends = [width, width + kv_width, width + 2 * kv_width, 2 * width + 2 * kv_width]
    gain_attn = flat[ends[2] : ends[3]]
    gain_mlp = flat[ends[3] : ends[3] + width]

    n_first = (inputs * inv_first * gain_attn).astype(BF)
    qkv = times(n_first, w_qkv) + flat[: ends[2]]
    q_rot = turn(qkv[:, :width].reshape(tok_rows, heads, HEAD_DIM), cosine, sine)
    q_rot = q_rot.astype(BF).reshape(tok_rows, width)
    k_rot = turn(qkv[:, width : ends[1]].reshape(tok_rows, KV_HEADS, HEAD_DIM), cosine, sine)
    k_rot = k_rot.astype(BF).reshape(tok_rows, kv_width)
    kv_mine = jnp.concatenate([k_rot, qkv[:, ends[1] :].astype(BF)], axis=1)
    kv = (lax.all_gather(kv_mine, "ctx", axis=0, tiled=True),)
    info = info.at[0].set(1)
    attn, lse = attention(q_rot, kv, info, docs, seq_tokens, False)
    mid = inputs + times(attn, w_out)
    inv_second = lax.rsqrt(jnp.mean(mid * mid, axis=-1, keepdims=True) + EPS)
    n_second = (mid * inv_second * gain_mlp).astype(BF)
    gate = times(n_second, w_gate)
    up_val = times(n_second, w_up)
    sig = jax.nn.sigmoid(gate)
    act = gate * sig
    hidden = (act * up_val).astype(BF)
    layer_out = (mid + times(hidden, w_down)).astype(BF)

    grad_wdown = inner_rows(hidden, cotangent)
    grad_hidden = times_back(cotangent, w_down)
    grad_gate = (grad_hidden * up_val * (sig * (1.0 + gate * (1.0 - sig)))).astype(BF)
    grad_up = (grad_hidden * act).astype(BF)
    grad_wgate = inner_rows(n_second, grad_gate)
    grad_wup = inner_rows(n_second, grad_up)
    grad_n2 = times_back(grad_gate, w_gate) + times_back(grad_up, w_up)
    grad_mid_norm, grad_gain_mlp = norm_back(mid, inv_second, gain_mlp, grad_n2)
    grad_mid = cotangent.astype(F32) + grad_mid_norm
    grad_branch = grad_mid.astype(BF)
    grad_wout = inner_rows(attn, grad_branch)
    grad_attn = times_back(grad_branch, w_out).astype(BF)
    grad_q_rot, grad_kv = attention_back(
        q_rot, kv, grad_attn, lse, info, docs, seq_tokens, False, 0, KV_HEADS
    )
    grad_kv_mine = lax.psum_scatter(
        grad_kv.astype(BF), "ctx", scatter_dimension=0, tiled=True
    ).astype(F32)
    grad_q = turn(grad_q_rot.reshape(tok_rows, heads, HEAD_DIM), cosine, -sine)
    grad_k = turn(
        grad_kv_mine[:, :kv_width].reshape(tok_rows, KV_HEADS, HEAD_DIM), cosine, -sine
    )
    grad_qkv = jnp.concatenate(
        [
            grad_q.reshape(tok_rows, width).astype(BF),
            grad_k.reshape(tok_rows, kv_width).astype(BF),
            grad_kv_mine[:, kv_width:].astype(BF),
        ],
        axis=1,
    )
    grad_wqkv = inner_rows(n_first, grad_qkv)
    grad_bias = jnp.sum(grad_qkv.astype(F32), axis=0)
    grad_n1 = times_back(grad_qkv, w_qkv)
    grad_x_norm, grad_gain_attn = norm_back(inputs, inv_first, gain_attn, grad_n1)
    input_grad = grad_mid + grad_x_norm
    used = 3 * width + 2 * kv_width
    padding = jnp.zeros((vectors.shape[0] * count - used,), F32)
    vector_term = jnp.concatenate([grad_bias, grad_gain_attn, grad_gain_mlp, padding])

    def shares(term):
        return lax.psum_scatter(term.reshape(-1), AXES, scatter_dimension=0, tiled=True)

    return (
        layer_out, input_grad, shares(grad_wqkv[:, :width]),
        shares(grad_wqkv[:, width : ends[1]]), shares(grad_wqkv[:, ends[1] :]),
        shares(grad_wout), shares(grad_wgate), shares(grad_wup), shares(grad_wdown),
        shares(vector_term),
    )


def solution(mesh):
    split = P(AXES)
    rows = P(AXES, None)
    in_specs = (rows,) + (split,) * 8 + (P("dp", None), rows)
    out_specs = (rows, rows) + (split,) * 8
    return jax.shard_map(local, mesh=mesh, in_specs=in_specs, out_specs=out_specs, check_vma=False)
```

```python
import functools

import jax
import jax.numpy as jnp
import numpy as np
from jax import lax
from jax.experimental import pallas as pl
from jax.experimental.pallas import tpu as pltpu
from jax.sharding import PartitionSpec as P

KV_HEADS = 3
HEAD_DIM = 64

EPS = 1e-06
THETA = 100000.0
NEG_FILL = -1e30
AXES = ("dp", "ctx")
BF = jnp.bfloat16
F32 = jnp.float32


def times(left, right):
    return jnp.dot(left, right, preferred_element_type=F32)


def inner_rows(left, right):
    return lax.dot_general(left, right, (((0,), (0,)), ((), ())), preferred_element_type=F32)


def times_back(left, right):
    return lax.dot_general(left, right, (((1,), (1,)), ((), ())), preferred_element_type=F32)


def norm_back(values, inv, gain, grad):
    scaled = grad * gain
    dot = jnp.mean(scaled * values, axis=-1, keepdims=True)
    grad_values = inv * scaled - values * (inv * inv * inv * dot)
    grad_gain = jnp.sum(grad * values * inv, axis=0)
    return grad_values, grad_gain


def turn(values, cosine, sine):
    half = values.shape[-1] // 2
    first = values[..., :half]
    second = values[..., half:]
    return jnp.concatenate(
        [first * cosine - second * sine, second * cosine + first * sine], axis=-1
    )


def doc_layout(lengths, count):
    ends = jnp.cumsum(lengths)
    place = jnp.arange(count, dtype=jnp.int32)
    segment = jnp.sum((place[:, None] >= ends[None, :-1]).astype(jnp.int32), axis=1)
    starts = ends - lengths
    picked = segment[:, None] == jnp.arange(lengths.shape[0], dtype=jnp.int32)[None, :]
    first = jnp.sum(jnp.where(picked, starts[None, :], 0), axis=1)
    return place - first


def fill_bias(bias, info, docs, short, own=None):
    total, rows = bias.shape
    row_q = lax.broadcasted_iota(jnp.int32, (1, rows), 1) + info[2]
    first = jnp.zeros_like(row_q)
    for j in range(docs - 1):
        first = jnp.where(row_q >= info[3 + j], info[3 + j], first)
    parts = ((0, total, 0),)
    if own is not None:
        parts = ((0, total, info[2] if own else info[1]),)
    elif short < total:
        parts = ((0, total - short, info[1]), (total - short, total, info[2]))
    for start, stop, base in parts:
        row_k = lax.broadcasted_iota(jnp.int32, (stop - start, rows), 0)
        allowed = (row_k >= first - base) & (row_k <= row_q - base)
        bias[start:stop] = jnp.where(allowed, 0.0, NEG_FILL)


def key_range(full, total, short, rows, block, at, causal):
    start = 0 if full else total - short
    stop = total - rows + (at + 1) * block if causal else total
    return start, stop


def key_parts(kv_refs):
    at = 0
    for kv_ref in kv_refs:
        yield slice(at, at + kv_ref.shape[0]), kv_ref
        at += kv_ref.shape[0]


def attn_fwd_kernel(
    heads, block, short, causal, docs, info, q_ref, *refs,
):
    kv_refs, (out_ref, lse_ref, qs, ks, vts, bias, out_t) = refs[:-7], refs[-7:]
    rows = q_ref.shape[0]
    total = bias.shape[0]
    kv_width = KV_HEADS * HEAD_DIM
    group = heads // KV_HEADS
    fill_bias(bias, info, docs, short)
    for h in range(heads):
        qs[h] = q_ref[:, h * HEAD_DIM : (h + 1) * HEAD_DIM] * BF(HEAD_DIM**-0.5)
    for at, kv_ref in key_parts(kv_refs):
        for g in range(KV_HEADS):
            ks[g, at] = kv_ref[:, g * HEAD_DIM : (g + 1) * HEAD_DIM]
        vts[:, at] = jnp.transpose(kv_ref[:, kv_width:].astype(F32)).astype(BF)

    def run(full):
        @pl.loop(0, KV_HEADS)
        def _(g):
            v_rows = pl.ds(pl.multiple_of(g * HEAD_DIM, HEAD_DIM), HEAD_DIM)
            for j in range(group):
                h = g * group + j
                out_rows = pl.ds(pl.multiple_of(h * HEAD_DIM, HEAD_DIM), HEAD_DIM)
                for at in range(rows // block):
                    start, stop = key_range(full, total, short, rows, block, at, causal)
                    cols = slice(at * block, (at + 1) * block)
                    s = times_back(ks[g, start:stop], qs[h, cols])
                    s = s + bias[start:stop, cols]
                    top = jnp.max(s, axis=0, keepdims=True)
                    p = jnp.exp(s - top)
                    total_p = jnp.sum(p, axis=0, keepdims=True)
                    o = times(vts[v_rows, start:stop], p.astype(BF))
                    out_t[out_rows, cols] = o / total_p
                    lse_ref[h, :, cols] = top + jnp.log(total_p)

    pl.when(info[0] != 0)(lambda: run(True))
    pl.when(info[0] == 0)(lambda: run(False))
    out_ref[...] = jnp.transpose(out_t[...]).astype(BF)


def attn_own_kernel(
    heads, block, docs, info, q_ref, kv_ref, acc, top_ref, sum_ref, qs, ks, vts, bias
):
    rows = q_ref.shape[0]
    kv_width = KV_HEADS * HEAD_DIM
    group = heads // KV_HEADS
    fill_bias(bias, info, docs, rows, own=True)
    for h in range(heads):
        qs[h] = q_ref[:, h * HEAD_DIM : (h + 1) * HEAD_DIM] * BF(HEAD_DIM**-0.5)
    for g in range(KV_HEADS):
        ks[g] = kv_ref[:, g * HEAD_DIM : (g + 1) * HEAD_DIM]
    vts[...] = jnp.transpose(kv_ref[:, kv_width:].astype(F32)).astype(BF)

    @pl.loop(0, heads)
    def _(h):
        g = h // group
        v_rows = pl.ds(pl.multiple_of(g * HEAD_DIM, HEAD_DIM), HEAD_DIM)
        out_rows = pl.ds(pl.multiple_of(h * HEAD_DIM, HEAD_DIM), HEAD_DIM)
        for at in range(rows // block):
            stop = (at + 1) * block
            cols = slice(at * block, stop)
            s = times_back(ks[g, :stop], qs[h, cols]) + bias[:stop, cols]
            top = jnp.max(s, axis=0, keepdims=True)
            p = jnp.exp(s - top)
            top_ref[h, :, cols] = top
            sum_ref[h, :, cols] = jnp.sum(p, axis=0, keepdims=True)
            acc[out_rows, cols] = times(vts[v_rows, :stop], p.astype(BF))


def attn_others_kernel(
    heads, block, docs, info, q_ref, kv_ref, acc, top_ref, sum_ref, out_ref, lse_ref,
    qs, ks, vts, bias, out_t,
):
    rows = q_ref.shape[0]
    kv_width = KV_HEADS * HEAD_DIM
    group = heads // KV_HEADS

    @pl.when(info[0] == 0)
    def _():
        for h in range(heads):
            at = slice(h * HEAD_DIM, (h + 1) * HEAD_DIM)
            out_t[at] = acc[at] / sum_ref[h]
            lse_ref[h] = top_ref[h] + jnp.log(sum_ref[h])

    @pl.when(info[0] != 0)
    def _():
        fill_bias(bias, info, docs, rows, own=False)
        for h in range(heads):
            qs[h] = q_ref[:, h * HEAD_DIM : (h + 1) * HEAD_DIM] * BF(HEAD_DIM**-0.5)
        for g in range(KV_HEADS):
            ks[g] = kv_ref[:, g * HEAD_DIM : (g + 1) * HEAD_DIM]
        vts[...] = jnp.transpose(kv_ref[:, kv_width:].astype(F32)).astype(BF)

        @pl.loop(0, heads)
        def _(h):
            g = h // group
            v_rows = pl.ds(pl.multiple_of(g * HEAD_DIM, HEAD_DIM), HEAD_DIM)
            out_rows = pl.ds(pl.multiple_of(h * HEAD_DIM, HEAD_DIM), HEAD_DIM)
            for at in range(rows // block):
                cols = slice(at * block, (at + 1) * block)
                s = times_back(ks[g], qs[h, cols]) + bias[:, cols]
                own = top_ref[h, :, cols]
                top = jnp.maximum(own, jnp.max(s, axis=0, keepdims=True))
                scale = jnp.exp(own - top)
                p = jnp.exp(s - top)
                total_p = sum_ref[h, :, cols] * scale + jnp.sum(p, axis=0, keepdims=True)
                o = acc[out_rows, cols] * scale + times(vts[v_rows], p.astype(BF))
                out_t[out_rows, cols] = o / total_p
                lse_ref[h, :, cols] = top + jnp.log(total_p)

    out_ref[...] = jnp.transpose(out_t[...]).astype(BF)


def attn_grad_kernel(
    heads, block, docs, own, info, q_ref, kv_ref, do_ref, lse_ref, delta_ref, *refs
):
    refs, (qs, dos, ks, vs, kts, bias, dk, dv) = refs[:-8], refs[-8:]
    if own:
        before, dq_ref, dkv_ref, dq_t = refs
    else:
        dq_t, dkv_ref = refs
    rows = q_ref.shape[0]
    kv_width = KV_HEADS * HEAD_DIM
    group = heads // KV_HEADS
    dk[...] = jnp.zeros_like(dk)
    dv[...] = jnp.zeros_like(dv)

    def run():
        fill_bias(bias, info, docs, rows, own=own)
        for h in range(heads):
            at = slice(h * HEAD_DIM, (h + 1) * HEAD_DIM)
            qs[h] = q_ref[:, at] * BF(HEAD_DIM**-0.5)
            dos[h] = do_ref[:, at]
        for g in range(KV_HEADS):
            lo = g * HEAD_DIM
            ks[g] = kv_ref[:, lo : lo + HEAD_DIM]
            vs[g] = kv_ref[:, kv_width + lo : kv_width + lo + HEAD_DIM]
        kts[...] = jnp.transpose(kv_ref[:, :kv_width].astype(F32)).astype(BF)

        @pl.loop(0, heads)
        def _(h):
            g = h // group
            k_rows = pl.ds(pl.multiple_of(g * HEAD_DIM, HEAD_DIM), HEAD_DIM)
            out_rows = pl.ds(pl.multiple_of(h * HEAD_DIM, HEAD_DIM), HEAD_DIM)
            for at in range(rows // block):
                stop = (at + 1) * block if own else rows
                cols = slice(at * block, (at + 1) * block)
                q = qs[h, cols]
                do = dos[h, cols]
                s = times_back(ks[g, :stop], q) + bias[:stop, cols]
                p = jnp.exp(s - lse_ref[h, :, cols])
                dp = times_back(vs[g, :stop], do)
                ds = (p * (dp - delta_ref[h, :, cols])).astype(BF)
                dk[g, :stop] += times(ds, q)
                dv[g, :stop] += times(p.astype(BF), do)
                dq = times(kts[k_rows, :stop], ds) * HEAD_DIM**-0.5
                dq_t[out_rows, cols] = before[out_rows, cols] + dq if own else dq

    if own:
        run()
        dq_ref[...] = jnp.transpose(dq_t[...])
    else:
        pl.when(info[0] != 0)(run)

        @pl.when(info[0] == 0)
        def _():
            dq_t[...] = jnp.zeros_like(dq_t)

    for g in range(KV_HEADS):
        lo = g * HEAD_DIM
        dkv_ref[:, lo : lo + HEAD_DIM] = dk[g].astype(dkv_ref.dtype)
        dkv_ref[:, kv_width + lo : kv_width + lo + HEAD_DIM] = dv[g].astype(dkv_ref.dtype)


def attn_bwd_kernel(
    heads, block, short, causal, docs, g0, g1, parts, info, q_ref, do_ref, lse_ref, *refs,
):
    kv_refs, outs, scratch = refs[:parts], refs[parts:-9], refs[-9:]
    qs, ks, vs, kts, dos, bias, dq_t, dk, dv = scratch
    rows = q_ref.shape[0]
    total = bias.shape[0]
    kv_width = KV_HEADS * HEAD_DIM
    group = heads // KV_HEADS
    keys = g1 - g0
    fill_bias(bias, info, docs, short)
    for h in range(keys * group):
        lanes = slice((g0 * group + h) * HEAD_DIM, (g0 * group + h + 1) * HEAD_DIM)
        qs[h] = q_ref[:, lanes] * BF(HEAD_DIM**-0.5)
        dos[h] = do_ref[:, lanes]
    for g in range(keys):
        lo = (g0 + g) * HEAD_DIM
        for at, kv_ref in key_parts(kv_refs):
            ks[g, at] = kv_ref[:, lo : lo + HEAD_DIM]
            vs[g, at] = kv_ref[:, kv_width + lo : kv_width + lo + HEAD_DIM]
        kts[g] = jnp.transpose(ks[g].astype(F32)).astype(BF)
    dk[...] = jnp.zeros_like(dk)
    dv[...] = jnp.zeros_like(dv)

    def run(full):
        @pl.loop(0, keys * group)
        def _(h):
            g = h // group if keys > 1 else 0
            out_rows = pl.ds(pl.multiple_of(h * HEAD_DIM, HEAD_DIM), HEAD_DIM)
            for at in range(rows // block):
                start, stop = key_range(full, total, short, rows, block, at, causal)
                cols = slice(at * block, (at + 1) * block)
                q = qs[h, cols]
                do = dos[h, cols]
                s = times_back(ks[g, start:stop], q)
                p = jnp.exp(s + bias[start:stop, cols] - lse_ref[g0 * group + h, :, cols])
                dp = times_back(vs[g, start:stop], do)
                t = p * dp
                inner = jnp.sum(t, axis=0, keepdims=True)
                ds = (t - p * inner).astype(BF)
                dk[g, start:stop] += times(ds, q)
                dv[g, start:stop] += times(p.astype(BF), do)
                dq_t[out_rows, cols] = times(kts[g, :, start:stop], ds) * HEAD_DIM**-0.5

    pl.when(info[0] != 0)(lambda: run(True))
    pl.when(info[0] == 0)(lambda: run(False))
    outs[0][...] = jnp.transpose(dq_t[...])
    cut = total - outs[1].shape[0]
    for part, out in ((slice(cut, total), outs[1]),) + tuple((slice(0, cut), o) for o in outs[2:]):
        for g in range(keys):
            lo = g * HEAD_DIM
            out[:, lo : lo + HEAD_DIM] = dk[g, part].astype(out.dtype)
            lo += keys * HEAD_DIM
            out[:, lo : lo + HEAD_DIM] = dv[g, part].astype(out.dtype)


VM = pl.BlockSpec(memory_space=pltpu.VMEM)
SM = pl.BlockSpec(memory_space=pltpu.SMEM)


def cost_of(micros):
    return pl.CostEstimate(
        flops=int(micros * 1.1e9), bytes_accessed=2**20, transcendentals=0
    )


def attention(q, kv, info, docs, short, causal):
    rows, width = q.shape
    total = sum(part.shape[0] for part in kv)
    heads = width // HEAD_DIM
    block = min(rows, 256)
    return pl.pallas_call(
        functools.partial(attn_fwd_kernel, heads, block, short, causal, docs),
        out_shape=(
            jax.ShapeDtypeStruct((rows, width), BF),
            jax.ShapeDtypeStruct((heads, 1, rows), F32),
        ),
        in_specs=[SM] + [VM] * (1 + len(kv)),
        out_specs=(VM, VM),
        scratch_shapes=[
            pltpu.VMEM((heads, rows, HEAD_DIM), BF),
            pltpu.VMEM((KV_HEADS, total, HEAD_DIM), BF),
            pltpu.VMEM((KV_HEADS * HEAD_DIM, total), BF),
            pltpu.VMEM((total, rows), F32),
            pltpu.VMEM((width, rows), F32),
        ],
        compiler_params=pltpu.CompilerParams(vmem_limit_bytes=20 * 2**20),
        cost_estimate=cost_of(14),
        name="attn_fwd",
    )(info, q, *kv)


def attention_own(q, kv, info, docs):
    rows, width = q.shape
    heads = width // HEAD_DIM
    stat = jax.ShapeDtypeStruct((heads, 1, rows), F32)
    return pl.pallas_call(
        functools.partial(attn_own_kernel, heads, min(rows, 256), docs),
        out_shape=(jax.ShapeDtypeStruct((width, rows), F32), stat, stat),
        in_specs=[SM, VM, VM],
        out_specs=(VM, VM, VM),
        scratch_shapes=attn_scratch(rows, heads),
        compiler_params=pltpu.CompilerParams(vmem_limit_bytes=16 * 2**20),
        cost_estimate=cost_of(6),
        name="attn_own",
    )(info, q, kv)


def attn_scratch(rows, heads):
    return [
        pltpu.VMEM((heads, rows, HEAD_DIM), BF),
        pltpu.VMEM((KV_HEADS, rows, HEAD_DIM), BF),
        pltpu.VMEM((KV_HEADS * HEAD_DIM, rows), BF),
        pltpu.VMEM((rows, rows), F32),
    ]


def attention_grad(q, kv, grad_out, lse, delta, info, docs, before=None):
    rows, width = q.shape
    heads = width // HEAD_DIM
    own = before is not None
    turned = jax.ShapeDtypeStruct((width, rows), F32)
    if own:
        outs = [jax.ShapeDtypeStruct((rows, width), F32), jax.ShapeDtypeStruct(kv.shape, F32)]
    else:
        outs = [turned, jax.ShapeDtypeStruct(kv.shape, BF)]
    by_head = pltpu.VMEM((heads, rows, HEAD_DIM), BF)
    by_key = pltpu.VMEM((KV_HEADS, rows, HEAD_DIM), BF)
    sums = pltpu.VMEM((KV_HEADS, rows, HEAD_DIM), F32)
    return pl.pallas_call(
        functools.partial(attn_grad_kernel, heads, min(rows, 256), docs, own),
        out_shape=outs,
        in_specs=[SM] + [VM] * (6 if own else 5),
        out_specs=[VM] * 2,
        scratch_shapes=([pltpu.VMEM((width, rows), F32)] if own else []) + [
            by_head, by_head, by_key, by_key, pltpu.VMEM((KV_HEADS * HEAD_DIM, rows), BF),
            pltpu.VMEM((rows, rows), F32), sums, sums,
        ],
        compiler_params=pltpu.CompilerParams(vmem_limit_bytes=20 * 2**20),
        cost_estimate=cost_of(2.5),
        name="attn_grad_own" if own else "attn_grad_others",
    )(info, q, kv, grad_out, lse, delta, *([before] if own else []))


def attention_others(q, kv, acc, top, total, info, docs):
    rows, width = q.shape
    heads = width // HEAD_DIM
    return pl.pallas_call(
        functools.partial(attn_others_kernel, heads, min(rows, 256), docs),
        out_shape=(
            jax.ShapeDtypeStruct((rows, width), BF),
            jax.ShapeDtypeStruct((heads, 1, rows), F32),
        ),
        in_specs=[SM] + [VM] * 5,
        out_specs=(VM, VM),
        scratch_shapes=attn_scratch(rows, heads) + [pltpu.VMEM((width, rows), F32)],
        compiler_params=pltpu.CompilerParams(vmem_limit_bytes=16 * 2**20),
        cost_estimate=cost_of(10),
        name="attn_others",
    )(info, q, kv, acc, top, total)


def attention_back(q, kv, grad_out, lse, info, docs, short, causal, g0, g1):
    rows, width = q.shape
    total = sum(part.shape[0] for part in kv)
    heads = width // HEAD_DIM
    block = min(rows, 256)
    keys = g1 - g0
    mine = heads // KV_HEADS * keys
    outs = [jax.ShapeDtypeStruct((rows, mine * HEAD_DIM), F32)]
    if causal:
        outs.append(jax.ShapeDtypeStruct((rows, 2 * keys * HEAD_DIM), F32))
        outs.append(jax.ShapeDtypeStruct((total - rows, 2 * keys * HEAD_DIM), BF))
    else:
        outs.append(jax.ShapeDtypeStruct((total, 2 * keys * HEAD_DIM), F32))
    return pl.pallas_call(
        functools.partial(attn_bwd_kernel, heads, block, short, causal, docs, g0, g1, len(kv)),
        out_shape=outs,
        in_specs=[SM] + [VM] * (3 + len(kv)),
        out_specs=[VM] * len(outs),
        scratch_shapes=[
            pltpu.VMEM((mine, rows, HEAD_DIM), BF),
            pltpu.VMEM((keys, total, HEAD_DIM), BF),
            pltpu.VMEM((keys, total, HEAD_DIM), BF),
            pltpu.VMEM((keys, HEAD_DIM, total), BF),
            pltpu.VMEM((mine, rows, HEAD_DIM), BF),
            pltpu.VMEM((total, rows), F32),
            pltpu.VMEM((mine * HEAD_DIM, rows), F32),
            pltpu.VMEM((keys, total, HEAD_DIM), F32),
            pltpu.VMEM((keys, total, HEAD_DIM), F32),
        ],
        compiler_params=pltpu.CompilerParams(vmem_limit_bytes=20 * 2**20),
        cost_estimate=cost_of(20),
        name="attn_bwd",
    )(info, q, grad_out, lse, *kv)


TAIL = 2
MAIN = 16
PIECES = MAIN // TAIL


class Blocks:
    def __init__(self, dp_count, ctx_count):
        self.count = dp_count * ctx_count
        self.x = 1
        self.core = ctx_count
        self.y = 2 * ctx_count
        self.z = 4 * ctx_count
        self.zs = dp_count // 4
        self.masks = []
        for p in range(self.count):
            z, x = p % self.zs, p // self.zs % 2
            y, core = p // (2 * self.zs) % 2, p // (4 * self.zs)
            self.masks.append(x * self.x + y * self.y + core * self.core + z * self.z)

    def swap(self, values, mask):
        perm = [(i, i ^ mask) for i in range(self.count)]
        return lax.ppermute(values, AXES, perm)

    def along_z(self, mine):
        return jnp.stack([mine] + [self.swap(mine, d * self.z) for d in range(1, self.zs)])

    def add(self, keep, got):
        return (keep.astype(F32) + got.astype(F32)).astype(BF)

    def sum_z(self, held):
        got = [self.swap(held[d], d * self.z).astype(F32) for d in range(1, self.zs)]
        return functools.reduce(jnp.add, got, held[0].astype(F32))


class Sizes:
    def __init__(self, width, ff, dp, ctx, vec, kv_width):
        count = dp * ctx
        self.zs, self.ctx = dp // 4, ctx
        self.width, self.ff, self.count, self.vec = width, ff, count, vec
        self.rows = width // count
        self.f_rows = ff // count
        up = lambda n: (n + 127) // 128 * 128
        self.wide = up(width)
        self.qkv = width + 2 * kv_width
        self.a_width = up(self.qkv)
        self.tall = (self.rows + 1 + 7) // 8 * 8
        self.downs = self.f_rows // MAIN
        self.piece = 2 * ff // PIECES
        self.gate = 0
        self.tail = ff
        self.tail_o = self.tail + self.piece
        self.out = self.tail_o + 128
        self.down0 = self.out + self.wide
        self.first = self.down0 + self.wide
        self.second = ff + (self.downs - 1) * self.wide
        self.back_first = self.down0 + (self.downs - 1) * self.wide
        self.back_second = ff + self.wide
        self.flat = self.a_width + 2 * self.wide

    def down_at(self, c):
        return (0, self.down0) if c == 0 else (1, self.ff + (c - 1) * self.wide)

    def down_back_at(self, c):
        return (0, self.down0 + c * self.wide) if c < self.downs - 1 else (1, self.ff)

    def fits(self):
        return (
            self.rows == MAIN + TAIL
            and self.f_rows % MAIN == 0
            and self.piece % 128 == 0
            and self.ff % 256 == 0
            and self.wide <= 128 * PIECES
            and self.vec <= 128
        )


def wire_kernel(
    size, g_ref, u_ref, o_ref, d_ref, xt_ref, cott_ref, out1, out2, x_any, cot_any,
    tail, tail_o, x_ref, cot_ref, sems,
):
    ff, width = size.ff, size.width
    x_ref[...] = jnp.transpose(xt_ref[...].astype(F32)).astype(BF)
    cot_ref[...] = jnp.transpose(cott_ref[...].astype(F32)).astype(BF)
    copies = fetch((x_ref, cot_ref), (x_any, cot_any), sems)
    out1[:, : ff] = g_ref[:MAIN]
    out2[:, : ff] = u_ref[:MAIN]
    out1[:, size.out : size.out + size.wide] = jnp.zeros((MAIN, size.wide), BF)
    out1[:, size.out : size.out + width] = o_ref[:MAIN]
    tail_o[...] = jnp.zeros_like(tail_o)
    odd = [ref[MAIN:].astype(F32) for ref in (g_ref, u_ref, o_ref)]
    for c in range(PIECES):
        src = odd[c * size.piece // ff]
        at = c * size.piece % ff
        tail[c * TAIL : (c + 1) * TAIL] = src[:, at : at + size.piece]
        used = min(128, width - c * 128)
        if used > 0:
            tail_o[c * TAIL : (c + 1) * TAIL, :used] = odd[2][:, c * 128 : c * 128 + used]
    out1[:, size.tail : size.tail + size.piece] = tail[...].astype(BF)
    out1[:, size.tail_o : size.tail_o + 128] = tail_o[...].astype(BF)
    for c in range(size.downs):
        which, at = size.down_at(c)
        out = (out1, out2)[which]
        out[:, at : at + size.wide] = jnp.zeros((MAIN, size.wide), BF)
        out[:, at : at + width] = d_ref[c * MAIN : (c + 1) * MAIN]
    for copy in copies:
        copy.wait()


def over(values, by):
    scale = 2**16 // by + 1
    whole = (values * scale) >> 16
    return whole, values - whole * by


def mask_of(size, p):
    z, rest = p % size.zs, p // size.zs
    x, y, core = rest % 2, rest // 2 % 2, rest // 4
    return x + core * size.ctx + y * (2 * size.ctx) + z * (4 * size.ctx)


def lanes(count):
    return lax.broadcasted_iota(jnp.int32, (1, count), 1)


def place_matrix(size, me, tall):
    if tall:
        p, inside = over(lanes(size.count * size.tall), size.tall)
        feature = jnp.where(inside < size.rows, size.rows * (me ^ mask_of(size, p)) + inside, -1)
    else:
        s = lanes(size.count * (MAIN + TAIL))
        tail = s - size.count * MAIN
        p = jnp.where(tail < 0, s // MAIN, tail // TAIL)
        inside = jnp.where(tail < 0, s % MAIN, MAIN + tail % TAIL)
        feature = size.rows * (me ^ mask_of(size, p)) + inside
    at = lax.broadcasted_iota(jnp.int32, (size.width, feature.shape[1]), 0)
    return jnp.where(at == feature, 1.0, 0.0).astype(BF)


def vector_places(size, me):
    at = lanes(size.flat)
    ends = (size.a_width, size.a_width + size.wide)
    part = jnp.where(at < ends[0], 0, jnp.where(at < ends[1], 1, 2))
    inside = at - jnp.where(part == 0, 0, jnp.where(part == 1, ends[0], ends[1]))
    start = jnp.where(part == 0, 0, jnp.where(part == 1, size.qkv, size.qkv + size.width))
    used = inside < jnp.where(part == 0, size.qkv, size.width)
    owner, lane = over(start + inside, size.vec)
    rows = lax.broadcasted_iota(jnp.int32, (128, size.flat), 0)
    spread = jnp.where((rows == lane) & used, 1.0, 0.0).astype(BF)
    p = lax.broadcasted_iota(jnp.int32, (size.count, 1), 0)
    return spread, (owner == (me ^ mask_of(size, p))) & used


def swap_halves(u):
    rolled_back = pltpu.roll(u, 128 - HEAD_DIM // 2, 1)
    rolled = pltpu.roll(u, HEAD_DIM // 2, 1)
    lane = lax.broadcasted_iota(jnp.int32, u.shape, 1)
    return jnp.where(lane % HEAD_DIM < HEAD_DIM // 2, rolled_back, rolled)


def fetch(sources, targets, sems):
    copies = [
        pltpu.make_async_copy(src, dst, sems.at[i])
        for i, (src, dst) in enumerate(zip(sources, targets))
    ]
    for copy in copies:
        copy.start()
    return copies


def pre_kernel(
    size, me_ref, x_ref, wm_ref, wo_ref, cos_ref, sin_ref,
    q_ref, kv_ref, n1t_ref, flat_ref, w, qkv,
):
    me = me_ref[0]
    half = wm_ref.shape[0]
    w[:half] = wm_ref[...]
    w[half:] = wo_ref[...]
    place = place_matrix(size, me, True)
    spread, mine = vector_places(size, me)
    shape = (size.count, 2 * half)
    row = lax.broadcasted_iota(jnp.int32, shape, 0) * size.tall + size.rows
    row = jnp.where(lax.broadcasted_iota(jnp.int32, shape, 1) == row, 1.0, 0.0).astype(BF)
    packed = times(row, w[:, :128]).astype(BF)
    flat = jnp.sum(jnp.where(mine, times(packed, spread), 0.0), axis=0, keepdims=True)
    flat_ref[...] = flat
    gain = flat[:, size.a_width : size.a_width + size.width]
    x = x_ref[...].astype(F32)
    inv = lax.rsqrt(jnp.mean(x * x, axis=-1, keepdims=True) + EPS)
    n1 = (x * inv * gain).astype(BF)
    n1a = times(n1, place)
    n1t_ref[...] = jnp.transpose(n1a).astype(BF)
    qkv[...] = times(n1a.astype(BF), w[...]) + flat[:, : size.a_width]
    kv_width = kv_ref.shape[1] // 2
    for t in range((size.width + kv_width) // 128):
        u = qkv[:, t * 128 : (t + 1) * 128]
        qkv[:, t * 128 : (t + 1) * 128] = u * cos_ref[...] + swap_halves(u) * sin_ref[...]
    q_ref[...] = qkv[:, : size.width].astype(BF)
    kv_ref[...] = qkv[:, size.width : size.qkv].astype(BF)


def tail_place(size, back):
    odd, count = size.count * TAIL, size.count * MAIN
    row = lax.broadcasted_iota(jnp.int32, (count, count), 1 if back else 0)
    at = lax.broadcasted_iota(jnp.int32, (count, count), 0 if back else 1)
    c, q = row // odd, row % odd
    want = (q // TAIL) * MAIN + c * TAIL + q % TAIL
    return jnp.where(at == want, 1.0, 0.0).astype(BF)


def mlp_kernel(
    size, me_ref, attn_ref, x_ref, cot_ref, flat_ref,
    b1_00, b1_01, b1_10, b1_11, b2_00, b2_01, b2_10, b2_11,
    out_ref, keep1, give1, keep2, give2, gmid_ref, gattn_ref, ggain_ref, delta_ref,
    wg, wu, wo, wd, mid, n2s, n2t, place, acc, gacc, dwd, tails, tail_o, packed,
):
    me = me_ref[0]
    width, ff = size.width, size.ff
    part = b1_00.shape[0]
    half, main = 2 * part, 4 * part
    rows_z = part // 2
    place[...] = place_matrix(size, me, False)
    first = (b1_00, b1_01, b1_10, b1_11)
    second = (b2_00, b2_01, b2_10, b2_11)
    room = size.piece + 128
    for i, b1 in enumerate(first):
        rows = slice(i * part, (i + 1) * part)
        wg[rows] = b1[:, :ff]
        wo[rows] = b1[:, size.out : size.out + size.wide]
        packed[rows] = b1[:, size.tail : size.tail + room]
    for i, b2 in enumerate(second):
        for y in range(2):
            at = (i // 2) * half + y * part + (i % 2) * rows_z
            wu[at : at + rows_z] = b2[y * rows_z : (y + 1) * rows_z, :ff]
    odd = size.count * TAIL
    got = times(tail_place(size, False), packed[...]).astype(BF)
    for c in range(PIECES):
        rows = slice(c * odd, (c + 1) * odd)
        target = wg if c * size.piece < ff else wu
        at = c * size.piece % ff
        target[main:, at : at + size.piece] = got[rows, : size.piece]
        if c * 128 < size.wide:
            wo[main:, c * 128 : (c + 1) * 128] = got[rows, size.piece :]
    zs = rows_z // MAIN
    for p in range(size.count):
        z, x, y, core = p % zs, p // zs % 2, p // (2 * zs) % 2, p // (4 * zs)
        owner = me ^ mask_of(size, p)
        for c in range(size.downs):
            which, at = size.down_at(c)
            src, row = (second[2 * core + x], y * zs + z) if which else (
                first[2 * core + y], x * zs + z
            )
            to = pl.multiple_of(owner * size.f_rows + c * MAIN, MAIN)
            wd[pl.ds(to, MAIN), :] = src[row * MAIN : (row + 1) * MAIN, at : at + size.wide]
    attn_s = times(attn_ref[...], place[...])
    m = x_ref[...].astype(F32) + times(attn_s.astype(BF), wo[:, :width])
    mid[...] = m
    inv = lax.rsqrt(jnp.mean(m * m, axis=-1, keepdims=True) + EPS)
    lo = size.a_width + size.wide
    gain = flat_ref[:, lo : lo + width]
    n2 = (m * inv * gain).astype(BF)
    spread = times(n2, place[...])
    n2s[...] = spread.astype(BF)
    n2t[...] = jnp.transpose(spread).astype(BF)
    acc[...] = jnp.zeros_like(acc)
    gacc[...] = jnp.zeros_like(gacc)
    step = 512 if ff % 512 == 0 else 256

    @pl.loop(0, ff // step)
    def _(b):
        at = pl.multiple_of(b * step, step)
        cols = pl.ds(at, step)
        gate = times(n2s[...], wg[:, cols])
        up = times(n2s[...], wu[:, cols])
        sig = 1.0 / (1.0 + jnp.exp(-gate))
        act = gate * sig
        h = act * up
        gh = times_back(cot_ref[...], wd[cols, :width])
        gg = (gh * up * (sig * (1.0 + gate * (1.0 - sig)))).astype(BF)
        gu = (gh * act).astype(BF)
        acc[...] += times(h.astype(BF), wd[cols, :width])
        dwd[cols, :width] = times(jnp.transpose(h).astype(BF), cot_ref[...]).astype(BF)
        gacc[...] += times_back(gg, wg[:, cols]) + times_back(gu, wu[:, cols])
        for k, (grad, keep, give) in enumerate(((gg, keep1, give1), (gu, keep2, give2))):
            dw = times(n2t[...], grad).astype(BF)
            keep[:, cols] = dw[:half]
            give[:, cols] = dw[half:main]
            tails[:, pl.ds(pl.multiple_of(k * ff + at, 128), step)] = dw[main:]

    m = mid[...]
    inv = lax.rsqrt(jnp.mean(m * m, axis=-1, keepdims=True) + EPS)
    out_ref[...] = jnp.transpose(m + acc[...]).astype(BF)
    gn2 = times_back(gacc[...].astype(BF), place[...])
    scaled = gn2 * gain
    dot = jnp.mean(scaled * m, axis=-1, keepdims=True)
    ggain_ref[...] = jnp.sum(gn2 * m * inv, axis=0, keepdims=True)
    gmid = cot_ref[...].astype(F32) + inv * scaled - m * (inv * inv * inv * dot)
    gmid_ref[...] = gmid
    branch = gmid.astype(BF)
    gattn = times_back(branch, wo[:, :width]).astype(BF)
    gattn = times_back(gattn, place[...]).astype(BF)
    gattn_ref[...] = gattn
    both = jnp.transpose(gattn.astype(F32) * attn_ref[...].astype(F32))
    for h in range(width // HEAD_DIM):
        at = slice(h * HEAD_DIM, (h + 1) * HEAD_DIM)
        delta_ref[h] = jnp.sum(both[at], axis=0, keepdims=True)
    dwo = times(jnp.transpose(attn_s).astype(BF), branch).astype(BF)
    tail_o[...] = jnp.zeros_like(tail_o)
    tail_o[:, :width] = dwo[main:]
    terms = ((keep1, keep2), (give1, give2))
    for i, (term, _) in enumerate(terms):
        term[:, size.out : size.out + width] = dwo[i * half : (i + 1) * half]
    packed[...] = jnp.zeros_like(packed)
    for c in range(PIECES):
        rows = slice(c * odd, (c + 1) * odd)
        packed[rows, : size.piece] = tails[:, c * size.piece : (c + 1) * size.piece]
        if c * 128 < size.wide:
            packed[rows, size.piece :] = tail_o[:, c * 128 : (c + 1) * 128]
    wire = times(tail_place(size, True), packed[...]).astype(BF)
    for i, (term, _) in enumerate(terms):
        rows = slice(i * half, (i + 1) * half)
        term[:, size.tail : size.tail + room] = wire[rows]
    for p in range(size.count):
        to = terms[p // (size.count // 2)]
        rows = slice(p * MAIN % half, p * MAIN % half + MAIN)
        owner = me ^ mask_of(size, p)
        for c in range(size.downs):
            which, at = size.down_back_at(c)
            src = pl.multiple_of(owner * size.f_rows + c * MAIN, MAIN)
            to[which][rows, at : at + size.wide] = dwd[pl.ds(src, MAIN), :]


def post_kernel(
    size, me_ref, dq_ref, dkv_ref, got_ref, cos_ref, sin_ref, n1t_ref,
    wm_ref, wo_ref, x_ref, gmid_ref, flat_ref, ggain_ref,
    gx_ref, keep_ref, give_ref, turn_buf, grad, vec_row,
):
    me = me_ref[0]
    width = size.width
    half = wm_ref.shape[0]
    place = place_matrix(size, me, True)
    kv_width = KV_HEADS * HEAD_DIM
    turned = width + kv_width
    dkv = dkv_ref[...] + got_ref[...].astype(F32)
    turn_buf[:, :width] = dq_ref[...]
    turn_buf[:, width:] = dkv[:, :kv_width]
    grad[...] = jnp.zeros_like(grad)
    grad[:, turned : turned + kv_width] = dkv[:, kv_width:].astype(BF)
    for t in range(turned // 128):
        u = turn_buf[:, t * 128 : (t + 1) * 128]
        back = u * cos_ref[...] - swap_halves(u) * sin_ref[...]
        grad[:, t * 128 : (t + 1) * 128] = back.astype(BF)
    g = grad[...]
    gn1 = jnp.zeros((g.shape[0], width), F32)
    for part, w_ref in enumerate((wm_ref, wo_ref)):
        values = times_back(g, w_ref[...]).astype(BF)
        gn1 += times_back(values, place[:, part * half : (part + 1) * half])
    x = x_ref[...].astype(F32)
    inv = lax.rsqrt(jnp.mean(x * x, axis=-1, keepdims=True) + EPS)
    gain = flat_ref[:, size.a_width : size.a_width + width]
    scaled = gn1 * gain
    dot = jnp.mean(scaled * x, axis=-1, keepdims=True)
    gx_ref[...] = jnp.transpose(gmid_ref[...] + inv * scaled - x * (inv * inv * inv * dot))
    vec_row[...] = jnp.zeros_like(vec_row)
    vec_row[:, : size.a_width] = jnp.sum(g.astype(F32), axis=0, keepdims=True)
    vec_row[:, size.a_width : size.a_width + width] = jnp.sum(gn1 * x * inv, axis=0, keepdims=True)
    lo = size.a_width + size.wide
    vec_row[:, lo : lo + width] = ggain_ref[...]
    spread, mine = vector_places(size, me)
    packed = times_back(jnp.where(mine, vec_row[...], 0.0).astype(BF), spread)
    shape = (half, size.count)
    for part, term in ((0, keep_ref), (1, give_ref)):
        rows = slice(part * half, (part + 1) * half)
        dw = times(n1t_ref[rows], g)
        term[...] = dw.astype(BF)
        want = lax.broadcasted_iota(jnp.int32, shape, 1) * size.tall + size.rows - part * half
        here = lax.broadcasted_iota(jnp.int32, shape, 0) == want
        extra = times(jnp.where(here, 1.0, 0.0).astype(BF), packed.astype(BF))
        term[:, :128] = (dw[:, :128] + extra).astype(BF)


def call(kernel, name, out_shape, scratch, micros, args, vmem, any_in=(), any_out=(), scalar=True):
    shapes = [jax.ShapeDtypeStruct(s, t) for s, t in out_shape]
    here = pl.BlockSpec(memory_space=pl.ANY)
    specs = [here if i in any_in else VM for i in range(len(args))]
    if scalar:
        specs[0] = SM
    return pl.pallas_call(
        kernel,
        out_shape=shapes,
        in_specs=specs,
        out_specs=[here if i in any_out else VM for i in range(len(shapes))],
        scratch_shapes=[
            pltpu.SemaphoreType.DMA(s) if t is None else pltpu.VMEM(s, t) for s, t in scratch
        ],
        compiler_params=pltpu.CompilerParams(vmem_limit_bytes=vmem * 2**20),
        cost_estimate=cost_of(micros),
        name=name,
    )(*args)


def pad_to(values, rows, columns):
    return jnp.pad(values, ((0, rows - values.shape[0]), (0, columns - values.shape[1])))


def tail_pack(rows, piece):
    rows = pad_to(rows, TAIL, PIECES * piece)
    return rows.reshape(TAIL, PIECES, piece).transpose(1, 0, 2).reshape(MAIN, piece)


def tail_unpack(wire, used):
    piece = wire.shape[1]
    rows = wire.reshape(PIECES, TAIL, piece).transpose(1, 0, 2).reshape(TAIL, PIECES * piece)
    return rows[:, :used]


def tie(*values):
    return lax.optimization_barrier(values)


def local_blocks(size, blocks, pos, args):
    (
        tokens, q_weight, k_weight, v_weight, o_weight, gate_weight, up_weight, down_weight,
        vectors, cotangent,
    ) = args
    tok_rows, width = tokens.shape
    ff, rows = size.ff, size.rows
    kv_width = KV_HEADS * HEAD_DIM
    ctx_index = lax.axis_index("ctx")
    me = (lax.axis_index("dp") * lax.axis_size("ctx") + ctx_index).astype(jnp.int32).reshape(1)
    half = size.count // 2
    info, docs, cos, sin = pos

    joined_w = jnp.concatenate(
        [w.reshape(rows, -1) for w in (q_weight, k_weight, v_weight)], axis=1
    )
    vec_row = pad_to(vectors.reshape(1, -1), size.tall - rows, size.a_width)
    wire_a = jnp.concatenate([pad_to(joined_w, rows, size.a_width), vec_row], axis=0)
    za = blocks.along_z(wire_a)
    xa = jnp.stack([za, blocks.swap(za, blocks.x)])
    _, flat_w = tie(za, (gate_weight, up_weight, o_weight, down_weight))
    w_rows = [w.reshape(rows, -1) for w in flat_w[:3]]
    wire_1, wire_2, tokens, cotangent = call(
        functools.partial(wire_kernel, size),
        "wire",
        [
            ((MAIN, size.first), BF), ((MAIN, size.second), BF), ((tok_rows, width), BF),
            ((tok_rows, width), BF),
        ],
        [
            ((MAIN, size.piece), F32), ((MAIN, 128), F32), ((tok_rows, width), BF),
            ((tok_rows, width), BF), ((2,), None),
        ],
        1,
        w_rows + [flat_w[3].reshape(size.f_rows, width), tokens.T, cotangent.T],
        10,
        any_out=(2, 3),
        scalar=False,
    )
    xa, wire_1, wire_2 = tie(xa, wire_1, wire_2)
    ya = blocks.swap(xa, blocks.y)
    z1 = blocks.along_z(wire_1)
    z1, wire_2, ya = tie(z1, wire_2, ya)
    z2 = blocks.along_z(wire_2)
    x1 = jnp.stack([z1, blocks.swap(z1, blocks.x)])
    a_mine = jnp.stack([xa, ya]).reshape(half * size.tall, size.a_width)
    a_other = blocks.swap(a_mine, blocks.core)

    a_rows = size.count * size.tall
    q_rot, kv_mine, n1t, flat = call(
        functools.partial(pre_kernel, size),
        "norm_qkv",
        [
            ((tok_rows, width), BF), ((tok_rows, 2 * kv_width), BF), ((a_rows, tok_rows), BF),
            ((1, size.flat), F32),
        ],
        [((a_rows, size.a_width), BF), ((tok_rows, size.a_width), F32)],
        3,
        (me, tokens, a_mine, a_other, cos, sin),
        16,
    )
    kv_got = blocks.swap(kv_mine, blocks.x)
    own = attention_own(q_rot, kv_mine, info, docs)
    z2, x1 = tie(z2, x1, kv_mine)[:2]
    y2 = jnp.stack([z2, blocks.swap(z2, blocks.y)])
    b1_parts = [b.reshape(half // 2 * MAIN, -1) for b in (x1, blocks.swap(x1, blocks.y))]
    b2_parts = [b.reshape(half // 2 * MAIN, -1) for b in (y2, blocks.swap(y2, blocks.x))]
    attn, lse = attention_others(q_rot, kv_got, *own, info, docs)

    b1_parts[1:] = [b1_parts[1], blocks.swap(b1_parts[0], blocks.core)]
    b2_parts[1:] = [b2_parts[1], blocks.swap(b2_parts[0], blocks.core)]
    attn, b2_parts[1] = tie(attn, b2_parts[1])
    attn, b1_parts[1] = tie(attn, b1_parts[1])
    b2_parts.append(blocks.swap(b2_parts[1], blocks.core))
    b1_parts.append(blocks.swap(b1_parts[1], blocks.core))
    main = size.count * MAIN
    slots = main + size.count * TAIL
    layer_out, keep1, give1, keep2, give2, grad_mid, grad_attn, grad_gain, delta = call(
        functools.partial(mlp_kernel, size),
        "feed_forward",
        [
            ((width, tok_rows), BF),
            ((main // 2, size.back_first), BF), ((main // 2, size.back_first), BF),
            ((main // 2, size.back_second), BF), ((main // 2, size.back_second), BF),
            ((tok_rows, width), F32), ((tok_rows, width), BF), ((1, width), F32),
            ((width // HEAD_DIM, 1, tok_rows), F32),
        ],
        [
            ((slots, ff), BF), ((slots, ff), BF), ((slots, size.wide), BF), ((ff, size.wide), BF),
            ((tok_rows, width), F32), ((tok_rows, slots), BF), ((slots, tok_rows), BF),
            ((width, slots), BF), ((tok_rows, width), F32), ((tok_rows, slots), F32),
            ((ff, size.wide), BF), ((size.count * TAIL, 2 * ff), BF),
            ((size.count * TAIL, size.wide), BF), ((main, size.piece + 128), BF),
        ],
        21,
        (
            me, attn, tokens, cotangent, flat, *b1_parts, *b2_parts,
        ),
        28,
    )

    got1 = blocks.swap(give1, blocks.core)
    got2 = blocks.swap(give2, blocks.core)
    shape = (2, 2, blocks.zs, MAIN, -1)
    h1 = blocks.add(keep1, got1).reshape(shape)
    h2 = blocks.add(keep2, got2).reshape(shape)
    dq_others, give_kv = attention_grad(q_rot, kv_got, grad_attn, lse, delta, info, docs)
    got_kv = blocks.swap(give_kv, blocks.x)
    dq_others, h1, h2 = tie(dq_others, h1, h2)
    h1 = blocks.add(h1[0], blocks.swap(h1[1], blocks.y))
    h2 = blocks.add(h2[:, 0], blocks.swap(h2[:, 1], blocks.x))
    grad_q_rot, own_kv = attention_grad(
        q_rot, kv_mine, grad_attn, lse, delta, info, docs, dq_others
    )

    gx, keep_a, give_a = call(
        functools.partial(post_kernel, size),
        "norm_qkv_back",
        [
            ((width, tok_rows), F32), ((a_rows // 2, size.a_width), BF),
            ((a_rows // 2, size.a_width), BF),
        ],
        [
            ((tok_rows, width + kv_width), F32), ((tok_rows, size.a_width), BF),
            ((1, size.flat), F32),
        ],
        1.5,
        (
            me, grad_q_rot, own_kv, got_kv, cos, sin, n1t, a_mine,
            a_other, tokens, grad_mid, flat, grad_gain,
        ),
        24,
    )
    got_a = blocks.swap(give_a, blocks.core)
    got_a, h1, h2 = tie(got_a, h1, h2)
    held = blocks.add(keep_a, got_a)
    h1 = blocks.add(h1[0], blocks.swap(h1[1], blocks.x))
    h2 = blocks.add(h2[0], blocks.swap(h2[1], blocks.y))
    held, h2 = tie(held, h2)
    held = held.reshape(2, 2, blocks.zs, size.tall, size.a_width)
    held = blocks.add(held[0], blocks.swap(held[1], blocks.y))
    held, share2 = tie(held, blocks.sum_z(h2))
    held = blocks.add(held[0], blocks.swap(held[1], blocks.x))
    held, share1 = tie(held, blocks.sum_z(h1))
    share_a = blocks.sum_z(held)

    tails = tail_unpack(share1[:, size.tail : size.tail + size.piece], 2 * ff)
    tail_o = tail_unpack(share1[:, size.tail_o : size.tail_o + 128], width)
    share_out = jnp.concatenate([share1[:, size.out : size.out + width], tail_o], axis=0)
    share_gate = jnp.concatenate([share1[:, :ff], tails[:, :ff]], axis=0)
    share_up = jnp.concatenate([share2[:, :ff], tails[:, ff:]], axis=0)
    downs = [size.down_back_at(c) for c in range(size.downs)]
    share_down = jnp.concatenate(
        [(share1, share2)[which][:, at : at + width] for which, at in downs], axis=0
    )
    ends = (width, width + kv_width, size.qkv)
    return (
        layer_out.T, gx.T, share_a[:rows, : ends[0]].reshape(-1),
        share_a[:rows, ends[0] : ends[1]].reshape(-1),
        share_a[:rows, ends[1] : ends[2]].reshape(-1),
        share_out.reshape(-1), share_gate.reshape(-1), share_up.reshape(-1),
        share_down.reshape(-1), share_a[rows, : size.vec],
    )


def local(
    tokens, q_weight, k_weight, v_weight, o_weight, gate_weight, up_weight, down_weight,
    vectors, doc_lengths, cotangent,
):
    tok_rows, width = tokens.shape
    ctx_count = lax.axis_size("ctx")
    dp_count = lax.axis_size("dp")
    count = dp_count * ctx_count
    seq_tokens = tok_rows * ctx_count
    ctx_index = lax.axis_index("ctx")
    heads = width // HEAD_DIM
    kv_width = KV_HEADS * HEAD_DIM
    ff = gate_weight.shape[0] * count // width

    position_all = doc_layout(doc_lengths[0], seq_tokens)
    offset = ctx_index * tok_rows
    position_mine = lax.dynamic_slice_in_dim(position_all, offset, tok_rows)
    docs = doc_lengths.shape[1]
    others = (ctx_count - 1 - ctx_index) * tok_rows
    heads_of = jnp.stack([ctx_index, others, offset]).astype(jnp.int32)
    info = jnp.concatenate([heads_of, jnp.cumsum(doc_lengths[0])[:-1].astype(jnp.int32)])
    half = HEAD_DIM // 2
    freq = THETA ** (-jnp.arange(half, dtype=F32) * 2.0 / HEAD_DIM)
    position_f = position_mine.astype(F32)[:, None]

    whole_rows = width % count == 0 and ff % count == 0
    if whole_rows and ctx_count == 2 and dp_count % 4 == 0 and count & (count - 1) == 0:
        size = Sizes(width, ff, dp_count, ctx_count, vectors.shape[0], kv_width)
        if size.fits() and (width + kv_width) % 128 == 0:
            angle = position_f * jnp.tile(freq, 128 // half)[None, :]
            sign = np.where(np.arange(128) % HEAD_DIM < half, -1.0, 1.0).astype(np.float32)
            pos = (info, docs, jnp.cos(angle), jnp.sin(angle) * sign)
            args = (
                tokens, q_weight, k_weight, v_weight, o_weight, gate_weight, up_weight,
                down_weight, vectors, cotangent,
            )
            return local_blocks(size, Blocks(dp_count, ctx_count), pos, args)

    angle = position_f * freq[None, :]
    cosine = jnp.cos(angle)[:, None, :]
    sine = jnp.sin(angle)[:, None, :]
    inputs = tokens.astype(F32)
    inv_first = lax.rsqrt(jnp.mean(inputs * inputs, axis=-1, keepdims=True) + EPS)

    def whole(part):
        return lax.all_gather(part, AXES, axis=0, tiled=True)

    w_qkv = jnp.concatenate(
        [whole(w).reshape(width, -1) for w in (q_weight, k_weight, v_weight)], axis=1
    )
    w_out = whole(o_weight).reshape(width, width)
    w_gate = whole(gate_weight).reshape(width, ff)
    w_up = whole(up_weight).reshape(width, ff)
    w_down = whole(down_weight).reshape(ff, width)
    flat = whole(vectors).astype(F32)
    ends = [width, width + kv_width, width + 2 * kv_width, 2 * width + 2 * kv_width]
    gain_attn = flat[ends[2] : ends[3]]
    gain_mlp = flat[ends[3] : ends[3] + width]

    n_first = (inputs * inv_first * gain_attn).astype(BF)
    qkv = times(n_first, w_qkv) + flat[: ends[2]]
    q_rot = turn(qkv[:, :width].reshape(tok_rows, heads, HEAD_DIM), cosine, sine)
    q_rot = q_rot.astype(BF).reshape(tok_rows, width)
    k_rot = turn(qkv[:, width : ends[1]].reshape(tok_rows, KV_HEADS, HEAD_DIM), cosine, sine)
    k_rot = k_rot.astype(BF).reshape(tok_rows, kv_width)
    kv_mine = jnp.concatenate([k_rot, qkv[:, ends[1] :].astype(BF)], axis=1)
    kv = (lax.all_gather(kv_mine, "ctx", axis=0, tiled=True),)
    info = info.at[0].set(1)
    attn, lse = attention(q_rot, kv, info, docs, seq_tokens, False)
    mid = inputs + times(attn, w_out)
    inv_second = lax.rsqrt(jnp.mean(mid * mid, axis=-1, keepdims=True) + EPS)
    n_second = (mid * inv_second * gain_mlp).astype(BF)
    gate = times(n_second, w_gate)
    up_val = times(n_second, w_up)
    sig = jax.nn.sigmoid(gate)
    act = gate * sig
    hidden = (act * up_val).astype(BF)
    layer_out = (mid + times(hidden, w_down)).astype(BF)

    grad_wdown = inner_rows(hidden, cotangent)
    grad_hidden = times_back(cotangent, w_down)
    grad_gate = (grad_hidden * up_val * (sig * (1.0 + gate * (1.0 - sig)))).astype(BF)
    grad_up = (grad_hidden * act).astype(BF)
    grad_wgate = inner_rows(n_second, grad_gate)
    grad_wup = inner_rows(n_second, grad_up)
    grad_n2 = times_back(grad_gate, w_gate) + times_back(grad_up, w_up)
    grad_mid_norm, grad_gain_mlp = norm_back(mid, inv_second, gain_mlp, grad_n2)
    grad_mid = cotangent.astype(F32) + grad_mid_norm
    grad_branch = grad_mid.astype(BF)
    grad_wout = inner_rows(attn, grad_branch)
    grad_attn = times_back(grad_branch, w_out).astype(BF)
    grad_q_rot, grad_kv = attention_back(
        q_rot, kv, grad_attn, lse, info, docs, seq_tokens, False, 0, KV_HEADS
    )
    grad_kv_mine = lax.psum_scatter(
        grad_kv.astype(BF), "ctx", scatter_dimension=0, tiled=True
    ).astype(F32)
    grad_q = turn(grad_q_rot.reshape(tok_rows, heads, HEAD_DIM), cosine, -sine)
    grad_k = turn(
        grad_kv_mine[:, :kv_width].reshape(tok_rows, KV_HEADS, HEAD_DIM), cosine, -sine
    )
    grad_qkv = jnp.concatenate(
        [
            grad_q.reshape(tok_rows, width).astype(BF),
            grad_k.reshape(tok_rows, kv_width).astype(BF),
            grad_kv_mine[:, kv_width:].astype(BF),
        ],
        axis=1,
    )
    grad_wqkv = inner_rows(n_first, grad_qkv)
    grad_bias = jnp.sum(grad_qkv.astype(F32), axis=0)
    grad_n1 = times_back(grad_qkv, w_qkv)
    grad_x_norm, grad_gain_attn = norm_back(inputs, inv_first, gain_attn, grad_n1)
    input_grad = grad_mid + grad_x_norm
    used = 3 * width + 2 * kv_width
    padding = jnp.zeros((vectors.shape[0] * count - used,), F32)
    vector_term = jnp.concatenate([grad_bias, grad_gain_attn, grad_gain_mlp, padding])

    def shares(term):
        return lax.psum_scatter(term.reshape(-1), AXES, scatter_dimension=0, tiled=True)

    return (
        layer_out, input_grad, shares(grad_wqkv[:, :width]),
        shares(grad_wqkv[:, width : ends[1]]), shares(grad_wqkv[:, ends[1] :]),
        shares(grad_wout), shares(grad_wgate), shares(grad_wup), shares(grad_wdown),
        shares(vector_term),
    )


def solution(mesh):
    split = P(AXES)
    rows = P(AXES, None)
    in_specs = (rows,) + (split,) * 8 + (P("dp", None), rows)
    out_specs = (rows, rows) + (split,) * 8
    return jax.shard_map(local, mesh=mesh, in_specs=in_specs, out_specs=out_specs, check_vma=False)
```

```python
import functools

import jax
import jax.numpy as jnp
import numpy as np
from jax import lax
from jax.experimental import pallas as pl
from jax.experimental.pallas import tpu as pltpu
from jax.sharding import PartitionSpec as P

KV_HEADS = 3
HEAD_DIM = 64

EPS = 1e-06
THETA = 100000.0
NEG_FILL = -1e30
AXES = ("dp", "ctx")
BF = jnp.bfloat16
F32 = jnp.float32


def times(left, right):
    return jnp.dot(left, right, preferred_element_type=F32)


def inner_rows(left, right):
    return lax.dot_general(left, right, (((0,), (0,)), ((), ())), preferred_element_type=F32)


def times_back(left, right):
    return lax.dot_general(left, right, (((1,), (1,)), ((), ())), preferred_element_type=F32)


def norm_back(values, inv, gain, grad):
    scaled = grad * gain
    dot = jnp.mean(scaled * values, axis=-1, keepdims=True)
    grad_values = inv * scaled - values * (inv * inv * inv * dot)
    grad_gain = jnp.sum(grad * values * inv, axis=0)
    return grad_values, grad_gain


def turn(values, cosine, sine):
    half = values.shape[-1] // 2
    first = values[..., :half]
    second = values[..., half:]
    return jnp.concatenate(
        [first * cosine - second * sine, second * cosine + first * sine], axis=-1
    )


def doc_layout(lengths, count):
    ends = jnp.cumsum(lengths)
    place = jnp.arange(count, dtype=jnp.int32)
    segment = jnp.sum((place[:, None] >= ends[None, :-1]).astype(jnp.int32), axis=1)
    starts = ends - lengths
    picked = segment[:, None] == jnp.arange(lengths.shape[0], dtype=jnp.int32)[None, :]
    first = jnp.sum(jnp.where(picked, starts[None, :], 0), axis=1)
    return place - first


def fill_bias(bias, info, docs, short, own=None):
    total, rows = bias.shape
    row_q = lax.broadcasted_iota(jnp.int32, (1, rows), 1) + info[2]
    first = jnp.zeros_like(row_q)
    for j in range(docs - 1):
        first = jnp.where(row_q >= info[3 + j], info[3 + j], first)
    parts = ((0, total, 0),)
    if own is not None:
        parts = ((0, total, info[2] if own else info[1]),)
    elif short < total:
        parts = ((0, total - short, info[1]), (total - short, total, info[2]))
    for start, stop, base in parts:
        row_k = lax.broadcasted_iota(jnp.int32, (stop - start, rows), 0)
        allowed = (row_k >= first - base) & (row_k <= row_q - base)
        bias[start:stop] = jnp.where(allowed, 0.0, NEG_FILL)


def key_range(full, total, short, rows, block, at, causal):
    start = 0 if full else total - short
    stop = total - rows + (at + 1) * block if causal else total
    return start, stop


def key_parts(kv_refs):
    at = 0
    for kv_ref in kv_refs:
        yield slice(at, at + kv_ref.shape[0]), kv_ref
        at += kv_ref.shape[0]


def attn_fwd_kernel(
    heads, block, short, causal, docs, info, q_ref, *refs,
):
    kv_refs, (out_ref, lse_ref, qs, ks, vts, bias, out_t) = refs[:-7], refs[-7:]
    rows = q_ref.shape[0]
    total = bias.shape[0]
    kv_width = KV_HEADS * HEAD_DIM
    group = heads // KV_HEADS
    fill_bias(bias, info, docs, short)
    for h in range(heads):
        qs[h] = q_ref[:, h * HEAD_DIM : (h + 1) * HEAD_DIM] * BF(HEAD_DIM**-0.5)
    for at, kv_ref in key_parts(kv_refs):
        for g in range(KV_HEADS):
            ks[g, at] = kv_ref[:, g * HEAD_DIM : (g + 1) * HEAD_DIM]
        vts[:, at] = jnp.transpose(kv_ref[:, kv_width:].astype(F32)).astype(BF)

    def run(full):
        @pl.loop(0, KV_HEADS)
        def _(g):
            v_rows = pl.ds(pl.multiple_of(g * HEAD_DIM, HEAD_DIM), HEAD_DIM)
            for j in range(group):
                h = g * group + j
                out_rows = pl.ds(pl.multiple_of(h * HEAD_DIM, HEAD_DIM), HEAD_DIM)
                for at in range(rows // block):
                    start, stop = key_range(full, total, short, rows, block, at, causal)
                    cols = slice(at * block, (at + 1) * block)
                    s = times_back(ks[g, start:stop], qs[h, cols])
                    s = s + bias[start:stop, cols]
                    top = jnp.max(s, axis=0, keepdims=True)
                    p = jnp.exp(s - top)
                    total_p = jnp.sum(p, axis=0, keepdims=True)
                    o = times(vts[v_rows, start:stop], p.astype(BF))
                    out_t[out_rows, cols] = o / total_p
                    lse_ref[h, :, cols] = top + jnp.log(total_p)

    pl.when(info[0] != 0)(lambda: run(True))
    pl.when(info[0] == 0)(lambda: run(False))
    out_ref[...] = jnp.transpose(out_t[...]).astype(BF)


def attn_own_kernel(
    heads, block, docs, info, q_ref, kv_ref, acc, top_ref, sum_ref, qs, ks, vts, bias
):
    rows = q_ref.shape[0]
    kv_width = KV_HEADS * HEAD_DIM
    group = heads // KV_HEADS
    fill_bias(bias, info, docs, rows, own=True)
    for h in range(heads):
        qs[h] = q_ref[:, h * HEAD_DIM : (h + 1) * HEAD_DIM] * BF(HEAD_DIM**-0.5)
    for g in range(KV_HEADS):
        ks[g] = kv_ref[:, g * HEAD_DIM : (g + 1) * HEAD_DIM]
    vts[...] = jnp.transpose(kv_ref[:, kv_width:].astype(F32)).astype(BF)

    @pl.loop(0, heads)
    def _(h):
        g = h // group
        v_rows = pl.ds(pl.multiple_of(g * HEAD_DIM, HEAD_DIM), HEAD_DIM)
        out_rows = pl.ds(pl.multiple_of(h * HEAD_DIM, HEAD_DIM), HEAD_DIM)
        for at in range(rows // block):
            stop = (at + 1) * block
            cols = slice(at * block, stop)
            s = times_back(ks[g, :stop], qs[h, cols]) + bias[:stop, cols]
            top = jnp.max(s, axis=0, keepdims=True)
            p = jnp.exp(s - top)
            top_ref[h, :, cols] = top
            sum_ref[h, :, cols] = jnp.sum(p, axis=0, keepdims=True)
            acc[out_rows, cols] = times(vts[v_rows, :stop], p.astype(BF))


def attn_others_kernel(
    heads, block, docs, info, q_ref, kv_ref, acc, top_ref, sum_ref, out_ref, lse_ref,
    qs, ks, vts, bias, out_t,
):
    rows = q_ref.shape[0]
    kv_width = KV_HEADS * HEAD_DIM
    group = heads // KV_HEADS

    @pl.when(info[0] == 0)
    def _():
        for h in range(heads):
            at = slice(h * HEAD_DIM, (h + 1) * HEAD_DIM)
            out_t[at] = acc[at] / sum_ref[h]
            lse_ref[h] = top_ref[h] + jnp.log(sum_ref[h])

    @pl.when(info[0] != 0)
    def _():
        fill_bias(bias, info, docs, rows, own=False)
        for h in range(heads):
            qs[h] = q_ref[:, h * HEAD_DIM : (h + 1) * HEAD_DIM] * BF(HEAD_DIM**-0.5)
        for g in range(KV_HEADS):
            ks[g] = kv_ref[:, g * HEAD_DIM : (g + 1) * HEAD_DIM]
        vts[...] = jnp.transpose(kv_ref[:, kv_width:].astype(F32)).astype(BF)

        @pl.loop(0, heads)
        def _(h):
            g = h // group
            v_rows = pl.ds(pl.multiple_of(g * HEAD_DIM, HEAD_DIM), HEAD_DIM)
            out_rows = pl.ds(pl.multiple_of(h * HEAD_DIM, HEAD_DIM), HEAD_DIM)
            for at in range(rows // block):
                cols = slice(at * block, (at + 1) * block)
                s = times_back(ks[g], qs[h, cols]) + bias[:, cols]
                own = top_ref[h, :, cols]
                top = jnp.maximum(own, jnp.max(s, axis=0, keepdims=True))
                scale = jnp.exp(own - top)
                p = jnp.exp(s - top)
                total_p = sum_ref[h, :, cols] * scale + jnp.sum(p, axis=0, keepdims=True)
                o = acc[out_rows, cols] * scale + times(vts[v_rows], p.astype(BF))
                out_t[out_rows, cols] = o / total_p
                lse_ref[h, :, cols] = top + jnp.log(total_p)

    out_ref[...] = jnp.transpose(out_t[...]).astype(BF)


def attn_grad_kernel(
    heads, block, docs, own, info, q_ref, kv_ref, do_ref, lse_ref, delta_ref, *refs
):
    refs, (qs, dos, ks, vs, kts, bias, dk, dv) = refs[:-8], refs[-8:]
    if own:
        before, dq_ref, dkv_ref, dq_t = refs
    else:
        dq_t, dkv_ref = refs
    rows = q_ref.shape[0]
    kv_width = KV_HEADS * HEAD_DIM
    group = heads // KV_HEADS
    dk[...] = jnp.zeros_like(dk)
    dv[...] = jnp.zeros_like(dv)

    def run():
        fill_bias(bias, info, docs, rows, own=own)
        for h in range(heads):
            at = slice(h * HEAD_DIM, (h + 1) * HEAD_DIM)
            qs[h] = q_ref[:, at] * BF(HEAD_DIM**-0.5)
            dos[h] = do_ref[:, at]
        for g in range(KV_HEADS):
            lo = g * HEAD_DIM
            ks[g] = kv_ref[:, lo : lo + HEAD_DIM]
            vs[g] = kv_ref[:, kv_width + lo : kv_width + lo + HEAD_DIM]
        kts[...] = jnp.transpose(kv_ref[:, :kv_width].astype(F32)).astype(BF)

        @pl.loop(0, KV_HEADS)
        def _(g):
            k_rows = pl.ds(pl.multiple_of(g * HEAD_DIM, HEAD_DIM), HEAD_DIM)
            for j in range(group):
                h = g * group + j
                out_rows = pl.ds(pl.multiple_of(h * HEAD_DIM, HEAD_DIM), HEAD_DIM)
                for at in range(rows // block):
                    stop = (at + 1) * block if own else rows
                    cols = slice(at * block, (at + 1) * block)
                    q = qs[h, cols]
                    do = dos[h, cols]
                    s = times_back(ks[g, :stop], q) + bias[:stop, cols]
                    p = jnp.exp(s - lse_ref[h, :, cols])
                    dp = times_back(vs[g, :stop], do)
                    ds = (p * (dp - delta_ref[h, :, cols])).astype(BF)
                    dk[g, :stop] += times(ds, q)
                    dv[g, :stop] += times(p.astype(BF), do)
                    dq = times(kts[k_rows, :stop], ds) * HEAD_DIM**-0.5
                    dq_t[out_rows, cols] = before[out_rows, cols] + dq if own else dq

    if own:
        run()
        dq_ref[...] = jnp.transpose(dq_t[...])
    else:
        pl.when(info[0] != 0)(run)

        @pl.when(info[0] == 0)
        def _():
            dq_t[...] = jnp.zeros_like(dq_t)

    for g in range(KV_HEADS):
        lo = g * HEAD_DIM
        dkv_ref[:, lo : lo + HEAD_DIM] = dk[g].astype(dkv_ref.dtype)
        dkv_ref[:, kv_width + lo : kv_width + lo + HEAD_DIM] = dv[g].astype(dkv_ref.dtype)


def attn_bwd_kernel(
    heads, block, short, causal, docs, g0, g1, parts, info, q_ref, do_ref, lse_ref, *refs,
):
    kv_refs, outs, scratch = refs[:parts], refs[parts:-9], refs[-9:]
    qs, ks, vs, kts, dos, bias, dq_t, dk, dv = scratch
    rows = q_ref.shape[0]
    total = bias.shape[0]
    kv_width = KV_HEADS * HEAD_DIM
    group = heads // KV_HEADS
    keys = g1 - g0
    fill_bias(bias, info, docs, short)
    for h in range(keys * group):
        lanes = slice((g0 * group + h) * HEAD_DIM, (g0 * group + h + 1) * HEAD_DIM)
        qs[h] = q_ref[:, lanes] * BF(HEAD_DIM**-0.5)
        dos[h] = do_ref[:, lanes]
    for g in range(keys):
        lo = (g0 + g) * HEAD_DIM
        for at, kv_ref in key_parts(kv_refs):
            ks[g, at] = kv_ref[:, lo : lo + HEAD_DIM]
            vs[g, at] = kv_ref[:, kv_width + lo : kv_width + lo + HEAD_DIM]
        kts[g] = jnp.transpose(ks[g].astype(F32)).astype(BF)
    dk[...] = jnp.zeros_like(dk)
    dv[...] = jnp.zeros_like(dv)

    def run(full):
        @pl.loop(0, keys * group)
        def _(h):
            g = h // group if keys > 1 else 0
            out_rows = pl.ds(pl.multiple_of(h * HEAD_DIM, HEAD_DIM), HEAD_DIM)
            for at in range(rows // block):
                start, stop = key_range(full, total, short, rows, block, at, causal)
                cols = slice(at * block, (at + 1) * block)
                q = qs[h, cols]
                do = dos[h, cols]
                s = times_back(ks[g, start:stop], q)
                p = jnp.exp(s + bias[start:stop, cols] - lse_ref[g0 * group + h, :, cols])
                dp = times_back(vs[g, start:stop], do)
                t = p * dp
                inner = jnp.sum(t, axis=0, keepdims=True)
                ds = (t - p * inner).astype(BF)
                dk[g, start:stop] += times(ds, q)
                dv[g, start:stop] += times(p.astype(BF), do)
                dq_t[out_rows, cols] = times(kts[g, :, start:stop], ds) * HEAD_DIM**-0.5

    pl.when(info[0] != 0)(lambda: run(True))
    pl.when(info[0] == 0)(lambda: run(False))
    outs[0][...] = jnp.transpose(dq_t[...])
    cut = total - outs[1].shape[0]
    for part, out in ((slice(cut, total), outs[1]),) + tuple((slice(0, cut), o) for o in outs[2:]):
        for g in range(keys):
            lo = g * HEAD_DIM
            out[:, lo : lo + HEAD_DIM] = dk[g, part].astype(out.dtype)
            lo += keys * HEAD_DIM
            out[:, lo : lo + HEAD_DIM] = dv[g, part].astype(out.dtype)


VM = pl.BlockSpec(memory_space=pltpu.VMEM)
SM = pl.BlockSpec(memory_space=pltpu.SMEM)


def cost_of(micros):
    return pl.CostEstimate(
        flops=int(micros * 1.1e9), bytes_accessed=2**20, transcendentals=0
    )


def attention(q, kv, info, docs, short, causal):
    rows, width = q.shape
    total = sum(part.shape[0] for part in kv)
    heads = width // HEAD_DIM
    block = min(rows, 256)
    return pl.pallas_call(
        functools.partial(attn_fwd_kernel, heads, block, short, causal, docs),
        out_shape=(
            jax.ShapeDtypeStruct((rows, width), BF),
            jax.ShapeDtypeStruct((heads, 1, rows), F32),
        ),
        in_specs=[SM] + [VM] * (1 + len(kv)),
        out_specs=(VM, VM),
        scratch_shapes=[
            pltpu.VMEM((heads, rows, HEAD_DIM), BF),
            pltpu.VMEM((KV_HEADS, total, HEAD_DIM), BF),
            pltpu.VMEM((KV_HEADS * HEAD_DIM, total), BF),
            pltpu.VMEM((total, rows), F32),
            pltpu.VMEM((width, rows), F32),
        ],
        compiler_params=pltpu.CompilerParams(vmem_limit_bytes=20 * 2**20),
        cost_estimate=cost_of(14),
        name="attn_fwd",
    )(info, q, *kv)


def attention_own(q, kv, info, docs):
    rows, width = q.shape
    heads = width // HEAD_DIM
    stat = jax.ShapeDtypeStruct((heads, 1, rows), F32)
    return pl.pallas_call(
        functools.partial(attn_own_kernel, heads, min(rows, 256), docs),
        out_shape=(jax.ShapeDtypeStruct((width, rows), F32), stat, stat),
        in_specs=[SM, VM, VM],
        out_specs=(VM, VM, VM),
        scratch_shapes=attn_scratch(rows, heads),
        compiler_params=pltpu.CompilerParams(vmem_limit_bytes=16 * 2**20),
        cost_estimate=cost_of(6),
        name="attn_own",
    )(info, q, kv)


def attn_scratch(rows, heads):
    return [
        pltpu.VMEM((heads, rows, HEAD_DIM), BF),
        pltpu.VMEM((KV_HEADS, rows, HEAD_DIM), BF),
        pltpu.VMEM((KV_HEADS * HEAD_DIM, rows), BF),
        pltpu.VMEM((rows, rows), F32),
    ]


def attention_grad(q, kv, grad_out, lse, delta, info, docs, before=None):
    rows, width = q.shape
    heads = width // HEAD_DIM
    own = before is not None
    turned = jax.ShapeDtypeStruct((width, rows), F32)
    if own:
        outs = [jax.ShapeDtypeStruct((rows, width), F32), jax.ShapeDtypeStruct(kv.shape, F32)]
    else:
        outs = [turned, jax.ShapeDtypeStruct(kv.shape, BF)]
    by_head = pltpu.VMEM((heads, rows, HEAD_DIM), BF)
    by_key = pltpu.VMEM((KV_HEADS, rows, HEAD_DIM), BF)
    sums = pltpu.VMEM((KV_HEADS, rows, HEAD_DIM), F32)
    return pl.pallas_call(
        functools.partial(attn_grad_kernel, heads, min(rows, 256), docs, own),
        out_shape=outs,
        in_specs=[SM] + [VM] * (6 if own else 5),
        out_specs=[VM] * 2,
        scratch_shapes=([pltpu.VMEM((width, rows), F32)] if own else []) + [
            by_head, by_head, by_key, by_key, pltpu.VMEM((KV_HEADS * HEAD_DIM, rows), BF),
            pltpu.VMEM((rows, rows), F32), sums, sums,
        ],
        compiler_params=pltpu.CompilerParams(vmem_limit_bytes=20 * 2**20),
        cost_estimate=cost_of(2.5),
        name="attn_grad_own" if own else "attn_grad_others",
    )(info, q, kv, grad_out, lse, delta, *([before] if own else []))


def attention_others(q, kv, acc, top, total, info, docs):
    rows, width = q.shape
    heads = width // HEAD_DIM
    return pl.pallas_call(
        functools.partial(attn_others_kernel, heads, min(rows, 256), docs),
        out_shape=(
            jax.ShapeDtypeStruct((rows, width), BF),
            jax.ShapeDtypeStruct((heads, 1, rows), F32),
        ),
        in_specs=[SM] + [VM] * 5,
        out_specs=(VM, VM),
        scratch_shapes=attn_scratch(rows, heads) + [pltpu.VMEM((width, rows), F32)],
        compiler_params=pltpu.CompilerParams(vmem_limit_bytes=16 * 2**20),
        cost_estimate=cost_of(10),
        name="attn_others",
    )(info, q, kv, acc, top, total)


def attention_back(q, kv, grad_out, lse, info, docs, short, causal, g0, g1):
    rows, width = q.shape
    total = sum(part.shape[0] for part in kv)
    heads = width // HEAD_DIM
    block = min(rows, 256)
    keys = g1 - g0
    mine = heads // KV_HEADS * keys
    outs = [jax.ShapeDtypeStruct((rows, mine * HEAD_DIM), F32)]
    if causal:
        outs.append(jax.ShapeDtypeStruct((rows, 2 * keys * HEAD_DIM), F32))
        outs.append(jax.ShapeDtypeStruct((total - rows, 2 * keys * HEAD_DIM), BF))
    else:
        outs.append(jax.ShapeDtypeStruct((total, 2 * keys * HEAD_DIM), F32))
    return pl.pallas_call(
        functools.partial(attn_bwd_kernel, heads, block, short, causal, docs, g0, g1, len(kv)),
        out_shape=outs,
        in_specs=[SM] + [VM] * (3 + len(kv)),
        out_specs=[VM] * len(outs),
        scratch_shapes=[
            pltpu.VMEM((mine, rows, HEAD_DIM), BF),
            pltpu.VMEM((keys, total, HEAD_DIM), BF),
            pltpu.VMEM((keys, total, HEAD_DIM), BF),
            pltpu.VMEM((keys, HEAD_DIM, total), BF),
            pltpu.VMEM((mine, rows, HEAD_DIM), BF),
            pltpu.VMEM((total, rows), F32),
            pltpu.VMEM((mine * HEAD_DIM, rows), F32),
            pltpu.VMEM((keys, total, HEAD_DIM), F32),
            pltpu.VMEM((keys, total, HEAD_DIM), F32),
        ],
        compiler_params=pltpu.CompilerParams(vmem_limit_bytes=20 * 2**20),
        cost_estimate=cost_of(20),
        name="attn_bwd",
    )(info, q, grad_out, lse, *kv)


TAIL = 2
MAIN = 16
PIECES = MAIN // TAIL


class Blocks:
    def __init__(self, dp_count, ctx_count):
        self.count = dp_count * ctx_count
        self.x = 1
        self.core = ctx_count
        self.y = 2 * ctx_count
        self.z = 4 * ctx_count
        self.zs = dp_count // 4
        self.masks = []
        for p in range(self.count):
            z, x = p % self.zs, p // self.zs % 2
            y, core = p // (2 * self.zs) % 2, p // (4 * self.zs)
            self.masks.append(x * self.x + y * self.y + core * self.core + z * self.z)

    def swap(self, values, mask):
        perm = [(i, i ^ mask) for i in range(self.count)]
        return lax.ppermute(values, AXES, perm)

    def along_z(self, mine):
        return jnp.stack([mine] + [self.swap(mine, d * self.z) for d in range(1, self.zs)])

    def add(self, keep, got):
        return (keep.astype(F32) + got.astype(F32)).astype(BF)

    def sum_z(self, held):
        got = [self.swap(held[d], d * self.z).astype(F32) for d in range(1, self.zs)]
        return functools.reduce(jnp.add, got, held[0].astype(F32))


class Sizes:
    def __init__(self, width, ff, dp, ctx, vec, kv_width):
        count = dp * ctx
        self.zs, self.ctx = dp // 4, ctx
        self.width, self.ff, self.count, self.vec = width, ff, count, vec
        self.rows = width // count
        self.f_rows = ff // count
        up = lambda n: (n + 127) // 128 * 128
        self.wide = up(width)
        self.qkv = width + 2 * kv_width
        self.a_width = up(self.qkv)
        self.tall = (self.rows + 1 + 7) // 8 * 8
        self.downs = self.f_rows // MAIN
        self.piece = 2 * ff // PIECES
        self.gate = 0
        self.tail = ff
        self.tail_o = self.tail + self.piece
        self.out = self.tail_o + 128
        self.down0 = self.out + self.wide
        self.first = self.down0 + self.wide
        self.second = ff + (self.downs - 1) * self.wide
        self.back_first = self.down0 + (self.downs - 1) * self.wide
        self.back_second = ff + self.wide
        self.flat = self.a_width + 2 * self.wide

    def down_at(self, c):
        return (0, self.down0) if c == 0 else (1, self.ff + (c - 1) * self.wide)

    def down_back_at(self, c):
        return (0, self.down0 + c * self.wide) if c < self.downs - 1 else (1, self.ff)

    def fits(self):
        return (
            self.rows == MAIN + TAIL
            and self.f_rows % MAIN == 0
            and self.piece % 128 == 0
            and self.ff % 256 == 0
            and self.wide <= 128 * PIECES
            and self.vec <= 128
        )


def wire_kernel(
    size, g_ref, u_ref, o_ref, d_ref, xt_ref, cott_ref, out1, out2, x_any, cot_any,
    tail, tail_o, x_ref, cot_ref, sems,
):
    ff, width = size.ff, size.width
    x_ref[...] = jnp.transpose(xt_ref[...].astype(F32)).astype(BF)
    cot_ref[...] = jnp.transpose(cott_ref[...].astype(F32)).astype(BF)
    copies = fetch((x_ref, cot_ref), (x_any, cot_any), sems)
    out1[:, : ff] = g_ref[:MAIN]
    out2[:, : ff] = u_ref[:MAIN]
    out1[:, size.out : size.out + size.wide] = jnp.zeros((MAIN, size.wide), BF)
    out1[:, size.out : size.out + width] = o_ref[:MAIN]
    tail_o[...] = jnp.zeros_like(tail_o)
    odd = [ref[MAIN:].astype(F32) for ref in (g_ref, u_ref, o_ref)]
    for c in range(PIECES):
        src = odd[c * size.piece // ff]
        at = c * size.piece % ff
        tail[c * TAIL : (c + 1) * TAIL] = src[:, at : at + size.piece]
        used = min(128, width - c * 128)
        if used > 0:
            tail_o[c * TAIL : (c + 1) * TAIL, :used] = odd[2][:, c * 128 : c * 128 + used]
    out1[:, size.tail : size.tail + size.piece] = tail[...].astype(BF)
    out1[:, size.tail_o : size.tail_o + 128] = tail_o[...].astype(BF)
    for c in range(size.downs):
        which, at = size.down_at(c)
        out = (out1, out2)[which]
        out[:, at : at + size.wide] = jnp.zeros((MAIN, size.wide), BF)
        out[:, at : at + width] = d_ref[c * MAIN : (c + 1) * MAIN]
    for copy in copies:
        copy.wait()


def over(values, by):
    scale = 2**16 // by + 1
    whole = (values * scale) >> 16
    return whole, values - whole * by


def mask_of(size, p):
    z, rest = p % size.zs, p // size.zs
    x, y, core = rest % 2, rest // 2 % 2, rest // 4
    return x + core * size.ctx + y * (2 * size.ctx) + z * (4 * size.ctx)


def lanes(count):
    return lax.broadcasted_iota(jnp.int32, (1, count), 1)


def place_matrix(size, me, tall):
    if tall:
        p, inside = over(lanes(size.count * size.tall), size.tall)
        feature = jnp.where(inside < size.rows, size.rows * (me ^ mask_of(size, p)) + inside, -1)
    else:
        s = lanes(size.count * (MAIN + TAIL))
        tail = s - size.count * MAIN
        p = jnp.where(tail < 0, s // MAIN, tail // TAIL)
        inside = jnp.where(tail < 0, s % MAIN, MAIN + tail % TAIL)
        feature = size.rows * (me ^ mask_of(size, p)) + inside
    at = lax.broadcasted_iota(jnp.int32, (size.width, feature.shape[1]), 0)
    return jnp.where(at == feature, 1.0, 0.0).astype(BF)


def vector_places(size, me):
    at = lanes(size.flat)
    ends = (size.a_width, size.a_width + size.wide)
    part = jnp.where(at < ends[0], 0, jnp.where(at < ends[1], 1, 2))
    inside = at - jnp.where(part == 0, 0, jnp.where(part == 1, ends[0], ends[1]))
    start = jnp.where(part == 0, 0, jnp.where(part == 1, size.qkv, size.qkv + size.width))
    used = inside < jnp.where(part == 0, size.qkv, size.width)
    owner, lane = over(start + inside, size.vec)
    rows = lax.broadcasted_iota(jnp.int32, (128, size.flat), 0)
    spread = jnp.where((rows == lane) & used, 1.0, 0.0).astype(BF)
    p = lax.broadcasted_iota(jnp.int32, (size.count, 1), 0)
    return spread, (owner == (me ^ mask_of(size, p))) & used


def swap_halves(u):
    rolled_back = pltpu.roll(u, 128 - HEAD_DIM // 2, 1)
    rolled = pltpu.roll(u, HEAD_DIM // 2, 1)
    lane = lax.broadcasted_iota(jnp.int32, u.shape, 1)
    return jnp.where(lane % HEAD_DIM < HEAD_DIM // 2, rolled_back, rolled)


def fetch(sources, targets, sems):
    copies = [
        pltpu.make_async_copy(src, dst, sems.at[i])
        for i, (src, dst) in enumerate(zip(sources, targets))
    ]
    for copy in copies:
        copy.start()
    return copies


def pre_kernel(
    size, me_ref, x_ref, wm_ref, wo_ref, cos_ref, sin_ref,
    q_ref, kv_ref, n1t_ref, flat_ref, w, qkv,
):
    me = me_ref[0]
    half = wm_ref.shape[0]
    w[:half] = wm_ref[...]
    w[half:] = wo_ref[...]
    place = place_matrix(size, me, True)
    spread, mine = vector_places(size, me)
    shape = (size.count, 2 * half)
    row = lax.broadcasted_iota(jnp.int32, shape, 0) * size.tall + size.rows
    row = jnp.where(lax.broadcasted_iota(jnp.int32, shape, 1) == row, 1.0, 0.0).astype(BF)
    packed = times(row, w[:, :128]).astype(BF)
    flat = jnp.sum(jnp.where(mine, times(packed, spread), 0.0), axis=0, keepdims=True)
    flat_ref[...] = flat
    gain = flat[:, size.a_width : size.a_width + size.width]
    x = x_ref[...].astype(F32)
    inv = lax.rsqrt(jnp.mean(x * x, axis=-1, keepdims=True) + EPS)
    n1 = (x * inv * gain).astype(BF)
    n1a = times(n1, place)
    n1t_ref[...] = jnp.transpose(n1a).astype(BF)
    qkv[...] = times(n1a.astype(BF), w[...]) + flat[:, : size.a_width]
    kv_width = kv_ref.shape[1] // 2
    for t in range((size.width + kv_width) // 128):
        u = qkv[:, t * 128 : (t + 1) * 128]
        qkv[:, t * 128 : (t + 1) * 128] = u * cos_ref[...] + swap_halves(u) * sin_ref[...]
    q_ref[...] = qkv[:, : size.width].astype(BF)
    kv_ref[...] = qkv[:, size.width : size.qkv].astype(BF)


def tail_place(size, back):
    odd, count = size.count * TAIL, size.count * MAIN
    row = lax.broadcasted_iota(jnp.int32, (count, count), 1 if back else 0)
    at = lax.broadcasted_iota(jnp.int32, (count, count), 0 if back else 1)
    c, q = row // odd, row % odd
    want = (q // TAIL) * MAIN + c * TAIL + q % TAIL
    return jnp.where(at == want, 1.0, 0.0).astype(BF)


def mlp_kernel(
    size, me_ref, attn_ref, x_ref, cot_ref, flat_ref,
    b1_00, b1_01, b1_10, b1_11, b2_00, b2_01, b2_10, b2_11,
    out_ref, keep1, give1, keep2, give2, gmid_ref, gattn_ref, ggain_ref, delta_ref,
    wg, wu, wo, wd, mid, n2s, n2t, place, acc, gacc, dwd, tails, tail_o, packed,
):
    me = me_ref[0]
    width, ff = size.width, size.ff
    part = b1_00.shape[0]
    half, main = 2 * part, 4 * part
    rows_z = part // 2
    place[...] = place_matrix(size, me, False)
    first = (b1_00, b1_01, b1_10, b1_11)
    second = (b2_00, b2_01, b2_10, b2_11)
    room = size.piece + 128
    for i, b1 in enumerate(first):
        rows = slice(i * part, (i + 1) * part)
        wg[rows] = b1[:, :ff]
        wo[rows] = b1[:, size.out : size.out + size.wide]
        packed[rows] = b1[:, size.tail : size.tail + room]
    for i, b2 in enumerate(second):
        for y in range(2):
            at = (i // 2) * half + y * part + (i % 2) * rows_z
            wu[at : at + rows_z] = b2[y * rows_z : (y + 1) * rows_z, :ff]
    odd = size.count * TAIL
    got = times(tail_place(size, False), packed[...]).astype(BF)
    for c in range(PIECES):
        rows = slice(c * odd, (c + 1) * odd)
        target = wg if c * size.piece < ff else wu
        at = c * size.piece % ff
        target[main:, at : at + size.piece] = got[rows, : size.piece]
        if c * 128 < size.wide:
            wo[main:, c * 128 : (c + 1) * 128] = got[rows, size.piece :]
    zs = rows_z // MAIN
    for p in range(size.count):
        z, x, y, core = p % zs, p // zs % 2, p // (2 * zs) % 2, p // (4 * zs)
        owner = me ^ mask_of(size, p)
        for c in range(size.downs):
            which, at = size.down_at(c)
            src, row = (second[2 * core + x], y * zs + z) if which else (
                first[2 * core + y], x * zs + z
            )
            to = pl.multiple_of(owner * size.f_rows + c * MAIN, MAIN)
            wd[pl.ds(to, MAIN), :] = src[row * MAIN : (row + 1) * MAIN, at : at + size.wide]
    attn_s = times(attn_ref[...], place[...])
    m = x_ref[...].astype(F32) + times(attn_s.astype(BF), wo[:, :width])
    mid[...] = m
    inv = lax.rsqrt(jnp.mean(m * m, axis=-1, keepdims=True) + EPS)
    lo = size.a_width + size.wide
    gain = flat_ref[:, lo : lo + width]
    n2 = (m * inv * gain).astype(BF)
    spread = times(n2, place[...])
    n2s[...] = spread.astype(BF)
    n2t[...] = jnp.transpose(spread).astype(BF)
    acc[...] = jnp.zeros_like(acc)
    gacc[...] = jnp.zeros_like(gacc)
    step = 512 if ff % 512 == 0 else 256

    @pl.loop(0, ff // step)
    def _(b):
        at = pl.multiple_of(b * step, step)
        cols = pl.ds(at, step)
        gate = times(n2s[...], wg[:, cols])
        up = times(n2s[...], wu[:, cols])
        sig = 1.0 / (1.0 + jnp.exp(-gate))
        act = gate * sig
        h = act * up
        gh = times_back(cot_ref[...], wd[cols, :width])
        gg = (gh * up * (sig * (1.0 + gate * (1.0 - sig)))).astype(BF)
        gu = (gh * act).astype(BF)
        acc[...] += times(h.astype(BF), wd[cols, :width])
        dwd[cols, :width] = times(jnp.transpose(h).astype(BF), cot_ref[...]).astype(BF)
        gacc[...] += times_back(gg, wg[:, cols]) + times_back(gu, wu[:, cols])
        for k, (grad, keep, give) in enumerate(((gg, keep1, give1), (gu, keep2, give2))):
            dw = times(n2t[...], grad).astype(BF)
            keep[:, cols] = dw[:half]
            give[:, cols] = dw[half:main]
            tails[:, pl.ds(pl.multiple_of(k * ff + at, 128), step)] = dw[main:]

    m = mid[...]
    inv = lax.rsqrt(jnp.mean(m * m, axis=-1, keepdims=True) + EPS)
    out_ref[...] = jnp.transpose(m + acc[...]).astype(BF)
    gn2 = times_back(gacc[...].astype(BF), place[...])
    scaled = gn2 * gain
    dot = jnp.mean(scaled * m, axis=-1, keepdims=True)
    ggain_ref[...] = jnp.sum(gn2 * m * inv, axis=0, keepdims=True)
    gmid = cot_ref[...].astype(F32) + inv * scaled - m * (inv * inv * inv * dot)
    gmid_ref[...] = gmid
    branch = gmid.astype(BF)
    gattn = times_back(branch, wo[:, :width]).astype(BF)
    gattn = times_back(gattn, place[...]).astype(BF)
    gattn_ref[...] = gattn
    both = jnp.transpose(gattn.astype(F32) * attn_ref[...].astype(F32))
    for h in range(width // HEAD_DIM):
        at = slice(h * HEAD_DIM, (h + 1) * HEAD_DIM)
        delta_ref[h] = jnp.sum(both[at], axis=0, keepdims=True)
    dwo = times(jnp.transpose(attn_s).astype(BF), branch).astype(BF)
    tail_o[...] = jnp.zeros_like(tail_o)
    tail_o[:, :width] = dwo[main:]
    terms = ((keep1, keep2), (give1, give2))
    for i, (term, _) in enumerate(terms):
        term[:, size.out : size.out + width] = dwo[i * half : (i + 1) * half]
    packed[...] = jnp.zeros_like(packed)
    for c in range(PIECES):
        rows = slice(c * odd, (c + 1) * odd)
        packed[rows, : size.piece] = tails[:, c * size.piece : (c + 1) * size.piece]
        if c * 128 < size.wide:
            packed[rows, size.piece :] = tail_o[:, c * 128 : (c + 1) * 128]
    wire = times(tail_place(size, True), packed[...]).astype(BF)
    for i, (term, _) in enumerate(terms):
        rows = slice(i * half, (i + 1) * half)
        term[:, size.tail : size.tail + room] = wire[rows]
    for p in range(size.count):
        to = terms[p // (size.count // 2)]
        rows = slice(p * MAIN % half, p * MAIN % half + MAIN)
        owner = me ^ mask_of(size, p)
        for c in range(size.downs):
            which, at = size.down_back_at(c)
            src = pl.multiple_of(owner * size.f_rows + c * MAIN, MAIN)
            to[which][rows, at : at + size.wide] = dwd[pl.ds(src, MAIN), :]


def post_kernel(
    size, me_ref, dq_ref, dkv_ref, got_ref, cos_ref, sin_ref, n1t_ref,
    wm_ref, wo_ref, x_ref, gmid_ref, flat_ref, ggain_ref,
    gx_ref, keep_ref, give_ref, turn_buf, grad, vec_row,
):
    me = me_ref[0]
    width = size.width
    half = wm_ref.shape[0]
    place = place_matrix(size, me, True)
    kv_width = KV_HEADS * HEAD_DIM
    turned = width + kv_width
    dkv = dkv_ref[...] + got_ref[...].astype(F32)
    turn_buf[:, :width] = dq_ref[...]
    turn_buf[:, width:] = dkv[:, :kv_width]
    grad[...] = jnp.zeros_like(grad)
    grad[:, turned : turned + kv_width] = dkv[:, kv_width:].astype(BF)
    for t in range(turned // 128):
        u = turn_buf[:, t * 128 : (t + 1) * 128]
        back = u * cos_ref[...] - swap_halves(u) * sin_ref[...]
        grad[:, t * 128 : (t + 1) * 128] = back.astype(BF)
    g = grad[...]
    gn1 = jnp.zeros((g.shape[0], width), F32)
    for part, w_ref in enumerate((wm_ref, wo_ref)):
        values = times_back(g, w_ref[...]).astype(BF)
        gn1 += times_back(values, place[:, part * half : (part + 1) * half])
    x = x_ref[...].astype(F32)
    inv = lax.rsqrt(jnp.mean(x * x, axis=-1, keepdims=True) + EPS)
    gain = flat_ref[:, size.a_width : size.a_width + width]
    scaled = gn1 * gain
    dot = jnp.mean(scaled * x, axis=-1, keepdims=True)
    gx_ref[...] = jnp.transpose(gmid_ref[...] + inv * scaled - x * (inv * inv * inv * dot))
    vec_row[...] = jnp.zeros_like(vec_row)
    vec_row[:, : size.a_width] = jnp.sum(g.astype(F32), axis=0, keepdims=True)
    vec_row[:, size.a_width : size.a_width + width] = jnp.sum(gn1 * x * inv, axis=0, keepdims=True)
    lo = size.a_width + size.wide
    vec_row[:, lo : lo + width] = ggain_ref[...]
    spread, mine = vector_places(size, me)
    packed = times_back(jnp.where(mine, vec_row[...], 0.0).astype(BF), spread)
    shape = (half, size.count)
    for part, term in ((0, keep_ref), (1, give_ref)):
        rows = slice(part * half, (part + 1) * half)
        dw = times(n1t_ref[rows], g)
        term[...] = dw.astype(BF)
        want = lax.broadcasted_iota(jnp.int32, shape, 1) * size.tall + size.rows - part * half
        here = lax.broadcasted_iota(jnp.int32, shape, 0) == want
        extra = times(jnp.where(here, 1.0, 0.0).astype(BF), packed.astype(BF))
        term[:, :128] = (dw[:, :128] + extra).astype(BF)


def call(kernel, name, out_shape, scratch, micros, args, vmem, any_in=(), any_out=(), scalar=True):
    shapes = [jax.ShapeDtypeStruct(s, t) for s, t in out_shape]
    here = pl.BlockSpec(memory_space=pl.ANY)
    specs = [here if i in any_in else VM for i in range(len(args))]
    if scalar:
        specs[0] = SM
    return pl.pallas_call(
        kernel,
        out_shape=shapes,
        in_specs=specs,
        out_specs=[here if i in any_out else VM for i in range(len(shapes))],
        scratch_shapes=[
            pltpu.SemaphoreType.DMA(s) if t is None else pltpu.VMEM(s, t) for s, t in scratch
        ],
        compiler_params=pltpu.CompilerParams(vmem_limit_bytes=vmem * 2**20),
        cost_estimate=cost_of(micros),
        name=name,
    )(*args)


def pad_to(values, rows, columns):
    return jnp.pad(values, ((0, rows - values.shape[0]), (0, columns - values.shape[1])))


def tail_pack(rows, piece):
    rows = pad_to(rows, TAIL, PIECES * piece)
    return rows.reshape(TAIL, PIECES, piece).transpose(1, 0, 2).reshape(MAIN, piece)


def tail_unpack(wire, used):
    piece = wire.shape[1]
    rows = wire.reshape(PIECES, TAIL, piece).transpose(1, 0, 2).reshape(TAIL, PIECES * piece)
    return rows[:, :used]


def tie(*values):
    return lax.optimization_barrier(values)


def local_blocks(size, blocks, pos, args):
    (
        tokens, q_weight, k_weight, v_weight, o_weight, gate_weight, up_weight, down_weight,
        vectors, cotangent,
    ) = args
    tok_rows, width = tokens.shape
    ff, rows = size.ff, size.rows
    kv_width = KV_HEADS * HEAD_DIM
    ctx_index = lax.axis_index("ctx")
    me = (lax.axis_index("dp") * lax.axis_size("ctx") + ctx_index).astype(jnp.int32).reshape(1)
    half = size.count // 2
    info, docs, cos, sin = pos

    joined_w = jnp.concatenate(
        [w.reshape(rows, -1) for w in (q_weight, k_weight, v_weight)], axis=1
    )
    vec_row = pad_to(vectors.reshape(1, -1), size.tall - rows, size.a_width)
    wire_a = jnp.concatenate([pad_to(joined_w, rows, size.a_width), vec_row], axis=0)
    za = blocks.along_z(wire_a)
    xa = jnp.stack([za, blocks.swap(za, blocks.x)])
    _, flat_w = tie(za, (gate_weight, up_weight, o_weight, down_weight))
    w_rows = [w.reshape(rows, -1) for w in flat_w[:3]]
    wire_1, wire_2, tokens, cotangent = call(
        functools.partial(wire_kernel, size),
        "wire",
        [
            ((MAIN, size.first), BF), ((MAIN, size.second), BF), ((tok_rows, width), BF),
            ((tok_rows, width), BF),
        ],
        [
            ((MAIN, size.piece), F32), ((MAIN, 128), F32), ((tok_rows, width), BF),
            ((tok_rows, width), BF), ((2,), None),
        ],
        1,
        w_rows + [flat_w[3].reshape(size.f_rows, width), tokens.T, cotangent.T],
        10,
        any_out=(2, 3),
        scalar=False,
    )
    xa, wire_1, wire_2 = tie(xa, wire_1, wire_2)
    ya = blocks.swap(xa, blocks.y)
    z1 = blocks.along_z(wire_1)
    z1, wire_2, ya = tie(z1, wire_2, ya)
    z2 = blocks.along_z(wire_2)
    x1 = jnp.stack([z1, blocks.swap(z1, blocks.x)])
    a_mine = jnp.stack([xa, ya]).reshape(half * size.tall, size.a_width)
    a_other = blocks.swap(a_mine, blocks.core)

    a_rows = size.count * size.tall
    q_rot, kv_mine, n1t, flat = call(
        functools.partial(pre_kernel, size),
        "norm_qkv",
        [
            ((tok_rows, width), BF), ((tok_rows, 2 * kv_width), BF), ((a_rows, tok_rows), BF),
            ((1, size.flat), F32),
        ],
        [((a_rows, size.a_width), BF), ((tok_rows, size.a_width), F32)],
        3,
        (me, tokens, a_mine, a_other, cos, sin),
        16,
    )
    kv_got = blocks.swap(kv_mine, blocks.x)
    own = attention_own(q_rot, kv_mine, info, docs)
    z2, x1 = tie(z2, x1, kv_mine)[:2]
    y2 = jnp.stack([z2, blocks.swap(z2, blocks.y)])
    b1_parts = [b.reshape(half // 2 * MAIN, -1) for b in (x1, blocks.swap(x1, blocks.y))]
    b2_parts = [b.reshape(half // 2 * MAIN, -1) for b in (y2, blocks.swap(y2, blocks.x))]
    attn, lse = attention_others(q_rot, kv_got, *own, info, docs)

    b1_parts[1:] = [b1_parts[1], blocks.swap(b1_parts[0], blocks.core)]
    b2_parts[1:] = [b2_parts[1], blocks.swap(b2_parts[0], blocks.core)]
    attn, b2_parts[1] = tie(attn, b2_parts[1])
    attn, b1_parts[1] = tie(attn, b1_parts[1])
    b2_parts.append(blocks.swap(b2_parts[1], blocks.core))
    b1_parts.append(blocks.swap(b1_parts[1], blocks.core))
    main = size.count * MAIN
    slots = main + size.count * TAIL
    layer_out, keep1, give1, keep2, give2, grad_mid, grad_attn, grad_gain, delta = call(
        functools.partial(mlp_kernel, size),
        "feed_forward",
        [
            ((width, tok_rows), BF),
            ((main // 2, size.back_first), BF), ((main // 2, size.back_first), BF),
            ((main // 2, size.back_second), BF), ((main // 2, size.back_second), BF),
            ((tok_rows, width), F32), ((tok_rows, width), BF), ((1, width), F32),
            ((width // HEAD_DIM, 1, tok_rows), F32),
        ],
        [
            ((slots, ff), BF), ((slots, ff), BF), ((slots, size.wide), BF), ((ff, size.wide), BF),
            ((tok_rows, width), F32), ((tok_rows, slots), BF), ((slots, tok_rows), BF),
            ((width, slots), BF), ((tok_rows, width), F32), ((tok_rows, slots), F32),
            ((ff, size.wide), BF), ((size.count * TAIL, 2 * ff), BF),
            ((size.count * TAIL, size.wide), BF), ((main, size.piece + 128), BF),
        ],
        21,
        (
            me, attn, tokens, cotangent, flat, *b1_parts, *b2_parts,
        ),
        28,
    )

    got1 = blocks.swap(give1, blocks.core)
    got2 = blocks.swap(give2, blocks.core)
    shape = (2, 2, blocks.zs, MAIN, -1)
    h1 = blocks.add(keep1, got1).reshape(shape)
    h2 = blocks.add(keep2, got2).reshape(shape)
    dq_others, give_kv = attention_grad(q_rot, kv_got, grad_attn, lse, delta, info, docs)
    got_kv = blocks.swap(give_kv, blocks.x)
    dq_others, h1, h2 = tie(dq_others, h1, h2)
    h1 = blocks.add(h1[0], blocks.swap(h1[1], blocks.y))
    h2 = blocks.add(h2[:, 0], blocks.swap(h2[:, 1], blocks.x))
    grad_q_rot, own_kv = attention_grad(
        q_rot, kv_mine, grad_attn, lse, delta, info, docs, dq_others
    )

    gx, keep_a, give_a = call(
        functools.partial(post_kernel, size),
        "norm_qkv_back",
        [
            ((width, tok_rows), F32), ((a_rows // 2, size.a_width), BF),
            ((a_rows // 2, size.a_width), BF),
        ],
        [
            ((tok_rows, width + kv_width), F32), ((tok_rows, size.a_width), BF),
            ((1, size.flat), F32),
        ],
        1.5,
        (
            me, grad_q_rot, own_kv, got_kv, cos, sin, n1t, a_mine,
            a_other, tokens, grad_mid, flat, grad_gain,
        ),
        24,
    )
    got_a = blocks.swap(give_a, blocks.core)
    got_a, h1, h2 = tie(got_a, h1, h2)
    held = blocks.add(keep_a, got_a)
    h1 = blocks.add(h1[0], blocks.swap(h1[1], blocks.x))
    h2 = blocks.add(h2[0], blocks.swap(h2[1], blocks.y))
    held, h2 = tie(held, h2)
    held = held.reshape(2, 2, blocks.zs, size.tall, size.a_width)
    held = blocks.add(held[0], blocks.swap(held[1], blocks.y))
    held, share2 = tie(held, blocks.sum_z(h2))
    held = blocks.add(held[0], blocks.swap(held[1], blocks.x))
    held, share1 = tie(held, blocks.sum_z(h1))
    share_a = blocks.sum_z(held)

    tails = tail_unpack(share1[:, size.tail : size.tail + size.piece], 2 * ff)
    tail_o = tail_unpack(share1[:, size.tail_o : size.tail_o + 128], width)
    share_out = jnp.concatenate([share1[:, size.out : size.out + width], tail_o], axis=0)
    share_gate = jnp.concatenate([share1[:, :ff], tails[:, :ff]], axis=0)
    share_up = jnp.concatenate([share2[:, :ff], tails[:, ff:]], axis=0)
    downs = [size.down_back_at(c) for c in range(size.downs)]
    share_down = jnp.concatenate(
        [(share1, share2)[which][:, at : at + width] for which, at in downs], axis=0
    )
    ends = (width, width + kv_width, size.qkv)
    return (
        layer_out.T, gx.T, share_a[:rows, : ends[0]].reshape(-1),
        share_a[:rows, ends[0] : ends[1]].reshape(-1),
        share_a[:rows, ends[1] : ends[2]].reshape(-1),
        share_out.reshape(-1), share_gate.reshape(-1), share_up.reshape(-1),
        share_down.reshape(-1), share_a[rows, : size.vec],
    )


def local(
    tokens, q_weight, k_weight, v_weight, o_weight, gate_weight, up_weight, down_weight,
    vectors, doc_lengths, cotangent,
):
    tok_rows, width = tokens.shape
    ctx_count = lax.axis_size("ctx")
    dp_count = lax.axis_size("dp")
    count = dp_count * ctx_count
    seq_tokens = tok_rows * ctx_count
    ctx_index = lax.axis_index("ctx")
    heads = width // HEAD_DIM
    kv_width = KV_HEADS * HEAD_DIM
    ff = gate_weight.shape[0] * count // width

    position_all = doc_layout(doc_lengths[0], seq_tokens)
    offset = ctx_index * tok_rows
    position_mine = lax.dynamic_slice_in_dim(position_all, offset, tok_rows)
    docs = doc_lengths.shape[1]
    others = (ctx_count - 1 - ctx_index) * tok_rows
    heads_of = jnp.stack([ctx_index, others, offset]).astype(jnp.int32)
    info = jnp.concatenate([heads_of, jnp.cumsum(doc_lengths[0])[:-1].astype(jnp.int32)])
    half = HEAD_DIM // 2
    freq = THETA ** (-jnp.arange(half, dtype=F32) * 2.0 / HEAD_DIM)
    position_f = position_mine.astype(F32)[:, None]

    whole_rows = width % count == 0 and ff % count == 0
    if whole_rows and ctx_count == 2 and dp_count % 4 == 0 and count & (count - 1) == 0:
        size = Sizes(width, ff, dp_count, ctx_count, vectors.shape[0], kv_width)
        if size.fits() and (width + kv_width) % 128 == 0:
            angle = position_f * jnp.tile(freq, 128 // half)[None, :]
            sign = np.where(np.arange(128) % HEAD_DIM < half, -1.0, 1.0).astype(np.float32)
            pos = (info, docs, jnp.cos(angle), jnp.sin(angle) * sign)
            args = (
                tokens, q_weight, k_weight, v_weight, o_weight, gate_weight, up_weight,
                down_weight, vectors, cotangent,
            )
            return local_blocks(size, Blocks(dp_count, ctx_count), pos, args)

    angle = position_f * freq[None, :]
    cosine = jnp.cos(angle)[:, None, :]
    sine = jnp.sin(angle)[:, None, :]
    inputs = tokens.astype(F32)
    inv_first = lax.rsqrt(jnp.mean(inputs * inputs, axis=-1, keepdims=True) + EPS)

    def whole(part):
        return lax.all_gather(part, AXES, axis=0, tiled=True)

    w_qkv = jnp.concatenate(
        [whole(w).reshape(width, -1) for w in (q_weight, k_weight, v_weight)], axis=1
    )
    w_out = whole(o_weight).reshape(width, width)
    w_gate = whole(gate_weight).reshape(width, ff)
    w_up = whole(up_weight).reshape(width, ff)
    w_down = whole(down_weight).reshape(ff, width)
    flat = whole(vectors).astype(F32)
    ends = [width, width + kv_width, width + 2 * kv_width, 2 * width + 2 * kv_width]
    gain_attn = flat[ends[2] : ends[3]]
    gain_mlp = flat[ends[3] : ends[3] + width]

    n_first = (inputs * inv_first * gain_attn).astype(BF)
    qkv = times(n_first, w_qkv) + flat[: ends[2]]
    q_rot = turn(qkv[:, :width].reshape(tok_rows, heads, HEAD_DIM), cosine, sine)
    q_rot = q_rot.astype(BF).reshape(tok_rows, width)
    k_rot = turn(qkv[:, width : ends[1]].reshape(tok_rows, KV_HEADS, HEAD_DIM), cosine, sine)
    k_rot = k_rot.astype(BF).reshape(tok_rows, kv_width)
    kv_mine = jnp.concatenate([k_rot, qkv[:, ends[1] :].astype(BF)], axis=1)
    kv = (lax.all_gather(kv_mine, "ctx", axis=0, tiled=True),)
    info = info.at[0].set(1)
    attn, lse = attention(q_rot, kv, info, docs, seq_tokens, False)
    mid = inputs + times(attn, w_out)
    inv_second = lax.rsqrt(jnp.mean(mid * mid, axis=-1, keepdims=True) + EPS)
    n_second = (mid * inv_second * gain_mlp).astype(BF)
    gate = times(n_second, w_gate)
    up_val = times(n_second, w_up)
    sig = jax.nn.sigmoid(gate)
    act = gate * sig
    hidden = (act * up_val).astype(BF)
    layer_out = (mid + times(hidden, w_down)).astype(BF)

    grad_wdown = inner_rows(hidden, cotangent)
    grad_hidden = times_back(cotangent, w_down)
    grad_gate = (grad_hidden * up_val * (sig * (1.0 + gate * (1.0 - sig)))).astype(BF)
    grad_up = (grad_hidden * act).astype(BF)
    grad_wgate = inner_rows(n_second, grad_gate)
    grad_wup = inner_rows(n_second, grad_up)
    grad_n2 = times_back(grad_gate, w_gate) + times_back(grad_up, w_up)
    grad_mid_norm, grad_gain_mlp = norm_back(mid, inv_second, gain_mlp, grad_n2)
    grad_mid = cotangent.astype(F32) + grad_mid_norm
    grad_branch = grad_mid.astype(BF)
    grad_wout = inner_rows(attn, grad_branch)
    grad_attn = times_back(grad_branch, w_out).astype(BF)
    grad_q_rot, grad_kv = attention_back(
        q_rot, kv, grad_attn, lse, info, docs, seq_tokens, False, 0, KV_HEADS
    )
    grad_kv_mine = lax.psum_scatter(
        grad_kv.astype(BF), "ctx", scatter_dimension=0, tiled=True
    ).astype(F32)
    grad_q = turn(grad_q_rot.reshape(tok_rows, heads, HEAD_DIM), cosine, -sine)
    grad_k = turn(
        grad_kv_mine[:, :kv_width].reshape(tok_rows, KV_HEADS, HEAD_DIM), cosine, -sine
    )
    grad_qkv = jnp.concatenate(
        [
            grad_q.reshape(tok_rows, width).astype(BF),
            grad_k.reshape(tok_rows, kv_width).astype(BF),
            grad_kv_mine[:, kv_width:].astype(BF),
        ],
        axis=1,
    )
    grad_wqkv = inner_rows(n_first, grad_qkv)
    grad_bias = jnp.sum(grad_qkv.astype(F32), axis=0)
    grad_n1 = times_back(grad_qkv, w_qkv)
    grad_x_norm, grad_gain_attn = norm_back(inputs, inv_first, gain_attn, grad_n1)
    input_grad = grad_mid + grad_x_norm
    used = 3 * width + 2 * kv_width
    padding = jnp.zeros((vectors.shape[0] * count - used,), F32)
    vector_term = jnp.concatenate([grad_bias, grad_gain_attn, grad_gain_mlp, padding])

    def shares(term):
        return lax.psum_scatter(term.reshape(-1), AXES, scatter_dimension=0, tiled=True)

    return (
        layer_out, input_grad, shares(grad_wqkv[:, :width]),
        shares(grad_wqkv[:, width : ends[1]]), shares(grad_wqkv[:, ends[1] :]),
        shares(grad_wout), shares(grad_wgate), shares(grad_wup), shares(grad_wdown),
        shares(vector_term),
    )


def solution(mesh):
    split = P(AXES)
    rows = P(AXES, None)
    in_specs = (rows,) + (split,) * 8 + (P("dp", None), rows)
    out_specs = (rows, rows) + (split,) * 8
    return jax.shard_map(local, mesh=mesh, in_specs=in_specs, out_specs=out_specs, check_vma=False)
```
